32 devices in a mesh: tile: 16 (over z, x, core), head: 2 (over y).
Axes of the slice: x: 2, y: 2, z: 4, core: 2. Of those that a mesh axis runs over, the one named last changes fastest.
Arguments:
- attn_proj: bfloat16 [16, 3, 192, 3, 3072], P('tile', None, 'head')
- mlp_proj: bfloat16 [16, 3, 192, 6144], P('tile', None, 'head'), may hold values from -6 to 6
- stream: bfloat16 [16, 3, 192, 3072], P('tile', None, 'head'), may hold values from -6 to 6
- text_len: int32 [16], P('tile'), may hold values from 1 to 192, as said below
- q_gain: float32 [128], replicated
- k_gain: float32 [128], replicated
- w_out_attn: bfloat16 [3072, 3072], P('head', 'tile'), may hold values from -0.0625 to 0.0625
- w_out_mlp: bfloat16 [6144, 3072], P('head', 'tile'), may hold values from -0.0625 to 0.0625
- bias_out: float32 [3072], replicated, may hold values from -3 to 3
- gate_mod: float32 [16, 3072], P('tile'), may hold values from -4 to 4
- final_shift: float32 [16, 3072], P('tile'), may hold values from -3 to 3
- final_scale: float32 [16, 3072], P('tile'), may hold values from -3 to 3
- w_final: bfloat16 [3072, 64], replicated, may hold values from -0.109375 to 0.109375
- b_final: float32 [64], replicated, may hold values from -3 to 3
- latent: float32 [16, 2, 192, 64], P('tile', None, 'head'), may hold values from -6 to 6
- step_size: float32 [16], P('tile'), may hold values from -0.4 to -0.1
Outputs:
- hidden_out: bfloat16 [16, 3, 192, 3072], P('tile', None, 'head')
- latent_next: float32 [16, 2, 192, 64], P('tile', None, 'head')
The draws below stay inside these ranges and needn't reach their ends.
Inputs may be any that keep to these rules, and one draw needn't show every extreme that they name: `text_len`: live text slots of each request; some request has all 192 text slots live in every draw.
All inputs are finite; a program needn't handle non-finite values.
Results may differ from the reference program's by a relative error of at most 0.0098.
Values may be sent and summed in bfloat16 or wider, within the bound.
No kernel may reach another device: no remote copies, remote signals or barrier semaphores. Data moves between devices by JAX's collectives and lax.ppermute only.
A program may use at most 128 MiB of HBM per device.

```python
import math
import jax
import jax.numpy as jnp
from jax import lax

D = 3072
HEADS = 24
HEAD_DIM = 128
CHANNELS = 64
FFW = 6144
SLOTS = 192
GRID_W = 32
REQUESTS = 16


def draw_attn_proj(key, part):
    shape = (REQUESTS, 3, SLOTS, 3, D)
    first_key = jax.random.fold_in(key, 11)
    base = jax.random.normal(first_key, shape, jnp.float32)
    return base.astype(jnp.bfloat16)


def draw_gain_common(key, salt):
    gain_key = jax.random.fold_in(key, salt)
    values = jax.random.uniform(gain_key, (HEAD_DIM,), jnp.float32, 0.6, 1.8)
    return values


def draw_q_gain(key, part):
    return draw_gain_common(key, 21)


def draw_k_gain(key, part):
    return draw_gain_common(key, 22)


def draw_text_len(key, part):
    length_key = jax.random.fold_in(key, 31)
    which_key = jax.random.fold_in(key, 32)
    lengths = jax.random.randint(length_key, (REQUESTS,), 1, SLOTS + 1)
    which = jax.random.randint(which_key, (), 0, REQUESTS)
    return jnp.where(jnp.arange(REQUESTS) == which, SLOTS, lengths).astype(jnp.int32)


def level_of(rng, extent, shards, smallest, high):
    factor_of = 1.0
    for position, blocks in shards:
        heights = jax.random.uniform(jax.random.fold_in(jax.random.fold_in(rng, 6), position), (blocks,), jnp.float32, smallest / len(shards), high / len(shards))
        factor_of = factor_of * jnp.repeat(jnp.exp(heights), extent[position] // blocks).reshape((-1,) + (1,) * (len(extent) - 1 - position))
    return factor_of


def centred(own_key, dims, width, limit, cuts=(), kind=jnp.bfloat16):
    level = level_of(own_key, dims, cuts, -0.22, 0.18) if cuts else 1.0
    values = jax.random.normal(own_key, dims, jnp.float32) * width * level
    return jnp.minimum(jnp.maximum(values, -limit), limit).astype(kind)


def setup_inputs(seed: int = 0) -> dict:
    seeds = jax.random.split(jax.random.key(seed), 17)
    return {
        "attn_proj": draw_attn_proj(jax.random.fold_in(seeds[16], 71), 0),
        "mlp_proj": centred(seeds[1], (REQUESTS, 3, SLOTS, FFW), 1.0, 6.0, ((0, 16), (2, 2))),
        "stream": centred(seeds[2], (REQUESTS, 3, SLOTS, D), 1.0, 6.0, ((0, 16), (2, 2))),
        "text_len": draw_text_len(jax.random.fold_in(seeds[16], 71), 0),
        "q_gain": draw_q_gain(jax.random.fold_in(seeds[16], 71), 0),
        "k_gain": draw_k_gain(jax.random.fold_in(seeds[16], 71), 0),
        "w_out_attn": centred(seeds[6], (D, D), (D + FFW) ** -0.5, 0.0625, ((0, 2), (1, 16))),
        "w_out_mlp": centred(seeds[7], (FFW, D), (D + FFW) ** -0.5, 0.0625, ((0, 2), (1, 16))),
        "bias_out": centred(seeds[8], (D,), 0.5, 3.0, (), jnp.float32),
        "gate_mod": centred(seeds[9], (REQUESTS, D), 1.0, 4.0, ((0, 16),), jnp.float32),
        "final_shift": centred(seeds[10], (REQUESTS, D), 0.5, 3.0, ((0, 16),), jnp.float32),
        "final_scale": centred(seeds[11], (REQUESTS, D), 0.5, 3.0, ((0, 16),), jnp.float32),
        "w_final": centred(seeds[12], (D, CHANNELS), D ** -0.5, 0.109375),
        "b_final": centred(seeds[13], (CHANNELS,), 0.5, 3.0, (), jnp.float32),
        "latent": centred(seeds[14], (REQUESTS, 2, SLOTS, CHANNELS), 1.0, 6.0, ((0, 16), (2, 2)), jnp.float32),
        "step_size": jnp.clip(-0.4 + 0.3 * jax.random.uniform(seeds[15], (REQUESTS,), jnp.float32) ** level_of(seeds[15], (REQUESTS,), ((0, 16),), -0.2, 0.2), -0.4, -0.1),
    }


def rope_tables(positions):
    pairs_zero = HEAD_DIM // 16
    pairs_axis = (HEAD_DIM // 2 - pairs_zero) // 2
    freqs = 10000.0 ** (-jnp.arange(pairs_axis, dtype=jnp.float32) / pairs_axis)
    count = positions.shape[0]
    angles = [jnp.zeros((count, HEAD_DIM // 2), jnp.float32)]
    for block in range(1, 3):
        image_index = (block - 1) * SLOTS + positions
        rows = (image_index // GRID_W).astype(jnp.float32)
        columns = (image_index % GRID_W).astype(jnp.float32)
        angles.append(jnp.concatenate([jnp.zeros((count, pairs_zero), jnp.float32), rows[:, None] * freqs[None, :], columns[:, None] * freqs[None, :]], axis=1))
    stacked = jnp.stack(angles)
    return (jnp.cos(stacked), jnp.sin(stacked))

def prepare(raw, gain, cosine, sine):
    normed = raw * lax.rsqrt(lax.optimization_barrier(jnp.mean(raw * raw, axis=-1, keepdims=True)) + 1e-06) * gain
    halves = normed.reshape(normed.shape[:-1] + (HEAD_DIM // 2, 2))
    first = halves[..., 0]
    second = halves[..., 1]
    cosine = cosine[None, :, :, None, :]
    sine = sine[None, :, :, None, :]
    rotated = jnp.stack([first * cosine - second * sine, first * sine + second * cosine], axis=-1)
    return rotated.reshape(raw.shape).astype(jnp.bfloat16)

def attend_request(inputs):
    queries, keys, values, live = inputs
    scores = jnp.einsum('qhd,khd->hqk', queries.astype(jnp.float32), keys.astype(jnp.float32)) / math.sqrt(HEAD_DIM)
    scores = jnp.where(live[None, None, :], scores, -jnp.inf)
    top = lax.optimization_barrier(jnp.max(scores, axis=-1, keepdims=True))
    weights = jnp.exp(scores - top)
    total = lax.optimization_barrier(jnp.sum(weights, axis=-1))
    mixed = jnp.einsum('hqk,khd->qhd', weights.astype(jnp.bfloat16).astype(jnp.float32), values.astype(jnp.float32))
    return (mixed / jnp.transpose(total)[:, :, None]).astype(jnp.bfloat16)

def reference(attn_proj, mlp_proj, stream, text_len, q_gain, k_gain, w_out_attn, w_out_mlp, bias_out, gate_mod, final_shift, final_scale, w_final, b_final, latent, step_size):
    positions = jnp.arange(SLOTS, dtype=jnp.int32)
    cosine, sine = rope_tables(positions)
    head_shape = (REQUESTS, 3, SLOTS, HEADS, HEAD_DIM)
    queries = prepare(attn_proj[:, :, :, 0].astype(jnp.float32).reshape(head_shape), q_gain, cosine, sine)
    keys = prepare(attn_proj[:, :, :, 1].astype(jnp.float32).reshape(head_shape), k_gain, cosine, sine)
    values = attn_proj[:, :, :, 2].reshape(head_shape)
    text_live = positions[None, :] < text_len[:, None]
    image_live = jnp.ones_like(text_live)
    live = jnp.stack([text_live, image_live, image_live], axis=1).reshape(REQUESTS, 3 * SLOTS)
    flat_shape = (REQUESTS, 3 * SLOTS, HEADS, HEAD_DIM)
    attn_out = lax.map(attend_request, (queries.reshape(flat_shape), keys.reshape(flat_shape), values.reshape(flat_shape), live))
    attn_out = attn_out.reshape(REQUESTS * 3 * SLOTS, D)
    mlp_act = jax.nn.gelu(mlp_proj.astype(jnp.float32), approximate=True).astype(jnp.bfloat16)
    proj = jnp.dot(attn_out, w_out_attn, preferred_element_type=jnp.float32) + jnp.dot(mlp_act.reshape(REQUESTS * 3 * SLOTS, FFW), w_out_mlp, preferred_element_type=jnp.float32)
    proj = proj.reshape(REQUESTS, 3, SLOTS, D)
    updated = stream.astype(jnp.float32) + gate_mod[:, None, None, :] * (proj + bias_out)
    hidden_out = updated.astype(jnp.bfloat16)
    image = updated[:, 1:]
    center = image - lax.optimization_barrier(jnp.mean(image, axis=-1, keepdims=True))
    variance = lax.optimization_barrier(jnp.mean(center * center, axis=-1, keepdims=True))
    normed = center * lax.rsqrt(variance + 1e-06)
    modulated = ((1.0 + final_scale[:, None, None, :]) * normed + final_shift[:, None, None, :]).astype(jnp.bfloat16)
    velocity = jnp.dot(modulated.reshape(REQUESTS * 2 * SLOTS, D), w_final, preferred_element_type=jnp.float32).reshape(REQUESTS, 2, SLOTS, CHANNELS) + b_final
    latent_next = latent + step_size[:, None, None, None] * velocity
    return (hidden_out, latent_next)
```

```python
import functools
import math

import jax
import jax.numpy as jnp
from jax import lax
from jax.experimental import pallas as pl
from jax.experimental.pallas import tpu as pltpu
from jax.sharding import PartitionSpec as P

HEAD_DIM = 128
SLOTS = 192
GRID_W = 32


def rope_tables(positions):
    pairs_zero = HEAD_DIM // 16
    pairs_axis = (HEAD_DIM // 2 - pairs_zero) // 2
    freqs = 10000.0 ** (-jnp.arange(pairs_axis, dtype=jnp.float32) / pairs_axis)
    count = positions.shape[0]
    angles = [jnp.zeros((count, HEAD_DIM // 2), jnp.float32)]
    for block in range(1, 3):
        image_index = (block - 1) * SLOTS + positions
        rows = (image_index // GRID_W).astype(jnp.float32)
        columns = (image_index % GRID_W).astype(jnp.float32)
        angles.append(
            jnp.concatenate(
                [
                    jnp.zeros((count, pairs_zero), jnp.float32),
                    rows[:, None] * freqs[None, :],
                    columns[:, None] * freqs[None, :],
                ],
                axis=1,
            )
        )
    stacked = jnp.stack(angles)
    return (jnp.cos(stacked), jnp.sin(stacked))


def prepare(raw, gain, cosine, sine):
    normed = raw * lax.rsqrt(jnp.mean(raw * raw, axis=-1, keepdims=True) + 1e-06) * gain
    halves = normed.reshape(normed.shape[:-1] + (HEAD_DIM // 2, 2))
    first = halves[..., 0]
    second = halves[..., 1]
    cosine = cosine[None, :, :, None, :]
    sine = sine[None, :, :, None, :]
    rotated = jnp.stack([first * cosine - second * sine, first * sine + second * cosine], axis=-1)
    return rotated.reshape(raw.shape).astype(jnp.bfloat16)


def attend_head(inputs):
    queries, keys, values, live = inputs
    scores = jnp.einsum("qd,kd->qk", queries, keys, preferred_element_type=jnp.float32) / math.sqrt(
        HEAD_DIM
    )
    scores = jnp.where(live[None, :], scores, -jnp.inf)
    top = jnp.max(scores, axis=-1, keepdims=True)
    weights = jnp.exp(scores - top)
    total = jnp.sum(weights, axis=-1, keepdims=True)
    mixed = jnp.dot(weights.astype(jnp.bfloat16), values, preferred_element_type=jnp.float32)
    return (mixed / total).astype(jnp.bfloat16)


def attend_request(inputs):
    queries, keys, values, live = inputs
    count = queries.shape[1]
    broad_live = jnp.broadcast_to(live[None, :], (count, live.shape[0]))
    result = lax.map(
        attend_head,
        (
            jnp.moveaxis(queries, 1, 0),
            jnp.moveaxis(keys, 1, 0),
            jnp.moveaxis(values, 1, 0),
            broad_live,
        ),
    )
    return jnp.moveaxis(result, 0, 1)


def general(
    attn_proj,
    mlp_proj,
    stream,
    text_len,
    q_gain,
    k_gain,
    w_out_attn,
    w_out_mlp,
    bias_out,
    gate_mod,
    final_shift,
    final_scale,
    w_final,
    b_final,
    latent,
    step_size,
):
    requests = attn_proj.shape[0]
    own_slots = attn_proj.shape[2]
    width = attn_proj.shape[4]
    heads = width // HEAD_DIM
    start_slot = lax.axis_index("head") * own_slots
    positions = start_slot + jnp.arange(own_slots, dtype=jnp.int32)
    cosine, sine = rope_tables(positions)
    head_shape = (requests, 3, own_slots, heads, HEAD_DIM)
    queries = prepare(
        attn_proj[:, :, :, 0].astype(jnp.float32).reshape(head_shape), q_gain, cosine, sine
    )
    keys = prepare(
        attn_proj[:, :, :, 1].astype(jnp.float32).reshape(head_shape), k_gain, cosine, sine
    )
    packed = jnp.stack(
        [
            queries.reshape(requests, 3, own_slots, width),
            keys.reshape(requests, 3, own_slots, width),
            attn_proj[:, :, :, 2],
        ],
        axis=3,
    )
    units = mlp_proj[:, :, :, None, :]
    moved, hidden_units = (
        lax.all_to_all(packed, "head", split_axis=4, concat_axis=2, tiled=True),
        lax.all_to_all(units, "head", split_axis=4, concat_axis=2, tiled=True),
    )
    hidden_units = hidden_units[:, :, :, 0]
    tile_slots = moved.shape[2]
    local_width = moved.shape[4]
    local_heads = local_width // HEAD_DIM
    flat_shape = (requests, 3 * tile_slots, local_heads, HEAD_DIM)
    all_positions = jnp.arange(tile_slots, dtype=jnp.int32)
    text_live = all_positions[None, :] < text_len[:, None]
    image_live = jnp.ones_like(text_live)
    live = jnp.stack([text_live, image_live, image_live], axis=1).reshape(requests, 3 * tile_slots)
    attn_out = lax.map(
        attend_request,
        (
            moved[:, :, :, 0].reshape(flat_shape),
            moved[:, :, :, 1].reshape(flat_shape),
            moved[:, :, :, 2].reshape(flat_shape),
            live,
        ),
    )
    attn_out = attn_out.reshape(requests, 3, tile_slots, local_width)
    mlp_act = jax.nn.gelu(hidden_units.astype(jnp.float32), approximate=True).astype(jnp.bfloat16)
    term = jnp.einsum(
        "rbsk,kd->rbsd",
        attn_out,
        lax.all_gather(w_out_attn, "tile", axis=1, tiled=True),
        preferred_element_type=jnp.float32,
    )
    term = term + jnp.einsum(
        "rbsk,kd->rbsd",
        mlp_act,
        lax.all_gather(w_out_mlp, "tile", axis=1, tiled=True),
        preferred_element_type=jnp.float32,
    )
    proj = lax.psum_scatter(term, "head", scatter_dimension=2, tiled=True)
    updated = stream.astype(jnp.float32) + gate_mod[:, None, None, :] * (proj + bias_out)
    hidden_out = updated.astype(jnp.bfloat16)
    image = updated[:, 1:]
    center = image - jnp.mean(image, axis=-1, keepdims=True)
    variance = jnp.mean(center * center, axis=-1, keepdims=True)
    normed = center * lax.rsqrt(variance + 1e-06)
    modulated = (
        (1.0 + final_scale[:, None, None, :]) * normed + final_shift[:, None, None, :]
    ).astype(jnp.bfloat16)
    velocity = (
        jnp.einsum("rbsd,dc->rbsc", modulated, w_final, preferred_element_type=jnp.float32)
        + b_final
    )
    latent_next = latent + step_size[:, None, None, None] * velocity
    return (hidden_out, latent_next)


EPS = 1e-06
SCALE = math.log2(math.e) / math.sqrt(HEAD_DIM)
VMEM = 60 * 1024 * 1024
NT = (((1,), (1,)), ((), ()))


def fits(axis):
    return axis == 2


def rotary(positions, gain):
    cosine, sine = rope_tables(positions)
    rows = cosine.shape[0] * cosine.shape[1]
    cosine = jnp.repeat(cosine.reshape(rows, HEAD_DIM // 2), 2, axis=1)
    sine = jnp.repeat(sine.reshape(rows, HEAD_DIM // 2), 2, axis=1)
    odd = jnp.arange(HEAD_DIM) % 2 == 1
    partner = jnp.where(odd, jnp.roll(gain, 1), -jnp.roll(gain, -1))
    return cosine * gain, sine * partner


def attend_kernel(half_ref, own_ref, far_ref, cq_ref, sq_ref, ck_ref, sk_ref, swap_ref, mask_ref, out_ref):
    rows = own_ref.shape[0] * own_ref.shape[2]

    def load(part):
        return jnp.concatenate(
            [own_ref[:, part].reshape(rows, HEAD_DIM), far_ref[:, part].reshape(rows, HEAD_DIM)], axis=0
        )

    def turn(raw, straight, crossed):
        wide = raw.astype(jnp.float32)
        scale = lax.rsqrt(jnp.mean(wide * wide, axis=-1, keepdims=True) + EPS)
        partner = jnp.dot(raw, swap_ref[...], preferred_element_type=jnp.float32)
        return ((wide * straight + partner * crossed) * scale).astype(jnp.bfloat16)

    queries = turn(load(0), cq_ref[...], sq_ref[...])
    keys = turn(load(1), ck_ref[...], sk_ref[...])
    scores = lax.dot_general(queries, keys, NT, preferred_element_type=jnp.float32)
    scores = scores * SCALE + mask_ref[...]
    weights = jnp.exp2(scores - jnp.max(scores, axis=-1, keepdims=True))
    total = jnp.sum(weights, axis=-1, keepdims=True)
    mixed = jnp.dot(weights.astype(jnp.bfloat16), load(2), preferred_element_type=jnp.float32)
    out_ref[...] = (mixed / total).astype(jnp.bfloat16)


def attend(half, own, far, tables, mask):
    blocks, parts, slots, width = far.shape
    heads = width // HEAD_DIM
    rows = 2 * blocks * slots
    order = jnp.arange(HEAD_DIM)
    swap = (order[:, None] == (order ^ 1)[None, :]).astype(jnp.bfloat16)
    shape = (blocks, parts, slots, HEAD_DIM)
    whole = pl.BlockSpec((rows, HEAD_DIM), lambda g, half: (0, 0))
    return pl.pallas_call(
        attend_kernel,
        grid_spec=pltpu.PrefetchScalarGridSpec(
            num_scalar_prefetch=1,
            grid=(heads,),
            in_specs=[
                pl.BlockSpec(shape, lambda g, half: (0, 0, 0, half[0] * heads + g)),
                pl.BlockSpec(shape, lambda g, half: (0, 0, 0, g)),
                whole,
                whole,
                whole,
                whole,
                pl.BlockSpec((HEAD_DIM, HEAD_DIM), lambda g, half: (0, 0)),
                pl.BlockSpec((1, rows), lambda g, half: (0, 0)),
            ],
            out_specs=pl.BlockSpec((rows, HEAD_DIM), lambda g, half: (0, g)),
        ),
        out_shape=jax.ShapeDtypeStruct((rows, width), jnp.bfloat16),
        compiler_params=pltpu.CompilerParams(vmem_limit_bytes=VMEM),
        cost_estimate=pl.CostEstimate(
            flops=heads * rows * rows * HEAD_DIM * 4 * 4,
            bytes_accessed=rows * width * 8,
            transcendentals=heads * rows * rows,
        ),
        name="attend",
    )(half, own, far, *tables, swap, mask)


def gelu_kernel(half_ref, own_ref, far_ref, out_ref):
    @pl.when(pl.program_id(0) == 0)
    def _():
        out_ref[...] = jax.nn.gelu(own_ref[0].astype(jnp.float32), approximate=True).astype(jnp.bfloat16)

    @pl.when(pl.program_id(0) == 1)
    def _():
        out_ref[...] = jax.nn.gelu(far_ref[0].astype(jnp.float32), approximate=True).astype(jnp.bfloat16)


def activate(half, own, far):
    blocks, slots, width = far.shape
    return pl.pallas_call(
        gelu_kernel,
        grid_spec=pltpu.PrefetchScalarGridSpec(
            num_scalar_prefetch=1,
            grid=(2, blocks),
            in_specs=[
                pl.BlockSpec((1, slots, width), lambda s, b, half: (jnp.where(s == 0, b, blocks - 1), 0, half[0])),
                pl.BlockSpec((1, slots, width), lambda s, b, half: (jnp.where(s == 0, 0, b), 0, 0)),
            ],
            out_specs=pl.BlockSpec((slots, width), lambda s, b, half: (s * blocks + b, 0)),
        ),
        out_shape=jax.ShapeDtypeStruct((2 * blocks * slots, width), jnp.bfloat16),
        compiler_params=pltpu.CompilerParams(vmem_limit_bytes=VMEM),
        cost_estimate=pl.CostEstimate(
            flops=2 * blocks * slots * width * 20,
            bytes_accessed=2 * blocks * slots * width * 4,
            transcendentals=2 * blocks * slots * width,
        ),
        name="activate",
    )(half, own, far)


def project_kernel(attn_ref, act_ref, w_ref, own_ref, far_ref):
    depth = attn_ref.shape[1]
    rows = own_ref.shape[0]
    total = lax.dot_general(attn_ref[...], w_ref[:, :depth], NT, preferred_element_type=jnp.float32)
    total = total + lax.dot_general(act_ref[...], w_ref[:, depth:], NT, preferred_element_type=jnp.float32)
    own_ref[...] = total[:rows]
    far_ref[...] = total[rows:].astype(jnp.bfloat16)


def project(attn, act, weights, tile=256):
    rows = attn.shape[0]
    columns, depth = weights.shape
    return pl.pallas_call(
        project_kernel,
        grid=(columns // tile,),
        in_specs=[
            pl.BlockSpec(attn.shape, lambda n: (0, 0)),
            pl.BlockSpec(act.shape, lambda n: (0, 0)),
            pl.BlockSpec((tile, depth), lambda n: (n, 0)),
        ],
        out_specs=[
            pl.BlockSpec((rows // 2, tile), lambda n: (0, n)),
            pl.BlockSpec((rows // 2, tile), lambda n: (0, n)),
        ],
        out_shape=[
            jax.ShapeDtypeStruct((rows // 2, columns), jnp.float32),
            jax.ShapeDtypeStruct((rows // 2, columns), jnp.bfloat16),
        ],
        compiler_params=pltpu.CompilerParams(vmem_limit_bytes=VMEM),
        cost_estimate=pl.CostEstimate(
            flops=2 * rows * columns * depth, bytes_accessed=2 * columns * depth + 2 * rows * depth, transcendentals=0
        ),
        name="project",
    )(attn, act, weights)


def finish_kernel(
    own_a_ref, far_a_ref, own_b_ref, far_b_ref, stream_ref, bias_ref, gate_ref, scale_ref, shift_ref, w_ref,
    b_ref, latent_ref, step_ref, hidden_ref, next_ref, proj_ref,
):
    slots, width = proj_ref.shape
    lower = lax.broadcasted_iota(jnp.int32, (slots, 128), 1) < 64
    for pair in range(width // 384):
        first = pl.ds(256 * pair, 128)
        second = pl.ds(256 * pair + 128, 128)
        rest = pl.ds(128 * pair, 128)
        even = own_a_ref[:, first] + far_a_ref[:, first].astype(jnp.float32)
        odd = own_a_ref[:, second] + far_a_ref[:, second].astype(jnp.float32)
        tail = own_b_ref[:, rest] + far_b_ref[:, rest].astype(jnp.float32)
        odd = pltpu.roll(odd, 64, 1)
        proj_ref[:, pl.ds(384 * pair, 128)] = even
        proj_ref[:, pl.ds(384 * pair + 128, 128)] = jnp.where(lower, tail, odd)
        proj_ref[:, pl.ds(384 * pair + 256, 128)] = jnp.where(lower, odd, tail)
    updated = stream_ref[0].astype(jnp.float32) + gate_ref[...] * (proj_ref[...] + bias_ref[...])
    hidden_ref[0] = updated.astype(jnp.bfloat16)

    @pl.when(pl.program_id(0) > 0)
    def _():
        center = updated - jnp.mean(updated, axis=-1, keepdims=True)
        variance = jnp.mean(center * center, axis=-1, keepdims=True)
        normed = center * lax.rsqrt(variance + EPS)
        modulated = ((1.0 + scale_ref[...]) * normed + shift_ref[...]).astype(jnp.bfloat16)
        velocity = lax.dot_general(w_ref[...], modulated, NT, preferred_element_type=jnp.float32)
        next_ref[0] = latent_ref[0] + step_ref[0] * (velocity + b_ref[...])


def finish(own_a, far_a, own_b, far_b, stream, bias, gate, scale, shift, w_final, b_final, latent, step):
    blocks, slots, width = stream.shape
    channels = w_final.shape[0]

    def rows(array):
        return pl.BlockSpec((slots, array.shape[1]), lambda b: (b, 0))

    def whole(array):
        return pl.BlockSpec(array.shape, lambda b: (0, 0))

    image = pl.BlockSpec((1, channels, slots), lambda b: (jnp.maximum(b - 1, 0), 0, 0))
    return pl.pallas_call(
        finish_kernel,
        grid=(blocks,),
        in_specs=[
            rows(own_a),
            rows(far_a),
            rows(own_b),
            rows(far_b),
            pl.BlockSpec((1, slots, width), lambda b: (b, 0, 0)),
            whole(bias),
            whole(gate),
            whole(scale),
            whole(shift),
            whole(w_final),
            whole(b_final),
            image,
            pl.BlockSpec(memory_space=pltpu.SMEM),
        ],
        out_specs=[pl.BlockSpec((1, slots, width), lambda b: (b, 0, 0)), image],
        out_shape=[
            jax.ShapeDtypeStruct(stream.shape, jnp.bfloat16),
            jax.ShapeDtypeStruct(latent.shape, jnp.float32),
        ],
        scratch_shapes=[pltpu.VMEM((slots, width), jnp.float32)],
        compiler_params=pltpu.CompilerParams(vmem_limit_bytes=VMEM),
        cost_estimate=pl.CostEstimate(
            flops=blocks * slots * width * 160, bytes_accessed=blocks * slots * width * 10, transcendentals=0
        ),
        name="finish",
    )(own_a, far_a, own_b, far_b, stream, bias, gate, scale, shift, w_final, b_final, latent, step)


def paired(
    partners,
    attn_proj,
    mlp_proj,
    stream,
    text_len,
    q_gain,
    k_gain,
    w_out_attn,
    w_out_mlp,
    bias_out,
    gate_mod,
    final_shift,
    final_scale,
    w_final,
    b_final,
    latent,
    step_size,
):
    me = lax.axis_index("head")
    half = me[None].astype(jnp.int32)
    trade = functools.partial(lax.ppermute, axis_name="head", perm=[(0, 1), (1, 0)])

    columns = jnp.concatenate([w_out_attn.T, w_out_mlp.T], axis=1)
    weights_a = lax.all_gather(columns[:128], "tile", axis=0, tiled=True)
    weights_b = lax.all_gather(columns[128:], "tile", axis=0, tiled=True)

    own_attn = jnp.transpose(attn_proj[0], (0, 2, 1, 3))
    own_units = mlp_proj[0]
    slots = own_attn.shape[2]
    width = own_attn.shape[3] // partners
    units = own_units.shape[2] // partners
    far_attn = trade(lax.dynamic_slice_in_dim(own_attn, (1 - me) * width, width, axis=3))
    far_units = trade(lax.dynamic_slice_in_dim(own_units, (1 - me) * units, units, axis=2))

    positions = jnp.arange(slots, dtype=jnp.int32)
    near, away = me * slots + positions, (1 - me) * slots + positions

    def both(gain):
        return [jnp.concatenate(pair, axis=0) for pair in zip(rotary(near, gain), rotary(away, gain))]

    text = jnp.concatenate([near, jnp.full(2 * slots, -1), away, jnp.full(2 * slots, -1)])
    mask = jnp.where(text < text_len[0], 0.0, -jnp.inf)[None, :].astype(jnp.float32)
    attn = attend(half, own_attn, far_attn, both(q_gain) + both(k_gain), mask)
    act = activate(half, own_units, far_units)

    own_a, sent_a = project(attn, act, weights_a)
    far_a = trade(sent_a)
    own_b, sent_b = project(attn, act, weights_b)
    far_b = trade(sent_b)
    hidden, following = finish(
        own_a,
        far_a,
        own_b,
        far_b,
        stream[0],
        bias_out[None, :],
        gate_mod,
        final_scale,
        final_shift,
        w_final.T,
        b_final[:, None],
        jnp.transpose(latent[0], (0, 2, 1)),
        step_size,
    )
    return hidden[None], jnp.transpose(following, (0, 2, 1))[None]


def solution(mesh):
    placed = (
        P("tile", None, "head", None, None),
        P("tile", None, "head", None),
        P("tile", None, "head", None),
        P("tile"),
        P(),
        P(),
        P("head", "tile"),
        P("head", "tile"),
        P(),
        P("tile", None),
        P("tile", None),
        P("tile", None),
        P(),
        P(),
        P("tile", None, "head", None),
        P("tile"),
    )
    return jax.shard_map(
        functools.partial(paired, mesh.shape["head"]) if fits(mesh.shape["head"]) else general,
        mesh=mesh,
        in_specs=placed,
        out_specs=(P("tile", None, "head", None), P("tile", None, "head", None)),
        check_vma=False,
    )
```

```python
import functools
import math

import jax
import jax.numpy as jnp
from jax import lax
from jax.experimental import pallas as pl
from jax.experimental.pallas import tpu as pltpu
from jax.sharding import PartitionSpec as P

HEAD_DIM = 128
SLOTS = 192
GRID_W = 32


def rope_tables(positions):
    pairs_zero = HEAD_DIM // 16
    pairs_axis = (HEAD_DIM // 2 - pairs_zero) // 2
    freqs = 10000.0 ** (-jnp.arange(pairs_axis, dtype=jnp.float32) / pairs_axis)
    count = positions.shape[0]
    angles = [jnp.zeros((count, HEAD_DIM // 2), jnp.float32)]
    for block in range(1, 3):
        image_index = (block - 1) * SLOTS + positions
        rows = (image_index // GRID_W).astype(jnp.float32)
        columns = (image_index % GRID_W).astype(jnp.float32)
        angles.append(
            jnp.concatenate(
                [
                    jnp.zeros((count, pairs_zero), jnp.float32),
                    rows[:, None] * freqs[None, :],
                    columns[:, None] * freqs[None, :],
                ],
                axis=1,
            )
        )
    stacked = jnp.stack(angles)
    return (jnp.cos(stacked), jnp.sin(stacked))


def prepare(raw, gain, cosine, sine):
    normed = raw * lax.rsqrt(jnp.mean(raw * raw, axis=-1, keepdims=True) + 1e-06) * gain
    halves = normed.reshape(normed.shape[:-1] + (HEAD_DIM // 2, 2))
    first = halves[..., 0]
    second = halves[..., 1]
    cosine = cosine[None, :, :, None, :]
    sine = sine[None, :, :, None, :]
    rotated = jnp.stack([first * cosine - second * sine, first * sine + second * cosine], axis=-1)
    return rotated.reshape(raw.shape).astype(jnp.bfloat16)


def attend_head(inputs):
    queries, keys, values, live = inputs
    scores = jnp.einsum("qd,kd->qk", queries, keys, preferred_element_type=jnp.float32) / math.sqrt(
        HEAD_DIM
    )
    scores = jnp.where(live[None, :], scores, -jnp.inf)
    top = jnp.max(scores, axis=-1, keepdims=True)
    weights = jnp.exp(scores - top)
    total = jnp.sum(weights, axis=-1, keepdims=True)
    mixed = jnp.dot(weights.astype(jnp.bfloat16), values, preferred_element_type=jnp.float32)
    return (mixed / total).astype(jnp.bfloat16)


def attend_request(inputs):
    queries, keys, values, live = inputs
    count = queries.shape[1]
    broad_live = jnp.broadcast_to(live[None, :], (count, live.shape[0]))
    result = lax.map(
        attend_head,
        (
            jnp.moveaxis(queries, 1, 0),
            jnp.moveaxis(keys, 1, 0),
            jnp.moveaxis(values, 1, 0),
            broad_live,
        ),
    )
    return jnp.moveaxis(result, 0, 1)


def general(
    attn_proj,
    mlp_proj,
    stream,
    text_len,
    q_gain,
    k_gain,
    w_out_attn,
    w_out_mlp,
    bias_out,
    gate_mod,
    final_shift,
    final_scale,
    w_final,
    b_final,
    latent,
    step_size,
):
    requests = attn_proj.shape[0]
    own_slots = attn_proj.shape[2]
    width = attn_proj.shape[4]
    heads = width // HEAD_DIM
    start_slot = lax.axis_index("head") * own_slots
    positions = start_slot + jnp.arange(own_slots, dtype=jnp.int32)
    cosine, sine = rope_tables(positions)
    head_shape = (requests, 3, own_slots, heads, HEAD_DIM)
    queries = prepare(
        attn_proj[:, :, :, 0].astype(jnp.float32).reshape(head_shape), q_gain, cosine, sine
    )
    keys = prepare(
        attn_proj[:, :, :, 1].astype(jnp.float32).reshape(head_shape), k_gain, cosine, sine
    )
    packed = jnp.stack(
        [
            queries.reshape(requests, 3, own_slots, width),
            keys.reshape(requests, 3, own_slots, width),
            attn_proj[:, :, :, 2],
        ],
        axis=3,
    )
    units = mlp_proj[:, :, :, None, :]
    moved, hidden_units = (
        lax.all_to_all(packed, "head", split_axis=4, concat_axis=2, tiled=True),
        lax.all_to_all(units, "head", split_axis=4, concat_axis=2, tiled=True),
    )
    hidden_units = hidden_units[:, :, :, 0]
    tile_slots = moved.shape[2]
    local_width = moved.shape[4]
    local_heads = local_width // HEAD_DIM
    flat_shape = (requests, 3 * tile_slots, local_heads, HEAD_DIM)
    all_positions = jnp.arange(tile_slots, dtype=jnp.int32)
    text_live = all_positions[None, :] < text_len[:, None]
    image_live = jnp.ones_like(text_live)
    live = jnp.stack([text_live, image_live, image_live], axis=1).reshape(requests, 3 * tile_slots)
    attn_out = lax.map(
        attend_request,
        (
            moved[:, :, :, 0].reshape(flat_shape),
            moved[:, :, :, 1].reshape(flat_shape),
            moved[:, :, :, 2].reshape(flat_shape),
            live,
        ),
    )
    attn_out = attn_out.reshape(requests, 3, tile_slots, local_width)
    mlp_act = jax.nn.gelu(hidden_units.astype(jnp.float32), approximate=True).astype(jnp.bfloat16)
    term = jnp.einsum(
        "rbsk,kd->rbsd",
        attn_out,
        lax.all_gather(w_out_attn, "tile", axis=1, tiled=True),
        preferred_element_type=jnp.float32,
    )
    term = term + jnp.einsum(
        "rbsk,kd->rbsd",
        mlp_act,
        lax.all_gather(w_out_mlp, "tile", axis=1, tiled=True),
        preferred_element_type=jnp.float32,
    )
    proj = lax.psum_scatter(term, "head", scatter_dimension=2, tiled=True)
    updated = stream.astype(jnp.float32) + gate_mod[:, None, None, :] * (proj + bias_out)
    hidden_out = updated.astype(jnp.bfloat16)
    image = updated[:, 1:]
    center = image - jnp.mean(image, axis=-1, keepdims=True)
    variance = jnp.mean(center * center, axis=-1, keepdims=True)
    normed = center * lax.rsqrt(variance + 1e-06)
    modulated = (
        (1.0 + final_scale[:, None, None, :]) * normed + final_shift[:, None, None, :]
    ).astype(jnp.bfloat16)
    velocity = (
        jnp.einsum("rbsd,dc->rbsc", modulated, w_final, preferred_element_type=jnp.float32)
        + b_final
    )
    latent_next = latent + step_size[:, None, None, None] * velocity
    return (hidden_out, latent_next)


EPS = 1e-06
SCALE = math.log2(math.e) / math.sqrt(HEAD_DIM)
VMEM = 60 * 1024 * 1024
NT = (((1,), (1,)), ((), ()))


def fits(sizes):
    return sizes["head"] == 2 and sizes["tile"] == 2 * len(PATH)


def rotary(positions, gain):
    cosine, sine = rope_tables(positions)
    rows = cosine.shape[0] * cosine.shape[1]
    cosine = jnp.repeat(cosine.reshape(rows, HEAD_DIM // 2), 2, axis=1)
    sine = jnp.repeat(sine.reshape(rows, HEAD_DIM // 2), 2, axis=1)
    odd = jnp.arange(HEAD_DIM) % 2 == 1
    partner = jnp.where(odd, jnp.roll(gain, 1), -jnp.roll(gain, -1))
    return cosine * gain, sine * partner


def attend_kernel(half_ref, own_ref, far_ref, cq_ref, sq_ref, ck_ref, sk_ref, swap_ref, mask_ref, out_ref):
    rows = own_ref.shape[0] * own_ref.shape[2]

    def load(part):
        return jnp.concatenate(
            [own_ref[:, part].reshape(rows, HEAD_DIM), far_ref[:, part].reshape(rows, HEAD_DIM)], axis=0
        )

    def turn(raw, straight, crossed):
        wide = raw.astype(jnp.float32)
        scale = lax.rsqrt(jnp.mean(wide * wide, axis=-1, keepdims=True) + EPS)
        partner = jnp.dot(raw, swap_ref[...], preferred_element_type=jnp.float32)
        return ((wide * straight + partner * crossed) * scale).astype(jnp.bfloat16)

    queries = turn(load(0), cq_ref[...], sq_ref[...])
    keys = turn(load(1), ck_ref[...], sk_ref[...])
    scores = lax.dot_general(queries, keys, NT, preferred_element_type=jnp.float32)
    scores = scores * SCALE + mask_ref[...]
    weights = jnp.exp2(scores - jnp.max(scores, axis=-1, keepdims=True))
    total = jnp.sum(weights, axis=-1, keepdims=True)
    mixed = jnp.dot(weights.astype(jnp.bfloat16), load(2), preferred_element_type=jnp.float32)
    out_ref[...] = (mixed / total).astype(jnp.bfloat16)


def attend(half, own, far, tables, mask):
    blocks, parts, slots, width = far.shape
    heads = width // HEAD_DIM
    rows = 2 * blocks * slots
    order = jnp.arange(HEAD_DIM)
    swap = (order[:, None] == (order ^ 1)[None, :]).astype(jnp.bfloat16)
    shape = (blocks, parts, slots, HEAD_DIM)
    whole = pl.BlockSpec((rows, HEAD_DIM), lambda g, half: (0, 0))
    return pl.pallas_call(
        attend_kernel,
        grid_spec=pltpu.PrefetchScalarGridSpec(
            num_scalar_prefetch=1,
            grid=(heads,),
            in_specs=[
                pl.BlockSpec(shape, lambda g, half: (0, 0, 0, half[0] * heads + g)),
                pl.BlockSpec(shape, lambda g, half: (0, 0, 0, g)),
                whole,
                whole,
                whole,
                whole,
                pl.BlockSpec((HEAD_DIM, HEAD_DIM), lambda g, half: (0, 0)),
                pl.BlockSpec((1, rows), lambda g, half: (0, 0)),
            ],
            out_specs=pl.BlockSpec((rows, HEAD_DIM), lambda g, half: (0, g)),
        ),
        out_shape=jax.ShapeDtypeStruct((rows, width), jnp.bfloat16),
        compiler_params=pltpu.CompilerParams(vmem_limit_bytes=VMEM),
        cost_estimate=pl.CostEstimate(
            flops=heads * rows * rows * HEAD_DIM * 4,
            bytes_accessed=rows * width * 8,
            transcendentals=0,
        ),
        name="attend",
    )(half, own, far, *tables, swap, mask)


def gelu_kernel(half_ref, own_ref, far_ref, out_ref):
    @pl.when(pl.program_id(0) == 0)
    def _():
        out_ref[...] = jax.nn.gelu(own_ref[0].astype(jnp.float32), approximate=True).astype(jnp.bfloat16)

    @pl.when(pl.program_id(0) == 1)
    def _():
        out_ref[...] = jax.nn.gelu(far_ref[0].astype(jnp.float32), approximate=True).astype(jnp.bfloat16)


def activate(half, own, far):
    blocks, slots, width = far.shape
    return pl.pallas_call(
        gelu_kernel,
        grid_spec=pltpu.PrefetchScalarGridSpec(
            num_scalar_prefetch=1,
            grid=(2, blocks),
            in_specs=[
                pl.BlockSpec((1, slots, width), lambda s, b, half: (jnp.where(s == 0, b, blocks - 1), 0, half[0])),
                pl.BlockSpec((1, slots, width), lambda s, b, half: (jnp.where(s == 0, 0, b), 0, 0)),
            ],
            out_specs=pl.BlockSpec((slots, width), lambda s, b, half: (s * blocks + b, 0)),
        ),
        out_shape=jax.ShapeDtypeStruct((2 * blocks * slots, width), jnp.bfloat16),
        compiler_params=pltpu.CompilerParams(vmem_limit_bytes=VMEM),
        cost_estimate=pl.CostEstimate(
            flops=2 * blocks * slots * width * 4,
            bytes_accessed=2 * blocks * slots * width,
            transcendentals=0,
        ),
        name="activate",
    )(half, own, far)


def project_kernel(attn_ref, act_ref, *refs):
    *blocks, own_ref, far_ref = refs
    depth = attn_ref.shape[1]
    rows = own_ref.shape[0]
    weights = blocks[0][...] if len(blocks) == 1 else jnp.concatenate([block[...] for block in blocks], axis=0)
    total = lax.dot_general(attn_ref[...], weights[:, :depth], NT, preferred_element_type=jnp.float32)
    total = total + lax.dot_general(act_ref[...], weights[:, depth:], NT, preferred_element_type=jnp.float32)
    own_ref[...] = total[:rows]
    far_ref[...] = total[rows:].astype(jnp.bfloat16)


def project(attn, act, weights, tiles=1, first=0, tile=None):
    rows = attn.shape[0]
    depth = weights[0].shape[1]
    tile = tile or sum(block.shape[0] for block in weights)
    columns = tiles * tile
    return pl.pallas_call(
        project_kernel,
        grid=(tiles,),
        in_specs=[
            pl.BlockSpec(attn.shape, lambda n: (0, 0)),
            pl.BlockSpec(act.shape, lambda n: (0, 0)),
        ]
        + [
            pl.BlockSpec((tile if len(weights) == 1 else block.shape[0], depth), lambda n: (first + n, 0))
            for block in weights
        ],
        out_specs=[
            pl.BlockSpec((rows // 2, tile), lambda n: (0, n)),
            pl.BlockSpec((rows // 2, tile), lambda n: (0, n)),
        ],
        out_shape=[
            jax.ShapeDtypeStruct((rows // 2, columns), jnp.float32),
            jax.ShapeDtypeStruct((rows // 2, columns), jnp.bfloat16),
        ],
        compiler_params=pltpu.CompilerParams(vmem_limit_bytes=VMEM),
        cost_estimate=pl.CostEstimate(
            flops=rows * columns * depth // 4, bytes_accessed=columns * depth // 4, transcendentals=0
        ),
        name="project",
    )(attn, act, *weights)


def finish_kernel(counts, slot_ref, step_ref, *refs):
    wide, narrow = counts
    chunks = [refs[2 * i : 2 * i + 2] for i in range(wide + narrow)]
    (
        stream_ref, bias_ref, gate_ref, scale_ref, shift_ref, w_ref, b_ref, latent_ref, hidden_ref, next_ref,
        proj_ref, rest_ref,
    ) = refs[2 * (wide + narrow) :]
    slots, width = proj_ref.shape
    lower = lax.broadcasted_iota(jnp.int32, (slots, 128), 1) < 64
    start = 0
    for own_ref, far_ref in chunks[wide:]:
        size = own_ref.shape[1]
        rest_ref[:, start : start + size] = own_ref[...] + far_ref[...].astype(jnp.float32)
        start += size
    share = chunks[0][0].shape[1] // 256
    for pair in range(width // 384):
        own_ref, far_ref = chunks[pair // share]
        first = pl.ds(256 * (pair % share), 128)
        second = pl.ds(256 * (pair % share) + 128, 128)
        even = own_ref[:, first] + far_ref[:, first].astype(jnp.float32)
        odd = own_ref[:, second] + far_ref[:, second].astype(jnp.float32)
        tail = rest_ref[:, pl.ds(pl.multiple_of(128 * slot_ref[pair], 128), 128)]
        odd = pltpu.roll(odd, 64, 1)
        swapped = pltpu.roll(tail, 64, 1)
        straight = slot_ref[width // 384] == 0
        tail = jnp.where(straight, tail, swapped)
        proj_ref[:, pl.ds(384 * pair, 128)] = even
        proj_ref[:, pl.ds(384 * pair + 128, 128)] = jnp.where(lower, tail, odd)
        proj_ref[:, pl.ds(384 * pair + 256, 128)] = jnp.where(lower, odd, tail)
    updated = stream_ref[0].astype(jnp.float32) + gate_ref[...] * (proj_ref[...] + bias_ref[...])
    hidden_ref[0] = updated.astype(jnp.bfloat16)

    @pl.when(pl.program_id(0) > 0)
    def _():
        center = updated - jnp.mean(updated, axis=-1, keepdims=True)
        variance = jnp.mean(center * center, axis=-1, keepdims=True)
        normed = center * lax.rsqrt(variance + EPS)
        modulated = ((1.0 + scale_ref[...]) * normed + shift_ref[...]).astype(jnp.bfloat16)
        velocity = lax.dot_general(w_ref[...], modulated, NT, preferred_element_type=jnp.float32)
        next_ref[0] = latent_ref[0] + step_ref[0] * (velocity + b_ref[...])


def finish(slot, step, wide, narrow, stream, bias, gate, scale, shift, w_final, b_final, latent):
    blocks, slots, width = stream.shape
    channels = w_final.shape[0]
    chunks = [array for pair in wide + narrow for array in pair]

    def whole(array):
        return pl.BlockSpec(array.shape, lambda b, *_: (0, 0))

    tokens = pl.BlockSpec((1, slots, width), lambda b, *_: (b, 0, 0))
    image = pl.BlockSpec((1, channels, slots), lambda b, *_: (jnp.maximum(b - 1, 0), 0, 0))
    return pl.pallas_call(
        functools.partial(finish_kernel, (len(wide), len(narrow))),
        grid_spec=pltpu.PrefetchScalarGridSpec(
            num_scalar_prefetch=2,
            grid=(blocks,),
            in_specs=[pl.BlockSpec((slots, array.shape[1]), lambda b, *_: (b, 0)) for array in chunks]
            + [
                tokens,
                whole(bias),
                whole(gate),
                whole(scale),
                whole(shift),
                whole(w_final),
                whole(b_final),
                image,
            ],
            out_specs=[tokens, image],
            scratch_shapes=[
                pltpu.VMEM((slots, width), jnp.float32),
                pltpu.VMEM((slots, width // 3), jnp.float32),
            ],
        ),
        out_shape=[
            jax.ShapeDtypeStruct(stream.shape, jnp.bfloat16),
            jax.ShapeDtypeStruct(latent.shape, jnp.float32),
        ],
        compiler_params=pltpu.CompilerParams(vmem_limit_bytes=VMEM),
        cost_estimate=pl.CostEstimate(
            flops=blocks * slots * width * 160, bytes_accessed=blocks * slots * width * 10, transcendentals=0
        ),
        name="finish",
    )(slot, step, *chunks, stream, bias, gate, scale, shift, w_final, b_final, latent)


PATH = (0, 1, 3, 5, 7, 6, 4, 2)


def after(array, *others):
    return lax.optimization_barrier((array, *others))[0]


def hop(array, by):
    places = len(PATH)
    pairs = [(2 * PATH[i] + c, 2 * PATH[(i + by) % places] + c) for i in range(places) for c in range(2)]
    return lax.ppermute(array, "tile", pairs)


def sibling(array):
    return lax.ppermute(array, "tile", [(t, t ^ 1) for t in range(2 * len(PATH))])


def paired(
    partners,
    attn_proj,
    mlp_proj,
    stream,
    text_len,
    q_gain,
    k_gain,
    w_out_attn,
    w_out_mlp,
    bias_out,
    gate_mod,
    final_shift,
    final_scale,
    w_final,
    b_final,
    latent,
    step_size,
):
    me = lax.axis_index("head")
    half = me[None].astype(jnp.int32)
    trade = functools.partial(lax.ppermute, axis_name="head", perm=[(0, 1), (1, 0)])

    columns = jnp.concatenate([w_out_attn.T, w_out_mlp.T], axis=1)
    weights_a = lax.all_gather(columns[:128], "tile", axis=0, tiled=True)
    block = columns[128:]

    own_attn = jnp.transpose(attn_proj[0], (0, 2, 1, 3))
    own_units = mlp_proj[0]
    slots = own_attn.shape[2]
    width = own_attn.shape[3] // partners
    units = own_units.shape[2] // partners
    far_attn = trade(lax.dynamic_slice_in_dim(own_attn, (1 - me) * width, width, axis=3))
    far_units = trade(after(lax.dynamic_slice_in_dim(own_units, (1 - me) * units, units, axis=2), far_attn))

    onward, back = hop(block, 1), hop(block, -1)
    first = [block, sibling(block), onward, sibling(onward), back, sibling(back)]
    positions = jnp.arange(slots, dtype=jnp.int32)
    near, away = me * slots + positions, (1 - me) * slots + positions

    def both(gain):
        return [jnp.concatenate(pair, axis=0) for pair in zip(rotary(near, gain), rotary(away, gain))]

    text = jnp.concatenate([near, jnp.full(2 * slots, -1), away, jnp.full(2 * slots, -1)])
    mask = jnp.where(text < text_len[0], 0.0, -jnp.inf)[None, :].astype(jnp.float32)
    attn = attend(half, own_attn, far_attn, both(q_gain) + both(k_gain), mask)
    act = activate(half, own_units, far_units)

    onward, back, weights_a, attn, act = lax.optimization_barrier((onward, back, weights_a, attn, act))
    onward, back = hop(onward, 1), hop(back, -1)
    own, sent = project(attn, act, [weights_a], tiles=4, first=0, tile=256)
    onward, back, attn, act, sent = lax.optimization_barrier((onward, back, attn, act, sent))
    wide = [(own, trade(sent))]
    second = [onward, sibling(onward), back, sibling(back)]
    onward, back = hop(onward, 1), hop(back, -1)
    own, sent = project(attn, act, [weights_a], tiles=4, first=4, tile=256)
    onward, back, attn, act, sent = lax.optimization_barrier((onward, back, attn, act, sent))
    wide.append((own, trade(sent)))
    third = [onward, sibling(onward), back, sibling(back)]
    onward, back = hop(onward[:32], 1), hop(back[32:], -1)
    own, sent = project(attn, act, first)
    narrow = [(own, trade(sent))]
    own, sent = project(attn, act, second)
    onward, back, attn, act, sent, far = lax.optimization_barrier((onward, back, attn, act, sent, wide[0][1]))
    wide[0] = (wide[0][0], far)
    narrow.append((own, trade(sent)))
    last = [onward, back, sibling(onward), sibling(back)]
    for blocks in (third, last):
        own, sent = project(attn, act, blocks)
        narrow.append((own, trade(sent)))

    tile = lax.axis_index("tile")
    place = jnp.array([PATH.index(chip) for chip in range(len(PATH))], jnp.int32)
    behind = (place[tile // 2] - place) % len(PATH)
    slot = jnp.array([0, 1, 3, 5, 7, 6, 4, 2], jnp.int32)[behind]
    slot = jnp.concatenate([slot, (tile % 2)[None].astype(jnp.int32)])
    hidden, following = finish(
        slot,
        step_size,
        wide,
        narrow,
        stream[0],
        bias_out[None, :],
        gate_mod,
        final_scale,
        final_shift,
        w_final.T,
        b_final[:, None],
        jnp.transpose(latent[0], (0, 2, 1)),
    )
    return hidden[None], jnp.transpose(following, (0, 2, 1))[None]


def solution(mesh):
    placed = (
        P("tile", None, "head", None, None),
        P("tile", None, "head", None),
        P("tile", None, "head", None),
        P("tile"),
        P(),
        P(),
        P("head", "tile"),
        P("head", "tile"),
        P(),
        P("tile", None),
        P("tile", None),
        P("tile", None),
        P(),
        P(),
        P("tile", None, "head", None),
        P("tile"),
    )
    return jax.shard_map(
        functools.partial(paired, mesh.shape["head"]) if fits(mesh.shape) else general,
        mesh=mesh,
        in_specs=placed,
        out_specs=(P("tile", None, "head", None), P("tile", None, "head", None)),
        check_vma=False,
    )
```

```python
import functools
import math

import jax
import jax.numpy as jnp
from jax import lax
from jax.experimental import pallas as pl
from jax.experimental.pallas import tpu as pltpu
from jax.sharding import PartitionSpec as P

HEAD_DIM = 128
SLOTS = 192
GRID_W = 32


def rope_tables(positions):
    pairs_zero = HEAD_DIM // 16
    pairs_axis = (HEAD_DIM // 2 - pairs_zero) // 2
    freqs = 10000.0 ** (-jnp.arange(pairs_axis, dtype=jnp.float32) / pairs_axis)
    count = positions.shape[0]
    angles = [jnp.zeros((count, HEAD_DIM // 2), jnp.float32)]
    for block in range(1, 3):
        image_index = (block - 1) * SLOTS + positions
        rows = (image_index // GRID_W).astype(jnp.float32)
        columns = (image_index % GRID_W).astype(jnp.float32)
        angles.append(
            jnp.concatenate(
                [
                    jnp.zeros((count, pairs_zero), jnp.float32),
                    rows[:, None] * freqs[None, :],
                    columns[:, None] * freqs[None, :],
                ],
                axis=1,
            )
        )
    stacked = jnp.stack(angles)
    return (jnp.cos(stacked), jnp.sin(stacked))


def prepare(raw, gain, cosine, sine):
    normed = raw * lax.rsqrt(jnp.mean(raw * raw, axis=-1, keepdims=True) + 1e-06) * gain
    halves = normed.reshape(normed.shape[:-1] + (HEAD_DIM // 2, 2))
    first = halves[..., 0]
    second = halves[..., 1]
    cosine = cosine[None, :, :, None, :]
    sine = sine[None, :, :, None, :]
    rotated = jnp.stack([first * cosine - second * sine, first * sine + second * cosine], axis=-1)
    return rotated.reshape(raw.shape).astype(jnp.bfloat16)


def attend_head(inputs):
    queries, keys, values, live = inputs
    scores = jnp.einsum("qd,kd->qk", queries, keys, preferred_element_type=jnp.float32) / math.sqrt(
        HEAD_DIM
    )
    scores = jnp.where(live[None, :], scores, -jnp.inf)
    top = jnp.max(scores, axis=-1, keepdims=True)
    weights = jnp.exp(scores - top)
    total = jnp.sum(weights, axis=-1, keepdims=True)
    mixed = jnp.dot(weights.astype(jnp.bfloat16), values, preferred_element_type=jnp.float32)
    return (mixed / total).astype(jnp.bfloat16)


def attend_request(inputs):
    queries, keys, values, live = inputs
    count = queries.shape[1]
    broad_live = jnp.broadcast_to(live[None, :], (count, live.shape[0]))
    result = lax.map(
        attend_head,
        (
            jnp.moveaxis(queries, 1, 0),
            jnp.moveaxis(keys, 1, 0),
            jnp.moveaxis(values, 1, 0),
            broad_live,
        ),
    )
    return jnp.moveaxis(result, 0, 1)


def general(
    attn_proj,
    mlp_proj,
    stream,
    text_len,
    q_gain,
    k_gain,
    w_out_attn,
    w_out_mlp,
    bias_out,
    gate_mod,
    final_shift,
    final_scale,
    w_final,
    b_final,
    latent,
    step_size,
):
    requests = attn_proj.shape[0]
    own_slots = attn_proj.shape[2]
    width = attn_proj.shape[4]
    heads = width // HEAD_DIM
    start_slot = lax.axis_index("head") * own_slots
    positions = start_slot + jnp.arange(own_slots, dtype=jnp.int32)
    cosine, sine = rope_tables(positions)
    head_shape = (requests, 3, own_slots, heads, HEAD_DIM)
    queries = prepare(
        attn_proj[:, :, :, 0].astype(jnp.float32).reshape(head_shape), q_gain, cosine, sine
    )
    keys = prepare(
        attn_proj[:, :, :, 1].astype(jnp.float32).reshape(head_shape), k_gain, cosine, sine
    )
    packed = jnp.stack(
        [
            queries.reshape(requests, 3, own_slots, width),
            keys.reshape(requests, 3, own_slots, width),
            attn_proj[:, :, :, 2],
        ],
        axis=3,
    )
    units = mlp_proj[:, :, :, None, :]
    moved, hidden_units = (
        lax.all_to_all(packed, "head", split_axis=4, concat_axis=2, tiled=True),
        lax.all_to_all(units, "head", split_axis=4, concat_axis=2, tiled=True),
    )
    hidden_units = hidden_units[:, :, :, 0]
    tile_slots = moved.shape[2]
    local_width = moved.shape[4]
    local_heads = local_width // HEAD_DIM
    flat_shape = (requests, 3 * tile_slots, local_heads, HEAD_DIM)
    all_positions = jnp.arange(tile_slots, dtype=jnp.int32)
    text_live = all_positions[None, :] < text_len[:, None]
    image_live = jnp.ones_like(text_live)
    live = jnp.stack([text_live, image_live, image_live], axis=1).reshape(requests, 3 * tile_slots)
    attn_out = lax.map(
        attend_request,
        (
            moved[:, :, :, 0].reshape(flat_shape),
            moved[:, :, :, 1].reshape(flat_shape),
            moved[:, :, :, 2].reshape(flat_shape),
            live,
        ),
    )
    attn_out = attn_out.reshape(requests, 3, tile_slots, local_width)
    mlp_act = jax.nn.gelu(hidden_units.astype(jnp.float32), approximate=True).astype(jnp.bfloat16)
    term = jnp.einsum(
        "rbsk,kd->rbsd",
        attn_out,
        lax.all_gather(w_out_attn, "tile", axis=1, tiled=True),
        preferred_element_type=jnp.float32,
    )
    term = term + jnp.einsum(
        "rbsk,kd->rbsd",
        mlp_act,
        lax.all_gather(w_out_mlp, "tile", axis=1, tiled=True),
        preferred_element_type=jnp.float32,
    )
    proj = lax.psum_scatter(term, "head", scatter_dimension=2, tiled=True)
    updated = stream.astype(jnp.float32) + gate_mod[:, None, None, :] * (proj + bias_out)
    hidden_out = updated.astype(jnp.bfloat16)
    image = updated[:, 1:]
    center = image - jnp.mean(image, axis=-1, keepdims=True)
    variance = jnp.mean(center * center, axis=-1, keepdims=True)
    normed = center * lax.rsqrt(variance + 1e-06)
    modulated = (
        (1.0 + final_scale[:, None, None, :]) * normed + final_shift[:, None, None, :]
    ).astype(jnp.bfloat16)
    velocity = (
        jnp.einsum("rbsd,dc->rbsc", modulated, w_final, preferred_element_type=jnp.float32)
        + b_final
    )
    latent_next = latent + step_size[:, None, None, None] * velocity
    return (hidden_out, latent_next)


EPS = 1e-06
SCALE = math.log2(math.e) / math.sqrt(HEAD_DIM)
VMEM = 60 * 1024 * 1024
NT = (((1,), (1,)), ((), ()))


def fits(sizes):
    return sizes["head"] == 2 and sizes["tile"] == 2 * len(PATH)


def rotary(positions, gain):
    cosine, sine = rope_tables(positions)
    rows = cosine.shape[0] * cosine.shape[1]
    cosine = jnp.repeat(cosine.reshape(rows, HEAD_DIM // 2), 2, axis=1)
    sine = jnp.repeat(sine.reshape(rows, HEAD_DIM // 2), 2, axis=1)
    odd = jnp.arange(HEAD_DIM) % 2 == 1
    partner = jnp.where(odd, jnp.roll(gain, 1), -jnp.roll(gain, -1))
    return cosine * gain, sine * partner


def pack_kernel(half_ref, attn_ref, attn_w_ref, act_w_ref, sent_ref, block_ref, sems):
    width = sent_ref.shape[3]
    depth = attn_w_ref.shape[1]
    other = pl.ds(pl.multiple_of((1 - half_ref[0]) * width, 128), width)
    copies = [
        pltpu.make_async_copy(attn_w_ref, block_ref.at[:, :depth], sems.at[0]),
        pltpu.make_async_copy(act_w_ref, block_ref.at[:, depth:], sems.at[1]),
    ]
    for b in range(sent_ref.shape[0]):
        for part in range(sent_ref.shape[1]):
            copies.append(
                pltpu.make_async_copy(attn_ref.at[b, part, :, other], sent_ref.at[b, part], sems.at[len(copies)])
            )
    for copy in copies:
        copy.start()
    for copy in copies:
        copy.wait()


def pack(half, attn, attn_w, act_w):
    blocks, parts, slots, width = attn.shape
    anywhere = pl.BlockSpec(memory_space=pl.ANY)
    return pl.pallas_call(
        pack_kernel,
        in_specs=[pl.BlockSpec(memory_space=pltpu.SMEM), anywhere, anywhere, anywhere],
        out_specs=[anywhere, anywhere],
        out_shape=[
            jax.ShapeDtypeStruct((blocks, parts, slots, width // 2), jnp.bfloat16),
            jax.ShapeDtypeStruct((attn_w.shape[0], attn_w.shape[1] + act_w.shape[1]), jnp.bfloat16),
        ],
        scratch_shapes=[pltpu.SemaphoreType.DMA((2 + blocks * parts,))],
        cost_estimate=pl.CostEstimate(flops=0, bytes_accessed=8 * attn_w.size, transcendentals=0),
        name="pack",
    )(half, attn, attn_w, act_w)


def attend_kernel(half_ref, own_ref, far_ref, cq_ref, sq_ref, ck_ref, sk_ref, swap_ref, mask_ref, out_ref):
    rows = own_ref.shape[0] * own_ref.shape[2]

    def load(part):
        return jnp.concatenate(
            [own_ref[:, part].reshape(rows, HEAD_DIM), far_ref[:, part].reshape(rows, HEAD_DIM)], axis=0
        )

    def turn(raw, straight, crossed):
        wide = raw.astype(jnp.float32)
        scale = lax.rsqrt(jnp.mean(wide * wide, axis=-1, keepdims=True) + EPS)
        partner = jnp.dot(raw, swap_ref[...], preferred_element_type=jnp.float32)
        return ((wide * straight + partner * crossed) * scale).astype(jnp.bfloat16)

    queries = turn(load(0), cq_ref[...], sq_ref[...])
    keys = turn(load(1), ck_ref[...], sk_ref[...])
    scores = lax.dot_general(queries, keys, NT, preferred_element_type=jnp.float32)
    scores = scores * SCALE + mask_ref[...]
    weights = jnp.exp2(scores - jnp.max(scores, axis=-1, keepdims=True))
    total = jnp.sum(weights, axis=-1, keepdims=True)
    mixed = jnp.dot(weights.astype(jnp.bfloat16), load(2), preferred_element_type=jnp.float32)
    out_ref[...] = (mixed / total).astype(jnp.bfloat16)


def attend(half, own, far, tables, mask):
    blocks, parts, slots, width = far.shape
    heads = width // HEAD_DIM
    rows = 2 * blocks * slots
    order = jnp.arange(HEAD_DIM)
    swap = (order[:, None] == (order ^ 1)[None, :]).astype(jnp.bfloat16)
    shape = (blocks, parts, slots, HEAD_DIM)
    whole = pl.BlockSpec((rows, HEAD_DIM), lambda g, half: (0, 0))
    return pl.pallas_call(
        attend_kernel,
        grid_spec=pltpu.PrefetchScalarGridSpec(
            num_scalar_prefetch=1,
            grid=(heads,),
            in_specs=[
                pl.BlockSpec(shape, lambda g, half: (0, 0, 0, half[0] * heads + g)),
                pl.BlockSpec(shape, lambda g, half: (0, 0, 0, g)),
                whole,
                whole,
                whole,
                whole,
                pl.BlockSpec((HEAD_DIM, HEAD_DIM), lambda g, half: (0, 0)),
                pl.BlockSpec((1, rows), lambda g, half: (0, 0)),
            ],
            out_specs=pl.BlockSpec((rows, HEAD_DIM), lambda g, half: (0, g)),
        ),
        out_shape=jax.ShapeDtypeStruct((rows, width), jnp.bfloat16),
        compiler_params=pltpu.CompilerParams(vmem_limit_bytes=VMEM),
        cost_estimate=pl.CostEstimate(
            flops=heads * rows * rows * HEAD_DIM * 4,
            bytes_accessed=rows * width * 8,
            transcendentals=0,
        ),
        name="attend",
    )(half, own, far, *tables, swap, mask)


def gelu_kernel(part_ref, units_ref, out_ref):
    out_ref[...] = jax.nn.gelu(units_ref[0].astype(jnp.float32), approximate=True).astype(jnp.bfloat16)


def activate(part, units, width):
    blocks, slots, _ = units.shape
    return pl.pallas_call(
        gelu_kernel,
        grid_spec=pltpu.PrefetchScalarGridSpec(
            num_scalar_prefetch=1,
            grid=(blocks,),
            in_specs=[pl.BlockSpec((1, slots, width), lambda b, part: (b, 0, part[0]))],
            out_specs=pl.BlockSpec((slots, width), lambda b, part: (b, 0)),
        ),
        out_shape=jax.ShapeDtypeStruct((blocks * slots, width), jnp.bfloat16),
        compiler_params=pltpu.CompilerParams(vmem_limit_bytes=VMEM),
        cost_estimate=pl.CostEstimate(
            flops=blocks * slots * width * 4, bytes_accessed=blocks * slots * width, transcendentals=0
        ),
        name="activate",
    )(part, units)


def project_kernel(layout, core_ref, attn_ref, near_ref, away_ref, *refs):
    *pieces, own_ref, far_ref, x_ref, w_ref, sems = refs
    depth = attn_ref.shape[1]
    rows = near_ref.shape[0]
    core = core_ref[0]
    copies = [
        pltpu.make_async_copy(attn_ref, x_ref.at[:, :depth], sems.at[0]),
        pltpu.make_async_copy(near_ref, x_ref.at[:rows, depth:], sems.at[1]),
        pltpu.make_async_copy(away_ref, x_ref.at[rows:, depth:], sems.at[2]),
    ]
    for (base, here, share), piece in zip(layout, pieces):
        start = base + (core if here else 1 - core) * share
        place = pl.ds(pl.multiple_of(start, 16), piece.shape[0])
        copies.append(pltpu.make_async_copy(piece, w_ref.at[place], sems.at[len(copies)]))
    for copy in copies:
        copy.start()
    for copy in copies:
        copy.wait()
    total = lax.dot_general(x_ref[...], w_ref[...], NT, preferred_element_type=jnp.float32)
    own_ref[...] = total[:rows]
    far_ref[...] = total[rows:].astype(jnp.bfloat16)


def project(core, attn, near, away, chips):
    share = sum(piece.shape[0] for here, _, piece in chips[0] if here)
    layout, flat = [], []
    for index, pieces in enumerate(chips):
        for here, first, piece in pieces:
            layout.append((2 * share * index + first, here, share))
            flat.append(piece)
    rows, depth = near.shape[0], attn.shape[1] + near.shape[1]
    columns = 2 * share * len(chips)
    anywhere = pl.BlockSpec(memory_space=pl.ANY)
    return pl.pallas_call(
        functools.partial(project_kernel, layout),
        in_specs=[pl.BlockSpec(memory_space=pltpu.SMEM)] + [anywhere] * (3 + len(flat)),
        out_specs=[pl.BlockSpec(memory_space=pltpu.VMEM)] * 2,
        out_shape=[
            jax.ShapeDtypeStruct((rows, columns), jnp.float32),
            jax.ShapeDtypeStruct((rows, columns), jnp.bfloat16),
        ],
        scratch_shapes=[
            pltpu.VMEM((2 * rows, depth), jnp.bfloat16),
            pltpu.VMEM((columns, depth), jnp.bfloat16),
            pltpu.SemaphoreType.DMA((3 + len(flat),)),
        ],
        compiler_params=pltpu.CompilerParams(vmem_limit_bytes=VMEM),
        cost_estimate=pl.CostEstimate(
            flops=rows * columns * depth // 2, bytes_accessed=columns * depth // 4, transcendentals=0
        ),
        name="project",
    )(core, attn, near, away, *flat)


def finish_kernel(chunks, slot_ref, step_ref, *refs):
    pairs = [refs[2 * i : 2 * i + 2] for i in range(chunks)]
    (
        stream_ref, bias_ref, gate_ref, scale_ref, shift_ref, w_ref, b_ref, latent_ref, hidden_ref, next_ref,
        proj_ref, sums_ref,
    ) = refs[2 * chunks :]
    slots, width = proj_ref.shape
    start = 0
    for own_ref, far_ref in pairs:
        size = own_ref.shape[1]
        sums_ref[:, start : start + size] = own_ref[...] + far_ref[...].astype(jnp.float32)
        start += size
    chip = width // len(PATH)
    for index in range(len(PATH)):
        source = pl.ds(pl.multiple_of(chip * slot_ref[index], 128), chip)
        proj_ref[:, chip * index : chip * (index + 1)] = sums_ref[:, source]
    updated = stream_ref[0].astype(jnp.float32) + gate_ref[...] * (proj_ref[...] + bias_ref[...])
    hidden_ref[0] = updated.astype(jnp.bfloat16)

    @pl.when(pl.program_id(0) > 0)
    def _():
        center = updated - jnp.mean(updated, axis=-1, keepdims=True)
        variance = jnp.mean(center * center, axis=-1, keepdims=True)
        normed = center * lax.rsqrt(variance + EPS)
        modulated = ((1.0 + scale_ref[...]) * normed + shift_ref[...]).astype(jnp.bfloat16)
        velocity = lax.dot_general(w_ref[...], modulated, NT, preferred_element_type=jnp.float32)
        next_ref[0] = latent_ref[0] + step_ref[0] * (velocity + b_ref[...])


def finish(slot, step, chunks, stream, bias, gate, scale, shift, w_final, b_final, latent):
    blocks, slots, width = stream.shape
    channels = w_final.shape[0]
    flat = [array for pair in chunks for array in pair]

    def whole(array):
        return pl.BlockSpec(array.shape, lambda b, *_: (0, 0))

    tokens = pl.BlockSpec((1, slots, width), lambda b, *_: (b, 0, 0))
    image = pl.BlockSpec((1, channels, slots), lambda b, *_: (jnp.maximum(b - 1, 0), 0, 0))
    return pl.pallas_call(
        functools.partial(finish_kernel, len(chunks)),
        grid_spec=pltpu.PrefetchScalarGridSpec(
            num_scalar_prefetch=2,
            grid=(blocks,),
            in_specs=[pl.BlockSpec((slots, array.shape[1]), lambda b, *_: (b, 0)) for array in flat]
            + [
                tokens,
                whole(bias),
                whole(gate),
                whole(scale),
                whole(shift),
                whole(w_final),
                whole(b_final),
                image,
            ],
            out_specs=[tokens, image],
            scratch_shapes=[
                pltpu.VMEM((slots, width), jnp.float32),
                pltpu.VMEM((slots, width), jnp.float32),
            ],
        ),
        out_shape=[
            jax.ShapeDtypeStruct(stream.shape, jnp.bfloat16),
            jax.ShapeDtypeStruct(latent.shape, jnp.float32),
        ],
        compiler_params=pltpu.CompilerParams(vmem_limit_bytes=VMEM),
        cost_estimate=pl.CostEstimate(
            flops=blocks * slots * width * 160, bytes_accessed=blocks * slots * width * 10, transcendentals=0
        ),
        name="finish",
    )(slot, step, *flat, stream, bias, gate, scale, shift, w_final, b_final, latent)


PATH = (0, 1, 3, 5, 7, 6, 4, 2)


def hop(array, by):
    places = len(PATH)
    pairs = [(2 * PATH[i] + c, 2 * PATH[(i + by) % places] + c) for i in range(places) for c in range(2)]
    return lax.ppermute(array, "tile", pairs)


def both_cores(array, first=0):
    other = lax.ppermute(array, "tile", [(t, t ^ 1) for t in range(2 * len(PATH))])
    return [(True, first, array), (False, first, other)]


def paired(
    partners,
    attn_proj,
    mlp_proj,
    stream,
    text_len,
    q_gain,
    k_gain,
    w_out_attn,
    w_out_mlp,
    bias_out,
    gate_mod,
    final_shift,
    final_scale,
    w_final,
    b_final,
    latent,
    step_size,
):
    me = lax.axis_index("head")
    half = me[None].astype(jnp.int32)
    trade = functools.partial(lax.ppermute, axis_name="head", perm=[(0, 1), (1, 0)])

    core = (lax.axis_index("tile") % 2)[None].astype(jnp.int32)
    own_attn = jnp.transpose(attn_proj[0], (0, 2, 1, 3))
    own_units = mlp_proj[0]
    slots = own_attn.shape[2]
    units = own_units.shape[2] // partners
    sent_attn, block = pack(half, own_attn, w_out_attn.T, w_out_mlp.T)
    far_attn = trade(sent_attn)

    onward, back = hop(block, 1), hop(block, -1)
    chips = [both_cores(block)]

    positions = jnp.arange(slots, dtype=jnp.int32)
    near, away = me * slots + positions, (1 - me) * slots + positions

    def both(gain):
        return [jnp.concatenate(pair, axis=0) for pair in zip(rotary(near, gain), rotary(away, gain))]

    text = jnp.concatenate([near, jnp.full(2 * slots, -1), away, jnp.full(2 * slots, -1)])
    mask = jnp.where(text < text_len[0], 0.0, -jnp.inf)[None, :].astype(jnp.float32)
    tables = both(q_gain) + both(k_gain)
    act_near = activate(half, own_units, units)
    sent_units = lax.dynamic_slice_in_dim(own_units, (1 - me) * units, units, axis=2)

    tile = lax.axis_index("tile")
    place = jnp.array([PATH.index(chip) for chip in range(len(PATH))], jnp.int32)
    behind = (place[tile // 2] - place) % len(PATH)
    slot = jnp.array([0, 1, 3, 5, 7, 6, 4, 2], jnp.int32)[behind]

    onward, back, tables, mask, act_near, sent_units, slot, chips = lax.optimization_barrier(
        (onward, back, tables, mask, act_near, sent_units, slot, [[piece[2] for piece in chip] for chip in chips])
    )
    chips = [[(True, 0, chip[0]), (False, 0, chip[1])] for chip in chips]
    chips += [both_cores(onward), both_cores(back)]
    onward, back = hop(onward, 1), hop(back, -1)
    far_attn, sent_units, mask = lax.optimization_barrier((far_attn, sent_units, mask))
    far_units = trade(sent_units)
    attn = attend(half, own_attn, far_attn, tables, mask)
    attn, onward, back = lax.optimization_barrier((attn, onward, back))
    chips += [both_cores(onward), both_cores(back)]
    onward, back = hop(onward, 1), hop(back, -1)
    far_units, attn = lax.optimization_barrier((far_units, attn))
    act_away = activate(jnp.zeros_like(half), far_units, units)

    chunks = []

    def send(group):
        own, sent = project(core, attn, act_near, act_away, group)
        chunks.append((own, trade(sent)))
        return sent

    send(chips[0:1])
    sent = send(chips[1:3])
    onward, back, attn, sent, chunks[0] = lax.optimization_barrier((onward, back, attn, sent, chunks[0]))
    middle = block.shape[0] // 2
    last = hop(onward[:middle], 1), hop(back[middle:], -1)
    chips += [both_cores(onward), both_cores(back)]
    sent = send(chips[3:5])
    attn, sent, chunks[1] = lax.optimization_barrier((attn, sent, chunks[1]))
    sent = send(chips[5:7])
    onward, back, attn, sent, chunks[2] = lax.optimization_barrier((*last, attn, sent, chunks[2]))
    chips.append(both_cores(onward) + both_cores(back, middle))
    send(chips[7:8])

    hidden, following = finish(
        slot,
        step_size,
        chunks,
        stream[0],
        bias_out[None, :],
        gate_mod,
        final_scale,
        final_shift,
        w_final.T,
        b_final[:, None],
        jnp.transpose(latent[0], (0, 2, 1)),
    )
    return hidden[None], jnp.transpose(following, (0, 2, 1))[None]


def solution(mesh):
    placed = (
        P("tile", None, "head", None, None),
        P("tile", None, "head", None),
        P("tile", None, "head", None),
        P("tile"),
        P(),
        P(),
        P("head", "tile"),
        P("head", "tile"),
        P(),
        P("tile", None),
        P("tile", None),
        P("tile", None),
        P(),
        P(),
        P("tile", None, "head", None),
        P("tile"),
    )
    return jax.shard_map(
        functools.partial(paired, mesh.shape["head"]) if fits(mesh.shape) else general,
        mesh=mesh,
        in_specs=placed,
        out_specs=(P("tile", None, "head", None), P("tile", None, "head", None)),
        check_vma=False,
    )
```

```python
import functools
import math

import jax
import jax.numpy as jnp
from jax import lax
from jax.experimental import pallas as pl
from jax.experimental.pallas import tpu as pltpu
from jax.sharding import PartitionSpec as P

HEAD_DIM = 128
SLOTS = 192
GRID_W = 32


def rope_tables(positions):
    pairs_zero = HEAD_DIM // 16
    pairs_axis = (HEAD_DIM // 2 - pairs_zero) // 2
    freqs = 10000.0 ** (-jnp.arange(pairs_axis, dtype=jnp.float32) / pairs_axis)
    count = positions.shape[0]
    angles = [jnp.zeros((count, HEAD_DIM // 2), jnp.float32)]
    for block in range(1, 3):
        image_index = (block - 1) * SLOTS + positions
        rows = (image_index // GRID_W).astype(jnp.float32)
        columns = (image_index % GRID_W).astype(jnp.float32)
        angles.append(
            jnp.concatenate(
                [
                    jnp.zeros((count, pairs_zero), jnp.float32),
                    rows[:, None] * freqs[None, :],
                    columns[:, None] * freqs[None, :],
                ],
                axis=1,
            )
        )
    stacked = jnp.stack(angles)
    return (jnp.cos(stacked), jnp.sin(stacked))


def prepare(raw, gain, cosine, sine):
    normed = raw * lax.rsqrt(jnp.mean(raw * raw, axis=-1, keepdims=True) + 1e-06) * gain
    halves = normed.reshape(normed.shape[:-1] + (HEAD_DIM // 2, 2))
    first = halves[..., 0]
    second = halves[..., 1]
    cosine = cosine[None, :, :, None, :]
    sine = sine[None, :, :, None, :]
    rotated = jnp.stack([first * cosine - second * sine, first * sine + second * cosine], axis=-1)
    return rotated.reshape(raw.shape).astype(jnp.bfloat16)


def attend_head(inputs):
    queries, keys, values, live = inputs
    scores = jnp.einsum("qd,kd->qk", queries, keys, preferred_element_type=jnp.float32) / math.sqrt(
        HEAD_DIM
    )
    scores = jnp.where(live[None, :], scores, -jnp.inf)
    top = jnp.max(scores, axis=-1, keepdims=True)
    weights = jnp.exp(scores - top)
    total = jnp.sum(weights, axis=-1, keepdims=True)
    mixed = jnp.dot(weights.astype(jnp.bfloat16), values, preferred_element_type=jnp.float32)
    return (mixed / total).astype(jnp.bfloat16)


def attend_request(inputs):
    queries, keys, values, live = inputs
    count = queries.shape[1]
    broad_live = jnp.broadcast_to(live[None, :], (count, live.shape[0]))
    result = lax.map(
        attend_head,
        (
            jnp.moveaxis(queries, 1, 0),
            jnp.moveaxis(keys, 1, 0),
            jnp.moveaxis(values, 1, 0),
            broad_live,
        ),
    )
    return jnp.moveaxis(result, 0, 1)


def general(
    attn_proj,
    mlp_proj,
    stream,
    text_len,
    q_gain,
    k_gain,
    w_out_attn,
    w_out_mlp,
    bias_out,
    gate_mod,
    final_shift,
    final_scale,
    w_final,
    b_final,
    latent,
    step_size,
):
    requests = attn_proj.shape[0]
    own_slots = attn_proj.shape[2]
    width = attn_proj.shape[4]
    heads = width // HEAD_DIM
    start_slot = lax.axis_index("head") * own_slots
    positions = start_slot + jnp.arange(own_slots, dtype=jnp.int32)
    cosine, sine = rope_tables(positions)
    head_shape = (requests, 3, own_slots, heads, HEAD_DIM)
    queries = prepare(
        attn_proj[:, :, :, 0].astype(jnp.float32).reshape(head_shape), q_gain, cosine, sine
    )
    keys = prepare(
        attn_proj[:, :, :, 1].astype(jnp.float32).reshape(head_shape), k_gain, cosine, sine
    )
    packed = jnp.stack(
        [
            queries.reshape(requests, 3, own_slots, width),
            keys.reshape(requests, 3, own_slots, width),
            attn_proj[:, :, :, 2],
        ],
        axis=3,
    )
    units = mlp_proj[:, :, :, None, :]
    moved, hidden_units = (
        lax.all_to_all(packed, "head", split_axis=4, concat_axis=2, tiled=True),
        lax.all_to_all(units, "head", split_axis=4, concat_axis=2, tiled=True),
    )
    hidden_units = hidden_units[:, :, :, 0]
    tile_slots = moved.shape[2]
    local_width = moved.shape[4]
    local_heads = local_width // HEAD_DIM
    flat_shape = (requests, 3 * tile_slots, local_heads, HEAD_DIM)
    all_positions = jnp.arange(tile_slots, dtype=jnp.int32)
    text_live = all_positions[None, :] < text_len[:, None]
    image_live = jnp.ones_like(text_live)
    live = jnp.stack([text_live, image_live, image_live], axis=1).reshape(requests, 3 * tile_slots)
    attn_out = lax.map(
        attend_request,
        (
            moved[:, :, :, 0].reshape(flat_shape),
            moved[:, :, :, 1].reshape(flat_shape),
            moved[:, :, :, 2].reshape(flat_shape),
            live,
        ),
    )
    attn_out = attn_out.reshape(requests, 3, tile_slots, local_width)
    mlp_act = jax.nn.gelu(hidden_units.astype(jnp.float32), approximate=True).astype(jnp.bfloat16)
    term = jnp.einsum(
        "rbsk,kd->rbsd",
        attn_out,
        lax.all_gather(w_out_attn, "tile", axis=1, tiled=True),
        preferred_element_type=jnp.float32,
    )
    term = term + jnp.einsum(
        "rbsk,kd->rbsd",
        mlp_act,
        lax.all_gather(w_out_mlp, "tile", axis=1, tiled=True),
        preferred_element_type=jnp.float32,
    )
    proj = lax.psum_scatter(term, "head", scatter_dimension=2, tiled=True)
    updated = stream.astype(jnp.float32) + gate_mod[:, None, None, :] * (proj + bias_out)
    hidden_out = updated.astype(jnp.bfloat16)
    image = updated[:, 1:]
    center = image - jnp.mean(image, axis=-1, keepdims=True)
    variance = jnp.mean(center * center, axis=-1, keepdims=True)
    normed = center * lax.rsqrt(variance + 1e-06)
    modulated = (
        (1.0 + final_scale[:, None, None, :]) * normed + final_shift[:, None, None, :]
    ).astype(jnp.bfloat16)
    velocity = (
        jnp.einsum("rbsd,dc->rbsc", modulated, w_final, preferred_element_type=jnp.float32)
        + b_final
    )
    latent_next = latent + step_size[:, None, None, None] * velocity
    return (hidden_out, latent_next)


EPS = 1e-06
SCALE = math.log2(math.e) / math.sqrt(HEAD_DIM)
VMEM = 60 * 1024 * 1024
NT = (((1,), (1,)), ((), ()))


def fits(sizes):
    return sizes["head"] == 2 and sizes["tile"] == 2 * len(PATH)


def rotary(positions, gain):
    cosine, sine = rope_tables(positions)
    rows = cosine.shape[0] * cosine.shape[1]
    cosine = jnp.repeat(cosine.reshape(rows, HEAD_DIM // 2), 2, axis=1)
    sine = jnp.repeat(sine.reshape(rows, HEAD_DIM // 2), 2, axis=1)
    odd = jnp.arange(HEAD_DIM) % 2 == 1
    partner = jnp.where(odd, jnp.roll(gain, 1), -jnp.roll(gain, -1))
    return cosine * gain, sine * partner


def attend_kernel(half_ref, own_ref, far_ref, cq_ref, sq_ref, ck_ref, sk_ref, swap_ref, mask_ref, out_ref):
    rows = own_ref.shape[0] * own_ref.shape[2]

    def load(part):
        return jnp.concatenate(
            [own_ref[:, part].reshape(rows, HEAD_DIM), far_ref[:, part].reshape(rows, HEAD_DIM)], axis=0
        )

    def turn(raw, straight, crossed):
        wide = raw.astype(jnp.float32)
        scale = lax.rsqrt(jnp.mean(wide * wide, axis=-1, keepdims=True) + EPS)
        partner = jnp.dot(raw, swap_ref[...], preferred_element_type=jnp.float32)
        return ((wide * straight + partner * crossed) * scale).astype(jnp.bfloat16)

    queries = turn(load(0), cq_ref[...], sq_ref[...])
    keys = turn(load(1), ck_ref[...], sk_ref[...])
    scores = lax.dot_general(queries, keys, NT, preferred_element_type=jnp.float32)
    scores = scores * SCALE + mask_ref[...]
    weights = jnp.exp2(scores - jnp.max(scores, axis=-1, keepdims=True))
    total = jnp.sum(weights, axis=-1, keepdims=True)
    mixed = jnp.dot(weights.astype(jnp.bfloat16), load(2), preferred_element_type=jnp.float32)
    out_ref[...] = (mixed / total).astype(jnp.bfloat16)


def attend(half, own, far, tables, mask):
    blocks, parts, slots, width = far.shape
    heads = width // HEAD_DIM
    rows = 2 * blocks * slots
    order = jnp.arange(HEAD_DIM)
    swap = (order[:, None] == (order ^ 1)[None, :]).astype(jnp.bfloat16)
    shape = (blocks, parts, slots, HEAD_DIM)
    whole = pl.BlockSpec((rows, HEAD_DIM), lambda g, half: (0, 0))
    return pl.pallas_call(
        attend_kernel,
        grid_spec=pltpu.PrefetchScalarGridSpec(
            num_scalar_prefetch=1,
            grid=(heads,),
            in_specs=[
                pl.BlockSpec(shape, lambda g, half: (0, 0, 0, half[0] * heads + g)),
                pl.BlockSpec(shape, lambda g, half: (0, 0, 0, g)),
                whole,
                whole,
                whole,
                whole,
                pl.BlockSpec((HEAD_DIM, HEAD_DIM), lambda g, half: (0, 0)),
                pl.BlockSpec((1, rows), lambda g, half: (0, 0)),
            ],
            out_specs=pl.BlockSpec((rows, HEAD_DIM), lambda g, half: (0, g)),
        ),
        out_shape=jax.ShapeDtypeStruct((rows, width), jnp.bfloat16),
        compiler_params=pltpu.CompilerParams(vmem_limit_bytes=VMEM),
        cost_estimate=pl.CostEstimate(
            flops=heads * rows * rows * HEAD_DIM * 4,
            bytes_accessed=rows * width * 8,
            transcendentals=0,
        ),
        name="attend",
    )(half, own, far, *tables, swap, mask)


def gelu_kernel(part_ref, units_ref, *refs):
    refs[-1][...] = jax.nn.gelu(units_ref[0].astype(jnp.float32), approximate=True).astype(jnp.bfloat16)


def activate(part, units, width, into=None):
    blocks, slots, _ = units.shape
    first = 0 if into is None else blocks
    return pl.pallas_call(
        gelu_kernel,
        grid_spec=pltpu.PrefetchScalarGridSpec(
            num_scalar_prefetch=1,
            grid=(blocks,),
            in_specs=[pl.BlockSpec((1, slots, width), lambda b, part: (b, 0, part[0]))]
            + ([] if into is None else [pl.BlockSpec(memory_space=pl.ANY)]),
            out_specs=pl.BlockSpec((slots, width), lambda b, part: (first + b, 0)),
        ),
        out_shape=jax.ShapeDtypeStruct((2 * blocks * slots, width), jnp.bfloat16),
        input_output_aliases={} if into is None else {2: 0},
        compiler_params=pltpu.CompilerParams(vmem_limit_bytes=VMEM),
        cost_estimate=pl.CostEstimate(
            flops=blocks * slots * width * 4, bytes_accessed=blocks * slots * width, transcendentals=0
        ),
        name="activate",
    )(part, units, *([] if into is None else [into]))


def project_kernel(layout, core_ref, attn_ref, act_ref, *refs):
    *pieces, own_ref, far_ref, x_ref, w_ref, sems = refs
    depth = attn_ref.shape[1]
    rows, columns = own_ref.shape
    core = core_ref[0]
    copies = [
        pltpu.make_async_copy(attn_ref, x_ref.at[:, :depth], sems.at[0]),
        pltpu.make_async_copy(act_ref, x_ref.at[:, depth:], sems.at[1]),
    ]
    for (base, here, share), piece in zip(layout, pieces):
        start = base + (core if here else 1 - core) * share
        place = pl.ds(pl.multiple_of(start, 16), piece.shape[0])
        copies.append(pltpu.make_async_copy(piece, w_ref.at[place], sems.at[len(copies)]))
    for copy in copies:
        copy.start()
    pending = [0, 0] + [base // (2 * share) * 2 * share for base, _, share in layout]
    for first in range(0, columns, 256):
        end = min(first + 256, columns)
        while pending and pending[0] < end:
            copies[-len(pending)].wait()
            pending.pop(0)
        total = lax.dot_general(x_ref[...], w_ref[first:end], NT, preferred_element_type=jnp.float32)
        own_ref[:, first:end] = total[:rows]
        far_ref[:, first:end] = total[rows:].astype(jnp.bfloat16)


def project(core, attn, act, chips):
    share = sum(piece.shape[0] for here, _, piece in chips[0] if here)
    layout, flat = [], []
    for index, pieces in enumerate(chips):
        for here, first, piece in pieces:
            layout.append((2 * share * index + first, here, share))
            flat.append(piece)
    rows, depth = attn.shape[0] // 2, attn.shape[1] + act.shape[1]
    columns = 2 * share * len(chips)
    anywhere = pl.BlockSpec(memory_space=pl.ANY)
    return pl.pallas_call(
        functools.partial(project_kernel, layout),
        in_specs=[pl.BlockSpec(memory_space=pltpu.SMEM), anywhere, anywhere] + [anywhere] * len(flat),
        out_specs=[pl.BlockSpec(memory_space=pltpu.VMEM)] * 2,
        out_shape=[
            jax.ShapeDtypeStruct((rows, columns), jnp.float32),
            jax.ShapeDtypeStruct((rows, columns), jnp.bfloat16),
        ],
        scratch_shapes=[
            pltpu.VMEM((2 * rows, depth), jnp.bfloat16),
            pltpu.VMEM((columns, depth), jnp.bfloat16),
            pltpu.SemaphoreType.DMA((2 + len(flat),)),
        ],
        compiler_params=pltpu.CompilerParams(vmem_limit_bytes=VMEM),
        cost_estimate=pl.CostEstimate(
            flops=rows * columns * depth // 2, bytes_accessed=columns * depth // 4, transcendentals=0
        ),
        name="project",
    )(core, attn, act, *flat)


def finish_kernel(chunks, slot_ref, step_ref, *refs):
    pairs = [refs[2 * i : 2 * i + 2] for i in range(chunks)]
    (
        stream_ref, bias_ref, gate_ref, scale_ref, shift_ref, w_ref, b_ref, latent_ref, hidden_ref, next_ref,
        proj_ref, sums_ref,
    ) = refs[2 * chunks :]
    slots, width = proj_ref.shape
    start = 0
    for own_ref, far_ref in pairs:
        size = own_ref.shape[1]
        sums_ref[:, start : start + size] = own_ref[...] + far_ref[...].astype(jnp.float32)
        start += size
    chip = width // len(PATH)
    for index in range(len(PATH)):
        source = pl.ds(pl.multiple_of(chip * slot_ref[index], 128), chip)
        proj_ref[:, chip * index : chip * (index + 1)] = sums_ref[:, source]
    updated = stream_ref[0].astype(jnp.float32) + gate_ref[...] * (proj_ref[...] + bias_ref[...])
    hidden_ref[0] = updated.astype(jnp.bfloat16)

    @pl.when(pl.program_id(0) > 0)
    def _():
        center = updated - jnp.mean(updated, axis=-1, keepdims=True)
        variance = jnp.mean(center * center, axis=-1, keepdims=True)
        normed = center * lax.rsqrt(variance + EPS)
        modulated = ((1.0 + scale_ref[...]) * normed + shift_ref[...]).astype(jnp.bfloat16)
        velocity = lax.dot_general(w_ref[...], modulated, NT, preferred_element_type=jnp.float32)
        next_ref[0] = latent_ref[0] + step_ref[0] * (velocity + b_ref[...])


def finish(slot, step, chunks, stream, bias, gate, scale, shift, w_final, b_final, latent):
    blocks, slots, width = stream.shape
    channels = w_final.shape[0]
    flat = [array for pair in chunks for array in pair]

    def whole(array):
        return pl.BlockSpec(array.shape, lambda b, *_: (0, 0))

    tokens = pl.BlockSpec((1, slots, width), lambda b, *_: (b, 0, 0))
    image = pl.BlockSpec((1, channels, slots), lambda b, *_: (jnp.maximum(b - 1, 0), 0, 0))
    return pl.pallas_call(
        functools.partial(finish_kernel, len(chunks)),
        grid_spec=pltpu.PrefetchScalarGridSpec(
            num_scalar_prefetch=2,
            grid=(blocks,),
            in_specs=[pl.BlockSpec((slots, array.shape[1]), lambda b, *_: (b, 0)) for array in flat]
            + [
                tokens,
                whole(bias),
                whole(gate),
                whole(scale),
                whole(shift),
                whole(w_final),
                whole(b_final),
                image,
            ],
            out_specs=[tokens, image],
            scratch_shapes=[
                pltpu.VMEM((slots, width), jnp.float32),
                pltpu.VMEM((slots, width), jnp.float32),
            ],
        ),
        out_shape=[
            jax.ShapeDtypeStruct(stream.shape, jnp.bfloat16),
            jax.ShapeDtypeStruct(latent.shape, jnp.float32),
        ],
        compiler_params=pltpu.CompilerParams(vmem_limit_bytes=VMEM),
        cost_estimate=pl.CostEstimate(
            flops=blocks * slots * width * 160, bytes_accessed=blocks * slots * width * 10, transcendentals=0
        ),
        name="finish",
    )(slot, step, *flat, stream, bias, gate, scale, shift, w_final, b_final, latent)


PATH = (0, 1, 3, 5, 7, 6, 4, 2)


def hop(array, by):
    places = len(PATH)
    pairs = [(2 * PATH[i] + c, 2 * PATH[(i + by) % places] + c) for i in range(places) for c in range(2)]
    return lax.ppermute(array, "tile", pairs)


def both_cores(array, first=0):
    other = lax.ppermute(array, "tile", [(t, t ^ 1) for t in range(2 * len(PATH))])
    return [(True, first, array), (False, first, other)]


def paired(
    partners,
    attn_proj,
    mlp_proj,
    stream,
    text_len,
    q_gain,
    k_gain,
    w_out_attn,
    w_out_mlp,
    bias_out,
    gate_mod,
    final_shift,
    final_scale,
    w_final,
    b_final,
    latent,
    step_size,
):
    me = lax.axis_index("head")
    half = me[None].astype(jnp.int32)
    trade = functools.partial(lax.ppermute, axis_name="head", perm=[(0, 1), (1, 0)])

    core = (lax.axis_index("tile") % 2)[None].astype(jnp.int32)
    own_attn = jnp.transpose(attn_proj[0], (0, 2, 1, 3))
    own_units = mlp_proj[0]
    slots = own_attn.shape[2]
    units = own_units.shape[2] // partners
    width = own_attn.shape[3] // partners
    sent_attn = lax.dynamic_slice_in_dim(own_attn, (1 - me) * width, width, axis=3)
    sent_attn, attn_w, act_w = lax.optimization_barrier((sent_attn, w_out_attn.T, w_out_mlp.T))
    far_attn = trade(sent_attn)
    block = jnp.concatenate([attn_w, act_w], axis=1)

    onward, back = hop(block, 1), hop(block, -1)
    chips = [both_cores(block)]

    positions = jnp.arange(slots, dtype=jnp.int32)
    near, away = me * slots + positions, (1 - me) * slots + positions

    def both(gain):
        return [jnp.concatenate(pair, axis=0) for pair in zip(rotary(near, gain), rotary(away, gain))]

    text = jnp.concatenate([near, jnp.full(2 * slots, -1), away, jnp.full(2 * slots, -1)])
    mask = jnp.where(text < text_len[0], 0.0, -jnp.inf)[None, :].astype(jnp.float32)
    tables = both(q_gain) + both(k_gain)
    act_near = activate(half, own_units, units)
    sent_units = lax.dynamic_slice_in_dim(own_units, (1 - me) * units, units, axis=2)

    tile = lax.axis_index("tile")
    place = jnp.array([PATH.index(chip) for chip in range(len(PATH))], jnp.int32)
    behind = (place[tile // 2] - place) % len(PATH)
    slot = jnp.array([0, 1, 3, 5, 7, 6, 4, 2], jnp.int32)[behind]

    onward, back, tables, mask, act_near, sent_units, slot, chips = lax.optimization_barrier(
        (onward, back, tables, mask, act_near, sent_units, slot, [[piece[2] for piece in chip] for chip in chips])
    )
    chips = [[(True, 0, chip[0]), (False, 0, chip[1])] for chip in chips]
    chips += [both_cores(onward), both_cores(back)]
    onward, back = hop(onward, 1), hop(back, -1)
    far_attn, sent_units, mask = lax.optimization_barrier((far_attn, sent_units, mask))
    far_units = trade(sent_units)
    attn = attend(half, own_attn, far_attn, tables, mask)
    attn, onward, back = lax.optimization_barrier((attn, onward, back))
    chips += [both_cores(onward), both_cores(back)]
    onward, back = hop(onward, 1), hop(back, -1)
    far_units, attn = lax.optimization_barrier((far_units, attn))
    act = activate(jnp.zeros_like(half), far_units, units, act_near)

    chunks = []

    def send(group):
        own, sent = project(core, attn, act, group)
        chunks.append((own, trade(sent)))
        return sent

    sent = send(chips[0:3])
    onward, back, attn, sent = lax.optimization_barrier((onward, back, attn, sent))
    middle = block.shape[0] // 2
    last = hop(onward[:middle], 1), hop(back[middle:], -1)
    chips += [both_cores(onward), both_cores(back)]
    sent = send(chips[3:5])
    attn, sent, chunks[0] = lax.optimization_barrier((attn, sent, chunks[0]))
    sent = send(chips[5:7])
    onward, back, attn, sent, chunks[1] = lax.optimization_barrier((*last, attn, sent, chunks[1]))
    chips.append(both_cores(onward) + both_cores(back, middle))
    send(chips[7:8])

    hidden, following = finish(
        slot,
        step_size,
        chunks,
        stream[0],
        bias_out[None, :],
        gate_mod,
        final_scale,
        final_shift,
        w_final.T,
        b_final[:, None],
        jnp.transpose(latent[0], (0, 2, 1)),
    )
    return hidden[None], jnp.transpose(following, (0, 2, 1))[None]


def solution(mesh):
    placed = (
        P("tile", None, "head", None, None),
        P("tile", None, "head", None),
        P("tile", None, "head", None),
        P("tile"),
        P(),
        P(),
        P("head", "tile"),
        P("head", "tile"),
        P(),
        P("tile", None),
        P("tile", None),
        P("tile", None),
        P(),
        P(),
        P("tile", None, "head", None),
        P("tile"),
    )
    return jax.shard_map(
        functools.partial(paired, mesh.shape["head"]) if fits(mesh.shape) else general,
        mesh=mesh,
        in_specs=placed,
        out_specs=(P("tile", None, "head", None), P("tile", None, "head", None)),
        check_vma=False,
    )
```

```python
import functools
import math

import jax
import jax.numpy as jnp
import numpy as np
from jax import lax
from jax.experimental import pallas as pl
from jax.experimental.pallas import tpu as pltpu
from jax.sharding import PartitionSpec as P

HEAD_DIM = 128
SLOTS = 192
GRID_W = 32


def rope_tables(positions):
    pairs_zero = HEAD_DIM // 16
    pairs_axis = (HEAD_DIM // 2 - pairs_zero) // 2
    freqs = 10000.0 ** (-jnp.arange(pairs_axis, dtype=jnp.float32) / pairs_axis)
    count = positions.shape[0]
    angles = [jnp.zeros((count, HEAD_DIM // 2), jnp.float32)]
    for block in range(1, 3):
        image_index = (block - 1) * SLOTS + positions
        rows = (image_index // GRID_W).astype(jnp.float32)
        columns = (image_index % GRID_W).astype(jnp.float32)
        angles.append(
            jnp.concatenate(
                [
                    jnp.zeros((count, pairs_zero), jnp.float32),
                    rows[:, None] * freqs[None, :],
                    columns[:, None] * freqs[None, :],
                ],
                axis=1,
            )
        )
    stacked = jnp.stack(angles)
    return (jnp.cos(stacked), jnp.sin(stacked))


def prepare(raw, gain, cosine, sine):
    normed = raw * lax.rsqrt(jnp.mean(raw * raw, axis=-1, keepdims=True) + 1e-06) * gain
    halves = normed.reshape(normed.shape[:-1] + (HEAD_DIM // 2, 2))
    first = halves[..., 0]
    second = halves[..., 1]
    cosine = cosine[None, :, :, None, :]
    sine = sine[None, :, :, None, :]
    rotated = jnp.stack([first * cosine - second * sine, first * sine + second * cosine], axis=-1)
    return rotated.reshape(raw.shape).astype(jnp.bfloat16)


def attend_head(inputs):
    queries, keys, values, live = inputs
    scores = jnp.einsum("qd,kd->qk", queries, keys, preferred_element_type=jnp.float32) / math.sqrt(
        HEAD_DIM
    )
    scores = jnp.where(live[None, :], scores, -jnp.inf)
    top = jnp.max(scores, axis=-1, keepdims=True)
    weights = jnp.exp(scores - top)
    total = jnp.sum(weights, axis=-1, keepdims=True)
    mixed = jnp.dot(weights.astype(jnp.bfloat16), values, preferred_element_type=jnp.float32)
    return (mixed / total).astype(jnp.bfloat16)


def attend_request(inputs):
    queries, keys, values, live = inputs
    count = queries.shape[1]
    broad_live = jnp.broadcast_to(live[None, :], (count, live.shape[0]))
    result = lax.map(
        attend_head,
        (
            jnp.moveaxis(queries, 1, 0),
            jnp.moveaxis(keys, 1, 0),
            jnp.moveaxis(values, 1, 0),
            broad_live,
        ),
    )
    return jnp.moveaxis(result, 0, 1)


def general(
    attn_proj,
    mlp_proj,
    stream,
    text_len,
    q_gain,
    k_gain,
    w_out_attn,
    w_out_mlp,
    bias_out,
    gate_mod,
    final_shift,
    final_scale,
    w_final,
    b_final,
    latent,
    step_size,
):
    requests = attn_proj.shape[0]
    own_slots = attn_proj.shape[2]
    width = attn_proj.shape[4]
    heads = width // HEAD_DIM
    start_slot = lax.axis_index("head") * own_slots
    positions = start_slot + jnp.arange(own_slots, dtype=jnp.int32)
    cosine, sine = rope_tables(positions)
    head_shape = (requests, 3, own_slots, heads, HEAD_DIM)
    queries = prepare(
        attn_proj[:, :, :, 0].astype(jnp.float32).reshape(head_shape), q_gain, cosine, sine
    )
    keys = prepare(
        attn_proj[:, :, :, 1].astype(jnp.float32).reshape(head_shape), k_gain, cosine, sine
    )
    packed = jnp.stack(
        [
            queries.reshape(requests, 3, own_slots, width),
            keys.reshape(requests, 3, own_slots, width),
            attn_proj[:, :, :, 2],
        ],
        axis=3,
    )
    units = mlp_proj[:, :, :, None, :]
    moved, hidden_units = (
        lax.all_to_all(packed, "head", split_axis=4, concat_axis=2, tiled=True),
        lax.all_to_all(units, "head", split_axis=4, concat_axis=2, tiled=True),
    )
    hidden_units = hidden_units[:, :, :, 0]
    tile_slots = moved.shape[2]
    local_width = moved.shape[4]
    local_heads = local_width // HEAD_DIM
    flat_shape = (requests, 3 * tile_slots, local_heads, HEAD_DIM)
    all_positions = jnp.arange(tile_slots, dtype=jnp.int32)
    text_live = all_positions[None, :] < text_len[:, None]
    image_live = jnp.ones_like(text_live)
    live = jnp.stack([text_live, image_live, image_live], axis=1).reshape(requests, 3 * tile_slots)
    attn_out = lax.map(
        attend_request,
        (
            moved[:, :, :, 0].reshape(flat_shape),
            moved[:, :, :, 1].reshape(flat_shape),
            moved[:, :, :, 2].reshape(flat_shape),
            live,
        ),
    )
    attn_out = attn_out.reshape(requests, 3, tile_slots, local_width)
    mlp_act = jax.nn.gelu(hidden_units.astype(jnp.float32), approximate=True).astype(jnp.bfloat16)
    term = jnp.einsum(
        "rbsk,kd->rbsd",
        attn_out,
        lax.all_gather(w_out_attn, "tile", axis=1, tiled=True),
        preferred_element_type=jnp.float32,
    )
    term = term + jnp.einsum(
        "rbsk,kd->rbsd",
        mlp_act,
        lax.all_gather(w_out_mlp, "tile", axis=1, tiled=True),
        preferred_element_type=jnp.float32,
    )
    proj = lax.psum_scatter(term, "head", scatter_dimension=2, tiled=True)
    updated = stream.astype(jnp.float32) + gate_mod[:, None, None, :] * (proj + bias_out)
    hidden_out = updated.astype(jnp.bfloat16)
    image = updated[:, 1:]
    center = image - jnp.mean(image, axis=-1, keepdims=True)
    variance = jnp.mean(center * center, axis=-1, keepdims=True)
    normed = center * lax.rsqrt(variance + 1e-06)
    modulated = (
        (1.0 + final_scale[:, None, None, :]) * normed + final_shift[:, None, None, :]
    ).astype(jnp.bfloat16)
    velocity = (
        jnp.einsum("rbsd,dc->rbsc", modulated, w_final, preferred_element_type=jnp.float32)
        + b_final
    )
    latent_next = latent + step_size[:, None, None, None] * velocity
    return (hidden_out, latent_next)


EPS = 1e-06
SCALE = math.log2(math.e) / math.sqrt(HEAD_DIM)
VMEM = 60 * 1024 * 1024
NT = (((1,), (1,)), ((), ()))


def fits(sizes):
    return sizes["head"] == 2 and sizes["tile"] == 2 * len(PATH)


def tables_kernel(half_ref, len_ref, row_freq_ref, col_freq_ref, q_ref, k_ref, cq_ref, sq_ref, ck_ref, sk_ref, mask_ref, swap_ref):
    rows = cq_ref.shape[0]
    slots = rows // 6

    def place(axis, shape):
        index = lax.broadcasted_iota(jnp.int32, shape, axis)
        away = index >= rows // 2
        block = (index - jnp.where(away, rows // 2, 0)) // slots
        slot = index % slots + slots * jnp.where(away, 1 - half_ref[0], half_ref[0])
        return block, slot

    shape = (rows, HEAD_DIM)
    block, slot = place(0, shape)
    image = (block - 1) * SLOTS + slot
    angle = (image // GRID_W).astype(jnp.float32) * row_freq_ref[...]
    angle += (image % GRID_W).astype(jnp.float32) * col_freq_ref[...]
    angle = jnp.where(block == 0, 0.0, angle)
    cosine, sine = jnp.cos(angle), jnp.sin(angle)
    odd = lax.broadcasted_iota(jnp.int32, shape, 1) % 2 == 1
    for gain_ref, c_ref, s_ref in ((q_ref, cq_ref, sq_ref), (k_ref, ck_ref, sk_ref)):
        gain = jnp.broadcast_to(gain_ref[...], shape)
        partner = jnp.where(odd, pltpu.roll(gain, 1, 1), -pltpu.roll(gain, HEAD_DIM - 1, 1))
        c_ref[...] = cosine * gain
        s_ref[...] = sine * partner
    block, slot = place(1, (1, rows))
    mask_ref[...] = jnp.where((block > 0) | (slot < len_ref[0]), 0.0, -jnp.inf)
    square = (HEAD_DIM, HEAD_DIM)
    column = lax.broadcasted_iota(jnp.int32, square, 1)
    other = column + 1 - 2 * (column % 2)
    swap_ref[...] = jnp.where(lax.broadcasted_iota(jnp.int32, square, 0) == other, 1.0, 0.0).astype(jnp.bfloat16)


def make_tables(half, text_len, q_gain, k_gain, rows):
    pairs_zero = HEAD_DIM // 16
    pairs_axis = (HEAD_DIM // 2 - pairs_zero) // 2
    freqs = 10000.0 ** (-np.arange(pairs_axis, dtype=np.float32) / np.float32(pairs_axis))
    row_freq, col_freq = np.zeros((2, 1, HEAD_DIM // 2), np.float32)
    row_freq[0, pairs_zero : pairs_zero + pairs_axis] = freqs
    col_freq[0, pairs_zero + pairs_axis :] = freqs
    scalars = pl.BlockSpec(memory_space=pltpu.SMEM)
    table = jax.ShapeDtypeStruct((rows, HEAD_DIM), jnp.float32)
    return pl.pallas_call(
        tables_kernel,
        in_specs=[scalars, scalars] + [pl.BlockSpec(memory_space=pltpu.VMEM)] * 4,
        out_shape=[
            table,
            table,
            table,
            table,
            jax.ShapeDtypeStruct((1, rows), jnp.float32),
            jax.ShapeDtypeStruct((HEAD_DIM, HEAD_DIM), jnp.bfloat16),
        ],
        compiler_params=pltpu.CompilerParams(vmem_limit_bytes=VMEM),
        cost_estimate=pl.CostEstimate(flops=rows * HEAD_DIM * 8, bytes_accessed=rows * HEAD_DIM * 4, transcendentals=0),
        name="tables",
    )(
        half,
        text_len,
        np.repeat(row_freq, 2, axis=1),
        np.repeat(col_freq, 2, axis=1),
        q_gain[None, :],
        k_gain[None, :],
    )


def attend_kernel(half_ref, own_ref, far_ref, cq_ref, sq_ref, ck_ref, sk_ref, mask_ref, swap_ref, out_ref):
    rows = own_ref.shape[0] * own_ref.shape[2]

    def load(part):
        return jnp.concatenate(
            [own_ref[:, part].reshape(rows, HEAD_DIM), far_ref[:, part].reshape(rows, HEAD_DIM)], axis=0
        )

    def turn(raw, straight, crossed):
        wide = raw.astype(jnp.float32)
        scale = lax.rsqrt(jnp.mean(wide * wide, axis=-1, keepdims=True) + EPS)
        partner = jnp.dot(raw, swap_ref[...], preferred_element_type=jnp.float32)
        return ((wide * straight + partner * crossed) * scale).astype(jnp.bfloat16)

    queries = turn(load(0), cq_ref[...], sq_ref[...])
    keys = turn(load(1), ck_ref[...], sk_ref[...])
    scores = lax.dot_general(queries, keys, NT, preferred_element_type=jnp.float32)
    scores = scores * SCALE + mask_ref[...]
    weights = jnp.exp2(scores - jnp.max(scores, axis=-1, keepdims=True))
    total = jnp.sum(weights, axis=-1, keepdims=True)
    mixed = jnp.dot(weights.astype(jnp.bfloat16), load(2), preferred_element_type=jnp.float32)
    out_ref[...] = (mixed / total).astype(jnp.bfloat16)


def attend(half, own, far, tables):
    blocks, parts, slots, width = far.shape
    heads = width // HEAD_DIM
    rows = 2 * blocks * slots
    shape = (blocks, parts, slots, HEAD_DIM)
    whole = pl.BlockSpec((rows, HEAD_DIM), lambda g, half: (0, 0))
    return pl.pallas_call(
        attend_kernel,
        grid_spec=pltpu.PrefetchScalarGridSpec(
            num_scalar_prefetch=1,
            grid=(heads,),
            in_specs=[
                pl.BlockSpec(shape, lambda g, half: (0, 0, 0, half[0] * heads + g)),
                pl.BlockSpec(shape, lambda g, half: (0, 0, 0, g)),
                whole,
                whole,
                whole,
                whole,
                pl.BlockSpec((1, rows), lambda g, half: (0, 0)),
                pl.BlockSpec((HEAD_DIM, HEAD_DIM), lambda g, half: (0, 0)),
            ],
            out_specs=pl.BlockSpec((rows, HEAD_DIM), lambda g, half: (0, g)),
        ),
        out_shape=jax.ShapeDtypeStruct((rows, width), jnp.bfloat16),
        compiler_params=pltpu.CompilerParams(vmem_limit_bytes=VMEM),
        cost_estimate=pl.CostEstimate(
            flops=heads * rows * rows * HEAD_DIM * 4,
            bytes_accessed=rows * width * 8,
            transcendentals=0,
        ),
        name="attend",
    )(half, own, far, *tables)


def gelu_kernel(part_ref, units_ref, *refs):
    refs[-1][...] = jax.nn.gelu(units_ref[0].astype(jnp.float32), approximate=True).astype(jnp.bfloat16)


def activate(part, units, width, into=None):
    blocks, slots, _ = units.shape
    first = 0 if into is None else blocks
    return pl.pallas_call(
        gelu_kernel,
        grid_spec=pltpu.PrefetchScalarGridSpec(
            num_scalar_prefetch=1,
            grid=(blocks,),
            in_specs=[pl.BlockSpec((1, slots, width), lambda b, part: (b, 0, part[0]))]
            + ([] if into is None else [pl.BlockSpec(memory_space=pl.ANY)]),
            out_specs=pl.BlockSpec((slots, width), lambda b, part: (first + b, 0)),
        ),
        out_shape=jax.ShapeDtypeStruct((2 * blocks * slots, width), jnp.bfloat16),
        input_output_aliases={} if into is None else {2: 0},
        compiler_params=pltpu.CompilerParams(vmem_limit_bytes=VMEM),
        cost_estimate=pl.CostEstimate(
            flops=blocks * slots * width * 4, bytes_accessed=blocks * slots * width, transcendentals=0
        ),
        name="activate",
    )(part, units, *([] if into is None else [into]))


def project_kernel(layout, sides, core_ref, attn_ref, act_ref, *refs):
    pieces, outs = refs[: len(layout)], refs[len(layout) : -3]
    x_ref, w_ref, sems = refs[-3:]
    depth = attn_ref.shape[1]
    rows, columns = outs[0].shape
    taken = pl.ds(rows * sides[0], rows * len(sides))
    core = core_ref[0]
    copies = [
        pltpu.make_async_copy(attn_ref.at[taken], x_ref.at[:, :depth], sems.at[0]),
        pltpu.make_async_copy(act_ref.at[taken], x_ref.at[:, depth:], sems.at[1]),
    ]
    for (base, here, share), piece in zip(layout, pieces):
        start = base + (core if here else 1 - core) * share
        place = pl.ds(pl.multiple_of(start, 16), piece.shape[0])
        copies.append(pltpu.make_async_copy(piece, w_ref.at[place], sems.at[len(copies)]))
    for copy in copies:
        copy.start()
    pending = [0, 0] + [base // (2 * share) * 2 * share for base, _, share in layout]
    for first in range(0, columns, 256):
        end = min(first + 256, columns)
        while pending and pending[0] < end:
            copies[-len(pending)].wait()
            pending.pop(0)
        total = lax.dot_general(x_ref[...], w_ref[first:end], NT, preferred_element_type=jnp.float32)
        for index, out_ref in enumerate(outs):
            out_ref[:, first:end] = total[rows * index : rows * (index + 1)].astype(out_ref.dtype)


def project(core, attn, act, chips, sides=(0, 1)):
    share = sum(piece.shape[0] for here, _, piece in chips[0] if here)
    layout, flat = [], []
    for index, pieces in enumerate(chips):
        for here, first, piece in pieces:
            layout.append((2 * share * index + first, here, share))
            flat.append(piece)
    rows, depth = attn.shape[0] // 2, attn.shape[1] + act.shape[1]
    columns = 2 * share * len(chips)
    anywhere = pl.BlockSpec(memory_space=pl.ANY)
    return pl.pallas_call(
        functools.partial(project_kernel, layout, sides),
        in_specs=[pl.BlockSpec(memory_space=pltpu.SMEM), anywhere, anywhere] + [anywhere] * len(flat),
        out_specs=[pl.BlockSpec(memory_space=pltpu.VMEM)] * len(sides),
        out_shape=[jax.ShapeDtypeStruct((rows, columns), (jnp.float32, jnp.bfloat16)[side]) for side in sides],
        scratch_shapes=[
            pltpu.VMEM((len(sides) * rows, depth), jnp.bfloat16),
            pltpu.VMEM((columns, depth), jnp.bfloat16),
            pltpu.SemaphoreType.DMA((2 + len(flat),)),
        ],
        compiler_params=pltpu.CompilerParams(vmem_limit_bytes=VMEM),
        cost_estimate=pl.CostEstimate(
            flops=len(sides) * rows * columns * depth // 4, bytes_accessed=columns * depth // 4, transcendentals=0
        ),
        name="project",
    )(core, attn, act, *flat)


def finish_kernel(chunks, tile_ref, place_ref, step_ref, *refs):
    pairs = [refs[2 * i : 2 * i + 2] for i in range(chunks)]
    (
        stream_ref, bias_ref, gate_ref, scale_ref, shift_ref, w_ref, b_ref, latent_ref, hidden_ref, next_ref, proj_ref,
    ) = refs[2 * chunks :]
    places = len(PATH)
    chip = proj_ref.shape[1] // places
    mine = place_ref[places + tile_ref[0] // 2]
    behind = [0] + [distance for step in range(1, places // 2) for distance in (step, -step)] + [places // 2]
    for own_ref, far_ref in pairs:
        for first in range(0, own_ref.shape[1], chip):
            source = place_ref[(mine - behind.pop(0) + places) % places]
            target = pl.ds(pl.multiple_of(chip * source, 128), chip)
            part = slice(first, first + chip)
            proj_ref[:, target] = own_ref[:, part] + far_ref[:, part].astype(jnp.float32)
    updated = stream_ref[0].astype(jnp.float32) + gate_ref[...] * (proj_ref[...] + bias_ref[...])
    hidden_ref[0] = updated.astype(jnp.bfloat16)

    @pl.when(pl.program_id(0) > 0)
    def _():
        center = updated - jnp.mean(updated, axis=-1, keepdims=True)
        variance = jnp.mean(center * center, axis=-1, keepdims=True)
        normed = center * lax.rsqrt(variance + EPS)
        modulated = ((1.0 + scale_ref[...]) * normed + shift_ref[...]).astype(jnp.bfloat16)
        velocity = lax.dot_general(w_ref[...], modulated, NT, preferred_element_type=jnp.float32)
        next_ref[0] = latent_ref[0] + step_ref[0] * (velocity + b_ref[...])


def finish(tile, step, chunks, stream, bias, gate, scale, shift, w_final, b_final, latent):
    blocks, slots, width = stream.shape
    channels = w_final.shape[0]
    flat = [array for pair in chunks for array in pair]

    def whole(array):
        return pl.BlockSpec(array.shape, lambda b, *_: (0, 0))

    tokens = pl.BlockSpec((1, slots, width), lambda b, *_: (b, 0, 0))
    image = pl.BlockSpec((1, channels, slots), lambda b, *_: (jnp.maximum(b - 1, 0), 0, 0))
    return pl.pallas_call(
        functools.partial(finish_kernel, len(chunks)),
        grid_spec=pltpu.PrefetchScalarGridSpec(
            num_scalar_prefetch=3,
            grid=(blocks,),
            in_specs=[pl.BlockSpec((slots, array.shape[1]), lambda b, *_: (b, 0)) for array in flat]
            + [
                tokens,
                whole(bias),
                whole(gate),
                whole(scale),
                whole(shift),
                whole(w_final),
                whole(b_final),
                image,
            ],
            out_specs=[tokens, image],
            scratch_shapes=[pltpu.VMEM((slots, width), jnp.float32)],
        ),
        out_shape=[
            jax.ShapeDtypeStruct(stream.shape, jnp.bfloat16),
            jax.ShapeDtypeStruct(latent.shape, jnp.float32),
        ],
        compiler_params=pltpu.CompilerParams(vmem_limit_bytes=VMEM),
        cost_estimate=pl.CostEstimate(
            flops=blocks * slots * width * 160, bytes_accessed=blocks * slots * width * 10, transcendentals=0
        ),
        name="finish",
    )(tile, np.array(PATH + PLACE, np.int32), step, *flat, stream, bias, gate, scale, shift, w_final, b_final, latent)


PATH = (0, 1, 3, 5, 7, 6, 4, 2)
PLACE = tuple(PATH.index(chip) for chip in range(len(PATH)))


def hop(array, by):
    places = len(PATH)
    pairs = [(2 * PATH[i] + c, 2 * PATH[(i + by) % places] + c) for i in range(places) for c in range(2)]
    return lax.ppermute(array, "tile", pairs)


def both_cores(array, first=0):
    other = lax.ppermute(array, "tile", [(t, t ^ 1) for t in range(2 * len(PATH))])
    return [(True, first, array), (False, first, other)]


def paired(
    partners,
    attn_proj,
    mlp_proj,
    stream,
    text_len,
    q_gain,
    k_gain,
    w_out_attn,
    w_out_mlp,
    bias_out,
    gate_mod,
    final_shift,
    final_scale,
    w_final,
    b_final,
    latent,
    step_size,
):
    me = lax.axis_index("head")
    half = me[None].astype(jnp.int32)
    trade = functools.partial(lax.ppermute, axis_name="head", perm=[(0, 1), (1, 0)])

    tile = lax.axis_index("tile").astype(jnp.int32)
    core = (tile % 2)[None]
    own_attn = jnp.transpose(attn_proj[0], (0, 2, 1, 3))
    own_units = mlp_proj[0]
    slots = own_attn.shape[2]
    units = own_units.shape[2] // partners
    width = own_attn.shape[3] // partners
    sent_attn = lax.dynamic_slice_in_dim(own_attn, (1 - me) * width, width, axis=3)
    sent_attn, attn_w, act_w = lax.optimization_barrier((sent_attn, w_out_attn.T, w_out_mlp.T))
    far_attn = trade(sent_attn)
    block = jnp.concatenate([attn_w, act_w], axis=1)

    onward, back = hop(block, 1), hop(block, -1)
    chips = [both_cores(block)]

    tables = make_tables(half, text_len, q_gain, k_gain, 6 * slots)
    act_near = activate(half, own_units, units)
    sent_units = lax.dynamic_slice_in_dim(own_units, (1 - me) * units, units, axis=2)

    onward, back, tables, act_near, sent_units, chips = lax.optimization_barrier(
        (onward, back, tables, act_near, sent_units, [[piece[2] for piece in chip] for chip in chips])
    )
    chips = [[(True, 0, chip[0]), (False, 0, chip[1])] for chip in chips]
    chips += [both_cores(onward), both_cores(back)]
    onward, back = hop(onward, 1), hop(back, -1)
    far_attn, sent_units = lax.optimization_barrier((far_attn, sent_units))
    far_units = trade(sent_units)
    attn = attend(half, own_attn, far_attn, tables)
    attn, onward, back = lax.optimization_barrier((attn, onward, back))
    chips += [both_cores(onward), both_cores(back)]
    onward, back = hop(onward, 1), hop(back, -1)
    far_units, attn = lax.optimization_barrier((far_units, attn))
    act = activate(jnp.zeros_like(half), far_units, units, act_near)

    chunks = []

    def send(group):
        own, sent = project(core, attn, act, group)
        chunks.append((own, trade(sent)))
        return sent

    sent = send(chips[0:3])
    onward, back, attn, sent = lax.optimization_barrier((onward, back, attn, sent))
    middle = block.shape[0] // 2
    last = hop(onward[:middle], 1), hop(back[middle:], -1)
    chips += [both_cores(onward), both_cores(back)]
    sent = send(chips[3:5])
    attn, sent, chunks[0] = lax.optimization_barrier((attn, sent, chunks[0]))
    sent = send(chips[5:7])
    onward, back, attn, sent, chunks[1] = lax.optimization_barrier((*last, attn, sent, chunks[1]))
    chips.append(both_cores(onward) + both_cores(back, middle))
    (sent,) = project(core, attn, act, chips[7:8], (1,))
    attn, sent = lax.optimization_barrier((attn, sent))
    far = trade(sent)
    chunks.append((project(core, attn, act, chips[7:8], (0,))[0], far))

    hidden, following = finish(
        tile[None],
        step_size,
        chunks,
        stream[0],
        bias_out[None, :],
        gate_mod,
        final_scale,
        final_shift,
        w_final.T,
        b_final[:, None],
        jnp.transpose(latent[0], (0, 2, 1)),
    )
    return hidden[None], jnp.transpose(following, (0, 2, 1))[None]


def solution(mesh):
    placed = (
        P("tile", None, "head", None, None),
        P("tile", None, "head", None),
        P("tile", None, "head", None),
        P("tile"),
        P(),
        P(),
        P("head", "tile"),
        P("head", "tile"),
        P(),
        P("tile", None),
        P("tile", None),
        P("tile", None),
        P(),
        P(),
        P("tile", None, "head", None),
        P("tile"),
    )
    return jax.shard_map(
        functools.partial(paired, mesh.shape["head"]) if fits(mesh.shape) else general,
        mesh=mesh,
        in_specs=placed,
        out_specs=(P("tile", None, "head", None), P("tile", None, "head", None)),
        check_vma=False,
    )
```

```python
import functools
import math

import jax
import jax.numpy as jnp
import numpy as np
from jax import lax
from jax.experimental import pallas as pl
from jax.experimental.pallas import tpu as pltpu
from jax.sharding import PartitionSpec as P

HEAD_DIM = 128
SLOTS = 192
GRID_W = 32


def rope_tables(positions):
    pairs_zero = HEAD_DIM // 16
    pairs_axis = (HEAD_DIM // 2 - pairs_zero) // 2
    freqs = 10000.0 ** (-jnp.arange(pairs_axis, dtype=jnp.float32) / pairs_axis)
    count = positions.shape[0]
    angles = [jnp.zeros((count, HEAD_DIM // 2), jnp.float32)]
    for block in range(1, 3):
        image_index = (block - 1) * SLOTS + positions
        rows = (image_index // GRID_W).astype(jnp.float32)
        columns = (image_index % GRID_W).astype(jnp.float32)
        angles.append(
            jnp.concatenate(
                [
                    jnp.zeros((count, pairs_zero), jnp.float32),
                    rows[:, None] * freqs[None, :],
                    columns[:, None] * freqs[None, :],
                ],
                axis=1,
            )
        )
    stacked = jnp.stack(angles)
    return (jnp.cos(stacked), jnp.sin(stacked))


def prepare(raw, gain, cosine, sine):
    normed = raw * lax.rsqrt(jnp.mean(raw * raw, axis=-1, keepdims=True) + 1e-06) * gain
    halves = normed.reshape(normed.shape[:-1] + (HEAD_DIM // 2, 2))
    first = halves[..., 0]
    second = halves[..., 1]
    cosine = cosine[None, :, :, None, :]
    sine = sine[None, :, :, None, :]
    rotated = jnp.stack([first * cosine - second * sine, first * sine + second * cosine], axis=-1)
    return rotated.reshape(raw.shape).astype(jnp.bfloat16)


def attend_head(inputs):
    queries, keys, values, live = inputs
    scores = jnp.einsum("qd,kd->qk", queries, keys, preferred_element_type=jnp.float32) / math.sqrt(
        HEAD_DIM
    )
    scores = jnp.where(live[None, :], scores, -jnp.inf)
    top = jnp.max(scores, axis=-1, keepdims=True)
    weights = jnp.exp(scores - top)
    total = jnp.sum(weights, axis=-1, keepdims=True)
    mixed = jnp.dot(weights.astype(jnp.bfloat16), values, preferred_element_type=jnp.float32)
    return (mixed / total).astype(jnp.bfloat16)


def attend_request(inputs):
    queries, keys, values, live = inputs
    count = queries.shape[1]
    broad_live = jnp.broadcast_to(live[None, :], (count, live.shape[0]))
    result = lax.map(
        attend_head,
        (
            jnp.moveaxis(queries, 1, 0),
            jnp.moveaxis(keys, 1, 0),
            jnp.moveaxis(values, 1, 0),
            broad_live,
        ),
    )
    return jnp.moveaxis(result, 0, 1)


def general(
    attn_proj,
    mlp_proj,
    stream,
    text_len,
    q_gain,
    k_gain,
    w_out_attn,
    w_out_mlp,
    bias_out,
    gate_mod,
    final_shift,
    final_scale,
    w_final,
    b_final,
    latent,
    step_size,
):
    requests = attn_proj.shape[0]
    own_slots = attn_proj.shape[2]
    width = attn_proj.shape[4]
    heads = width // HEAD_DIM
    start_slot = lax.axis_index("head") * own_slots
    positions = start_slot + jnp.arange(own_slots, dtype=jnp.int32)
    cosine, sine = rope_tables(positions)
    head_shape = (requests, 3, own_slots, heads, HEAD_DIM)
    queries = prepare(
        attn_proj[:, :, :, 0].astype(jnp.float32).reshape(head_shape), q_gain, cosine, sine
    )
    keys = prepare(
        attn_proj[:, :, :, 1].astype(jnp.float32).reshape(head_shape), k_gain, cosine, sine
    )
    packed = jnp.stack(
        [
            queries.reshape(requests, 3, own_slots, width),
            keys.reshape(requests, 3, own_slots, width),
            attn_proj[:, :, :, 2],
        ],
        axis=3,
    )
    units = mlp_proj[:, :, :, None, :]
    moved, hidden_units = (
        lax.all_to_all(packed, "head", split_axis=4, concat_axis=2, tiled=True),
        lax.all_to_all(units, "head", split_axis=4, concat_axis=2, tiled=True),
    )
    hidden_units = hidden_units[:, :, :, 0]
    tile_slots = moved.shape[2]
    local_width = moved.shape[4]
    local_heads = local_width // HEAD_DIM
    flat_shape = (requests, 3 * tile_slots, local_heads, HEAD_DIM)
    all_positions = jnp.arange(tile_slots, dtype=jnp.int32)
    text_live = all_positions[None, :] < text_len[:, None]
    image_live = jnp.ones_like(text_live)
    live = jnp.stack([text_live, image_live, image_live], axis=1).reshape(requests, 3 * tile_slots)
    attn_out = lax.map(
        attend_request,
        (
            moved[:, :, :, 0].reshape(flat_shape),
            moved[:, :, :, 1].reshape(flat_shape),
            moved[:, :, :, 2].reshape(flat_shape),
            live,
        ),
    )
    attn_out = attn_out.reshape(requests, 3, tile_slots, local_width)
    mlp_act = jax.nn.gelu(hidden_units.astype(jnp.float32), approximate=True).astype(jnp.bfloat16)
    term = jnp.einsum(
        "rbsk,kd->rbsd",
        attn_out,
        lax.all_gather(w_out_attn, "tile", axis=1, tiled=True),
        preferred_element_type=jnp.float32,
    )
    term = term + jnp.einsum(
        "rbsk,kd->rbsd",
        mlp_act,
        lax.all_gather(w_out_mlp, "tile", axis=1, tiled=True),
        preferred_element_type=jnp.float32,
    )
    proj = lax.psum_scatter(term, "head", scatter_dimension=2, tiled=True)
    updated = stream.astype(jnp.float32) + gate_mod[:, None, None, :] * (proj + bias_out)
    hidden_out = updated.astype(jnp.bfloat16)
    image = updated[:, 1:]
    center = image - jnp.mean(image, axis=-1, keepdims=True)
    variance = jnp.mean(center * center, axis=-1, keepdims=True)
    normed = center * lax.rsqrt(variance + 1e-06)
    modulated = (
        (1.0 + final_scale[:, None, None, :]) * normed + final_shift[:, None, None, :]
    ).astype(jnp.bfloat16)
    velocity = (
        jnp.einsum("rbsd,dc->rbsc", modulated, w_final, preferred_element_type=jnp.float32)
        + b_final
    )
    latent_next = latent + step_size[:, None, None, None] * velocity
    return (hidden_out, latent_next)


EPS = 1e-06
SCALE = math.log2(math.e) / math.sqrt(HEAD_DIM)
VMEM = 60 * 1024 * 1024


def cost(flops, size):
    return pl.CostEstimate(flops=flops, bytes_accessed=size, transcendentals=0)
NT = (((1,), (1,)), ((), ()))


def fits(sizes):
    return sizes["head"] == 2 and sizes["tile"] == 2 * len(PATH)


def pack_kernel(half_ref, attn_ref, attn_w_ref, act_w_ref, sent_ref, block_ref):
    depth = attn_w_ref.shape[1]
    sent_ref[...] = attn_ref[...]
    block_ref[:, :depth] = attn_w_ref[...]
    block_ref[:, depth:] = act_w_ref[...]


def pack(half, attn, attn_w, act_w):
    blocks, parts, slots, width = attn.shape
    shape = (1, parts, slots // 2, width // 2)
    share = attn_w.shape[0] // (2 * blocks)

    def rows(depth):
        return pl.BlockSpec((share, depth), lambda b, s, half: (2 * b + s, 0))

    depth = attn_w.shape[1] + act_w.shape[1]
    return pl.pallas_call(
        pack_kernel,
        grid_spec=pltpu.PrefetchScalarGridSpec(
            num_scalar_prefetch=1,
            grid=(blocks, 2),
            in_specs=[
                pl.BlockSpec(shape, lambda b, s, half: (b, 0, s, 1 - half[0])),
                rows(attn_w.shape[1]),
                rows(act_w.shape[1]),
            ],
            out_specs=[pl.BlockSpec(shape, lambda b, s, half: (b, 0, s, 0)), rows(depth)],
        ),
        out_shape=[
            jax.ShapeDtypeStruct((blocks, parts, slots, width // 2), jnp.bfloat16),
            jax.ShapeDtypeStruct((attn_w.shape[0], depth), jnp.bfloat16),
        ],
        compiler_params=pltpu.CompilerParams(vmem_limit_bytes=VMEM),
        cost_estimate=cost(0, 8 * attn_w.size),
        name="pack",
    )(half, attn, attn_w, act_w)


def tables_kernel(half_ref, len_ref, row_freq_ref, col_freq_ref, q_ref, k_ref, cq_ref, sq_ref, ck_ref, sk_ref, mask_ref, swap_ref):
    rows = cq_ref.shape[0]
    slots = rows // 6

    def place(axis, shape):
        index = lax.broadcasted_iota(jnp.int32, shape, axis)
        away = index >= rows // 2
        block = (index - jnp.where(away, rows // 2, 0)) // slots
        slot = index % slots + slots * jnp.where(away, 1 - half_ref[0], half_ref[0])
        return block, slot

    shape = (rows, HEAD_DIM)
    block, slot = place(0, shape)
    image = (block - 1) * SLOTS + slot
    angle = (image // GRID_W).astype(jnp.float32) * row_freq_ref[...]
    angle += (image % GRID_W).astype(jnp.float32) * col_freq_ref[...]
    angle = jnp.where(block == 0, 0.0, angle)
    cosine, sine = jnp.cos(angle), jnp.sin(angle)
    odd = lax.broadcasted_iota(jnp.int32, shape, 1) % 2 == 1
    for gain_ref, c_ref, s_ref in ((q_ref, cq_ref, sq_ref), (k_ref, ck_ref, sk_ref)):
        gain = jnp.broadcast_to(gain_ref[...], shape)
        partner = jnp.where(odd, pltpu.roll(gain, 1, 1), -pltpu.roll(gain, HEAD_DIM - 1, 1))
        c_ref[...] = cosine * gain
        s_ref[...] = sine * partner
    block, slot = place(1, (1, rows))
    mask_ref[...] = jnp.where((block > 0) | (slot < len_ref[0]), 0.0, -jnp.inf)
    square = (HEAD_DIM, HEAD_DIM)
    column = lax.broadcasted_iota(jnp.int32, square, 1)
    other = column + 1 - 2 * (column % 2)
    swap_ref[...] = jnp.where(lax.broadcasted_iota(jnp.int32, square, 0) == other, 1.0, 0.0).astype(jnp.bfloat16)


def make_tables(half, text_len, q_gain, k_gain, rows):
    pairs_zero = HEAD_DIM // 16
    pairs_axis = (HEAD_DIM // 2 - pairs_zero) // 2
    freqs = 10000.0 ** (-np.arange(pairs_axis, dtype=np.float32) / np.float32(pairs_axis))
    row_freq, col_freq = np.zeros((2, 1, HEAD_DIM // 2), np.float32)
    row_freq[0, pairs_zero : pairs_zero + pairs_axis] = freqs
    col_freq[0, pairs_zero + pairs_axis :] = freqs
    scalars = pl.BlockSpec(memory_space=pltpu.SMEM)
    table = jax.ShapeDtypeStruct((rows, HEAD_DIM), jnp.float32)
    return pl.pallas_call(
        tables_kernel,
        in_specs=[scalars, scalars] + [pl.BlockSpec(memory_space=pltpu.VMEM)] * 4,
        out_shape=[
            table,
            table,
            table,
            table,
            jax.ShapeDtypeStruct((1, rows), jnp.float32),
            jax.ShapeDtypeStruct((HEAD_DIM, HEAD_DIM), jnp.bfloat16),
        ],
        compiler_params=pltpu.CompilerParams(vmem_limit_bytes=VMEM),
        cost_estimate=cost(rows * HEAD_DIM * 8, rows * HEAD_DIM * 4),
        name="tables",
    )(
        half,
        text_len,
        np.repeat(row_freq, 2, axis=1),
        np.repeat(col_freq, 2, axis=1),
        q_gain[None, :],
        k_gain[None, :],
    )


def attend_kernel(half_ref, own_ref, far_ref, cq_ref, sq_ref, ck_ref, sk_ref, mask_ref, swap_ref, out_ref):
    rows = own_ref.shape[0] * own_ref.shape[2]

    def load(part):
        return jnp.concatenate(
            [own_ref[:, part].reshape(rows, HEAD_DIM), far_ref[:, part].reshape(rows, HEAD_DIM)], axis=0
        )

    def turn(raw, straight, crossed):
        wide = raw.astype(jnp.float32)
        scale = lax.rsqrt(jnp.mean(wide * wide, axis=-1, keepdims=True) + EPS)
        partner = jnp.dot(raw, swap_ref[...], preferred_element_type=jnp.float32)
        return ((wide * straight + partner * crossed) * scale).astype(jnp.bfloat16)

    queries = turn(load(0), cq_ref[...], sq_ref[...])
    keys = turn(load(1), ck_ref[...], sk_ref[...])
    scores = lax.dot_general(queries, keys, NT, preferred_element_type=jnp.float32)
    scores = scores * SCALE + mask_ref[...]
    weights = jnp.exp2(scores - jnp.max(scores, axis=-1, keepdims=True))
    total = jnp.sum(weights, axis=-1, keepdims=True)
    mixed = jnp.dot(weights.astype(jnp.bfloat16), load(2), preferred_element_type=jnp.float32)
    out_ref[...] = (mixed / total).astype(jnp.bfloat16)


def attend(half, own, far, tables):
    blocks, parts, slots, width = far.shape
    heads = width // HEAD_DIM
    rows = 2 * blocks * slots
    shape = (blocks, parts, slots, HEAD_DIM)
    whole = pl.BlockSpec((rows, HEAD_DIM), lambda g, half: (0, 0))
    return pl.pallas_call(
        attend_kernel,
        grid_spec=pltpu.PrefetchScalarGridSpec(
            num_scalar_prefetch=1,
            grid=(heads,),
            in_specs=[
                pl.BlockSpec(shape, lambda g, half: (0, 0, 0, half[0] * heads + g)),
                pl.BlockSpec(shape, lambda g, half: (0, 0, 0, g)),
                whole,
                whole,
                whole,
                whole,
                pl.BlockSpec((1, rows), lambda g, half: (0, 0)),
                pl.BlockSpec((HEAD_DIM, HEAD_DIM), lambda g, half: (0, 0)),
            ],
            out_specs=pl.BlockSpec((rows, HEAD_DIM), lambda g, half: (0, g)),
        ),
        out_shape=jax.ShapeDtypeStruct((rows, width), jnp.bfloat16),
        compiler_params=pltpu.CompilerParams(vmem_limit_bytes=VMEM),
        cost_estimate=cost(heads * rows * rows * HEAD_DIM * 4, rows * width * 8),
        name="attend",
    )(half, own, far, *tables)


def gelu_kernel(part_ref, units_ref, *refs):
    refs[-1][...] = jax.nn.gelu(units_ref[0].astype(jnp.float32), approximate=True).astype(jnp.bfloat16)


def activate(part, units, width, into=None):
    blocks, slots, _ = units.shape
    first = 0 if into is None else blocks
    return pl.pallas_call(
        gelu_kernel,
        grid_spec=pltpu.PrefetchScalarGridSpec(
            num_scalar_prefetch=1,
            grid=(blocks,),
            in_specs=[pl.BlockSpec((1, slots, width), lambda b, part: (b, 0, part[0]))]
            + ([] if into is None else [pl.BlockSpec(memory_space=pl.ANY)]),
            out_specs=pl.BlockSpec((slots, width), lambda b, part: (first + b, 0)),
        ),
        out_shape=jax.ShapeDtypeStruct((2 * blocks * slots, width), jnp.bfloat16),
        input_output_aliases={} if into is None else {2: 0},
        compiler_params=pltpu.CompilerParams(vmem_limit_bytes=VMEM),
        cost_estimate=cost(blocks * slots * width * 4, blocks * slots * width),
        name="activate",
    )(part, units, *([] if into is None else [into]))


def project_kernel(layout, sides, core_ref, attn_ref, act_ref, *refs):
    pieces, outs = refs[: -3 - len(sides)], refs[-3 - len(sides) : -3]
    x_ref, w_ref, sems = refs[-3:]
    depth = attn_ref.shape[1]
    rows, columns = outs[0].shape
    core = core_ref[0]
    taken = pl.ds(rows * sides[0], rows * len(sides))
    parts = slice(0, depth), slice(depth, x_ref.shape[1])
    lefts, rights = [], []
    for part, source in zip(parts, (attn_ref, act_ref)):
        lefts.append(pltpu.make_async_copy(source.at[taken], x_ref.at[:, part], sems.at[len(lefts)]))
    for base, *choice in layout:
        target = pl.ds(base, pieces[choice[0]].shape[0])
        for part in parts:
            sem = sems.at[len(lefts) + len(rights)]
            rights.append([pltpu.make_async_copy(pieces[i].at[:, part], w_ref.at[target, part], sem) for i in choice])

    def start(copies):
        pl.when(core == 0)(copies[0].start)
        pl.when(core != 0)(copies[1].start)

    ahead = sum(base < 256 for base, *_ in layout)
    early = [rights[2 * index] for index in range(ahead)]
    lefts[0].start()
    for copies in early:
        start(copies)
    lefts[0].wait()
    for copies in early:
        copies[0].wait()
    lefts[1].start()
    for index, copies in enumerate(rights):
        if index >= 2 * ahead or index % 2:
            start(copies)
    waited = 0
    for first in range(0, columns, 256):
        end = min(first + 256, columns)
        total = None
        for half, part in enumerate(parts):
            if first == 0 and half == 1:
                lefts[1].wait()
            if first > 0 or half == 1:
                for index, (base, *_) in enumerate(layout):
                    if waited <= base < end:
                        rights[2 * index + half][0].wait()
            term = lax.dot_general(x_ref[:, part], w_ref[first:end, part], NT, preferred_element_type=jnp.float32)
            total = term if total is None else total + term
        waited = end
        for index, out_ref in enumerate(outs):
            out_ref[:, first:end] = total[rows * index : rows * (index + 1)].astype(out_ref.dtype)


def project(core, attn, act, chips, sides=(0, 1)):
    flat, layout, columns = [], [], 0
    for chip in chips:
        for pair in chip:
            choice = []
            for array in pair:
                known = [index for index, other in enumerate(flat) if other is array]
                choice.append(known[0] if known else len(flat))
                flat += [] if known else [array]
            layout.append((columns, *choice))
            columns += pair[0].shape[0]
    rows, depth = attn.shape[0] // 2, attn.shape[1] + act.shape[1]
    anywhere = pl.BlockSpec(memory_space=pl.ANY)
    return pl.pallas_call(
        functools.partial(project_kernel, layout, sides),
        in_specs=[pl.BlockSpec(memory_space=pltpu.SMEM)] + [anywhere] * (2 + len(flat)),
        out_specs=[pl.BlockSpec(memory_space=pltpu.VMEM)] * len(sides),
        out_shape=[jax.ShapeDtypeStruct((rows, columns), (jnp.float32, jnp.bfloat16)[side]) for side in sides],
        scratch_shapes=[
            pltpu.VMEM((len(sides) * rows, depth), jnp.bfloat16),
            pltpu.VMEM((columns, depth), jnp.bfloat16),
            pltpu.SemaphoreType.DMA((2 + 2 * len(layout),)),
        ],
        compiler_params=pltpu.CompilerParams(vmem_limit_bytes=VMEM),
        cost_estimate=cost(len(sides) * rows * columns * depth // 4, columns * depth // 4),
        name="project",
    )(core, attn, act, *flat)


def finish_kernel(chunks, tile_ref, place_ref, step_ref, *refs):
    pairs = [refs[2 * i : 2 * i + 2] for i in range(chunks)]
    (
        stream_ref, bias_ref, gate_ref, scale_ref, shift_ref, w_ref, b_ref, latent_ref, hidden_ref, next_ref, proj_ref,
    ) = refs[2 * chunks :]
    places = len(PATH)
    chip = proj_ref.shape[1] // places
    mine = place_ref[places + tile_ref[0] // 2]
    behind = [0] + [distance for step in range(1, places // 2) for distance in (step, -step)] + [places // 2]
    for own_ref, far_ref in pairs:
        for first in range(0, own_ref.shape[1], chip):
            source = place_ref[(mine - behind.pop(0) + places) % places]
            target = pl.ds(pl.multiple_of(chip * source, 128), chip)
            part = slice(first, first + chip)
            proj_ref[:, target] = own_ref[:, part] + far_ref[:, part].astype(jnp.float32)
    updated = stream_ref[0].astype(jnp.float32) + gate_ref[...] * (proj_ref[...] + bias_ref[...])
    hidden_ref[0] = updated.astype(jnp.bfloat16)

    @pl.when(pl.program_id(0) > 0)
    def _():
        center = updated - jnp.mean(updated, axis=-1, keepdims=True)
        variance = jnp.mean(center * center, axis=-1, keepdims=True)
        normed = center * lax.rsqrt(variance + EPS)
        modulated = ((1.0 + scale_ref[...]) * normed + shift_ref[...]).astype(jnp.bfloat16)
        velocity = lax.dot_general(w_ref[...], modulated, NT, preferred_element_type=jnp.float32)
        next_ref[0] = latent_ref[0] + step_ref[0] * (velocity + b_ref[...])


def finish(tile, step, chunks, stream, bias, gate, scale, shift, w_final, b_final, latent):
    blocks, slots, width = stream.shape
    channels = w_final.shape[0]
    flat = [array for pair in chunks for array in pair]

    def whole(array):
        return pl.BlockSpec(array.shape, lambda b, *_: (0, 0))

    tokens = pl.BlockSpec((1, slots, width), lambda b, *_: (b, 0, 0))
    image = pl.BlockSpec((1, channels, slots), lambda b, *_: (jnp.maximum(b - 1, 0), 0, 0))
    return pl.pallas_call(
        functools.partial(finish_kernel, len(chunks)),
        grid_spec=pltpu.PrefetchScalarGridSpec(
            num_scalar_prefetch=3,
            grid=(blocks,),
            in_specs=[pl.BlockSpec((slots, array.shape[1]), lambda b, *_: (b, 0)) for array in flat]
            + [
                tokens,
                whole(bias),
                whole(gate),
                whole(scale),
                whole(shift),
                whole(w_final),
                whole(b_final),
                image,
            ],
            out_specs=[tokens, image],
            scratch_shapes=[pltpu.VMEM((slots, width), jnp.float32)],
        ),
        out_shape=[
            jax.ShapeDtypeStruct(stream.shape, jnp.bfloat16),
            jax.ShapeDtypeStruct(latent.shape, jnp.float32),
        ],
        compiler_params=pltpu.CompilerParams(vmem_limit_bytes=VMEM),
        cost_estimate=cost(blocks * slots * width * 160, blocks * slots * width * 10),
        name="finish",
    )(tile, np.array(PATH + PLACE, np.int32), step, *flat, stream, bias, gate, scale, shift, w_final, b_final, latent)


PATH = (0, 1, 3, 5, 7, 6, 4, 2)
PLACE = tuple(PATH.index(chip) for chip in range(len(PATH)))


def hop(array, by, cores=(0, 1)):
    places = len(PATH)
    pairs = [(2 * PATH[i] + c, 2 * PATH[(i + by) % places] + c) for i in range(places) for c in cores]
    return lax.ppermute(array, "tile", pairs)


def across(array, cores=(0, 1)):
    return lax.ppermute(array, "tile", [(2 * chip + c, 2 * chip + 1 - c) for chip in range(len(PATH)) for c in cores])


def spread(array):
    other = across(array)
    return [(array, other), (other, array)]


def paired(
    partners,
    attn_proj,
    mlp_proj,
    stream,
    text_len,
    q_gain,
    k_gain,
    w_out_attn,
    w_out_mlp,
    bias_out,
    gate_mod,
    final_shift,
    final_scale,
    w_final,
    b_final,
    latent,
    step_size,
):
    me = lax.axis_index("head")
    half = me[None].astype(jnp.int32)
    trade = functools.partial(lax.ppermute, axis_name="head", perm=[(0, 1), (1, 0)])

    tile = lax.axis_index("tile").astype(jnp.int32)
    core = (tile % 2)[None]
    own_attn = jnp.transpose(attn_proj[0], (0, 2, 1, 3))
    own_units = mlp_proj[0]
    units = own_units.shape[2] // partners
    units = own_units.shape[2] // partners
    sent_attn, block = pack(half, own_attn, w_out_attn.T, w_out_mlp.T)
    far_attn = trade(sent_attn)
    onward, back = hop(block, 1), hop(block, -1)
    tables = make_tables(half, text_len, q_gain, k_gain, 6 * own_attn.shape[2])
    act_near = activate(half, own_units, units)
    sent_units = lax.dynamic_slice_in_dim(own_units, (1 - me) * units, units, axis=2)

    onward, back, tables, act_near, sent_units, block, other = lax.optimization_barrier(
        (onward, back, tables, act_near, sent_units, block, across(block))
    )
    chips = [[(block, other), (other, block)]]
    chips += [spread(onward), spread(back)]
    onward, back = hop(onward, 1), hop(back, -1)
    far_attn, sent_units = lax.optimization_barrier((far_attn, sent_units))
    far_units = trade(sent_units)
    attn = attend(half, own_attn, far_attn, tables)
    attn, onward, back = lax.optimization_barrier((attn, onward, back))
    chips += [spread(onward), spread(back)]
    onward, back = hop(onward, 1), hop(back, -1)
    far_units, attn, chips = lax.optimization_barrier((far_units, attn, chips))
    act = activate(jnp.zeros_like(half), far_units, units, act_near)

    chunks = []

    def send(group):
        own, sent = project(core, attn, act, group)
        chunks.append([own, trade(sent)])
        return sent

    sent = send(chips[0:3])
    onward, back, attn, sent = lax.optimization_barrier((onward, back, attn, sent))
    onward4, back4 = hop(onward, 1, (0,)), hop(back, -1, (1,))
    chips += [spread(onward), spread(back)]
    sent = send(chips[3:5])
    attn, sent, chunks[0][1] = lax.optimization_barrier((attn, sent, chunks[0][1]))
    sent = send(chips[5:7])
    onward, back, attn, sent, chunks[1][1] = lax.optimization_barrier((onward4, back4, attn, sent, chunks[1][1]))
    chips.append([(onward, across(onward, (0,))), (across(back, (1,)), back)])
    (sent,) = project(core, attn, act, chips[7:8], (1,))
    attn, sent = lax.optimization_barrier((attn, sent))
    far = trade(sent)
    chunks.append((project(core, attn, act, chips[7:8], (0,))[0], far))

    hidden, following = finish(
        tile[None],
        step_size,
        chunks,
        stream[0],
        bias_out[None, :],
        gate_mod,
        final_scale,
        final_shift,
        w_final.T,
        b_final[:, None],
        jnp.transpose(latent[0], (0, 2, 1)),
    )
    return hidden[None], jnp.transpose(following, (0, 2, 1))[None]


def solution(mesh):
    placed = (
        P("tile", None, "head", None, None),
        P("tile", None, "head", None),
        P("tile", None, "head", None),
        P("tile"),
        P(),
        P(),
        P("head", "tile"),
        P("head", "tile"),
        P(),
        P("tile", None),
        P("tile", None),
        P("tile", None),
        P(),
        P(),
        P("tile", None, "head", None),
        P("tile"),
    )
    return jax.shard_map(
        functools.partial(paired, mesh.shape["head"]) if fits(mesh.shape) else general,
        mesh=mesh,
        in_specs=placed,
        out_specs=(P("tile", None, "head", None), P("tile", None, "head", None)),
        check_vma=False,
    )
```

```python
import functools
import math

import jax
import jax.numpy as jnp
import numpy as np
from jax import lax
from jax.experimental import pallas as pl
from jax.experimental.pallas import tpu as pltpu
from jax.sharding import PartitionSpec as P

HEAD_DIM = 128
SLOTS = 192
GRID_W = 32


def rope_tables(positions):
    pairs_zero = HEAD_DIM // 16
    pairs_axis = (HEAD_DIM // 2 - pairs_zero) // 2
    freqs = 10000.0 ** (-jnp.arange(pairs_axis, dtype=jnp.float32) / pairs_axis)
    count = positions.shape[0]
    angles = [jnp.zeros((count, HEAD_DIM // 2), jnp.float32)]
    for block in range(1, 3):
        image_index = (block - 1) * SLOTS + positions
        rows = (image_index // GRID_W).astype(jnp.float32)
        columns = (image_index % GRID_W).astype(jnp.float32)
        angles.append(
            jnp.concatenate(
                [
                    jnp.zeros((count, pairs_zero), jnp.float32),
                    rows[:, None] * freqs[None, :],
                    columns[:, None] * freqs[None, :],
                ],
                axis=1,
            )
        )
    stacked = jnp.stack(angles)
    return (jnp.cos(stacked), jnp.sin(stacked))


def prepare(raw, gain, cosine, sine):
    normed = raw * lax.rsqrt(jnp.mean(raw * raw, axis=-1, keepdims=True) + 1e-06) * gain
    halves = normed.reshape(normed.shape[:-1] + (HEAD_DIM // 2, 2))
    first = halves[..., 0]
    second = halves[..., 1]
    cosine = cosine[None, :, :, None, :]
    sine = sine[None, :, :, None, :]
    rotated = jnp.stack([first * cosine - second * sine, first * sine + second * cosine], axis=-1)
    return rotated.reshape(raw.shape).astype(jnp.bfloat16)


def attend_head(inputs):
    queries, keys, values, live = inputs
    scores = jnp.einsum("qd,kd->qk", queries, keys, preferred_element_type=jnp.float32) / math.sqrt(
        HEAD_DIM
    )
    scores = jnp.where(live[None, :], scores, -jnp.inf)
    top = jnp.max(scores, axis=-1, keepdims=True)
    weights = jnp.exp(scores - top)
    total = jnp.sum(weights, axis=-1, keepdims=True)
    mixed = jnp.dot(weights.astype(jnp.bfloat16), values, preferred_element_type=jnp.float32)
    return (mixed / total).astype(jnp.bfloat16)


def attend_request(inputs):
    queries, keys, values, live = inputs
    count = queries.shape[1]
    broad_live = jnp.broadcast_to(live[None, :], (count, live.shape[0]))
    result = lax.map(
        attend_head,
        (
            jnp.moveaxis(queries, 1, 0),
            jnp.moveaxis(keys, 1, 0),
            jnp.moveaxis(values, 1, 0),
            broad_live,
        ),
    )
    return jnp.moveaxis(result, 0, 1)


def general(
    attn_proj,
    mlp_proj,
    stream,
    text_len,
    q_gain,
    k_gain,
    w_out_attn,
    w_out_mlp,
    bias_out,
    gate_mod,
    final_shift,
    final_scale,
    w_final,
    b_final,
    latent,
    step_size,
):
    requests = attn_proj.shape[0]
    own_slots = attn_proj.shape[2]
    width = attn_proj.shape[4]
    heads = width // HEAD_DIM
    start_slot = lax.axis_index("head") * own_slots
    positions = start_slot + jnp.arange(own_slots, dtype=jnp.int32)
    cosine, sine = rope_tables(positions)
    head_shape = (requests, 3, own_slots, heads, HEAD_DIM)
    queries = prepare(
        attn_proj[:, :, :, 0].astype(jnp.float32).reshape(head_shape), q_gain, cosine, sine
    )
    keys = prepare(
        attn_proj[:, :, :, 1].astype(jnp.float32).reshape(head_shape), k_gain, cosine, sine
    )
    packed = jnp.stack(
        [
            queries.reshape(requests, 3, own_slots, width),
            keys.reshape(requests, 3, own_slots, width),
            attn_proj[:, :, :, 2],
        ],
        axis=3,
    )
    units = mlp_proj[:, :, :, None, :]
    moved, hidden_units = (
        lax.all_to_all(packed, "head", split_axis=4, concat_axis=2, tiled=True),
        lax.all_to_all(units, "head", split_axis=4, concat_axis=2, tiled=True),
    )
    hidden_units = hidden_units[:, :, :, 0]
    tile_slots = moved.shape[2]
    local_width = moved.shape[4]
    local_heads = local_width // HEAD_DIM
    flat_shape = (requests, 3 * tile_slots, local_heads, HEAD_DIM)
    all_positions = jnp.arange(tile_slots, dtype=jnp.int32)
    text_live = all_positions[None, :] < text_len[:, None]
    image_live = jnp.ones_like(text_live)
    live = jnp.stack([text_live, image_live, image_live], axis=1).reshape(requests, 3 * tile_slots)
    attn_out = lax.map(
        attend_request,
        (
            moved[:, :, :, 0].reshape(flat_shape),
            moved[:, :, :, 1].reshape(flat_shape),
            moved[:, :, :, 2].reshape(flat_shape),
            live,
        ),
    )
    attn_out = attn_out.reshape(requests, 3, tile_slots, local_width)
    mlp_act = jax.nn.gelu(hidden_units.astype(jnp.float32), approximate=True).astype(jnp.bfloat16)
    term = jnp.einsum(
        "rbsk,kd->rbsd",
        attn_out,
        lax.all_gather(w_out_attn, "tile", axis=1, tiled=True),
        preferred_element_type=jnp.float32,
    )
    term = term + jnp.einsum(
        "rbsk,kd->rbsd",
        mlp_act,
        lax.all_gather(w_out_mlp, "tile", axis=1, tiled=True),
        preferred_element_type=jnp.float32,
    )
    proj = lax.psum_scatter(term, "head", scatter_dimension=2, tiled=True)
    updated = stream.astype(jnp.float32) + gate_mod[:, None, None, :] * (proj + bias_out)
    hidden_out = updated.astype(jnp.bfloat16)
    image = updated[:, 1:]
    center = image - jnp.mean(image, axis=-1, keepdims=True)
    variance = jnp.mean(center * center, axis=-1, keepdims=True)
    normed = center * lax.rsqrt(variance + 1e-06)
    modulated = (
        (1.0 + final_scale[:, None, None, :]) * normed + final_shift[:, None, None, :]
    ).astype(jnp.bfloat16)
    velocity = (
        jnp.einsum("rbsd,dc->rbsc", modulated, w_final, preferred_element_type=jnp.float32)
        + b_final
    )
    latent_next = latent + step_size[:, None, None, None] * velocity
    return (hidden_out, latent_next)


EPS = 1e-06
SCALE = math.log2(math.e) / math.sqrt(HEAD_DIM)
MIB = 1024 * 1024


def cost(flops, size):
    return pl.CostEstimate(flops=flops, bytes_accessed=size, transcendentals=0)
NT = (((1,), (1,)), ((), ()))


def fits(sizes):
    return sizes["head"] == 2 and sizes["tile"] == 2 * len(PATH)


def pack_kernel(half_ref, attn_ref, attn_w_ref, act_w_ref, sent_ref, block_ref):
    depth = attn_w_ref.shape[1]
    sent_ref[...] = attn_ref[...]
    block_ref[:, :depth] = attn_w_ref[...]
    block_ref[:, depth:] = act_w_ref[...]


def pack(half, attn, attn_w, act_w):
    blocks, parts, slots, width = attn.shape
    shape = (1, parts, slots // 2, width // 2)
    share = attn_w.shape[0] // (2 * blocks)

    def rows(depth):
        return pl.BlockSpec((share, depth), lambda b, s, half: (2 * b + s, 0))

    depth = attn_w.shape[1] + act_w.shape[1]
    return pl.pallas_call(
        pack_kernel,
        grid_spec=pltpu.PrefetchScalarGridSpec(
            num_scalar_prefetch=1,
            grid=(blocks, 2),
            in_specs=[
                pl.BlockSpec(shape, lambda b, s, half: (b, 0, s, 1 - half[0])),
                rows(attn_w.shape[1]),
                rows(act_w.shape[1]),
            ],
            out_specs=[pl.BlockSpec(shape, lambda b, s, half: (b, 0, s, 0)), rows(depth)],
        ),
        out_shape=[
            jax.ShapeDtypeStruct((blocks, parts, slots, width // 2), jnp.bfloat16),
            jax.ShapeDtypeStruct((attn_w.shape[0], depth), jnp.bfloat16),
        ],
        compiler_params=pltpu.CompilerParams(vmem_limit_bytes=60 * MIB),
        cost_estimate=cost(0, 8 * attn_w.size),
        name="pack",
    )(half, attn, attn_w, act_w)


def tables_kernel(half_ref, len_ref, row_freq_ref, col_freq_ref, q_ref, k_ref, cq_ref, sq_ref, ck_ref, sk_ref, mask_ref, swap_ref):
    rows = cq_ref.shape[0]
    slots = rows // 6

    def place(axis, shape):
        index = lax.broadcasted_iota(jnp.int32, shape, axis)
        away = index >= rows // 2
        block = (index - jnp.where(away, rows // 2, 0)) // slots
        slot = index % slots + slots * jnp.where(away, 1 - half_ref[0], half_ref[0])
        return block, slot

    shape = (rows, HEAD_DIM)
    block, slot = place(0, shape)
    image = (block - 1) * SLOTS + slot
    angle = (image // GRID_W).astype(jnp.float32) * row_freq_ref[...]
    angle += (image % GRID_W).astype(jnp.float32) * col_freq_ref[...]
    angle = jnp.where(block == 0, 0.0, angle)
    cosine, sine = jnp.cos(angle), jnp.sin(angle)
    odd = lax.broadcasted_iota(jnp.int32, shape, 1) % 2 == 1
    for gain_ref, c_ref, s_ref in ((q_ref, cq_ref, sq_ref), (k_ref, ck_ref, sk_ref)):
        gain = jnp.broadcast_to(gain_ref[...], shape)
        partner = jnp.where(odd, pltpu.roll(gain, 1, 1), -pltpu.roll(gain, HEAD_DIM - 1, 1))
        c_ref[...] = cosine * gain
        s_ref[...] = sine * partner
    block, slot = place(1, (1, rows))
    mask_ref[...] = jnp.where((block > 0) | (slot < len_ref[0]), 0.0, -jnp.inf)
    square = (HEAD_DIM, HEAD_DIM)
    column = lax.broadcasted_iota(jnp.int32, square, 1)
    other = column + 1 - 2 * (column % 2)
    swap_ref[...] = jnp.where(lax.broadcasted_iota(jnp.int32, square, 0) == other, 1.0, 0.0).astype(jnp.bfloat16)


def make_tables(half, text_len, q_gain, k_gain, rows):
    pairs_zero = HEAD_DIM // 16
    pairs_axis = (HEAD_DIM // 2 - pairs_zero) // 2
    freqs = 10000.0 ** (-np.arange(pairs_axis, dtype=np.float32) / np.float32(pairs_axis))
    row_freq, col_freq = np.zeros((2, 1, HEAD_DIM // 2), np.float32)
    row_freq[0, pairs_zero : pairs_zero + pairs_axis] = freqs
    col_freq[0, pairs_zero + pairs_axis :] = freqs
    scalars = pl.BlockSpec(memory_space=pltpu.SMEM)
    table = jax.ShapeDtypeStruct((rows, HEAD_DIM), jnp.float32)
    return pl.pallas_call(
        tables_kernel,
        in_specs=[scalars, scalars] + [pl.BlockSpec(memory_space=pltpu.VMEM)] * 4,
        out_shape=[
            table,
            table,
            table,
            table,
            jax.ShapeDtypeStruct((1, rows), jnp.float32),
            jax.ShapeDtypeStruct((HEAD_DIM, HEAD_DIM), jnp.bfloat16),
        ],
        compiler_params=pltpu.CompilerParams(vmem_limit_bytes=8 * MIB),
        cost_estimate=cost(rows * HEAD_DIM * 8, rows * HEAD_DIM * 4),
        name="tables",
    )(
        half,
        text_len,
        np.repeat(row_freq, 2, axis=1),
        np.repeat(col_freq, 2, axis=1),
        q_gain[None, :],
        k_gain[None, :],
    )


def attend_kernel(half_ref, own_ref, far_ref, cq_ref, sq_ref, ck_ref, sk_ref, mask_ref, swap_ref, out_ref):
    rows = own_ref.shape[0] * own_ref.shape[2]

    def load(part):
        return jnp.concatenate(
            [own_ref[:, part].reshape(rows, HEAD_DIM), far_ref[:, part].reshape(rows, HEAD_DIM)], axis=0
        )

    def turn(raw, straight, crossed):
        wide = raw.astype(jnp.float32)
        scale = lax.rsqrt(jnp.mean(wide * wide, axis=-1, keepdims=True) + EPS)
        partner = jnp.dot(raw, swap_ref[...], preferred_element_type=jnp.float32)
        return ((wide * straight + partner * crossed) * scale).astype(jnp.bfloat16)

    queries = turn(load(0), cq_ref[...], sq_ref[...])
    keys = turn(load(1), ck_ref[...], sk_ref[...])
    scores = lax.dot_general(queries, keys, NT, preferred_element_type=jnp.float32)
    scores = scores * SCALE + mask_ref[...]
    weights = jnp.exp2(scores - jnp.max(scores, axis=-1, keepdims=True))
    total = jnp.sum(weights, axis=-1, keepdims=True)
    mixed = jnp.dot(weights.astype(jnp.bfloat16), load(2), preferred_element_type=jnp.float32)
    out_ref[...] = (mixed / total).astype(jnp.bfloat16)


def attend(half, own, far, tables):
    blocks, parts, slots, width = far.shape
    heads = width // HEAD_DIM
    rows = 2 * blocks * slots
    shape = (blocks, parts, slots, HEAD_DIM)
    whole = pl.BlockSpec((rows, HEAD_DIM), lambda g, half: (0, 0))
    return pl.pallas_call(
        attend_kernel,
        grid_spec=pltpu.PrefetchScalarGridSpec(
            num_scalar_prefetch=1,
            grid=(heads,),
            in_specs=[
                pl.BlockSpec(shape, lambda g, half: (0, 0, 0, half[0] * heads + g)),
                pl.BlockSpec(shape, lambda g, half: (0, 0, 0, g)),
                whole,
                whole,
                whole,
                whole,
                pl.BlockSpec((1, rows), lambda g, half: (0, 0)),
                pl.BlockSpec((HEAD_DIM, HEAD_DIM), lambda g, half: (0, 0)),
            ],
            out_specs=pl.BlockSpec((rows, HEAD_DIM), lambda g, half: (0, g)),
        ),
        out_shape=jax.ShapeDtypeStruct((rows, width), jnp.bfloat16),
        compiler_params=pltpu.CompilerParams(vmem_limit_bytes=14 * MIB),
        cost_estimate=cost(heads * rows * rows * HEAD_DIM * 4, rows * width * 8),
        name="attend",
    )(half, own, far, *tables)


def gelu_kernel(part_ref, units_ref, *refs):
    refs[-1][...] = jax.nn.gelu(units_ref[0].astype(jnp.float32), approximate=True).astype(jnp.bfloat16)


def activate(part, units, width, into=None):
    blocks, slots, _ = units.shape
    first = 0 if into is None else blocks
    return pl.pallas_call(
        gelu_kernel,
        grid_spec=pltpu.PrefetchScalarGridSpec(
            num_scalar_prefetch=1,
            grid=(blocks,),
            in_specs=[pl.BlockSpec((1, slots, width), lambda b, part: (b, 0, part[0]))]
            + ([] if into is None else [pl.BlockSpec(memory_space=pl.ANY)]),
            out_specs=pl.BlockSpec((slots, width), lambda b, part: (first + b, 0)),
        ),
        out_shape=jax.ShapeDtypeStruct((2 * blocks * slots, width), jnp.bfloat16),
        input_output_aliases={} if into is None else {2: 0},
        compiler_params=pltpu.CompilerParams(vmem_limit_bytes=10 * MIB),
        cost_estimate=cost(blocks * slots * width * 4, blocks * slots * width),
        name="activate",
    )(part, units, *([] if into is None else [into]))


def project_kernel(chips, core_ref, attn_ref, act_ref, *refs):
    pieces, outs = refs[:-2], refs[-2:]
    depth = attn_ref.shape[1]
    rows = outs[0].shape[0]
    share = outs[0].shape[1] // (2 * len(chips))
    core = core_ref[0]

    def together(blocks):
        return jnp.concatenate([block[...] for block in blocks], axis=0)

    def term(weights):
        total = lax.dot_general(attn_ref[...], weights[:, :depth], NT, preferred_element_type=jnp.float32)
        return total + lax.dot_general(act_ref[...], weights[:, depth:], NT, preferred_element_type=jnp.float32)

    def store(total, first):
        for index, out_ref in enumerate(outs):
            part = total[rows * index : rows * (index + 1)]
            out_ref[:, first : first + share] = part.astype(out_ref.dtype)

    taking = iter(pieces)
    for chip, count in enumerate(chips):
        mine = term(together([next(taking) for _ in range(count // 2)]))
        other = term(together([next(taking) for _ in range(count // 2)]))
        first = 2 * share * chip
        pl.when(core == 0)(lambda: store(mine, first))
        pl.when(core == 0)(lambda: store(other, first + share))
        pl.when(core != 0)(lambda: store(mine, first + share))
        pl.when(core != 0)(lambda: store(other, first))


def project(core, attn, act, chips):
    flat = [array for chip in chips for array in chip]
    rows, depth = attn.shape[0] // 2, flat[0].shape[1]
    columns = sum(array.shape[0] for array in flat)
    inside = pl.BlockSpec(memory_space=pltpu.VMEM)
    return pl.pallas_call(
        functools.partial(project_kernel, [len(chip) for chip in chips]),
        in_specs=[pl.BlockSpec(memory_space=pltpu.SMEM)] + [inside] * (2 + len(flat)),
        out_specs=[inside] * 2,
        out_shape=[jax.ShapeDtypeStruct((rows, columns), kind) for kind in (jnp.float32, jnp.bfloat16)],
        compiler_params=pltpu.CompilerParams(vmem_limit_bytes=14 * MIB),
        cost_estimate=cost(rows * columns * depth // 2, columns * depth // 4),
        name="project",
    )(core, attn, act, *flat)


def finish_kernel(chunks, tile_ref, place_ref, step_ref, *refs):
    pairs = [refs[2 * i : 2 * i + 2] for i in range(chunks)]
    (
        stream_ref, bias_ref, gate_ref, scale_ref, shift_ref, w_ref, b_ref, latent_ref, hidden_ref, next_ref, proj_ref,
    ) = refs[2 * chunks :]
    places = len(PATH)
    chip = proj_ref.shape[1] // places
    mine = place_ref[places + tile_ref[0] // 2]
    behind = [0] + [distance for step in range(1, places // 2) for distance in (step, -step)] + [places // 2]
    for own_ref, far_ref in pairs:
        for first in range(0, own_ref.shape[1], chip):
            source = place_ref[(mine - behind.pop(0) + places) % places]
            target = pl.ds(pl.multiple_of(chip * source, 128), chip)
            part = slice(first, first + chip)
            proj_ref[:, target] = own_ref[:, part] + far_ref[:, part].astype(jnp.float32)
    updated = stream_ref[0].astype(jnp.float32) + gate_ref[...] * (proj_ref[...] + bias_ref[...])
    hidden_ref[0] = updated.astype(jnp.bfloat16)

    @pl.when(pl.program_id(0) > 0)
    def _():
        center = updated - jnp.mean(updated, axis=-1, keepdims=True)
        variance = jnp.mean(center * center, axis=-1, keepdims=True)
        normed = center * lax.rsqrt(variance + EPS)
        modulated = ((1.0 + scale_ref[...]) * normed + shift_ref[...]).astype(jnp.bfloat16)
        velocity = lax.dot_general(w_ref[...], modulated, NT, preferred_element_type=jnp.float32)
        next_ref[0] = latent_ref[0] + step_ref[0] * (velocity + b_ref[...])


def finish(tile, step, chunks, stream, bias, gate, scale, shift, w_final, b_final, latent):
    blocks, slots, width = stream.shape
    channels = w_final.shape[0]
    flat = [array for pair in chunks for array in pair]

    def whole(array):
        return pl.BlockSpec(array.shape, lambda b, *_: (0, 0))

    tokens = pl.BlockSpec((1, slots, width), lambda b, *_: (b, 0, 0))
    image = pl.BlockSpec((1, channels, slots), lambda b, *_: (jnp.maximum(b - 1, 0), 0, 0))
    return pl.pallas_call(
        functools.partial(finish_kernel, len(chunks)),
        grid_spec=pltpu.PrefetchScalarGridSpec(
            num_scalar_prefetch=3,
            grid=(blocks,),
            in_specs=[pl.BlockSpec((slots, array.shape[1]), lambda b, *_: (b, 0)) for array in flat]
            + [
                tokens,
                whole(bias),
                whole(gate),
                whole(scale),
                whole(shift),
                whole(w_final),
                whole(b_final),
                image,
            ],
            out_specs=[tokens, image],
            scratch_shapes=[pltpu.VMEM((slots, width), jnp.float32)],
        ),
        out_shape=[
            jax.ShapeDtypeStruct(stream.shape, jnp.bfloat16),
            jax.ShapeDtypeStruct(latent.shape, jnp.float32),
        ],
        compiler_params=pltpu.CompilerParams(vmem_limit_bytes=60 * MIB),
        cost_estimate=cost(blocks * slots * width * 160, blocks * slots * width * 10),
        name="finish",
    )(tile, np.array(PATH + PLACE, np.int32), step, *flat, stream, bias, gate, scale, shift, w_final, b_final, latent)


PATH = (0, 1, 3, 5, 7, 6, 4, 2)
PLACE = tuple(PATH.index(chip) for chip in range(len(PATH)))


def hop(array, by):
    places = len(PATH)
    pairs = [(2 * PATH[i] + c, 2 * PATH[(i + by) % places] + c) for i in range(places) for c in range(2)]
    return lax.ppermute(array, "tile", pairs)


def across(array):
    return lax.ppermute(array, "tile", [(2 * chip + c, 2 * chip + 1 - c) for chip in range(len(PATH)) for c in range(2)])


def spread(array):
    return [array, across(array)]


def paired(
    partners,
    attn_proj,
    mlp_proj,
    stream,
    text_len,
    q_gain,
    k_gain,
    w_out_attn,
    w_out_mlp,
    bias_out,
    gate_mod,
    final_shift,
    final_scale,
    w_final,
    b_final,
    latent,
    step_size,
):
    me = lax.axis_index("head")
    half = me[None].astype(jnp.int32)
    trade = functools.partial(lax.ppermute, axis_name="head", perm=[(0, 1), (1, 0)])

    tile = lax.axis_index("tile").astype(jnp.int32)
    core = (tile % 2)[None]
    own_attn = jnp.transpose(attn_proj[0], (0, 2, 1, 3))
    own_units = mlp_proj[0]
    units = own_units.shape[2] // partners
    units = own_units.shape[2] // partners
    sent_attn, block = pack(half, own_attn, w_out_attn.T, w_out_mlp.T)
    far_attn = trade(sent_attn)
    onward, back = hop(block, 1), hop(block, -1)
    tables = make_tables(half, text_len, q_gain, k_gain, 6 * own_attn.shape[2])
    act_near = activate(half, own_units, units)
    sent_units = lax.dynamic_slice_in_dim(own_units, (1 - me) * units, units, axis=2)

    onward, back, tables, act_near, sent_units, block, other = lax.optimization_barrier(
        (onward, back, tables, act_near, sent_units, block, across(block))
    )
    chips = [[block, other]]
    chips += [spread(onward), spread(back)]
    onward, back = hop(onward, 1), hop(back, -1)
    far_attn, sent_units = lax.optimization_barrier((far_attn, sent_units))
    far_units = trade(sent_units)
    attn = attend(half, own_attn, far_attn, tables)
    attn, onward, back = lax.optimization_barrier((attn, onward, back))
    chips += [spread(onward), spread(back)]
    onward, back = hop(onward, 1), hop(back, -1)
    far_units, attn, chips = lax.optimization_barrier((far_units, attn, chips))
    act = activate(jnp.zeros_like(half), far_units, units, act_near)

    chunks = []

    def send(group):
        own, sent = project(core, attn, act, group)
        chunks.append([own, trade(sent)])
        return sent

    sent = send(chips[0:3])
    onward, back, attn, sent = lax.optimization_barrier((onward, back, attn, sent))
    middle = block.shape[0] // 2
    last = hop(onward[:middle], 1), hop(back[middle:], -1)
    chips += [spread(onward), spread(back)]
    sent = send(chips[3:5])
    attn, sent, chunks[0][1] = lax.optimization_barrier((attn, sent, chunks[0][1]))
    sent = send(chips[5:7])
    onward, back, attn, sent, chunks[1][1] = lax.optimization_barrier((*last, attn, sent, chunks[1][1]))
    chips.append([onward, back, across(onward), across(back)])
    send(chips[7:8])

    hidden, following = finish(
        tile[None],
        step_size,
        chunks,
        stream[0],
        bias_out[None, :],
        gate_mod,
        final_scale,
        final_shift,
        w_final.T,
        b_final[:, None],
        jnp.transpose(latent[0], (0, 2, 1)),
    )
    return hidden[None], jnp.transpose(following, (0, 2, 1))[None]


def solution(mesh):
    placed = (
        P("tile", None, "head", None, None),
        P("tile", None, "head", None),
        P("tile", None, "head", None),
        P("tile"),
        P(),
        P(),
        P("head", "tile"),
        P("head", "tile"),
        P(),
        P("tile", None),
        P("tile", None),
        P("tile", None),
        P(),
        P(),
        P("tile", None, "head", None),
        P("tile"),
    )
    return jax.shard_map(
        functools.partial(paired, mesh.shape["head"]) if fits(mesh.shape) else general,
        mesh=mesh,
        in_specs=placed,
        out_specs=(P("tile", None, "head", None), P("tile", None, "head", None)),
        check_vma=False,
    )
```

```python
import functools
import math

import jax
import jax.numpy as jnp
import numpy as np
from jax import lax
from jax.experimental import pallas as pl
from jax.experimental.pallas import tpu as pltpu
from jax.sharding import PartitionSpec as P

HEAD_DIM = 128
SLOTS = 192
GRID_W = 32


def rope_tables(positions):
    pairs_zero = HEAD_DIM // 16
    pairs_axis = (HEAD_DIM // 2 - pairs_zero) // 2
    freqs = 10000.0 ** (-jnp.arange(pairs_axis, dtype=jnp.float32) / pairs_axis)
    count = positions.shape[0]
    angles = [jnp.zeros((count, HEAD_DIM // 2), jnp.float32)]
    for block in range(1, 3):
        image_index = (block - 1) * SLOTS + positions
        rows = (image_index // GRID_W).astype(jnp.float32)
        columns = (image_index % GRID_W).astype(jnp.float32)
        angles.append(
            jnp.concatenate(
                [
                    jnp.zeros((count, pairs_zero), jnp.float32),
                    rows[:, None] * freqs[None, :],
                    columns[:, None] * freqs[None, :],
                ],
                axis=1,
            )
        )
    stacked = jnp.stack(angles)
    return (jnp.cos(stacked), jnp.sin(stacked))


def prepare(raw, gain, cosine, sine):
    normed = raw * lax.rsqrt(jnp.mean(raw * raw, axis=-1, keepdims=True) + 1e-06) * gain
    halves = normed.reshape(normed.shape[:-1] + (HEAD_DIM // 2, 2))
    first = halves[..., 0]
    second = halves[..., 1]
    cosine = cosine[None, :, :, None, :]
    sine = sine[None, :, :, None, :]
    rotated = jnp.stack([first * cosine - second * sine, first * sine + second * cosine], axis=-1)
    return rotated.reshape(raw.shape).astype(jnp.bfloat16)


def attend_head(inputs):
    queries, keys, values, live = inputs
    scores = jnp.einsum("qd,kd->qk", queries, keys, preferred_element_type=jnp.float32) / math.sqrt(
        HEAD_DIM
    )
    scores = jnp.where(live[None, :], scores, -jnp.inf)
    top = jnp.max(scores, axis=-1, keepdims=True)
    weights = jnp.exp(scores - top)
    total = jnp.sum(weights, axis=-1, keepdims=True)
    mixed = jnp.dot(weights.astype(jnp.bfloat16), values, preferred_element_type=jnp.float32)
    return (mixed / total).astype(jnp.bfloat16)


def attend_request(inputs):
    queries, keys, values, live = inputs
    count = queries.shape[1]
    broad_live = jnp.broadcast_to(live[None, :], (count, live.shape[0]))
    result = lax.map(
        attend_head,
        (
            jnp.moveaxis(queries, 1, 0),
            jnp.moveaxis(keys, 1, 0),
            jnp.moveaxis(values, 1, 0),
            broad_live,
        ),
    )
    return jnp.moveaxis(result, 0, 1)


def general(
    attn_proj,
    mlp_proj,
    stream,
    text_len,
    q_gain,
    k_gain,
    w_out_attn,
    w_out_mlp,
    bias_out,
    gate_mod,
    final_shift,
    final_scale,
    w_final,
    b_final,
    latent,
    step_size,
):
    requests = attn_proj.shape[0]
    own_slots = attn_proj.shape[2]
    width = attn_proj.shape[4]
    heads = width // HEAD_DIM
    start_slot = lax.axis_index("head") * own_slots
    positions = start_slot + jnp.arange(own_slots, dtype=jnp.int32)
    cosine, sine = rope_tables(positions)
    head_shape = (requests, 3, own_slots, heads, HEAD_DIM)
    queries = prepare(
        attn_proj[:, :, :, 0].astype(jnp.float32).reshape(head_shape), q_gain, cosine, sine
    )
    keys = prepare(
        attn_proj[:, :, :, 1].astype(jnp.float32).reshape(head_shape), k_gain, cosine, sine
    )
    packed = jnp.stack(
        [
            queries.reshape(requests, 3, own_slots, width),
            keys.reshape(requests, 3, own_slots, width),
            attn_proj[:, :, :, 2],
        ],
        axis=3,
    )
    units = mlp_proj[:, :, :, None, :]
    moved, hidden_units = (
        lax.all_to_all(packed, "head", split_axis=4, concat_axis=2, tiled=True),
        lax.all_to_all(units, "head", split_axis=4, concat_axis=2, tiled=True),
    )
    hidden_units = hidden_units[:, :, :, 0]
    tile_slots = moved.shape[2]
    local_width = moved.shape[4]
    local_heads = local_width // HEAD_DIM
    flat_shape = (requests, 3 * tile_slots, local_heads, HEAD_DIM)
    all_positions = jnp.arange(tile_slots, dtype=jnp.int32)
    text_live = all_positions[None, :] < text_len[:, None]
    image_live = jnp.ones_like(text_live)
    live = jnp.stack([text_live, image_live, image_live], axis=1).reshape(requests, 3 * tile_slots)
    attn_out = lax.map(
        attend_request,
        (
            moved[:, :, :, 0].reshape(flat_shape),
            moved[:, :, :, 1].reshape(flat_shape),
            moved[:, :, :, 2].reshape(flat_shape),
            live,
        ),
    )
    attn_out = attn_out.reshape(requests, 3, tile_slots, local_width)
    mlp_act = jax.nn.gelu(hidden_units.astype(jnp.float32), approximate=True).astype(jnp.bfloat16)
    term = jnp.einsum(
        "rbsk,kd->rbsd",
        attn_out,
        lax.all_gather(w_out_attn, "tile", axis=1, tiled=True),
        preferred_element_type=jnp.float32,
    )
    term = term + jnp.einsum(
        "rbsk,kd->rbsd",
        mlp_act,
        lax.all_gather(w_out_mlp, "tile", axis=1, tiled=True),
        preferred_element_type=jnp.float32,
    )
    proj = lax.psum_scatter(term, "head", scatter_dimension=2, tiled=True)
    updated = stream.astype(jnp.float32) + gate_mod[:, None, None, :] * (proj + bias_out)
    hidden_out = updated.astype(jnp.bfloat16)
    image = updated[:, 1:]
    center = image - jnp.mean(image, axis=-1, keepdims=True)
    variance = jnp.mean(center * center, axis=-1, keepdims=True)
    normed = center * lax.rsqrt(variance + 1e-06)
    modulated = (
        (1.0 + final_scale[:, None, None, :]) * normed + final_shift[:, None, None, :]
    ).astype(jnp.bfloat16)
    velocity = (
        jnp.einsum("rbsd,dc->rbsc", modulated, w_final, preferred_element_type=jnp.float32)
        + b_final
    )
    latent_next = latent + step_size[:, None, None, None] * velocity
    return (hidden_out, latent_next)


EPS = 1e-06
SCALE = math.log2(math.e) / math.sqrt(HEAD_DIM)
MIB = 1024 * 1024


def cost(flops, size):
    return pl.CostEstimate(flops=flops, bytes_accessed=size, transcendentals=0)
NT = (((1,), (1,)), ((), ()))


def fits(sizes):
    return sizes["head"] == 2 and sizes["tile"] == 2 * len(PATH)


def pack_kernel(attn_w_ref, act_w_ref, block_ref):
    depth = attn_w_ref.shape[1]
    block_ref[:, :depth] = attn_w_ref[...]
    block_ref[:, depth:] = act_w_ref[...]


def pack(attn_w, act_w, steps=4):
    count = attn_w.shape[0] // steps
    depth = attn_w.shape[1] + act_w.shape[1]

    def rows(size):
        return pl.BlockSpec((count, size), lambda s: (s, 0))

    return pl.pallas_call(
        pack_kernel,
        grid=(steps,),
        in_specs=[rows(attn_w.shape[1]), rows(act_w.shape[1])],
        out_specs=rows(depth),
        out_shape=jax.ShapeDtypeStruct((attn_w.shape[0], depth), jnp.bfloat16),
        compiler_params=pltpu.CompilerParams(vmem_limit_bytes=60 * MIB),
        cost_estimate=cost(0, 4 * attn_w.size),
        name="pack",
    )(attn_w, act_w)


def tables_kernel(half_ref, len_ref, row_freq_ref, col_freq_ref, q_ref, k_ref, cq_ref, sq_ref, ck_ref, sk_ref, mask_ref, swap_ref):
    rows = cq_ref.shape[0]
    slots = rows // 6

    def place(axis, shape):
        index = lax.broadcasted_iota(jnp.int32, shape, axis)
        away = index >= rows // 2
        block = (index - jnp.where(away, rows // 2, 0)) // slots
        slot = index % slots + slots * jnp.where(away, 1 - half_ref[0], half_ref[0])
        return block, slot

    shape = (rows, HEAD_DIM)
    block, slot = place(0, shape)
    image = (block - 1) * SLOTS + slot
    angle = (image // GRID_W).astype(jnp.float32) * row_freq_ref[...]
    angle += (image % GRID_W).astype(jnp.float32) * col_freq_ref[...]
    angle = jnp.where(block == 0, 0.0, angle)
    cosine, sine = jnp.cos(angle), jnp.sin(angle)
    odd = lax.broadcasted_iota(jnp.int32, shape, 1) % 2 == 1
    for gain_ref, c_ref, s_ref in ((q_ref, cq_ref, sq_ref), (k_ref, ck_ref, sk_ref)):
        gain = jnp.broadcast_to(gain_ref[...], shape)
        partner = jnp.where(odd, pltpu.roll(gain, 1, 1), -pltpu.roll(gain, HEAD_DIM - 1, 1))
        c_ref[...] = cosine * gain
        s_ref[...] = sine * partner
    block, slot = place(1, (1, rows))
    mask_ref[...] = jnp.where((block > 0) | (slot < len_ref[0]), 0.0, -jnp.inf)
    square = (HEAD_DIM, HEAD_DIM)
    column = lax.broadcasted_iota(jnp.int32, square, 1)
    other = column + 1 - 2 * (column % 2)
    swap_ref[...] = jnp.where(lax.broadcasted_iota(jnp.int32, square, 0) == other, 1.0, 0.0).astype(jnp.bfloat16)


def make_tables(half, text_len, q_gain, k_gain, rows):
    pairs_zero = HEAD_DIM // 16
    pairs_axis = (HEAD_DIM // 2 - pairs_zero) // 2
    freqs = 10000.0 ** (-np.arange(pairs_axis, dtype=np.float32) / np.float32(pairs_axis))
    row_freq, col_freq = np.zeros((2, 1, HEAD_DIM // 2), np.float32)
    row_freq[0, pairs_zero : pairs_zero + pairs_axis] = freqs
    col_freq[0, pairs_zero + pairs_axis :] = freqs
    scalars = pl.BlockSpec(memory_space=pltpu.SMEM)
    table = jax.ShapeDtypeStruct((rows, HEAD_DIM), jnp.float32)
    return pl.pallas_call(
        tables_kernel,
        in_specs=[scalars, scalars] + [pl.BlockSpec(memory_space=pltpu.VMEM)] * 4,
        out_shape=[
            table,
            table,
            table,
            table,
            jax.ShapeDtypeStruct((1, rows), jnp.float32),
            jax.ShapeDtypeStruct((HEAD_DIM, HEAD_DIM), jnp.bfloat16),
        ],
        compiler_params=pltpu.CompilerParams(vmem_limit_bytes=8 * MIB),
        cost_estimate=cost(rows * HEAD_DIM * 8, rows * HEAD_DIM * 4),
        name="tables",
    )(
        half,
        text_len,
        np.repeat(row_freq, 2, axis=1),
        np.repeat(col_freq, 2, axis=1),
        q_gain[None, :],
        k_gain[None, :],
    )


def attend_kernel(half_ref, own_ref, far_ref, cq_ref, sq_ref, ck_ref, sk_ref, mask_ref, swap_ref, out_ref):
    rows = own_ref.shape[0] * own_ref.shape[2]

    def load(part):
        return jnp.concatenate(
            [own_ref[:, part].reshape(rows, HEAD_DIM), far_ref[:, part].reshape(rows, HEAD_DIM)], axis=0
        )

    def turn(raw, straight, crossed):
        wide = raw.astype(jnp.float32)
        scale = lax.rsqrt(jnp.mean(wide * wide, axis=-1, keepdims=True) + EPS)
        partner = jnp.dot(raw, swap_ref[...], preferred_element_type=jnp.float32)
        return ((wide * straight + partner * crossed) * scale).astype(jnp.bfloat16)

    queries = turn(load(0), cq_ref[...], sq_ref[...])
    keys = turn(load(1), ck_ref[...], sk_ref[...])
    scores = lax.dot_general(queries, keys, NT, preferred_element_type=jnp.float32)
    scores = scores * SCALE + mask_ref[...]
    weights = jnp.exp2(scores - jnp.max(scores, axis=-1, keepdims=True))
    total = jnp.sum(weights, axis=-1, keepdims=True)
    mixed = jnp.dot(weights.astype(jnp.bfloat16), load(2), preferred_element_type=jnp.float32)
    out_ref[...] = (mixed / total).astype(jnp.bfloat16)


def attend(half, own, far, tables):
    blocks, parts, slots, width = far.shape
    heads = width // HEAD_DIM
    rows = 2 * blocks * slots
    shape = (blocks, parts, slots, HEAD_DIM)
    whole = pl.BlockSpec((rows, HEAD_DIM), lambda g, half: (0, 0))
    return pl.pallas_call(
        attend_kernel,
        grid_spec=pltpu.PrefetchScalarGridSpec(
            num_scalar_prefetch=1,
            grid=(heads,),
            in_specs=[
                pl.BlockSpec(shape, lambda g, half: (0, 0, 0, half[0] * heads + g)),
                pl.BlockSpec(shape, lambda g, half: (0, 0, 0, g)),
                whole,
                whole,
                whole,
                whole,
                pl.BlockSpec((1, rows), lambda g, half: (0, 0)),
                pl.BlockSpec((HEAD_DIM, HEAD_DIM), lambda g, half: (0, 0)),
            ],
            out_specs=pl.BlockSpec((rows, HEAD_DIM), lambda g, half: (0, g)),
        ),
        out_shape=jax.ShapeDtypeStruct((rows, width), jnp.bfloat16),
        compiler_params=pltpu.CompilerParams(vmem_limit_bytes=14 * MIB),
        cost_estimate=cost(heads * rows * rows * HEAD_DIM * 4, rows * width * 8),
        name="attend",
    )(half, own, far, *tables)


def gelu_kernel(part_ref, units_ref, *refs):
    refs[-1][...] = jax.nn.gelu(units_ref[0].astype(jnp.float32), approximate=True).astype(jnp.bfloat16)


def activate(part, units, width, into=None):
    blocks, slots, _ = units.shape
    first = 0 if into is None else blocks
    return pl.pallas_call(
        gelu_kernel,
        grid_spec=pltpu.PrefetchScalarGridSpec(
            num_scalar_prefetch=1,
            grid=(blocks,),
            in_specs=[pl.BlockSpec((1, slots, width), lambda b, part: (b, 0, part[0]))]
            + ([] if into is None else [pl.BlockSpec(memory_space=pl.ANY)]),
            out_specs=pl.BlockSpec((slots, width), lambda b, part: (first + b, 0)),
        ),
        out_shape=jax.ShapeDtypeStruct((2 * blocks * slots, width), jnp.bfloat16),
        input_output_aliases={} if into is None else {2: 0},
        compiler_params=pltpu.CompilerParams(vmem_limit_bytes=10 * MIB),
        cost_estimate=cost(blocks * slots * width * 4, blocks * slots * width),
        name="activate",
    )(part, units, *([] if into is None else [into]))


def project_kernel(chips, core_ref, attn_ref, act_ref, *refs):
    pieces, outs = refs[:-2], refs[-2:]
    depth = attn_ref.shape[1]
    rows = outs[0].shape[0]
    share = outs[0].shape[1] // (2 * len(chips))
    core = core_ref[0]

    def together(blocks):
        return jnp.concatenate([block[...] for block in blocks], axis=0)

    def term(weights):
        total = lax.dot_general(attn_ref[...], weights[:, :depth], NT, preferred_element_type=jnp.float32)
        return total + lax.dot_general(act_ref[...], weights[:, depth:], NT, preferred_element_type=jnp.float32)

    def store(total, first):
        for index, out_ref in enumerate(outs):
            part = total[rows * index : rows * (index + 1)]
            out_ref[:, first : first + share] = part.astype(out_ref.dtype)

    taking = iter(pieces)
    for chip, count in enumerate(chips):
        mine = term(together([next(taking) for _ in range(count // 2)]))
        other = term(together([next(taking) for _ in range(count // 2)]))
        first = 2 * share * chip
        pl.when(core == 0)(lambda: store(mine, first))
        pl.when(core == 0)(lambda: store(other, first + share))
        pl.when(core != 0)(lambda: store(mine, first + share))
        pl.when(core != 0)(lambda: store(other, first))


def project(core, attn, act, chips):
    flat = [array for chip in chips for array in chip]
    rows, depth = attn.shape[0] // 2, flat[0].shape[1]
    columns = sum(array.shape[0] for array in flat)
    inside = pl.BlockSpec(memory_space=pltpu.VMEM)
    return pl.pallas_call(
        functools.partial(project_kernel, [len(chip) for chip in chips]),
        in_specs=[pl.BlockSpec(memory_space=pltpu.SMEM)] + [inside] * (2 + len(flat)),
        out_specs=[inside] * 2,
        out_shape=[jax.ShapeDtypeStruct((rows, columns), kind) for kind in (jnp.float32, jnp.bfloat16)],
        compiler_params=pltpu.CompilerParams(vmem_limit_bytes=14 * MIB),
        cost_estimate=cost(rows * columns * depth // 2, columns * depth // 4),
        name="project",
    )(core, attn, act, *flat)


def collect_kernel(chunks, tile_ref, place_ref, *refs):
    *terms, out_ref = refs
    places = len(PATH)
    chip = out_ref.shape[1] // places
    mine = place_ref[places + tile_ref[0] // 2]
    behind = [0] + [distance for step in range(1, places // 2) for distance in (step, -step)] + [places // 2]
    for count in chunks:
        parts, terms = terms[:count], terms[count:]
        for first in range(0, parts[0].shape[1], chip):
            source = place_ref[(mine - behind.pop(0) + places) % places]
            target = pl.ds(pl.multiple_of(chip * source, 128), chip)
            part = slice(first, first + chip)
            total = parts[0][:, part]
            for term in parts[1:]:
                total += term[:, part].astype(jnp.float32)
            out_ref[:, target] = total


def collect(tile, chunks, slots):
    flat = [array for chunk in chunks for array in chunk]
    rows, width = flat[0].shape[0], sum(chunk[0].shape[1] for chunk in chunks)
    return pl.pallas_call(
        functools.partial(collect_kernel, [len(chunk) for chunk in chunks]),
        grid_spec=pltpu.PrefetchScalarGridSpec(
            num_scalar_prefetch=2,
            grid=(rows // slots,),
            in_specs=[pl.BlockSpec((slots, array.shape[1]), lambda b, *_: (b, 0)) for array in flat],
            out_specs=pl.BlockSpec((slots, width), lambda b, *_: (b, 0)),
        ),
        out_shape=jax.ShapeDtypeStruct((rows, width), jnp.float32),
        compiler_params=pltpu.CompilerParams(vmem_limit_bytes=16 * MIB),
        cost_estimate=cost(rows * width, rows * width * 6),
        name="collect",
    )(tile, np.array(PATH + PLACE, np.int32), *flat)


def finish_kernel(
    tile_ref, place_ref, step_ref, terms_ref, last_ref, stream_ref, bias_ref, gate_ref, scale_ref, shift_ref, w_ref,
    b_ref, latent_ref, hidden_ref, next_ref, proj_ref,
):
    places = len(PATH)
    chip = last_ref.shape[1]
    source = place_ref[(place_ref[places + tile_ref[0] // 2] + places // 2) % places]
    target = pl.ds(pl.multiple_of(chip * source, 128), chip)
    proj_ref[...] = terms_ref[...]
    proj_ref[:, target] += last_ref[...].astype(jnp.float32)
    updated = stream_ref[0].astype(jnp.float32) + gate_ref[...] * (proj_ref[...] + bias_ref[...])
    hidden_ref[0] = updated.astype(jnp.bfloat16)

    @pl.when(pl.program_id(0) > 0)
    def _():
        center = updated - jnp.mean(updated, axis=-1, keepdims=True)
        variance = jnp.mean(center * center, axis=-1, keepdims=True)
        normed = center * lax.rsqrt(variance + EPS)
        modulated = ((1.0 + scale_ref[...]) * normed + shift_ref[...]).astype(jnp.bfloat16)
        velocity = lax.dot_general(w_ref[...], modulated, NT, preferred_element_type=jnp.float32)
        next_ref[0] = latent_ref[0] + step_ref[0] * (velocity + b_ref[...])


def finish(tile, step, terms, last, stream, bias, gate, scale, shift, w_final, b_final, latent):
    blocks, slots, width = stream.shape
    channels = w_final.shape[0]

    def rows(array):
        return pl.BlockSpec((slots, array.shape[1]), lambda b, *_: (b, 0))

    def whole(array):
        return pl.BlockSpec(array.shape, lambda b, *_: (0, 0))

    tokens = pl.BlockSpec((1, slots, width), lambda b, *_: (b, 0, 0))
    image = pl.BlockSpec((1, channels, slots), lambda b, *_: (jnp.maximum(b - 1, 0), 0, 0))
    return pl.pallas_call(
        finish_kernel,
        grid_spec=pltpu.PrefetchScalarGridSpec(
            num_scalar_prefetch=3,
            grid=(blocks,),
            in_specs=[
                rows(terms),
                rows(last),
                tokens,
                whole(bias),
                whole(gate),
                whole(scale),
                whole(shift),
                whole(w_final),
                whole(b_final),
                image,
            ],
            out_specs=[tokens, image],
            scratch_shapes=[pltpu.VMEM((slots, width), jnp.float32)],
        ),
        out_shape=[
            jax.ShapeDtypeStruct(stream.shape, jnp.bfloat16),
            jax.ShapeDtypeStruct(latent.shape, jnp.float32),
        ],
        compiler_params=pltpu.CompilerParams(vmem_limit_bytes=20 * MIB),
        cost_estimate=cost(blocks * slots * width * 160, blocks * slots * width * 10),
        name="finish",
    )(
        tile,
        np.array(PATH + PLACE, np.int32),
        step,
        terms,
        last,
        stream,
        bias,
        gate,
        scale,
        shift,
        w_final,
        b_final,
        latent,
    )


PATH = (0, 1, 3, 5, 7, 6, 4, 2)
PLACE = tuple(PATH.index(chip) for chip in range(len(PATH)))


def hop(array, by):
    places = len(PATH)
    pairs = [(2 * PATH[i] + c, 2 * PATH[(i + by) % places] + c) for i in range(places) for c in range(2)]
    return lax.ppermute(array, "tile", pairs)


def across(array):
    return lax.ppermute(array, "tile", [(2 * chip + c, 2 * chip + 1 - c) for chip in range(len(PATH)) for c in range(2)])


def spread(array):
    return [array, across(array)]


def paired(
    partners,
    attn_proj,
    mlp_proj,
    stream,
    text_len,
    q_gain,
    k_gain,
    w_out_attn,
    w_out_mlp,
    bias_out,
    gate_mod,
    final_shift,
    final_scale,
    w_final,
    b_final,
    latent,
    step_size,
):
    me = lax.axis_index("head")
    half = me[None].astype(jnp.int32)
    trade = functools.partial(lax.ppermute, axis_name="head", perm=[(0, 1), (1, 0)])

    tile = lax.axis_index("tile").astype(jnp.int32)
    core = (tile % 2)[None]
    own_attn = jnp.transpose(attn_proj[0], (0, 2, 1, 3))
    own_units = mlp_proj[0]
    units = own_units.shape[2] // partners
    units = own_units.shape[2] // partners
    width = own_attn.shape[3] // partners
    block, own_attn = lax.optimization_barrier((pack(w_out_attn.T, w_out_mlp.T), own_attn))
    onward, back = hop(block, 1), hop(block, -1)
    far_attn = trade(lax.dynamic_slice_in_dim(own_attn, (1 - me) * width, width, axis=3))
    tables = make_tables(half, text_len, q_gain, k_gain, 6 * own_attn.shape[2])
    act_near = activate(half, own_units, units)
    sent_units = lax.dynamic_slice_in_dim(own_units, (1 - me) * units, units, axis=2)

    onward, back, tables, act_near, sent_units, block, other = lax.optimization_barrier(
        (onward, back, tables, act_near, sent_units, block, across(block))
    )
    chips = [[block, other]]
    chips += [spread(onward), spread(back)]
    onward, back = hop(onward, 1), hop(back, -1)
    far_attn, sent_units = lax.optimization_barrier((far_attn, sent_units))
    far_units = trade(sent_units)
    attn = attend(half, own_attn, far_attn, tables)
    attn, onward, back = lax.optimization_barrier((attn, onward, back))
    chips += [spread(onward), spread(back)]
    onward, back = hop(onward, 1), hop(back, -1)
    far_units, attn, chips = lax.optimization_barrier((far_units, attn, chips))
    act = activate(jnp.zeros_like(half), far_units, units, act_near)

    chunks = []

    def send(group):
        own, sent = project(core, attn, act, group)
        chunks.append([own, trade(sent)])
        return sent

    sent = send(chips[0:1])
    attn, sent = lax.optimization_barrier((attn, sent))
    sent = send(chips[1:3])
    onward, back, attn, sent, chunks[0][1] = lax.optimization_barrier((onward, back, attn, sent, chunks[0][1]))
    middle = block.shape[0] // 2
    last = hop(onward[:middle], 1), hop(back[middle:], -1)
    chips += [spread(onward), spread(back)]
    sent = send(chips[3:5])
    attn, sent, chunks[1][1] = lax.optimization_barrier((attn, sent, chunks[1][1]))
    sent = send(chips[5:7])
    onward, back, attn, sent, chunks[2][1] = lax.optimization_barrier((*last, attn, sent, chunks[2][1]))
    chips.append([onward, back, across(onward), across(back)])
    send(chips[7:8])
    own, far = chunks.pop()
    terms = collect(tile[None], chunks + [[own]], own_attn.shape[2])
    hidden, following = finish(
        tile[None],
        step_size,
        terms,
        far,
        stream[0],
        bias_out[None, :],
        gate_mod,
        final_scale,
        final_shift,
        w_final.T,
        b_final[:, None],
        jnp.transpose(latent[0], (0, 2, 1)),
    )
    return hidden[None], jnp.transpose(following, (0, 2, 1))[None]


def solution(mesh):
    placed = (
        P("tile", None, "head", None, None),
        P("tile", None, "head", None),
        P("tile", None, "head", None),
        P("tile"),
        P(),
        P(),
        P("head", "tile"),
        P("head", "tile"),
        P(),
        P("tile", None),
        P("tile", None),
        P("tile", None),
        P(),
        P(),
        P("tile", None, "head", None),
        P("tile"),
    )
    return jax.shard_map(
        functools.partial(paired, mesh.shape["head"]) if fits(mesh.shape) else general,
        mesh=mesh,
        in_specs=placed,
        out_specs=(P("tile", None, "head", None), P("tile", None, "head", None)),
        check_vma=False,
    )
```

```python
import functools
import math

import jax
import jax.numpy as jnp
import numpy as np
from jax import lax
from jax.experimental import pallas as pl
from jax.experimental.pallas import tpu as pltpu
from jax.sharding import PartitionSpec as P

HEAD_DIM = 128
SLOTS = 192
GRID_W = 32


def rope_tables(positions):
    pairs_zero = HEAD_DIM // 16
    pairs_axis = (HEAD_DIM // 2 - pairs_zero) // 2
    freqs = 10000.0 ** (-jnp.arange(pairs_axis, dtype=jnp.float32) / pairs_axis)
    count = positions.shape[0]
    angles = [jnp.zeros((count, HEAD_DIM // 2), jnp.float32)]
    for block in range(1, 3):
        image_index = (block - 1) * SLOTS + positions
        rows = (image_index // GRID_W).astype(jnp.float32)
        columns = (image_index % GRID_W).astype(jnp.float32)
        angles.append(
            jnp.concatenate(
                [
                    jnp.zeros((count, pairs_zero), jnp.float32),
                    rows[:, None] * freqs[None, :],
                    columns[:, None] * freqs[None, :],
                ],
                axis=1,
            )
        )
    stacked = jnp.stack(angles)
    return (jnp.cos(stacked), jnp.sin(stacked))


def prepare(raw, gain, cosine, sine):
    normed = raw * lax.rsqrt(jnp.mean(raw * raw, axis=-1, keepdims=True) + 1e-06) * gain
    halves = normed.reshape(normed.shape[:-1] + (HEAD_DIM // 2, 2))
    first = halves[..., 0]
    second = halves[..., 1]
    cosine = cosine[None, :, :, None, :]
    sine = sine[None, :, :, None, :]
    rotated = jnp.stack([first * cosine - second * sine, first * sine + second * cosine], axis=-1)
    return rotated.reshape(raw.shape).astype(jnp.bfloat16)


def attend_head(inputs):
    queries, keys, values, live = inputs
    scores = jnp.einsum("qd,kd->qk", queries, keys, preferred_element_type=jnp.float32) / math.sqrt(
        HEAD_DIM
    )
    scores = jnp.where(live[None, :], scores, -jnp.inf)
    top = jnp.max(scores, axis=-1, keepdims=True)
    weights = jnp.exp(scores - top)
    total = jnp.sum(weights, axis=-1, keepdims=True)
    mixed = jnp.dot(weights.astype(jnp.bfloat16), values, preferred_element_type=jnp.float32)
    return (mixed / total).astype(jnp.bfloat16)


def attend_request(inputs):
    queries, keys, values, live = inputs
    count = queries.shape[1]
    broad_live = jnp.broadcast_to(live[None, :], (count, live.shape[0]))
    result = lax.map(
        attend_head,
        (
            jnp.moveaxis(queries, 1, 0),
            jnp.moveaxis(keys, 1, 0),
            jnp.moveaxis(values, 1, 0),
            broad_live,
        ),
    )
    return jnp.moveaxis(result, 0, 1)


def general(
    attn_proj,
    mlp_proj,
    stream,
    text_len,
    q_gain,
    k_gain,
    w_out_attn,
    w_out_mlp,
    bias_out,
    gate_mod,
    final_shift,
    final_scale,
    w_final,
    b_final,
    latent,
    step_size,
):
    requests = attn_proj.shape[0]
    own_slots = attn_proj.shape[2]
    width = attn_proj.shape[4]
    heads = width // HEAD_DIM
    start_slot = lax.axis_index("head") * own_slots
    positions = start_slot + jnp.arange(own_slots, dtype=jnp.int32)
    cosine, sine = rope_tables(positions)
    head_shape = (requests, 3, own_slots, heads, HEAD_DIM)
    queries = prepare(
        attn_proj[:, :, :, 0].astype(jnp.float32).reshape(head_shape), q_gain, cosine, sine
    )
    keys = prepare(
        attn_proj[:, :, :, 1].astype(jnp.float32).reshape(head_shape), k_gain, cosine, sine
    )
    packed = jnp.stack(
        [
            queries.reshape(requests, 3, own_slots, width),
            keys.reshape(requests, 3, own_slots, width),
            attn_proj[:, :, :, 2],
        ],
        axis=3,
    )
    units = mlp_proj[:, :, :, None, :]
    moved, hidden_units = (
        lax.all_to_all(packed, "head", split_axis=4, concat_axis=2, tiled=True),
        lax.all_to_all(units, "head", split_axis=4, concat_axis=2, tiled=True),
    )
    hidden_units = hidden_units[:, :, :, 0]
    tile_slots = moved.shape[2]
    local_width = moved.shape[4]
    local_heads = local_width // HEAD_DIM
    flat_shape = (requests, 3 * tile_slots, local_heads, HEAD_DIM)
    all_positions = jnp.arange(tile_slots, dtype=jnp.int32)
    text_live = all_positions[None, :] < text_len[:, None]
    image_live = jnp.ones_like(text_live)
    live = jnp.stack([text_live, image_live, image_live], axis=1).reshape(requests, 3 * tile_slots)
    attn_out = lax.map(
        attend_request,
        (
            moved[:, :, :, 0].reshape(flat_shape),
            moved[:, :, :, 1].reshape(flat_shape),
            moved[:, :, :, 2].reshape(flat_shape),
            live,
        ),
    )
    attn_out = attn_out.reshape(requests, 3, tile_slots, local_width)
    mlp_act = jax.nn.gelu(hidden_units.astype(jnp.float32), approximate=True).astype(jnp.bfloat16)
    term = jnp.einsum(
        "rbsk,kd->rbsd",
        attn_out,
        lax.all_gather(w_out_attn, "tile", axis=1, tiled=True),
        preferred_element_type=jnp.float32,
    )
    term = term + jnp.einsum(
        "rbsk,kd->rbsd",
        mlp_act,
        lax.all_gather(w_out_mlp, "tile", axis=1, tiled=True),
        preferred_element_type=jnp.float32,
    )
    proj = lax.psum_scatter(term, "head", scatter_dimension=2, tiled=True)
    updated = stream.astype(jnp.float32) + gate_mod[:, None, None, :] * (proj + bias_out)
    hidden_out = updated.astype(jnp.bfloat16)
    image = updated[:, 1:]
    center = image - jnp.mean(image, axis=-1, keepdims=True)
    variance = jnp.mean(center * center, axis=-1, keepdims=True)
    normed = center * lax.rsqrt(variance + 1e-06)
    modulated = (
        (1.0 + final_scale[:, None, None, :]) * normed + final_shift[:, None, None, :]
    ).astype(jnp.bfloat16)
    velocity = (
        jnp.einsum("rbsd,dc->rbsc", modulated, w_final, preferred_element_type=jnp.float32)
        + b_final
    )
    latent_next = latent + step_size[:, None, None, None] * velocity
    return (hidden_out, latent_next)


EPS = 1e-06
SCALE = math.log2(math.e) / math.sqrt(HEAD_DIM)
VMEM = 60 * 1024 * 1024
LESS = 34 * 1024 * 1024
NT = (((1,), (1,)), ((), ()))


def fits(sizes):
    return sizes["head"] == 2 and sizes["tile"] == 2 * len(PATH)


def tables_kernel(half_ref, len_ref, row_freq_ref, col_freq_ref, q_ref, k_ref, cq_ref, sq_ref, ck_ref, sk_ref, mask_ref, swap_ref):
    rows = cq_ref.shape[0]
    slots = rows // 6

    def place(axis, shape):
        index = lax.broadcasted_iota(jnp.int32, shape, axis)
        away = index >= rows // 2
        block = (index - jnp.where(away, rows // 2, 0)) // slots
        slot = index % slots + slots * jnp.where(away, 1 - half_ref[0], half_ref[0])
        return block, slot

    shape = (rows, HEAD_DIM)
    block, slot = place(0, shape)
    image = (block - 1) * SLOTS + slot
    angle = (image // GRID_W).astype(jnp.float32) * row_freq_ref[...]
    angle += (image % GRID_W).astype(jnp.float32) * col_freq_ref[...]
    angle = jnp.where(block == 0, 0.0, angle)
    cosine, sine = jnp.cos(angle), jnp.sin(angle)
    odd = lax.broadcasted_iota(jnp.int32, shape, 1) % 2 == 1
    for gain_ref, c_ref, s_ref in ((q_ref, cq_ref, sq_ref), (k_ref, ck_ref, sk_ref)):
        gain = jnp.broadcast_to(gain_ref[...], shape)
        partner = jnp.where(odd, pltpu.roll(gain, 1, 1), -pltpu.roll(gain, HEAD_DIM - 1, 1))
        c_ref[...] = cosine * gain
        s_ref[...] = sine * partner
    block, slot = place(1, (1, rows))
    mask_ref[...] = jnp.where((block > 0) | (slot < len_ref[0]), 0.0, -jnp.inf)
    square = (HEAD_DIM, HEAD_DIM)
    column = lax.broadcasted_iota(jnp.int32, square, 1)
    other = column + 1 - 2 * (column % 2)
    swap_ref[...] = jnp.where(lax.broadcasted_iota(jnp.int32, square, 0) == other, 1.0, 0.0).astype(jnp.bfloat16)


def make_tables(half, text_len, q_gain, k_gain, rows):
    pairs_zero = HEAD_DIM // 16
    pairs_axis = (HEAD_DIM // 2 - pairs_zero) // 2
    freqs = 10000.0 ** (-np.arange(pairs_axis, dtype=np.float32) / np.float32(pairs_axis))
    row_freq, col_freq = np.zeros((2, 1, HEAD_DIM // 2), np.float32)
    row_freq[0, pairs_zero : pairs_zero + pairs_axis] = freqs
    col_freq[0, pairs_zero + pairs_axis :] = freqs
    scalars = pl.BlockSpec(memory_space=pltpu.SMEM)
    table = jax.ShapeDtypeStruct((rows, HEAD_DIM), jnp.float32)
    return pl.pallas_call(
        tables_kernel,
        in_specs=[scalars, scalars] + [pl.BlockSpec(memory_space=pltpu.VMEM)] * 4,
        out_shape=[
            table,
            table,
            table,
            table,
            jax.ShapeDtypeStruct((1, rows), jnp.float32),
            jax.ShapeDtypeStruct((HEAD_DIM, HEAD_DIM), jnp.bfloat16),
        ],
        compiler_params=pltpu.CompilerParams(vmem_limit_bytes=VMEM),
        cost_estimate=pl.CostEstimate(flops=rows * HEAD_DIM * 8, bytes_accessed=rows * HEAD_DIM * 4, transcendentals=0),
        name="tables",
    )(
        half,
        text_len,
        np.repeat(row_freq, 2, axis=1),
        np.repeat(col_freq, 2, axis=1),
        q_gain[None, :],
        k_gain[None, :],
    )


def attend_kernel(half_ref, own_ref, far_ref, cq_ref, sq_ref, ck_ref, sk_ref, mask_ref, swap_ref, out_ref):
    rows = own_ref.shape[0] * own_ref.shape[2]

    def load(part):
        return jnp.concatenate(
            [own_ref[:, part].reshape(rows, HEAD_DIM), far_ref[:, part].reshape(rows, HEAD_DIM)], axis=0
        )

    def turn(raw, straight, crossed):
        wide = raw.astype(jnp.float32)
        scale = lax.rsqrt(jnp.mean(wide * wide, axis=-1, keepdims=True) + EPS)
        partner = jnp.dot(raw, swap_ref[...], preferred_element_type=jnp.float32)
        return ((wide * straight + partner * crossed) * scale).astype(jnp.bfloat16)

    queries = turn(load(0), cq_ref[...], sq_ref[...])
    keys = turn(load(1), ck_ref[...], sk_ref[...])
    scores = lax.dot_general(queries, keys, NT, preferred_element_type=jnp.float32)
    scores = scores * SCALE + mask_ref[...]
    weights = jnp.exp2(scores - jnp.max(scores, axis=-1, keepdims=True))
    total = jnp.sum(weights, axis=-1, keepdims=True)
    mixed = jnp.dot(weights.astype(jnp.bfloat16), load(2), preferred_element_type=jnp.float32)
    out_ref[...] = (mixed / total).astype(jnp.bfloat16)


def attend(half, own, far, tables):
    blocks, parts, slots, width = far.shape
    heads = width // HEAD_DIM
    rows = 2 * blocks * slots
    shape = (blocks, parts, slots, HEAD_DIM)
    whole = pl.BlockSpec((rows, HEAD_DIM), lambda g, half: (0, 0))
    return pl.pallas_call(
        attend_kernel,
        grid_spec=pltpu.PrefetchScalarGridSpec(
            num_scalar_prefetch=1,
            grid=(heads,),
            in_specs=[
                pl.BlockSpec(shape, lambda g, half: (0, 0, 0, half[0] * heads + g)),
                pl.BlockSpec(shape, lambda g, half: (0, 0, 0, g)),
                whole,
                whole,
                whole,
                whole,
                pl.BlockSpec((1, rows), lambda g, half: (0, 0)),
                pl.BlockSpec((HEAD_DIM, HEAD_DIM), lambda g, half: (0, 0)),
            ],
            out_specs=pl.BlockSpec((rows, HEAD_DIM), lambda g, half: (0, g)),
        ),
        out_shape=jax.ShapeDtypeStruct((rows, width), jnp.bfloat16),
        compiler_params=pltpu.CompilerParams(vmem_limit_bytes=VMEM),
        cost_estimate=pl.CostEstimate(
            flops=heads * rows * rows * HEAD_DIM * 4,
            bytes_accessed=rows * width * 8,
            transcendentals=0,
        ),
        name="attend",
    )(half, own, far, *tables)


def gelu_kernel(part_ref, units_ref, *refs):
    refs[-1][...] = jax.nn.gelu(units_ref[0].astype(jnp.float32), approximate=True).astype(jnp.bfloat16)


def activate(part, units, width, into=None):
    blocks, slots, _ = units.shape
    first = 0 if into is None else blocks
    return pl.pallas_call(
        gelu_kernel,
        grid_spec=pltpu.PrefetchScalarGridSpec(
            num_scalar_prefetch=1,
            grid=(blocks,),
            in_specs=[pl.BlockSpec((1, slots, width), lambda b, part: (b, 0, part[0]))]
            + ([] if into is None else [pl.BlockSpec(memory_space=pl.ANY)]),
            out_specs=pl.BlockSpec((slots, width), lambda b, part: (first + b, 0)),
        ),
        out_shape=jax.ShapeDtypeStruct((2 * blocks * slots, width), jnp.bfloat16),
        input_output_aliases={} if into is None else {2: 0},
        compiler_params=pltpu.CompilerParams(vmem_limit_bytes=LESS),
        cost_estimate=pl.CostEstimate(
            flops=blocks * slots * width * 4, bytes_accessed=blocks * slots * width, transcendentals=0
        ),
        name="activate",
    )(part, units, *([] if into is None else [into]))


def project_kernel(layout, core_ref, attn_ref, act_ref, *refs):
    pieces, (own_ref, far_ref, w_ref, sems) = refs[:-4], refs[-4:]
    depth = attn_ref.shape[1]
    rows, columns = own_ref.shape
    core = core_ref[0]
    copies = []
    for (base, here, share), piece in zip(layout, pieces):
        start = base + (core if here else 1 - core) * share
        place = pl.ds(pl.multiple_of(start, 16), piece.shape[0])
        copies.append(pltpu.make_async_copy(piece, w_ref.at[place], sems.at[len(copies)]))
        copies[-1].start()
    pending = [base // (2 * share) * 2 * share for base, _, share in layout]
    for first in range(0, columns, 256):
        end = min(first + 256, columns)
        while pending and pending[0] < end:
            copies[-len(pending)].wait()
            pending.pop(0)
        total = lax.dot_general(attn_ref[...], w_ref[first:end, :depth], NT, preferred_element_type=jnp.float32)
        total += lax.dot_general(act_ref[...], w_ref[first:end, depth:], NT, preferred_element_type=jnp.float32)
        own_ref[:, first:end] = total[:rows]
        far_ref[:, first:end] = total[rows:].astype(jnp.bfloat16)


def project(core, attn, act, chips):
    share = sum(piece.shape[0] for here, _, piece in chips[0] if here)
    layout, flat = [], []
    for index, pieces in enumerate(chips):
        for here, first, piece in pieces:
            layout.append((2 * share * index + first, here, share))
            flat.append(piece)
    rows, depth = attn.shape[0] // 2, attn.shape[1] + act.shape[1]
    columns = 2 * share * len(chips)
    inside = pl.BlockSpec(memory_space=pltpu.VMEM)
    return pl.pallas_call(
        functools.partial(project_kernel, layout),
        in_specs=[pl.BlockSpec(memory_space=pltpu.SMEM), inside, inside]
        + [pl.BlockSpec(memory_space=pl.ANY)] * len(flat),
        out_specs=[inside, inside],
        out_shape=[
            jax.ShapeDtypeStruct((rows, columns), jnp.float32),
            jax.ShapeDtypeStruct((rows, columns), jnp.bfloat16),
        ],
        scratch_shapes=[
            pltpu.VMEM((columns, depth), jnp.bfloat16),
            pltpu.SemaphoreType.DMA((len(flat),)),
        ],
        compiler_params=pltpu.CompilerParams(vmem_limit_bytes=LESS),
        cost_estimate=pl.CostEstimate(
            flops=rows * columns * depth // 2, bytes_accessed=columns * depth // 4, transcendentals=0
        ),
        name="project",
    )(core, attn, act, *flat)


def finish_kernel(chunks, tile_ref, place_ref, step_ref, *refs):
    pairs = [refs[2 * i : 2 * i + 2] for i in range(chunks)]
    (
        stream_ref, bias_ref, gate_ref, scale_ref, shift_ref, w_ref, b_ref, latent_ref, hidden_ref, next_ref, proj_ref,
    ) = refs[2 * chunks :]
    places = len(PATH)
    chip = proj_ref.shape[1] // places
    mine = place_ref[places + tile_ref[0] // 2]
    behind = [0] + [distance for step in range(1, places // 2) for distance in (step, -step)] + [places // 2]
    for own_ref, far_ref in pairs:
        for first in range(0, own_ref.shape[1], chip):
            source = place_ref[(mine - behind.pop(0) + places) % places]
            target = pl.ds(pl.multiple_of(chip * source, 128), chip)
            part = slice(first, first + chip)
            proj_ref[:, target] = own_ref[:, part] + far_ref[:, part].astype(jnp.float32)
    updated = stream_ref[0].astype(jnp.float32) + gate_ref[...] * (proj_ref[...] + bias_ref[...])
    hidden_ref[0] = updated.astype(jnp.bfloat16)

    @pl.when(pl.program_id(0) > 0)
    def _():
        center = updated - jnp.mean(updated, axis=-1, keepdims=True)
        variance = jnp.mean(center * center, axis=-1, keepdims=True)
        normed = center * lax.rsqrt(variance + EPS)
        modulated = ((1.0 + scale_ref[...]) * normed + shift_ref[...]).astype(jnp.bfloat16)
        velocity = lax.dot_general(w_ref[...], modulated, NT, preferred_element_type=jnp.float32)
        next_ref[0] = latent_ref[0] + step_ref[0] * (velocity + b_ref[...])


def finish(tile, step, chunks, stream, bias, gate, scale, shift, w_final, b_final, latent):
    blocks, slots, width = stream.shape
    channels = w_final.shape[0]
    flat = [array for pair in chunks for array in pair]

    def whole(array):
        return pl.BlockSpec(array.shape, lambda b, *_: (0, 0))

    tokens = pl.BlockSpec((1, slots, width), lambda b, *_: (b, 0, 0))
    image = pl.BlockSpec((1, channels, slots), lambda b, *_: (jnp.maximum(b - 1, 0), 0, 0))
    return pl.pallas_call(
        functools.partial(finish_kernel, len(chunks)),
        grid_spec=pltpu.PrefetchScalarGridSpec(
            num_scalar_prefetch=3,
            grid=(blocks,),
            in_specs=[pl.BlockSpec((slots, array.shape[1]), lambda b, *_: (b, 0)) for array in flat]
            + [
                tokens,
                whole(bias),
                whole(gate),
                whole(scale),
                whole(shift),
                whole(w_final),
                whole(b_final),
                image,
            ],
            out_specs=[tokens, image],
            scratch_shapes=[pltpu.VMEM((slots, width), jnp.float32)],
        ),
        out_shape=[
            jax.ShapeDtypeStruct(stream.shape, jnp.bfloat16),
            jax.ShapeDtypeStruct(latent.shape, jnp.float32),
        ],
        compiler_params=pltpu.CompilerParams(vmem_limit_bytes=VMEM),
        cost_estimate=pl.CostEstimate(
            flops=blocks * slots * width * 160, bytes_accessed=blocks * slots * width * 10, transcendentals=0
        ),
        name="finish",
    )(tile, np.array(PATH + PLACE, np.int32), step, *flat, stream, bias, gate, scale, shift, w_final, b_final, latent)


PATH = (0, 1, 3, 5, 7, 6, 4, 2)
PLACE = tuple(PATH.index(chip) for chip in range(len(PATH)))


def hop(array, by):
    places = len(PATH)
    pairs = [(2 * PATH[i] + c, 2 * PATH[(i + by) % places] + c) for i in range(places) for c in range(2)]
    return lax.ppermute(array, "tile", pairs)


def both_cores(array, first=0):
    other = lax.ppermute(array, "tile", [(t, t ^ 1) for t in range(2 * len(PATH))])
    return [(True, first, array), (False, first, other)]


def paired(
    partners,
    attn_proj,
    mlp_proj,
    stream,
    text_len,
    q_gain,
    k_gain,
    w_out_attn,
    w_out_mlp,
    bias_out,
    gate_mod,
    final_shift,
    final_scale,
    w_final,
    b_final,
    latent,
    step_size,
):
    me = lax.axis_index("head")
    half = me[None].astype(jnp.int32)
    trade = functools.partial(lax.ppermute, axis_name="head", perm=[(0, 1), (1, 0)])

    tile = lax.axis_index("tile").astype(jnp.int32)
    core = (tile % 2)[None]
    own_attn = jnp.transpose(attn_proj[0], (0, 2, 1, 3))
    own_units = mlp_proj[0]
    slots = own_attn.shape[2]
    units = own_units.shape[2] // partners
    width = own_attn.shape[3] // partners
    sent_attn = lax.dynamic_slice_in_dim(own_attn, (1 - me) * width, width, axis=3)
    sent_attn, attn_w, act_w = lax.optimization_barrier((sent_attn, w_out_attn.T, w_out_mlp.T))
    far_attn = trade(sent_attn)
    block = jnp.concatenate([attn_w, act_w], axis=1)

    onward, back = hop(block, 1), hop(block, -1)
    chips = [both_cores(block)]

    tables = make_tables(half, text_len, q_gain, k_gain, 6 * slots)
    act_near = activate(half, own_units, units)
    sent_units = lax.dynamic_slice_in_dim(own_units, (1 - me) * units, units, axis=2)

    onward, back, tables, act_near, sent_units, chips = lax.optimization_barrier(
        (onward, back, tables, act_near, sent_units, [[piece[2] for piece in chip] for chip in chips])
    )
    chips = [[(True, 0, chip[0]), (False, 0, chip[1])] for chip in chips]
    chips += [both_cores(onward), both_cores(back)]
    onward, back = hop(onward, 1), hop(back, -1)
    far_attn, sent_units = lax.optimization_barrier((far_attn, sent_units))
    far_units = trade(sent_units)
    attn = attend(half, own_attn, far_attn, tables)
    attn, onward, back = lax.optimization_barrier((attn, onward, back))
    chips += [both_cores(onward), both_cores(back)]
    onward, back = hop(onward, 1), hop(back, -1)
    far_units, attn = lax.optimization_barrier((far_units, attn))
    act = activate(jnp.zeros_like(half), far_units, units, act_near)

    chunks = []

    def send(group):
        own, sent = project(core, attn, act, group)
        chunks.append((own, trade(sent)))
        return sent

    sent = send(chips[0:1])
    attn, sent = lax.optimization_barrier((attn, sent))
    sent = send(chips[1:3])
    onward, back, attn, sent, chunks[0] = lax.optimization_barrier((onward, back, attn, sent, chunks[0]))
    middle = block.shape[0] // 2
    last = hop(onward[:middle], 1), hop(back[middle:], -1)
    chips += [both_cores(onward), both_cores(back)]
    sent = send(chips[3:5])
    attn, sent, chunks[1] = lax.optimization_barrier((attn, sent, chunks[1]))
    sent = send(chips[5:7])
    onward, back, attn, sent, chunks[2] = lax.optimization_barrier((*last, attn, sent, chunks[2]))
    chips.append(both_cores(onward) + both_cores(back, middle))
    send(chips[7:8])

    hidden, following = finish(
        tile[None],
        step_size,
        chunks,
        stream[0],
        bias_out[None, :],
        gate_mod,
        final_scale,
        final_shift,
        w_final.T,
        b_final[:, None],
        jnp.transpose(latent[0], (0, 2, 1)),
    )
    return hidden[None], jnp.transpose(following, (0, 2, 1))[None]


def solution(mesh):
    placed = (
        P("tile", None, "head", None, None),
        P("tile", None, "head", None),
        P("tile", None, "head", None),
        P("tile"),
        P(),
        P(),
        P("head", "tile"),
        P("head", "tile"),
        P(),
        P("tile", None),
        P("tile", None),
        P("tile", None),
        P(),
        P(),
        P("tile", None, "head", None),
        P("tile"),
    )
    return jax.shard_map(
        functools.partial(paired, mesh.shape["head"]) if fits(mesh.shape) else general,
        mesh=mesh,
        in_specs=placed,
        out_specs=(P("tile", None, "head", None), P("tile", None, "head", None)),
        check_vma=False,
    )
```

```python
import functools
import math

import jax
import jax.numpy as jnp
import numpy as np
from jax import lax
from jax.experimental import pallas as pl
from jax.experimental.pallas import tpu as pltpu
from jax.sharding import PartitionSpec as P

HEAD_DIM = 128
SLOTS = 192
GRID_W = 32


def rope_tables(positions):
    pairs_zero = HEAD_DIM // 16
    pairs_axis = (HEAD_DIM // 2 - pairs_zero) // 2
    freqs = 10000.0 ** (-jnp.arange(pairs_axis, dtype=jnp.float32) / pairs_axis)
    count = positions.shape[0]
    angles = [jnp.zeros((count, HEAD_DIM // 2), jnp.float32)]
    for block in range(1, 3):
        image_index = (block - 1) * SLOTS + positions
        rows = (image_index // GRID_W).astype(jnp.float32)
        columns = (image_index % GRID_W).astype(jnp.float32)
        angles.append(
            jnp.concatenate(
                [
                    jnp.zeros((count, pairs_zero), jnp.float32),
                    rows[:, None] * freqs[None, :],
                    columns[:, None] * freqs[None, :],
                ],
                axis=1,
            )
        )
    stacked = jnp.stack(angles)
    return (jnp.cos(stacked), jnp.sin(stacked))


def prepare(raw, gain, cosine, sine):
    normed = raw * lax.rsqrt(jnp.mean(raw * raw, axis=-1, keepdims=True) + 1e-06) * gain
    halves = normed.reshape(normed.shape[:-1] + (HEAD_DIM // 2, 2))
    first = halves[..., 0]
    second = halves[..., 1]
    cosine = cosine[None, :, :, None, :]
    sine = sine[None, :, :, None, :]
    rotated = jnp.stack([first * cosine - second * sine, first * sine + second * cosine], axis=-1)
    return rotated.reshape(raw.shape).astype(jnp.bfloat16)


def attend_head(inputs):
    queries, keys, values, live = inputs
    scores = jnp.einsum("qd,kd->qk", queries, keys, preferred_element_type=jnp.float32) / math.sqrt(
        HEAD_DIM
    )
    scores = jnp.where(live[None, :], scores, -jnp.inf)
    top = jnp.max(scores, axis=-1, keepdims=True)
    weights = jnp.exp(scores - top)
    total = jnp.sum(weights, axis=-1, keepdims=True)
    mixed = jnp.dot(weights.astype(jnp.bfloat16), values, preferred_element_type=jnp.float32)
    return (mixed / total).astype(jnp.bfloat16)


def attend_request(inputs):
    queries, keys, values, live = inputs
    count = queries.shape[1]
    broad_live = jnp.broadcast_to(live[None, :], (count, live.shape[0]))
    result = lax.map(
        attend_head,
        (
            jnp.moveaxis(queries, 1, 0),
            jnp.moveaxis(keys, 1, 0),
            jnp.moveaxis(values, 1, 0),
            broad_live,
        ),
    )
    return jnp.moveaxis(result, 0, 1)


def general(
    attn_proj,
    mlp_proj,
    stream,
    text_len,
    q_gain,
    k_gain,
    w_out_attn,
    w_out_mlp,
    bias_out,
    gate_mod,
    final_shift,
    final_scale,
    w_final,
    b_final,
    latent,
    step_size,
):
    requests = attn_proj.shape[0]
    own_slots = attn_proj.shape[2]
    width = attn_proj.shape[4]
    heads = width // HEAD_DIM
    start_slot = lax.axis_index("head") * own_slots
    positions = start_slot + jnp.arange(own_slots, dtype=jnp.int32)
    cosine, sine = rope_tables(positions)
    head_shape = (requests, 3, own_slots, heads, HEAD_DIM)
    queries = prepare(
        attn_proj[:, :, :, 0].astype(jnp.float32).reshape(head_shape), q_gain, cosine, sine
    )
    keys = prepare(
        attn_proj[:, :, :, 1].astype(jnp.float32).reshape(head_shape), k_gain, cosine, sine
    )
    packed = jnp.stack(
        [
            queries.reshape(requests, 3, own_slots, width),
            keys.reshape(requests, 3, own_slots, width),
            attn_proj[:, :, :, 2],
        ],
        axis=3,
    )
    units = mlp_proj[:, :, :, None, :]
    moved, hidden_units = (
        lax.all_to_all(packed, "head", split_axis=4, concat_axis=2, tiled=True),
        lax.all_to_all(units, "head", split_axis=4, concat_axis=2, tiled=True),
    )
    hidden_units = hidden_units[:, :, :, 0]
    tile_slots = moved.shape[2]
    local_width = moved.shape[4]
    local_heads = local_width // HEAD_DIM
    flat_shape = (requests, 3 * tile_slots, local_heads, HEAD_DIM)
    all_positions = jnp.arange(tile_slots, dtype=jnp.int32)
    text_live = all_positions[None, :] < text_len[:, None]
    image_live = jnp.ones_like(text_live)
    live = jnp.stack([text_live, image_live, image_live], axis=1).reshape(requests, 3 * tile_slots)
    attn_out = lax.map(
        attend_request,
        (
            moved[:, :, :, 0].reshape(flat_shape),
            moved[:, :, :, 1].reshape(flat_shape),
            moved[:, :, :, 2].reshape(flat_shape),
            live,
        ),
    )
    attn_out = attn_out.reshape(requests, 3, tile_slots, local_width)
    mlp_act = jax.nn.gelu(hidden_units.astype(jnp.float32), approximate=True).astype(jnp.bfloat16)
    term = jnp.einsum(
        "rbsk,kd->rbsd",
        attn_out,
        lax.all_gather(w_out_attn, "tile", axis=1, tiled=True),
        preferred_element_type=jnp.float32,
    )
    term = term + jnp.einsum(
        "rbsk,kd->rbsd",
        mlp_act,
        lax.all_gather(w_out_mlp, "tile", axis=1, tiled=True),
        preferred_element_type=jnp.float32,
    )
    proj = lax.psum_scatter(term, "head", scatter_dimension=2, tiled=True)
    updated = stream.astype(jnp.float32) + gate_mod[:, None, None, :] * (proj + bias_out)
    hidden_out = updated.astype(jnp.bfloat16)
    image = updated[:, 1:]
    center = image - jnp.mean(image, axis=-1, keepdims=True)
    variance = jnp.mean(center * center, axis=-1, keepdims=True)
    normed = center * lax.rsqrt(variance + 1e-06)
    modulated = (
        (1.0 + final_scale[:, None, None, :]) * normed + final_shift[:, None, None, :]
    ).astype(jnp.bfloat16)
    velocity = (
        jnp.einsum("rbsd,dc->rbsc", modulated, w_final, preferred_element_type=jnp.float32)
        + b_final
    )
    latent_next = latent + step_size[:, None, None, None] * velocity
    return (hidden_out, latent_next)


EPS = 1e-06
SCALE = math.log2(math.e) / math.sqrt(HEAD_DIM)
VMEM = 60 * 1024 * 1024
LESS = 34 * 1024 * 1024
NT = (((1,), (1,)), ((), ()))


def fits(sizes):
    return sizes["head"] == 2 and sizes["tile"] == 2 * len(PATH)


def tables_kernel(half_ref, len_ref, row_freq_ref, col_freq_ref, q_ref, k_ref, cq_ref, sq_ref, ck_ref, sk_ref, mask_ref, swap_ref):
    rows = cq_ref.shape[0]
    slots = rows // 6

    def place(axis, shape):
        index = lax.broadcasted_iota(jnp.int32, shape, axis)
        away = index >= rows // 2
        block = (index - jnp.where(away, rows // 2, 0)) // slots
        slot = index % slots + slots * jnp.where(away, 1 - half_ref[0], half_ref[0])
        return block, slot

    shape = (rows, HEAD_DIM)
    block, slot = place(0, shape)
    image = (block - 1) * SLOTS + slot
    angle = (image // GRID_W).astype(jnp.float32) * row_freq_ref[...]
    angle += (image % GRID_W).astype(jnp.float32) * col_freq_ref[...]
    angle = jnp.where(block == 0, 0.0, angle)
    cosine, sine = jnp.cos(angle), jnp.sin(angle)
    odd = lax.broadcasted_iota(jnp.int32, shape, 1) % 2 == 1
    for gain_ref, c_ref, s_ref in ((q_ref, cq_ref, sq_ref), (k_ref, ck_ref, sk_ref)):
        gain = jnp.broadcast_to(gain_ref[...], shape)
        partner = jnp.where(odd, pltpu.roll(gain, 1, 1), -pltpu.roll(gain, HEAD_DIM - 1, 1))
        c_ref[...] = cosine * gain
        s_ref[...] = sine * partner
    block, slot = place(1, (1, rows))
    mask_ref[...] = jnp.where((block > 0) | (slot < len_ref[0]), 0.0, -jnp.inf)
    square = (HEAD_DIM, HEAD_DIM)
    column = lax.broadcasted_iota(jnp.int32, square, 1)
    other = column + 1 - 2 * (column % 2)
    swap_ref[...] = jnp.where(lax.broadcasted_iota(jnp.int32, square, 0) == other, 1.0, 0.0).astype(jnp.bfloat16)


def make_tables(half, text_len, q_gain, k_gain, rows):
    pairs_zero = HEAD_DIM // 16
    pairs_axis = (HEAD_DIM // 2 - pairs_zero) // 2
    freqs = 10000.0 ** (-np.arange(pairs_axis, dtype=np.float32) / np.float32(pairs_axis))
    row_freq, col_freq = np.zeros((2, 1, HEAD_DIM // 2), np.float32)
    row_freq[0, pairs_zero : pairs_zero + pairs_axis] = freqs
    col_freq[0, pairs_zero + pairs_axis :] = freqs
    scalars = pl.BlockSpec(memory_space=pltpu.SMEM)
    table = jax.ShapeDtypeStruct((rows, HEAD_DIM), jnp.float32)
    return pl.pallas_call(
        tables_kernel,
        in_specs=[scalars, scalars] + [pl.BlockSpec(memory_space=pltpu.VMEM)] * 4,
        out_shape=[
            table,
            table,
            table,
            table,
            jax.ShapeDtypeStruct((1, rows), jnp.float32),
            jax.ShapeDtypeStruct((HEAD_DIM, HEAD_DIM), jnp.bfloat16),
        ],
        compiler_params=pltpu.CompilerParams(vmem_limit_bytes=VMEM),
        cost_estimate=pl.CostEstimate(flops=rows * HEAD_DIM * 8, bytes_accessed=rows * HEAD_DIM * 4, transcendentals=0),
        name="tables",
    )(
        half,
        text_len,
        np.repeat(row_freq, 2, axis=1),
        np.repeat(col_freq, 2, axis=1),
        q_gain[None, :],
        k_gain[None, :],
    )


def attend_kernel(half_ref, own_ref, far_ref, cq_ref, sq_ref, ck_ref, sk_ref, mask_ref, swap_ref, *refs):
    out_ref = refs[-1]
    rows = own_ref.shape[0] * own_ref.shape[2]

    def load(part):
        return jnp.concatenate(
            [own_ref[:, part].reshape(rows, HEAD_DIM), far_ref[:, part].reshape(rows, HEAD_DIM)], axis=0
        )

    def turn(raw, straight, crossed):
        wide = raw.astype(jnp.float32)
        scale = lax.rsqrt(jnp.mean(wide * wide, axis=-1, keepdims=True) + EPS)
        partner = jnp.dot(raw, swap_ref[...], preferred_element_type=jnp.float32)
        return ((wide * straight + partner * crossed) * scale).astype(jnp.bfloat16)

    queries = turn(load(0), cq_ref[...], sq_ref[...])
    keys = turn(load(1), ck_ref[...], sk_ref[...])
    scores = lax.dot_general(queries, keys, NT, preferred_element_type=jnp.float32)
    scores = scores * SCALE + mask_ref[...]
    weights = jnp.exp2(scores - jnp.max(scores, axis=-1, keepdims=True))
    total = jnp.sum(weights, axis=-1, keepdims=True)
    mixed = jnp.dot(weights.astype(jnp.bfloat16), load(2), preferred_element_type=jnp.float32)
    out_ref[...] = (mixed / total).astype(jnp.bfloat16)


def attend(half, own, far, tables, part, parts, into=None):
    blocks, kinds, slots, width = far.shape
    heads = width // HEAD_DIM
    count = heads // parts
    first = part * count
    rows = 2 * blocks * slots
    shape = (blocks, kinds, slots, HEAD_DIM)
    whole = pl.BlockSpec((rows, HEAD_DIM), lambda g, half: (0, 0))
    return pl.pallas_call(
        attend_kernel,
        grid_spec=pltpu.PrefetchScalarGridSpec(
            num_scalar_prefetch=1,
            grid=(count,),
            in_specs=[
                pl.BlockSpec(shape, lambda g, half: (0, 0, 0, half[0] * heads + first + g)),
                pl.BlockSpec(shape, lambda g, half: (0, 0, 0, first + g)),
                whole,
                whole,
                whole,
                whole,
                pl.BlockSpec((1, rows), lambda g, half: (0, 0)),
                pl.BlockSpec((HEAD_DIM, HEAD_DIM), lambda g, half: (0, 0)),
            ]
            + ([] if into is None else [pl.BlockSpec(memory_space=pl.ANY)]),
            out_specs=pl.BlockSpec((rows, HEAD_DIM), lambda g, half: (0, first + g)),
        ),
        out_shape=jax.ShapeDtypeStruct((rows, width), jnp.bfloat16),
        input_output_aliases={} if into is None else {9: 0},
        compiler_params=pltpu.CompilerParams(vmem_limit_bytes=VMEM),
        cost_estimate=pl.CostEstimate(
            flops=count * rows * rows * HEAD_DIM * 4,
            bytes_accessed=rows * width * 8,
            transcendentals=0,
        ),
        name="attend",
    )(half, own, far, *tables, *([] if into is None else [into]))


def gelu_kernel(part_ref, units_ref, *refs):
    refs[-1][...] = jax.nn.gelu(units_ref[0].astype(jnp.float32), approximate=True).astype(jnp.bfloat16)


def activate(part, units, width, into=None):
    blocks, slots, _ = units.shape
    first = 0 if into is None else blocks
    return pl.pallas_call(
        gelu_kernel,
        grid_spec=pltpu.PrefetchScalarGridSpec(
            num_scalar_prefetch=1,
            grid=(blocks,),
            in_specs=[pl.BlockSpec((1, slots, width), lambda b, part: (b, 0, part[0]))]
            + ([] if into is None else [pl.BlockSpec(memory_space=pl.ANY)]),
            out_specs=pl.BlockSpec((slots, width), lambda b, part: (first + b, 0)),
        ),
        out_shape=jax.ShapeDtypeStruct((2 * blocks * slots, width), jnp.bfloat16),
        input_output_aliases={} if into is None else {2: 0},
        compiler_params=pltpu.CompilerParams(vmem_limit_bytes=LESS),
        cost_estimate=pl.CostEstimate(
            flops=blocks * slots * width * 4, bytes_accessed=blocks * slots * width, transcendentals=0
        ),
        name="activate",
    )(part, units, *([] if into is None else [into]))


def project_kernel(layout, core_ref, attn_ref, act_ref, *refs):
    pieces, (own_ref, far_ref, w_ref, sems) = refs[:-4], refs[-4:]
    depth = attn_ref.shape[1]
    rows, columns = own_ref.shape
    core = core_ref[0]
    copies = []
    for (base, here, share), piece in zip(layout, pieces):
        start = base + (core if here else 1 - core) * share
        place = pl.ds(pl.multiple_of(start, 16), piece.shape[0])
        copies.append(pltpu.make_async_copy(piece, w_ref.at[place], sems.at[len(copies)]))
        copies[-1].start()
    pending = [base // (2 * share) * 2 * share for base, _, share in layout]
    for first in range(0, columns, 256):
        end = min(first + 256, columns)
        while pending and pending[0] < end:
            copies[-len(pending)].wait()
            pending.pop(0)
        total = lax.dot_general(attn_ref[...], w_ref[first:end, :depth], NT, preferred_element_type=jnp.float32)
        total += lax.dot_general(act_ref[...], w_ref[first:end, depth:], NT, preferred_element_type=jnp.float32)
        own_ref[:, first:end] = total[:rows]
        far_ref[:, first:end] = total[rows:].astype(jnp.bfloat16)


def project(core, attn, act, chips):
    share = sum(piece.shape[0] for here, _, piece in chips[0] if here)
    layout, flat = [], []
    for index, pieces in enumerate(chips):
        for here, first, piece in pieces:
            layout.append((2 * share * index + first, here, share))
            flat.append(piece)
    rows, depth = attn.shape[0] // 2, attn.shape[1] + act.shape[1]
    columns = 2 * share * len(chips)
    inside = pl.BlockSpec(memory_space=pltpu.VMEM)
    return pl.pallas_call(
        functools.partial(project_kernel, layout),
        in_specs=[pl.BlockSpec(memory_space=pltpu.SMEM), inside, inside]
        + [pl.BlockSpec(memory_space=pl.ANY)] * len(flat),
        out_specs=[inside, inside],
        out_shape=[
            jax.ShapeDtypeStruct((rows, columns), jnp.float32),
            jax.ShapeDtypeStruct((rows, columns), jnp.bfloat16),
        ],
        scratch_shapes=[
            pltpu.VMEM((columns, depth), jnp.bfloat16),
            pltpu.SemaphoreType.DMA((len(flat),)),
        ],
        compiler_params=pltpu.CompilerParams(vmem_limit_bytes=LESS),
        cost_estimate=pl.CostEstimate(
            flops=rows * columns * depth // 2, bytes_accessed=columns * depth // 4, transcendentals=0
        ),
        name="project",
    )(core, attn, act, *flat)


def finish_kernel(chunks, tile_ref, place_ref, step_ref, *refs):
    pairs = [refs[2 * i : 2 * i + 2] for i in range(chunks)]
    (
        stream_ref, bias_ref, gate_ref, scale_ref, shift_ref, w_ref, b_ref, latent_ref, hidden_ref, next_ref, proj_ref,
    ) = refs[2 * chunks :]
    places = len(PATH)
    chip = proj_ref.shape[1] // places
    mine = place_ref[places + tile_ref[0] // 2]
    behind = [0] + [distance for step in range(1, places // 2) for distance in (step, -step)] + [places // 2]
    for own_ref, far_ref in pairs:
        for first in range(0, own_ref.shape[1], chip):
            source = place_ref[(mine - behind.pop(0) + places) % places]
            target = pl.ds(pl.multiple_of(chip * source, 128), chip)
            part = slice(first, first + chip)
            proj_ref[:, target] = own_ref[:, part] + far_ref[:, part].astype(jnp.float32)
    updated = stream_ref[0].astype(jnp.float32) + gate_ref[...] * (proj_ref[...] + bias_ref[...])
    hidden_ref[0] = updated.astype(jnp.bfloat16)

    @pl.when(pl.program_id(0) > 0)
    def _():
        center = updated - jnp.mean(updated, axis=-1, keepdims=True)
        variance = jnp.mean(center * center, axis=-1, keepdims=True)
        normed = center * lax.rsqrt(variance + EPS)
        modulated = ((1.0 + scale_ref[...]) * normed + shift_ref[...]).astype(jnp.bfloat16)
        velocity = lax.dot_general(w_ref[...], modulated, NT, preferred_element_type=jnp.float32)
        next_ref[0] = latent_ref[0] + step_ref[0] * (velocity + b_ref[...])


def finish(tile, step, chunks, stream, bias, gate, scale, shift, w_final, b_final, latent):
    blocks, slots, width = stream.shape
    channels = w_final.shape[0]
    flat = [array for pair in chunks for array in pair]

    def whole(array):
        return pl.BlockSpec(array.shape, lambda b, *_: (0, 0))

    tokens = pl.BlockSpec((1, slots, width), lambda b, *_: (b, 0, 0))
    image = pl.BlockSpec((1, channels, slots), lambda b, *_: (jnp.maximum(b - 1, 0), 0, 0))
    return pl.pallas_call(
        functools.partial(finish_kernel, len(chunks)),
        grid_spec=pltpu.PrefetchScalarGridSpec(
            num_scalar_prefetch=3,
            grid=(blocks,),
            in_specs=[pl.BlockSpec((slots, array.shape[1]), lambda b, *_: (b, 0)) for array in flat]
            + [
                tokens,
                whole(bias),
                whole(gate),
                whole(scale),
                whole(shift),
                whole(w_final),
                whole(b_final),
                image,
            ],
            out_specs=[tokens, image],
            scratch_shapes=[pltpu.VMEM((slots, width), jnp.float32)],
        ),
        out_shape=[
            jax.ShapeDtypeStruct(stream.shape, jnp.bfloat16),
            jax.ShapeDtypeStruct(latent.shape, jnp.float32),
        ],
        compiler_params=pltpu.CompilerParams(vmem_limit_bytes=VMEM),
        cost_estimate=pl.CostEstimate(
            flops=blocks * slots * width * 160, bytes_accessed=blocks * slots * width * 10, transcendentals=0
        ),
        name="finish",
    )(tile, np.array(PATH + PLACE, np.int32), step, *flat, stream, bias, gate, scale, shift, w_final, b_final, latent)


PATH = (0, 1, 3, 5, 7, 6, 4, 2)
PLACE = tuple(PATH.index(chip) for chip in range(len(PATH)))


def hop(array, by):
    places = len(PATH)
    pairs = [(2 * PATH[i] + c, 2 * PATH[(i + by) % places] + c) for i in range(places) for c in range(2)]
    return lax.ppermute(array, "tile", pairs)


def both_cores(array, first=0):
    other = lax.ppermute(array, "tile", [(t, t ^ 1) for t in range(2 * len(PATH))])
    return [(True, first, array), (False, first, other)]


def paired(
    partners,
    attn_proj,
    mlp_proj,
    stream,
    text_len,
    q_gain,
    k_gain,
    w_out_attn,
    w_out_mlp,
    bias_out,
    gate_mod,
    final_shift,
    final_scale,
    w_final,
    b_final,
    latent,
    step_size,
):
    me = lax.axis_index("head")
    half = me[None].astype(jnp.int32)
    trade = functools.partial(lax.ppermute, axis_name="head", perm=[(0, 1), (1, 0)])

    tile = lax.axis_index("tile").astype(jnp.int32)
    core = (tile % 2)[None]
    own_attn = jnp.transpose(attn_proj[0], (0, 2, 1, 3))
    own_units = mlp_proj[0]
    slots = own_attn.shape[2]
    units = own_units.shape[2] // partners
    width = own_attn.shape[3] // partners
    sent_attn = lax.dynamic_slice_in_dim(own_attn, (1 - me) * width, width, axis=3)
    block = jnp.concatenate([w_out_attn.T, w_out_mlp.T], axis=1)

    onward, back = hop(block, 1), hop(block, -1)
    far_attn = trade(sent_attn)
    chips = [both_cores(block)]

    tables = make_tables(half, text_len, q_gain, k_gain, 6 * slots)
    act_near = activate(half, own_units, units)
    sent_units = lax.dynamic_slice_in_dim(own_units, (1 - me) * units, units, axis=2)

    onward, back, tables, act_near, sent_units, chips = lax.optimization_barrier(
        (onward, back, tables, act_near, sent_units, [[piece[2] for piece in chip] for chip in chips])
    )
    chips = [[(True, 0, chip[0]), (False, 0, chip[1])] for chip in chips]
    chips += [both_cores(onward), both_cores(back)]
    onward, back = hop(onward, 1), hop(back, -1)
    far_attn, sent_units = lax.optimization_barrier((far_attn, sent_units))
    far_units = trade(sent_units)
    attn = attend(half, own_attn, far_attn, tables, 0, 2)
    blocks = [piece[2] for chip in chips[1:] for piece in chip]
    attn, onward, back, blocks = lax.optimization_barrier((attn, onward, back, blocks))
    chips[1:] = [[(True, 0, blocks[i]), (False, 0, blocks[i + 1])] for i in (0, 2)]
    chips += [both_cores(onward), both_cores(back)]
    onward, back = hop(onward, 1), hop(back, -1)
    attn = attend(half, own_attn, far_attn, tables, 1, 2, attn)
    far_units, attn = lax.optimization_barrier((far_units, attn))
    act = activate(jnp.zeros_like(half), far_units, units, act_near)

    chunks = []

    def send(group):
        own, sent = project(core, attn, act, group)
        chunks.append((own, trade(sent)))
        return sent

    sent = send(chips[0:1])
    attn, sent = lax.optimization_barrier((attn, sent))
    sent = send(chips[1:3])
    onward, back, attn, sent, chunks[0] = lax.optimization_barrier((onward, back, attn, sent, chunks[0]))
    middle = block.shape[0] // 2
    last = hop(onward[:middle], 1), hop(back[middle:], -1)
    chips += [both_cores(onward), both_cores(back)]
    sent = send(chips[3:5])
    attn, sent, chunks[1] = lax.optimization_barrier((attn, sent, chunks[1]))
    sent = send(chips[5:7])
    onward, back, attn, sent, chunks[2] = lax.optimization_barrier((*last, attn, sent, chunks[2]))
    chips.append(both_cores(onward) + both_cores(back, middle))
    send(chips[7:8])

    hidden, following = finish(
        tile[None],
        step_size,
        chunks,
        stream[0],
        bias_out[None, :],
        gate_mod,
        final_scale,
        final_shift,
        w_final.T,
        b_final[:, None],
        jnp.transpose(latent[0], (0, 2, 1)),
    )
    return hidden[None], jnp.transpose(following, (0, 2, 1))[None]


def solution(mesh):
    placed = (
        P("tile", None, "head", None, None),
        P("tile", None, "head", None),
        P("tile", None, "head", None),
        P("tile"),
        P(),
        P(),
        P("head", "tile"),
        P("head", "tile"),
        P(),
        P("tile", None),
        P("tile", None),
        P("tile", None),
        P(),
        P(),
        P("tile", None, "head", None),
        P("tile"),
    )
    return jax.shard_map(
        functools.partial(paired, mesh.shape["head"]) if fits(mesh.shape) else general,
        mesh=mesh,
        in_specs=placed,
        out_specs=(P("tile", None, "head", None), P("tile", None, "head", None)),
        check_vma=False,
    )
```

```python
import functools
import math

import jax
import jax.numpy as jnp
import numpy as np
from jax import lax
from jax.experimental import pallas as pl
from jax.experimental.pallas import tpu as pltpu
from jax.sharding import PartitionSpec as P

HEAD_DIM = 128
SLOTS = 192
GRID_W = 32


def rope_tables(positions):
    pairs_zero = HEAD_DIM // 16
    pairs_axis = (HEAD_DIM // 2 - pairs_zero) // 2
    freqs = 10000.0 ** (-jnp.arange(pairs_axis, dtype=jnp.float32) / pairs_axis)
    count = positions.shape[0]
    angles = [jnp.zeros((count, HEAD_DIM // 2), jnp.float32)]
    for block in range(1, 3):
        image_index = (block - 1) * SLOTS + positions
        rows = (image_index // GRID_W).astype(jnp.float32)
        columns = (image_index % GRID_W).astype(jnp.float32)
        angles.append(
            jnp.concatenate(
                [
                    jnp.zeros((count, pairs_zero), jnp.float32),
                    rows[:, None] * freqs[None, :],
                    columns[:, None] * freqs[None, :],
                ],
                axis=1,
            )
        )
    stacked = jnp.stack(angles)
    return (jnp.cos(stacked), jnp.sin(stacked))


def prepare(raw, gain, cosine, sine):
    normed = raw * lax.rsqrt(jnp.mean(raw * raw, axis=-1, keepdims=True) + 1e-06) * gain
    halves = normed.reshape(normed.shape[:-1] + (HEAD_DIM // 2, 2))
    first = halves[..., 0]
    second = halves[..., 1]
    cosine = cosine[None, :, :, None, :]
    sine = sine[None, :, :, None, :]
    rotated = jnp.stack([first * cosine - second * sine, first * sine + second * cosine], axis=-1)
    return rotated.reshape(raw.shape).astype(jnp.bfloat16)


def attend_head(inputs):
    queries, keys, values, live = inputs
    scores = jnp.einsum("qd,kd->qk", queries, keys, preferred_element_type=jnp.float32) / math.sqrt(
        HEAD_DIM
    )
    scores = jnp.where(live[None, :], scores, -jnp.inf)
    top = jnp.max(scores, axis=-1, keepdims=True)
    weights = jnp.exp(scores - top)
    total = jnp.sum(weights, axis=-1, keepdims=True)
    mixed = jnp.dot(weights.astype(jnp.bfloat16), values, preferred_element_type=jnp.float32)
    return (mixed / total).astype(jnp.bfloat16)


def attend_request(inputs):
    queries, keys, values, live = inputs
    count = queries.shape[1]
    broad_live = jnp.broadcast_to(live[None, :], (count, live.shape[0]))
    result = lax.map(
        attend_head,
        (
            jnp.moveaxis(queries, 1, 0),
            jnp.moveaxis(keys, 1, 0),
            jnp.moveaxis(values, 1, 0),
            broad_live,
        ),
    )
    return jnp.moveaxis(result, 0, 1)


def general(
    attn_proj,
    mlp_proj,
    stream,
    text_len,
    q_gain,
    k_gain,
    w_out_attn,
    w_out_mlp,
    bias_out,
    gate_mod,
    final_shift,
    final_scale,
    w_final,
    b_final,
    latent,
    step_size,
):
    requests = attn_proj.shape[0]
    own_slots = attn_proj.shape[2]
    width = attn_proj.shape[4]
    heads = width // HEAD_DIM
    start_slot = lax.axis_index("head") * own_slots
    positions = start_slot + jnp.arange(own_slots, dtype=jnp.int32)
    cosine, sine = rope_tables(positions)
    head_shape = (requests, 3, own_slots, heads, HEAD_DIM)
    queries = prepare(
        attn_proj[:, :, :, 0].astype(jnp.float32).reshape(head_shape), q_gain, cosine, sine
    )
    keys = prepare(
        attn_proj[:, :, :, 1].astype(jnp.float32).reshape(head_shape), k_gain, cosine, sine
    )
    packed = jnp.stack(
        [
            queries.reshape(requests, 3, own_slots, width),
            keys.reshape(requests, 3, own_slots, width),
            attn_proj[:, :, :, 2],
        ],
        axis=3,
    )
    units = mlp_proj[:, :, :, None, :]
    moved, hidden_units = (
        lax.all_to_all(packed, "head", split_axis=4, concat_axis=2, tiled=True),
        lax.all_to_all(units, "head", split_axis=4, concat_axis=2, tiled=True),
    )
    hidden_units = hidden_units[:, :, :, 0]
    tile_slots = moved.shape[2]
    local_width = moved.shape[4]
    local_heads = local_width // HEAD_DIM
    flat_shape = (requests, 3 * tile_slots, local_heads, HEAD_DIM)
    all_positions = jnp.arange(tile_slots, dtype=jnp.int32)
    text_live = all_positions[None, :] < text_len[:, None]
    image_live = jnp.ones_like(text_live)
    live = jnp.stack([text_live, image_live, image_live], axis=1).reshape(requests, 3 * tile_slots)
    attn_out = lax.map(
        attend_request,
        (
            moved[:, :, :, 0].reshape(flat_shape),
            moved[:, :, :, 1].reshape(flat_shape),
            moved[:, :, :, 2].reshape(flat_shape),
            live,
        ),
    )
    attn_out = attn_out.reshape(requests, 3, tile_slots, local_width)
    mlp_act = jax.nn.gelu(hidden_units.astype(jnp.float32), approximate=True).astype(jnp.bfloat16)
    term = jnp.einsum(
        "rbsk,kd->rbsd",
        attn_out,
        lax.all_gather(w_out_attn, "tile", axis=1, tiled=True),
        preferred_element_type=jnp.float32,
    )
    term = term + jnp.einsum(
        "rbsk,kd->rbsd",
        mlp_act,
        lax.all_gather(w_out_mlp, "tile", axis=1, tiled=True),
        preferred_element_type=jnp.float32,
    )
    proj = lax.psum_scatter(term, "head", scatter_dimension=2, tiled=True)
    updated = stream.astype(jnp.float32) + gate_mod[:, None, None, :] * (proj + bias_out)
    hidden_out = updated.astype(jnp.bfloat16)
    image = updated[:, 1:]
    center = image - jnp.mean(image, axis=-1, keepdims=True)
    variance = jnp.mean(center * center, axis=-1, keepdims=True)
    normed = center * lax.rsqrt(variance + 1e-06)
    modulated = (
        (1.0 + final_scale[:, None, None, :]) * normed + final_shift[:, None, None, :]
    ).astype(jnp.bfloat16)
    velocity = (
        jnp.einsum("rbsd,dc->rbsc", modulated, w_final, preferred_element_type=jnp.float32)
        + b_final
    )
    latent_next = latent + step_size[:, None, None, None] * velocity
    return (hidden_out, latent_next)


EPS = 1e-06
SCALE = math.log2(math.e) / math.sqrt(HEAD_DIM)
VMEM = 60 * 1024 * 1024
LESS = 34 * 1024 * 1024
NT = (((1,), (1,)), ((), ()))


def fits(sizes):
    return sizes["head"] == 2 and sizes["tile"] == 2 * len(PATH)


def tables_kernel(half_ref, len_ref, row_freq_ref, col_freq_ref, q_ref, k_ref, cq_ref, sq_ref, ck_ref, sk_ref, mask_ref, swap_ref):
    rows = cq_ref.shape[0]
    slots = rows // 6

    def place(axis, shape):
        index = lax.broadcasted_iota(jnp.int32, shape, axis)
        away = index >= rows // 2
        block = (index - jnp.where(away, rows // 2, 0)) // slots
        slot = index % slots + slots * jnp.where(away, 1 - half_ref[0], half_ref[0])
        return block, slot

    shape = (rows, HEAD_DIM)
    block, slot = place(0, shape)
    image = (block - 1) * SLOTS + slot
    angle = (image // GRID_W).astype(jnp.float32) * row_freq_ref[...]
    angle += (image % GRID_W).astype(jnp.float32) * col_freq_ref[...]
    angle = jnp.where(block == 0, 0.0, angle)
    cosine, sine = jnp.cos(angle), jnp.sin(angle)
    odd = lax.broadcasted_iota(jnp.int32, shape, 1) % 2 == 1
    for gain_ref, c_ref, s_ref in ((q_ref, cq_ref, sq_ref), (k_ref, ck_ref, sk_ref)):
        gain = jnp.broadcast_to(gain_ref[...], shape)
        partner = jnp.where(odd, pltpu.roll(gain, 1, 1), -pltpu.roll(gain, HEAD_DIM - 1, 1))
        c_ref[...] = cosine * gain
        s_ref[...] = sine * partner
    block, slot = place(1, (1, rows))
    mask_ref[...] = jnp.where((block > 0) | (slot < len_ref[0]), 0.0, -jnp.inf)
    square = (HEAD_DIM, HEAD_DIM)
    column = lax.broadcasted_iota(jnp.int32, square, 1)
    other = column + 1 - 2 * (column % 2)
    swap_ref[...] = jnp.where(lax.broadcasted_iota(jnp.int32, square, 0) == other, 1.0, 0.0).astype(jnp.bfloat16)


def make_tables(half, text_len, q_gain, k_gain, rows):
    pairs_zero = HEAD_DIM // 16
    pairs_axis = (HEAD_DIM // 2 - pairs_zero) // 2
    freqs = 10000.0 ** (-np.arange(pairs_axis, dtype=np.float32) / np.float32(pairs_axis))
    row_freq, col_freq = np.zeros((2, 1, HEAD_DIM // 2), np.float32)
    row_freq[0, pairs_zero : pairs_zero + pairs_axis] = freqs
    col_freq[0, pairs_zero + pairs_axis :] = freqs
    scalars = pl.BlockSpec(memory_space=pltpu.SMEM)
    table = jax.ShapeDtypeStruct((rows, HEAD_DIM), jnp.float32)
    return pl.pallas_call(
        tables_kernel,
        in_specs=[scalars, scalars] + [pl.BlockSpec(memory_space=pltpu.VMEM)] * 4,
        out_shape=[
            table,
            table,
            table,
            table,
            jax.ShapeDtypeStruct((1, rows), jnp.float32),
            jax.ShapeDtypeStruct((HEAD_DIM, HEAD_DIM), jnp.bfloat16),
        ],
        compiler_params=pltpu.CompilerParams(vmem_limit_bytes=VMEM),
        cost_estimate=pl.CostEstimate(flops=rows * HEAD_DIM * 8, bytes_accessed=rows * HEAD_DIM * 4, transcendentals=0),
        name="tables",
    )(
        half,
        text_len,
        np.repeat(row_freq, 2, axis=1),
        np.repeat(col_freq, 2, axis=1),
        q_gain[None, :],
        k_gain[None, :],
    )


def attend_kernel(half_ref, own_ref, far_ref, cq_ref, sq_ref, ck_ref, sk_ref, mask_ref, swap_ref, *refs):
    out_ref = refs[-1]
    rows = own_ref.shape[0] * own_ref.shape[2]

    def load(part):
        return jnp.concatenate(
            [own_ref[:, part].reshape(rows, HEAD_DIM), far_ref[:, part].reshape(rows, HEAD_DIM)], axis=0
        )

    def turn(raw, straight, crossed):
        wide = raw.astype(jnp.float32)
        scale = lax.rsqrt(jnp.mean(wide * wide, axis=-1, keepdims=True) + EPS)
        partner = jnp.dot(raw, swap_ref[...], preferred_element_type=jnp.float32)
        return ((wide * straight + partner * crossed) * scale).astype(jnp.bfloat16)

    queries = turn(load(0), cq_ref[...], sq_ref[...])
    keys = turn(load(1), ck_ref[...], sk_ref[...])
    scores = lax.dot_general(queries, keys, NT, preferred_element_type=jnp.float32)
    scores = scores * SCALE + mask_ref[...]
    weights = jnp.exp2(scores - jnp.max(scores, axis=-1, keepdims=True))
    total = jnp.sum(weights, axis=-1, keepdims=True)
    mixed = jnp.dot(weights.astype(jnp.bfloat16), load(2), preferred_element_type=jnp.float32)
    out_ref[...] = (mixed / total).astype(jnp.bfloat16)


def attend(half, own, far, tables, part, parts, into=None):
    blocks, kinds, slots, width = far.shape
    heads = width // HEAD_DIM
    count = heads // parts
    first = part * count
    rows = 2 * blocks * slots
    shape = (blocks, kinds, slots, HEAD_DIM)
    whole = pl.BlockSpec((rows, HEAD_DIM), lambda g, half: (0, 0))
    return pl.pallas_call(
        attend_kernel,
        grid_spec=pltpu.PrefetchScalarGridSpec(
            num_scalar_prefetch=1,
            grid=(count,),
            in_specs=[
                pl.BlockSpec(shape, lambda g, half: (0, 0, 0, half[0] * heads + first + g)),
                pl.BlockSpec(shape, lambda g, half: (0, 0, 0, first + g)),
                whole,
                whole,
                whole,
                whole,
                pl.BlockSpec((1, rows), lambda g, half: (0, 0)),
                pl.BlockSpec((HEAD_DIM, HEAD_DIM), lambda g, half: (0, 0)),
            ]
            + ([] if into is None else [pl.BlockSpec(memory_space=pl.ANY)]),
            out_specs=pl.BlockSpec((rows, HEAD_DIM), lambda g, half: (0, first + g)),
        ),
        out_shape=jax.ShapeDtypeStruct((rows, width), jnp.bfloat16),
        input_output_aliases={} if into is None else {9: 0},
        compiler_params=pltpu.CompilerParams(vmem_limit_bytes=VMEM),
        cost_estimate=pl.CostEstimate(
            flops=count * rows * rows * HEAD_DIM * 4,
            bytes_accessed=rows * width * 8,
            transcendentals=0,
        ),
        name="attend",
    )(half, own, far, *tables, *([] if into is None else [into]))


def gelu_kernel(part_ref, units_ref, *refs):
    refs[-1][...] = jax.nn.gelu(units_ref[0].astype(jnp.float32), approximate=True).astype(jnp.bfloat16)


def activate(part, units, width, into=None):
    blocks, slots, _ = units.shape
    first = 0 if into is None else blocks
    return pl.pallas_call(
        gelu_kernel,
        grid_spec=pltpu.PrefetchScalarGridSpec(
            num_scalar_prefetch=1,
            grid=(blocks,),
            in_specs=[pl.BlockSpec((1, slots, width), lambda b, part: (b, 0, part[0]))]
            + ([] if into is None else [pl.BlockSpec(memory_space=pl.ANY)]),
            out_specs=pl.BlockSpec((slots, width), lambda b, part: (first + b, 0)),
        ),
        out_shape=jax.ShapeDtypeStruct((2 * blocks * slots, width), jnp.bfloat16),
        input_output_aliases={} if into is None else {2: 0},
        compiler_params=pltpu.CompilerParams(vmem_limit_bytes=LESS),
        cost_estimate=pl.CostEstimate(
            flops=blocks * slots * width * 4, bytes_accessed=blocks * slots * width, transcendentals=0
        ),
        name="activate",
    )(part, units, *([] if into is None else [into]))


def project_kernel(layout, sides, core_ref, attn_ref, act_ref, *refs):
    pieces, outs, (w_ref, sems) = refs[: len(layout)], refs[len(layout) : -2], refs[-2:]
    depth = attn_ref.shape[1]
    rows, columns = outs[0].shape
    taken = pl.ds(rows * sides[0], rows * len(sides))
    core = core_ref[0]
    copies = []
    for (base, here, share), piece in zip(layout, pieces):
        start = base + (core if here else 1 - core) * share
        place = pl.ds(pl.multiple_of(start, 16), piece.shape[0])
        copies.append(pltpu.make_async_copy(piece, w_ref.at[place], sems.at[len(copies)]))
        copies[-1].start()
    pending = [base // (2 * share) * 2 * share for base, _, share in layout]
    for first in range(0, columns, 256):
        end = min(first + 256, columns)
        while pending and pending[0] < end:
            copies[-len(pending)].wait()
            pending.pop(0)
        total = lax.dot_general(attn_ref[taken], w_ref[first:end, :depth], NT, preferred_element_type=jnp.float32)
        total += lax.dot_general(act_ref[taken], w_ref[first:end, depth:], NT, preferred_element_type=jnp.float32)
        for index, out_ref in enumerate(outs):
            out_ref[:, first:end] = total[rows * index : rows * (index + 1)].astype(out_ref.dtype)


def project(core, attn, act, chips, sides=(0, 1)):
    share = sum(piece.shape[0] for here, _, piece in chips[0] if here)
    layout, flat = [], []
    for index, pieces in enumerate(chips):
        for here, first, piece in pieces:
            layout.append((2 * share * index + first, here, share))
            flat.append(piece)
    rows, depth = attn.shape[0] // 2, attn.shape[1] + act.shape[1]
    columns = 2 * share * len(chips)
    inside = pl.BlockSpec(memory_space=pltpu.VMEM)
    return pl.pallas_call(
        functools.partial(project_kernel, layout, sides),
        in_specs=[pl.BlockSpec(memory_space=pltpu.SMEM), inside, inside]
        + [pl.BlockSpec(memory_space=pl.ANY)] * len(flat),
        out_specs=[inside] * len(sides),
        out_shape=[jax.ShapeDtypeStruct((rows, columns), jnp.bfloat16)] * len(sides),
        scratch_shapes=[
            pltpu.VMEM((columns, depth), jnp.bfloat16),
            pltpu.SemaphoreType.DMA((len(flat),)),
        ],
        compiler_params=pltpu.CompilerParams(vmem_limit_bytes=LESS),
        cost_estimate=pl.CostEstimate(
            flops=rows * columns * depth // 2, bytes_accessed=columns * depth // 4, transcendentals=0
        ),
        name="project",
    )(core, attn, act, *flat)


def finish_kernel(chunks, tile_ref, place_ref, step_ref, *refs):
    pairs = [refs[2 * i : 2 * i + 2] for i in range(chunks)]
    (
        stream_ref, bias_ref, gate_ref, scale_ref, shift_ref, w_ref, b_ref, latent_ref, hidden_ref, next_ref, proj_ref,
    ) = refs[2 * chunks :]
    places = len(PATH)
    chip = proj_ref.shape[1] // places
    mine = place_ref[places + tile_ref[0] // 2]
    behind = [0] + [distance for step in range(1, places // 2) for distance in (step, -step)] + [places // 2]
    for own_ref, far_ref in pairs:
        for first in range(0, own_ref.shape[1], chip):
            source = place_ref[(mine - behind.pop(0) + places) % places]
            target = pl.ds(pl.multiple_of(chip * source, 128), chip)
            part = slice(first, first + chip)
            proj_ref[:, target] = own_ref[:, part].astype(jnp.float32) + far_ref[:, part].astype(jnp.float32)
    updated = stream_ref[0].astype(jnp.float32) + gate_ref[...] * (proj_ref[...] + bias_ref[...])
    hidden_ref[0] = updated.astype(jnp.bfloat16)

    @pl.when(pl.program_id(0) > 0)
    def _():
        center = updated - jnp.mean(updated, axis=-1, keepdims=True)
        variance = jnp.mean(center * center, axis=-1, keepdims=True)
        normed = center * lax.rsqrt(variance + EPS)
        modulated = ((1.0 + scale_ref[...]) * normed + shift_ref[...]).astype(jnp.bfloat16)
        velocity = lax.dot_general(w_ref[...], modulated, NT, preferred_element_type=jnp.float32)
        next_ref[0] = latent_ref[0] + step_ref[0] * (velocity + b_ref[...])


def finish(tile, step, chunks, stream, bias, gate, scale, shift, w_final, b_final, latent):
    blocks, slots, width = stream.shape
    channels = w_final.shape[0]
    flat = [array for pair in chunks for array in pair]

    def whole(array):
        return pl.BlockSpec(array.shape, lambda b, *_: (0, 0))

    tokens = pl.BlockSpec((1, slots, width), lambda b, *_: (b, 0, 0))
    image = pl.BlockSpec((1, channels, slots), lambda b, *_: (jnp.maximum(b - 1, 0), 0, 0))
    return pl.pallas_call(
        functools.partial(finish_kernel, len(chunks)),
        grid_spec=pltpu.PrefetchScalarGridSpec(
            num_scalar_prefetch=3,
            grid=(blocks,),
            in_specs=[pl.BlockSpec((slots, array.shape[1]), lambda b, *_: (b, 0)) for array in flat]
            + [
                tokens,
                whole(bias),
                whole(gate),
                whole(scale),
                whole(shift),
                whole(w_final),
                whole(b_final),
                image,
            ],
            out_specs=[tokens, image],
            scratch_shapes=[pltpu.VMEM((slots, width), jnp.float32)],
        ),
        out_shape=[
            jax.ShapeDtypeStruct(stream.shape, jnp.bfloat16),
            jax.ShapeDtypeStruct(latent.shape, jnp.float32),
        ],
        compiler_params=pltpu.CompilerParams(vmem_limit_bytes=VMEM),
        cost_estimate=pl.CostEstimate(
            flops=blocks * slots * width * 160, bytes_accessed=blocks * slots * width * 10, transcendentals=0
        ),
        name="finish",
    )(tile, np.array(PATH + PLACE, np.int32), step, *flat, stream, bias, gate, scale, shift, w_final, b_final, latent)


PATH = (0, 1, 3, 5, 7, 6, 4, 2)
PLACE = tuple(PATH.index(chip) for chip in range(len(PATH)))


def hop(array, by):
    places = len(PATH)
    pairs = [(2 * PATH[i] + c, 2 * PATH[(i + by) % places] + c) for i in range(places) for c in range(2)]
    return lax.ppermute(array, "tile", pairs)


def both_cores(array, first=0):
    other = lax.ppermute(array, "tile", [(t, t ^ 1) for t in range(2 * len(PATH))])
    return [(True, first, array), (False, first, other)]


def paired(
    partners,
    attn_proj,
    mlp_proj,
    stream,
    text_len,
    q_gain,
    k_gain,
    w_out_attn,
    w_out_mlp,
    bias_out,
    gate_mod,
    final_shift,
    final_scale,
    w_final,
    b_final,
    latent,
    step_size,
):
    me = lax.axis_index("head")
    half = me[None].astype(jnp.int32)
    trade = functools.partial(lax.ppermute, axis_name="head", perm=[(0, 1), (1, 0)])

    tile = lax.axis_index("tile").astype(jnp.int32)
    core = (tile % 2)[None]
    own_attn = jnp.transpose(attn_proj[0], (0, 2, 1, 3))
    own_units = mlp_proj[0]
    slots = own_attn.shape[2]
    units = own_units.shape[2] // partners
    width = own_attn.shape[3] // partners
    sent_attn = lax.dynamic_slice_in_dim(own_attn, (1 - me) * width, width, axis=3)
    block = jnp.concatenate([w_out_attn.T, w_out_mlp.T], axis=1)

    onward, back = hop(block, 1), hop(block, -1)
    far_attn = trade(sent_attn)
    chips = [both_cores(block)]

    tables = make_tables(half, text_len, q_gain, k_gain, 6 * slots)
    act_near = activate(half, own_units, units)
    sent_units = lax.dynamic_slice_in_dim(own_units, (1 - me) * units, units, axis=2)

    onward, back, tables, act_near, sent_units, chips = lax.optimization_barrier(
        (onward, back, tables, act_near, sent_units, [[piece[2] for piece in chip] for chip in chips])
    )
    chips = [[(True, 0, chip[0]), (False, 0, chip[1])] for chip in chips]
    chips += [both_cores(onward), both_cores(back)]
    onward, back = hop(onward, 1), hop(back, -1)
    far_attn, sent_units = lax.optimization_barrier((far_attn, sent_units))
    far_units = trade(sent_units)
    attn = attend(half, own_attn, far_attn, tables, 0, 2)
    blocks = [piece[2] for chip in chips[1:] for piece in chip]
    attn, onward, back, blocks = lax.optimization_barrier((attn, onward, back, blocks))
    chips[1:] = [[(True, 0, blocks[i]), (False, 0, blocks[i + 1])] for i in (0, 2)]
    chips += [both_cores(onward), both_cores(back)]
    onward, back = hop(onward, 1), hop(back, -1)
    attn = attend(half, own_attn, far_attn, tables, 1, 2, attn)
    far_units, attn = lax.optimization_barrier((far_units, attn))
    act = activate(jnp.zeros_like(half), far_units, units, act_near)

    chunks = []

    def send(group):
        own, sent = project(core, attn, act, group)
        chunks.append((own, trade(sent)))
        return sent

    (sent,) = project(core, attn, act, chips[0:1], (1,))
    chunks.append([None, trade(sent)])
    attn, sent = lax.optimization_barrier((attn, sent))
    sent = send(chips[1:3])
    onward, back, attn, sent, chunks[0][1] = lax.optimization_barrier((onward, back, attn, sent, chunks[0][1]))
    middle = block.shape[0] // 2
    last = hop(onward[:middle], 1), hop(back[middle:], -1)
    chips += [both_cores(onward), both_cores(back)]
    sent = send(chips[3:5])
    attn, sent, chunks[1] = lax.optimization_barrier((attn, sent, chunks[1]))
    sent = send(chips[5:7])
    onward, back, attn, sent, chunks[2] = lax.optimization_barrier((*last, attn, sent, chunks[2]))
    chips.append(both_cores(onward) + both_cores(back, middle))
    sent = send(chips[7:8])
    attn, sent = lax.optimization_barrier((attn, sent))
    (chunks[0][0],) = project(core, attn, act, chips[0:1], (0,))

    hidden, following = finish(
        tile[None],
        step_size,
        chunks,
        stream[0],
        bias_out[None, :],
        gate_mod,
        final_scale,
        final_shift,
        w_final.T,
        b_final[:, None],
        jnp.transpose(latent[0], (0, 2, 1)),
    )
    return hidden[None], jnp.transpose(following, (0, 2, 1))[None]


def solution(mesh):
    placed = (
        P("tile", None, "head", None, None),
        P("tile", None, "head", None),
        P("tile", None, "head", None),
        P("tile"),
        P(),
        P(),
        P("head", "tile"),
        P("head", "tile"),
        P(),
        P("tile", None),
        P("tile", None),
        P("tile", None),
        P(),
        P(),
        P("tile", None, "head", None),
        P("tile"),
    )
    return jax.shard_map(
        functools.partial(paired, mesh.shape["head"]) if fits(mesh.shape) else general,
        mesh=mesh,
        in_specs=placed,
        out_specs=(P("tile", None, "head", None), P("tile", None, "head", None)),
        check_vma=False,
    )
```

```python
import functools
import math

import jax
import jax.numpy as jnp
import numpy as np
from jax import lax
from jax.experimental import pallas as pl
from jax.experimental.pallas import tpu as pltpu
from jax.sharding import PartitionSpec as P

HEAD_DIM = 128
SLOTS = 192
GRID_W = 32


def rope_tables(positions):
    pairs_zero = HEAD_DIM // 16
    pairs_axis = (HEAD_DIM // 2 - pairs_zero) // 2
    freqs = 10000.0 ** (-jnp.arange(pairs_axis, dtype=jnp.float32) / pairs_axis)
    count = positions.shape[0]
    angles = [jnp.zeros((count, HEAD_DIM // 2), jnp.float32)]
    for block in range(1, 3):
        image_index = (block - 1) * SLOTS + positions
        rows = (image_index // GRID_W).astype(jnp.float32)
        columns = (image_index % GRID_W).astype(jnp.float32)
        angles.append(
            jnp.concatenate(
                [
                    jnp.zeros((count, pairs_zero), jnp.float32),
                    rows[:, None] * freqs[None, :],
                    columns[:, None] * freqs[None, :],
                ],
                axis=1,
            )
        )
    stacked = jnp.stack(angles)
    return (jnp.cos(stacked), jnp.sin(stacked))


def prepare(raw, gain, cosine, sine):
    normed = raw * lax.rsqrt(jnp.mean(raw * raw, axis=-1, keepdims=True) + 1e-06) * gain
    halves = normed.reshape(normed.shape[:-1] + (HEAD_DIM // 2, 2))
    first = halves[..., 0]
    second = halves[..., 1]
    cosine = cosine[None, :, :, None, :]
    sine = sine[None, :, :, None, :]
    rotated = jnp.stack([first * cosine - second * sine, first * sine + second * cosine], axis=-1)
    return rotated.reshape(raw.shape).astype(jnp.bfloat16)


def attend_head(inputs):
    queries, keys, values, live = inputs
    scores = jnp.einsum("qd,kd->qk", queries, keys, preferred_element_type=jnp.float32) / math.sqrt(
        HEAD_DIM
    )
    scores = jnp.where(live[None, :], scores, -jnp.inf)
    top = jnp.max(scores, axis=-1, keepdims=True)
    weights = jnp.exp(scores - top)
    total = jnp.sum(weights, axis=-1, keepdims=True)
    mixed = jnp.dot(weights.astype(jnp.bfloat16), values, preferred_element_type=jnp.float32)
    return (mixed / total).astype(jnp.bfloat16)


def attend_request(inputs):
    queries, keys, values, live = inputs
    count = queries.shape[1]
    broad_live = jnp.broadcast_to(live[None, :], (count, live.shape[0]))
    result = lax.map(
        attend_head,
        (
            jnp.moveaxis(queries, 1, 0),
            jnp.moveaxis(keys, 1, 0),
            jnp.moveaxis(values, 1, 0),
            broad_live,
        ),
    )
    return jnp.moveaxis(result, 0, 1)


def general(
    attn_proj,
    mlp_proj,
    stream,
    text_len,
    q_gain,
    k_gain,
    w_out_attn,
    w_out_mlp,
    bias_out,
    gate_mod,
    final_shift,
    final_scale,
    w_final,
    b_final,
    latent,
    step_size,
):
    requests = attn_proj.shape[0]
    own_slots = attn_proj.shape[2]
    width = attn_proj.shape[4]
    heads = width // HEAD_DIM
    start_slot = lax.axis_index("head") * own_slots
    positions = start_slot + jnp.arange(own_slots, dtype=jnp.int32)
    cosine, sine = rope_tables(positions)
    head_shape = (requests, 3, own_slots, heads, HEAD_DIM)
    queries = prepare(
        attn_proj[:, :, :, 0].astype(jnp.float32).reshape(head_shape), q_gain, cosine, sine
    )
    keys = prepare(
        attn_proj[:, :, :, 1].astype(jnp.float32).reshape(head_shape), k_gain, cosine, sine
    )
    packed = jnp.stack(
        [
            queries.reshape(requests, 3, own_slots, width),
            keys.reshape(requests, 3, own_slots, width),
            attn_proj[:, :, :, 2],
        ],
        axis=3,
    )
    units = mlp_proj[:, :, :, None, :]
    moved, hidden_units = (
        lax.all_to_all(packed, "head", split_axis=4, concat_axis=2, tiled=True),
        lax.all_to_all(units, "head", split_axis=4, concat_axis=2, tiled=True),
    )
    hidden_units = hidden_units[:, :, :, 0]
    tile_slots = moved.shape[2]
    local_width = moved.shape[4]
    local_heads = local_width // HEAD_DIM
    flat_shape = (requests, 3 * tile_slots, local_heads, HEAD_DIM)
    all_positions = jnp.arange(tile_slots, dtype=jnp.int32)
    text_live = all_positions[None, :] < text_len[:, None]
    image_live = jnp.ones_like(text_live)
    live = jnp.stack([text_live, image_live, image_live], axis=1).reshape(requests, 3 * tile_slots)
    attn_out = lax.map(
        attend_request,
        (
            moved[:, :, :, 0].reshape(flat_shape),
            moved[:, :, :, 1].reshape(flat_shape),
            moved[:, :, :, 2].reshape(flat_shape),
            live,
        ),
    )
    attn_out = attn_out.reshape(requests, 3, tile_slots, local_width)
    mlp_act = jax.nn.gelu(hidden_units.astype(jnp.float32), approximate=True).astype(jnp.bfloat16)
    term = jnp.einsum(
        "rbsk,kd->rbsd",
        attn_out,
        lax.all_gather(w_out_attn, "tile", axis=1, tiled=True),
        preferred_element_type=jnp.float32,
    )
    term = term + jnp.einsum(
        "rbsk,kd->rbsd",
        mlp_act,
        lax.all_gather(w_out_mlp, "tile", axis=1, tiled=True),
        preferred_element_type=jnp.float32,
    )
    proj = lax.psum_scatter(term, "head", scatter_dimension=2, tiled=True)
    updated = stream.astype(jnp.float32) + gate_mod[:, None, None, :] * (proj + bias_out)
    hidden_out = updated.astype(jnp.bfloat16)
    image = updated[:, 1:]
    center = image - jnp.mean(image, axis=-1, keepdims=True)
    variance = jnp.mean(center * center, axis=-1, keepdims=True)
    normed = center * lax.rsqrt(variance + 1e-06)
    modulated = (
        (1.0 + final_scale[:, None, None, :]) * normed + final_shift[:, None, None, :]
    ).astype(jnp.bfloat16)
    velocity = (
        jnp.einsum("rbsd,dc->rbsc", modulated, w_final, preferred_element_type=jnp.float32)
        + b_final
    )
    latent_next = latent + step_size[:, None, None, None] * velocity
    return (hidden_out, latent_next)


EPS = 1e-06
SCALE = math.log2(math.e) / math.sqrt(HEAD_DIM)
VMEM = 60 * 1024 * 1024
LIGHT = 24 * 1024 * 1024
LESS = 34 * 1024 * 1024
NT = (((1,), (1,)), ((), ()))


def fits(sizes):
    return sizes["head"] == 2 and sizes["tile"] == 2 * len(PATH)


def tables_kernel(half_ref, len_ref, row_freq_ref, col_freq_ref, q_ref, k_ref, cq_ref, sq_ref, ck_ref, sk_ref, mask_ref, swap_ref):
    rows = cq_ref.shape[0]
    slots = rows // 6

    def place(axis, shape):
        index = lax.broadcasted_iota(jnp.int32, shape, axis)
        away = index >= rows // 2
        block = (index - jnp.where(away, rows // 2, 0)) // slots
        slot = index % slots + slots * jnp.where(away, 1 - half_ref[0], half_ref[0])
        return block, slot

    shape = (rows, HEAD_DIM)
    block, slot = place(0, shape)
    image = (block - 1) * SLOTS + slot
    angle = (image // GRID_W).astype(jnp.float32) * row_freq_ref[...]
    angle += (image % GRID_W).astype(jnp.float32) * col_freq_ref[...]
    angle = jnp.where(block == 0, 0.0, angle)
    cosine, sine = jnp.cos(angle), jnp.sin(angle)
    odd = lax.broadcasted_iota(jnp.int32, shape, 1) % 2 == 1
    for gain_ref, c_ref, s_ref in ((q_ref, cq_ref, sq_ref), (k_ref, ck_ref, sk_ref)):
        gain = jnp.broadcast_to(gain_ref[...], shape)
        partner = jnp.where(odd, pltpu.roll(gain, 1, 1), -pltpu.roll(gain, HEAD_DIM - 1, 1))
        c_ref[...] = cosine * gain
        s_ref[...] = sine * partner
    block, slot = place(1, (1, rows))
    mask_ref[...] = jnp.where((block > 0) | (slot < len_ref[0]), 0.0, -jnp.inf)
    square = (HEAD_DIM, HEAD_DIM)
    column = lax.broadcasted_iota(jnp.int32, square, 1)
    other = column + 1 - 2 * (column % 2)
    swap_ref[...] = jnp.where(lax.broadcasted_iota(jnp.int32, square, 0) == other, 1.0, 0.0).astype(jnp.bfloat16)


def make_tables(half, text_len, q_gain, k_gain, rows):
    pairs_zero = HEAD_DIM // 16
    pairs_axis = (HEAD_DIM // 2 - pairs_zero) // 2
    freqs = 10000.0 ** (-np.arange(pairs_axis, dtype=np.float32) / np.float32(pairs_axis))
    row_freq, col_freq = np.zeros((2, 1, HEAD_DIM // 2), np.float32)
    row_freq[0, pairs_zero : pairs_zero + pairs_axis] = freqs
    col_freq[0, pairs_zero + pairs_axis :] = freqs
    scalars = pl.BlockSpec(memory_space=pltpu.SMEM)
    table = jax.ShapeDtypeStruct((rows, HEAD_DIM), jnp.float32)
    return pl.pallas_call(
        tables_kernel,
        in_specs=[scalars, scalars] + [pl.BlockSpec(memory_space=pltpu.VMEM)] * 4,
        out_shape=[
            table,
            table,
            table,
            table,
            jax.ShapeDtypeStruct((1, rows), jnp.float32),
            jax.ShapeDtypeStruct((HEAD_DIM, HEAD_DIM), jnp.bfloat16),
        ],
        compiler_params=pltpu.CompilerParams(vmem_limit_bytes=VMEM),
        cost_estimate=pl.CostEstimate(flops=rows * HEAD_DIM * 8, bytes_accessed=rows * HEAD_DIM * 4, transcendentals=0),
        name="tables",
    )(
        half,
        text_len,
        np.repeat(row_freq, 2, axis=1),
        np.repeat(col_freq, 2, axis=1),
        q_gain[None, :],
        k_gain[None, :],
    )


def attend_kernel(half_ref, own_ref, far_ref, cq_ref, sq_ref, ck_ref, sk_ref, mask_ref, swap_ref, *refs):
    out_ref = refs[-1]
    rows = own_ref.shape[0] * own_ref.shape[2]

    def load(part):
        return jnp.concatenate(
            [own_ref[:, part].reshape(rows, HEAD_DIM), far_ref[:, part].reshape(rows, HEAD_DIM)], axis=0
        )

    def turn(raw, straight, crossed):
        wide = raw.astype(jnp.float32)
        scale = lax.rsqrt(jnp.mean(wide * wide, axis=-1, keepdims=True) + EPS)
        partner = jnp.dot(raw, swap_ref[...], preferred_element_type=jnp.float32)
        return ((wide * straight + partner * crossed) * scale).astype(jnp.bfloat16)

    queries = turn(load(0), cq_ref[...], sq_ref[...])
    keys = turn(load(1), ck_ref[...], sk_ref[...])
    scores = lax.dot_general(queries, keys, NT, preferred_element_type=jnp.float32)
    scores = scores * SCALE + mask_ref[...]
    weights = jnp.exp2(scores - jnp.max(scores, axis=-1, keepdims=True))
    total = jnp.sum(weights, axis=-1, keepdims=True)
    mixed = jnp.dot(weights.astype(jnp.bfloat16), load(2), preferred_element_type=jnp.float32)
    out_ref[...] = (mixed / total).astype(jnp.bfloat16)


def attend(half, own, far, tables, part, parts, into=None):
    blocks, kinds, slots, width = far.shape
    heads = width // HEAD_DIM
    count = heads // parts
    first = part * count
    rows = 2 * blocks * slots
    shape = (blocks, kinds, slots, HEAD_DIM)
    whole = pl.BlockSpec((rows, HEAD_DIM), lambda g, half: (0, 0))
    return pl.pallas_call(
        attend_kernel,
        grid_spec=pltpu.PrefetchScalarGridSpec(
            num_scalar_prefetch=1,
            grid=(count,),
            in_specs=[
                pl.BlockSpec(shape, lambda g, half: (0, 0, 0, half[0] * heads + first + g)),
                pl.BlockSpec(shape, lambda g, half: (0, 0, 0, first + g)),
                whole,
                whole,
                whole,
                whole,
                pl.BlockSpec((1, rows), lambda g, half: (0, 0)),
                pl.BlockSpec((HEAD_DIM, HEAD_DIM), lambda g, half: (0, 0)),
            ]
            + ([] if into is None else [pl.BlockSpec(memory_space=pl.ANY)]),
            out_specs=pl.BlockSpec((rows, HEAD_DIM), lambda g, half: (0, first + g)),
        ),
        out_shape=jax.ShapeDtypeStruct((rows, width), jnp.bfloat16),
        input_output_aliases={} if into is None else {9: 0},
        compiler_params=pltpu.CompilerParams(vmem_limit_bytes=VMEM),
        cost_estimate=pl.CostEstimate(
            flops=count * rows * rows * HEAD_DIM * 4,
            bytes_accessed=rows * width * 8,
            transcendentals=0,
        ),
        name="attend",
    )(half, own, far, *tables, *([] if into is None else [into]))


def gelu_kernel(part_ref, units_ref, *refs):
    refs[-1][...] = jax.nn.gelu(units_ref[0].astype(jnp.float32), approximate=True).astype(jnp.bfloat16)


def activate(part, units, width, into=None):
    blocks, slots, _ = units.shape
    first = 0 if into is None else blocks
    return pl.pallas_call(
        gelu_kernel,
        grid_spec=pltpu.PrefetchScalarGridSpec(
            num_scalar_prefetch=1,
            grid=(blocks,),
            in_specs=[pl.BlockSpec((1, slots, width), lambda b, part: (b, 0, part[0]))]
            + ([] if into is None else [pl.BlockSpec(memory_space=pl.ANY)]),
            out_specs=pl.BlockSpec((slots, width), lambda b, part: (first + b, 0)),
        ),
        out_shape=jax.ShapeDtypeStruct((2 * blocks * slots, width), jnp.bfloat16),
        input_output_aliases={} if into is None else {2: 0},
        compiler_params=pltpu.CompilerParams(vmem_limit_bytes=LESS),
        cost_estimate=pl.CostEstimate(
            flops=blocks * slots * width * 4, bytes_accessed=blocks * slots * width, transcendentals=0
        ),
        name="activate",
    )(part, units, *([] if into is None else [into]))


def project_kernel(layout, sides, core_ref, attn_ref, act_ref, *refs):
    pieces, outs, (w_ref, sems) = refs[: len(layout)], refs[len(layout) : -2], refs[-2:]
    depth = attn_ref.shape[1]
    rows, columns = outs[0].shape
    taken = pl.ds(rows * sides[0], rows * len(sides))
    core = core_ref[0]
    copies = []
    for (base, here, share), piece in zip(layout, pieces):
        start = base + (core if here else 1 - core) * share
        place = pl.ds(pl.multiple_of(start, 16), piece.shape[0])
        copies.append(pltpu.make_async_copy(piece, w_ref.at[place], sems.at[len(copies)]))
        copies[-1].start()
    pending = [base // (2 * share) * 2 * share for base, _, share in layout]
    for first in range(0, columns, 256):
        end = min(first + 256, columns)
        while pending and pending[0] < end:
            copies[-len(pending)].wait()
            pending.pop(0)
        total = lax.dot_general(attn_ref[taken], w_ref[first:end, :depth], NT, preferred_element_type=jnp.float32)
        total += lax.dot_general(act_ref[taken], w_ref[first:end, depth:], NT, preferred_element_type=jnp.float32)
        for index, out_ref in enumerate(outs):
            out_ref[:, first:end] = total[rows * index : rows * (index + 1)].astype(out_ref.dtype)


def project(core, attn, act, chips, sides=(0, 1)):
    share = sum(piece.shape[0] for here, _, piece in chips[0] if here)
    layout, flat = [], []
    for index, pieces in enumerate(chips):
        for here, first, piece in pieces:
            layout.append((2 * share * index + first, here, share))
            flat.append(piece)
    rows, depth = attn.shape[0] // 2, attn.shape[1] + act.shape[1]
    columns = 2 * share * len(chips)
    inside = pl.BlockSpec(memory_space=pltpu.VMEM)
    return pl.pallas_call(
        functools.partial(project_kernel, layout, sides),
        in_specs=[pl.BlockSpec(memory_space=pltpu.SMEM), inside, inside]
        + [pl.BlockSpec(memory_space=pl.ANY)] * len(flat),
        out_specs=[inside] * len(sides),
        out_shape=[jax.ShapeDtypeStruct((rows, columns), jnp.bfloat16)] * len(sides),
        scratch_shapes=[
            pltpu.VMEM((columns, depth), jnp.bfloat16),
            pltpu.SemaphoreType.DMA((len(flat),)),
        ],
        compiler_params=pltpu.CompilerParams(vmem_limit_bytes=LESS),
        cost_estimate=pl.CostEstimate(
            flops=rows * columns * depth // 2, bytes_accessed=columns * depth // 4, transcendentals=0
        ),
        name="project",
    )(core, attn, act, *flat)


def finish_kernel(chunks, tile_ref, place_ref, step_ref, *refs):
    pairs = [refs[2 * i : 2 * i + 2] for i in range(chunks)]
    (
        stream_ref, bias_ref, gate_ref, scale_ref, shift_ref, w_ref, b_ref, latent_ref, hidden_ref, next_ref, proj_ref,
    ) = refs[2 * chunks :]
    places = len(PATH)
    chip = proj_ref.shape[1] // places
    mine = place_ref[places + tile_ref[0] // 2]
    behind = [0] + [distance for step in range(1, places // 2) for distance in (step, -step)] + [places // 2]
    for own_ref, far_ref in pairs:
        for first in range(0, own_ref.shape[1], chip):
            source = place_ref[(mine - behind.pop(0) + places) % places]
            target = pl.ds(pl.multiple_of(chip * source, 128), chip)
            part = slice(first, first + chip)
            proj_ref[:, target] = own_ref[:, part].astype(jnp.float32) + far_ref[:, part].astype(jnp.float32)
    updated = stream_ref[0].astype(jnp.float32) + gate_ref[...] * (proj_ref[...] + bias_ref[...])
    hidden_ref[0] = updated.astype(jnp.bfloat16)

    @pl.when(pl.program_id(0) > 0)
    def _():
        center = updated - jnp.mean(updated, axis=-1, keepdims=True)
        variance = jnp.mean(center * center, axis=-1, keepdims=True)
        normed = center * lax.rsqrt(variance + EPS)
        modulated = ((1.0 + scale_ref[...]) * normed + shift_ref[...]).astype(jnp.bfloat16)
        velocity = lax.dot_general(w_ref[...], modulated, NT, preferred_element_type=jnp.float32)
        next_ref[0] = latent_ref[0] + step_ref[0] * (velocity + b_ref[...])


def finish(tile, step, chunks, stream, bias, gate, scale, shift, w_final, b_final, latent):
    blocks, slots, width = stream.shape
    channels = w_final.shape[0]
    flat = [array for pair in chunks for array in pair]

    def whole(array):
        return pl.BlockSpec(array.shape, lambda b, *_: (0, 0))

    tokens = pl.BlockSpec((1, slots, width), lambda b, *_: (b, 0, 0))
    image = pl.BlockSpec((1, channels, slots), lambda b, *_: (jnp.maximum(b - 1, 0), 0, 0))
    return pl.pallas_call(
        functools.partial(finish_kernel, len(chunks)),
        grid_spec=pltpu.PrefetchScalarGridSpec(
            num_scalar_prefetch=3,
            grid=(blocks,),
            in_specs=[pl.BlockSpec((slots, array.shape[1]), lambda b, *_: (b, 0)) for array in flat]
            + [
                tokens,
                whole(bias),
                whole(gate),
                whole(scale),
                whole(shift),
                whole(w_final),
                whole(b_final),
                image,
            ],
            out_specs=[tokens, image],
            scratch_shapes=[pltpu.VMEM((slots, width), jnp.float32)],
        ),
        out_shape=[
            jax.ShapeDtypeStruct(stream.shape, jnp.bfloat16),
            jax.ShapeDtypeStruct(latent.shape, jnp.float32),
        ],
        compiler_params=pltpu.CompilerParams(vmem_limit_bytes=LIGHT),
        cost_estimate=pl.CostEstimate(
            flops=blocks * slots * width * 160, bytes_accessed=blocks * slots * width * 10, transcendentals=0
        ),
        name="finish",
    )(tile, np.array(PATH + PLACE, np.int32), step, *flat, stream, bias, gate, scale, shift, w_final, b_final, latent)


PATH = (0, 1, 3, 5, 7, 6, 4, 2)
PLACE = tuple(PATH.index(chip) for chip in range(len(PATH)))


def hop(array, by):
    places = len(PATH)
    pairs = [(2 * PATH[i] + c, 2 * PATH[(i + by) % places] + c) for i in range(places) for c in range(2)]
    return lax.ppermute(array, "tile", pairs)


def both_cores(array, first=0):
    other = lax.ppermute(array, "tile", [(t, t ^ 1) for t in range(2 * len(PATH))])
    return [(True, first, array), (False, first, other)]


def paired(
    partners,
    attn_proj,
    mlp_proj,
    stream,
    text_len,
    q_gain,
    k_gain,
    w_out_attn,
    w_out_mlp,
    bias_out,
    gate_mod,
    final_shift,
    final_scale,
    w_final,
    b_final,
    latent,
    step_size,
):
    me = lax.axis_index("head")
    half = me[None].astype(jnp.int32)
    trade = functools.partial(lax.ppermute, axis_name="head", perm=[(0, 1), (1, 0)])

    tile = lax.axis_index("tile").astype(jnp.int32)
    core = (tile % 2)[None]
    own_attn = jnp.transpose(attn_proj[0], (0, 2, 1, 3))
    own_units = mlp_proj[0]
    slots = own_attn.shape[2]
    units = own_units.shape[2] // partners
    width = own_attn.shape[3] // partners
    sent_attn = lax.dynamic_slice_in_dim(own_attn, (1 - me) * width, width, axis=3)
    block = jnp.concatenate([w_out_attn.T, w_out_mlp.T], axis=1)

    onward, back = hop(block, 1), hop(block, -1)
    far_attn = trade(sent_attn)
    chips = [both_cores(block)]

    tables = make_tables(half, text_len, q_gain, k_gain, 6 * slots)
    act_near = activate(half, own_units, units)
    sent_units = lax.dynamic_slice_in_dim(own_units, (1 - me) * units, units, axis=2)

    onward, back, tables, act_near, sent_units, chips = lax.optimization_barrier(
        (onward, back, tables, act_near, sent_units, [[piece[2] for piece in chip] for chip in chips])
    )
    chips = [[(True, 0, chip[0]), (False, 0, chip[1])] for chip in chips]
    chips += [both_cores(onward), both_cores(back)]
    onward, back = hop(onward, 1), hop(back, -1)
    far_attn, sent_units = lax.optimization_barrier((far_attn, sent_units))
    far_units = trade(sent_units)
    attn = attend(half, own_attn, far_attn, tables, 0, 2)
    blocks = [piece[2] for chip in chips[1:] for piece in chip]
    attn, onward, back, blocks = lax.optimization_barrier((attn, onward, back, blocks))
    chips[1:] = [[(True, 0, blocks[i]), (False, 0, blocks[i + 1])] for i in (0, 2)]
    chips += [both_cores(onward), both_cores(back)]
    onward, back = hop(onward, 1), hop(back, -1)
    attn = attend(half, own_attn, far_attn, tables, 1, 2, attn)
    far_units, attn = lax.optimization_barrier((far_units, attn))
    act = activate(jnp.zeros_like(half), far_units, units, act_near)

    chunks = []

    def send(group):
        own, sent = project(core, attn, act, group)
        chunks.append((own, trade(sent)))
        return sent

    (sent,) = project(core, attn, act, chips[0:1], (1,))
    chunks.append([None, trade(sent)])
    attn, sent = lax.optimization_barrier((attn, sent))
    sent = send(chips[1:3])
    onward, back, attn, sent, chunks[0][1] = lax.optimization_barrier((onward, back, attn, sent, chunks[0][1]))
    middle = block.shape[0] // 2
    last = hop(onward[:middle], 1), hop(back[middle:], -1)
    chips += [both_cores(onward), both_cores(back)]
    sent = send(chips[3:5])
    attn, sent, chunks[1] = lax.optimization_barrier((attn, sent, chunks[1]))
    sent = send(chips[5:7])
    onward, back, attn, sent, chunks[2] = lax.optimization_barrier((*last, attn, sent, chunks[2]))
    chips.append(both_cores(onward) + both_cores(back, middle))
    sent = send(chips[7:8])
    attn, sent = lax.optimization_barrier((attn, sent))
    (chunks[0][0],) = project(core, attn, act, chips[0:1], (0,))

    hidden, following = finish(
        tile[None],
        step_size,
        chunks,
        stream[0],
        bias_out[None, :],
        gate_mod,
        final_scale,
        final_shift,
        w_final.T,
        b_final[:, None],
        jnp.transpose(latent[0], (0, 2, 1)),
    )
    return hidden[None], jnp.transpose(following, (0, 2, 1))[None]


def solution(mesh):
    placed = (
        P("tile", None, "head", None, None),
        P("tile", None, "head", None),
        P("tile", None, "head", None),
        P("tile"),
        P(),
        P(),
        P("head", "tile"),
        P("head", "tile"),
        P(),
        P("tile", None),
        P("tile", None),
        P("tile", None),
        P(),
        P(),
        P("tile", None, "head", None),
        P("tile"),
    )
    return jax.shard_map(
        functools.partial(paired, mesh.shape["head"]) if fits(mesh.shape) else general,
        mesh=mesh,
        in_specs=placed,
        out_specs=(P("tile", None, "head", None), P("tile", None, "head", None)),
        check_vma=False,
    )
```

```python
import functools
import math

import jax
import jax.numpy as jnp
import numpy as np
from jax import lax
from jax.experimental import pallas as pl
from jax.experimental.pallas import tpu as pltpu
from jax.sharding import PartitionSpec as P

HEAD_DIM = 128
SLOTS = 192
GRID_W = 32


def rope_tables(positions):
    pairs_zero = HEAD_DIM // 16
    pairs_axis = (HEAD_DIM // 2 - pairs_zero) // 2
    freqs = 10000.0 ** (-jnp.arange(pairs_axis, dtype=jnp.float32) / pairs_axis)
    count = positions.shape[0]
    angles = [jnp.zeros((count, HEAD_DIM // 2), jnp.float32)]
    for block in range(1, 3):
        image_index = (block - 1) * SLOTS + positions
        rows = (image_index // GRID_W).astype(jnp.float32)
        columns = (image_index % GRID_W).astype(jnp.float32)
        angles.append(
            jnp.concatenate(
                [
                    jnp.zeros((count, pairs_zero), jnp.float32),
                    rows[:, None] * freqs[None, :],
                    columns[:, None] * freqs[None, :],
                ],
                axis=1,
            )
        )
    stacked = jnp.stack(angles)
    return (jnp.cos(stacked), jnp.sin(stacked))


def prepare(raw, gain, cosine, sine):
    normed = raw * lax.rsqrt(jnp.mean(raw * raw, axis=-1, keepdims=True) + 1e-06) * gain
    halves = normed.reshape(normed.shape[:-1] + (HEAD_DIM // 2, 2))
    first = halves[..., 0]
    second = halves[..., 1]
    cosine = cosine[None, :, :, None, :]
    sine = sine[None, :, :, None, :]
    rotated = jnp.stack([first * cosine - second * sine, first * sine + second * cosine], axis=-1)
    return rotated.reshape(raw.shape).astype(jnp.bfloat16)


def attend_head(inputs):
    queries, keys, values, live = inputs
    scores = jnp.einsum("qd,kd->qk", queries, keys, preferred_element_type=jnp.float32) / math.sqrt(
        HEAD_DIM
    )
    scores = jnp.where(live[None, :], scores, -jnp.inf)
    top = jnp.max(scores, axis=-1, keepdims=True)
    weights = jnp.exp(scores - top)
    total = jnp.sum(weights, axis=-1, keepdims=True)
    mixed = jnp.dot(weights.astype(jnp.bfloat16), values, preferred_element_type=jnp.float32)
    return (mixed / total).astype(jnp.bfloat16)


def attend_request(inputs):
    queries, keys, values, live = inputs
    count = queries.shape[1]
    broad_live = jnp.broadcast_to(live[None, :], (count, live.shape[0]))
    result = lax.map(
        attend_head,
        (
            jnp.moveaxis(queries, 1, 0),
            jnp.moveaxis(keys, 1, 0),
            jnp.moveaxis(values, 1, 0),
            broad_live,
        ),
    )
    return jnp.moveaxis(result, 0, 1)


def general(
    attn_proj,
    mlp_proj,
    stream,
    text_len,
    q_gain,
    k_gain,
    w_out_attn,
    w_out_mlp,
    bias_out,
    gate_mod,
    final_shift,
    final_scale,
    w_final,
    b_final,
    latent,
    step_size,
):
    requests = attn_proj.shape[0]
    own_slots = attn_proj.shape[2]
    width = attn_proj.shape[4]
    heads = width // HEAD_DIM
    start_slot = lax.axis_index("head") * own_slots
    positions = start_slot + jnp.arange(own_slots, dtype=jnp.int32)
    cosine, sine = rope_tables(positions)
    head_shape = (requests, 3, own_slots, heads, HEAD_DIM)
    queries = prepare(
        attn_proj[:, :, :, 0].astype(jnp.float32).reshape(head_shape), q_gain, cosine, sine
    )
    keys = prepare(
        attn_proj[:, :, :, 1].astype(jnp.float32).reshape(head_shape), k_gain, cosine, sine
    )
    packed = jnp.stack(
        [
            queries.reshape(requests, 3, own_slots, width),
            keys.reshape(requests, 3, own_slots, width),
            attn_proj[:, :, :, 2],
        ],
        axis=3,
    )
    units = mlp_proj[:, :, :, None, :]
    moved, hidden_units = (
        lax.all_to_all(packed, "head", split_axis=4, concat_axis=2, tiled=True),
        lax.all_to_all(units, "head", split_axis=4, concat_axis=2, tiled=True),
    )
    hidden_units = hidden_units[:, :, :, 0]
    tile_slots = moved.shape[2]
    local_width = moved.shape[4]
    local_heads = local_width // HEAD_DIM
    flat_shape = (requests, 3 * tile_slots, local_heads, HEAD_DIM)
    all_positions = jnp.arange(tile_slots, dtype=jnp.int32)
    text_live = all_positions[None, :] < text_len[:, None]
    image_live = jnp.ones_like(text_live)
    live = jnp.stack([text_live, image_live, image_live], axis=1).reshape(requests, 3 * tile_slots)
    attn_out = lax.map(
        attend_request,
        (
            moved[:, :, :, 0].reshape(flat_shape),
            moved[:, :, :, 1].reshape(flat_shape),
            moved[:, :, :, 2].reshape(flat_shape),
            live,
        ),
    )
    attn_out = attn_out.reshape(requests, 3, tile_slots, local_width)
    mlp_act = jax.nn.gelu(hidden_units.astype(jnp.float32), approximate=True).astype(jnp.bfloat16)
    term = jnp.einsum(
        "rbsk,kd->rbsd",
        attn_out,
        lax.all_gather(w_out_attn, "tile", axis=1, tiled=True),
        preferred_element_type=jnp.float32,
    )
    term = term + jnp.einsum(
        "rbsk,kd->rbsd",
        mlp_act,
        lax.all_gather(w_out_mlp, "tile", axis=1, tiled=True),
        preferred_element_type=jnp.float32,
    )
    proj = lax.psum_scatter(term, "head", scatter_dimension=2, tiled=True)
    updated = stream.astype(jnp.float32) + gate_mod[:, None, None, :] * (proj + bias_out)
    hidden_out = updated.astype(jnp.bfloat16)
    image = updated[:, 1:]
    center = image - jnp.mean(image, axis=-1, keepdims=True)
    variance = jnp.mean(center * center, axis=-1, keepdims=True)
    normed = center * lax.rsqrt(variance + 1e-06)
    modulated = (
        (1.0 + final_scale[:, None, None, :]) * normed + final_shift[:, None, None, :]
    ).astype(jnp.bfloat16)
    velocity = (
        jnp.einsum("rbsd,dc->rbsc", modulated, w_final, preferred_element_type=jnp.float32)
        + b_final
    )
    latent_next = latent + step_size[:, None, None, None] * velocity
    return (hidden_out, latent_next)


EPS = 1e-06
SCALE = math.log2(math.e) / math.sqrt(HEAD_DIM)
VMEM = 60 * 1024 * 1024
LIGHT = 24 * 1024 * 1024
LESS = 34 * 1024 * 1024
NT = (((1,), (1,)), ((), ()))


def fits(sizes):
    return sizes["head"] == 2 and sizes["tile"] == 2 * len(PATH)


def tables_kernel(half_ref, len_ref, row_freq_ref, col_freq_ref, q_ref, k_ref, cq_ref, sq_ref, ck_ref, sk_ref, mask_ref, swap_ref):
    rows = cq_ref.shape[0]
    slots = rows // 6

    def place(axis, shape):
        index = lax.broadcasted_iota(jnp.int32, shape, axis)
        away = index >= rows // 2
        block = (index - jnp.where(away, rows // 2, 0)) // slots
        slot = index % slots + slots * jnp.where(away, 1 - half_ref[0], half_ref[0])
        return block, slot

    shape = (rows, HEAD_DIM)
    block, slot = place(0, shape)
    image = (block - 1) * SLOTS + slot
    angle = (image // GRID_W).astype(jnp.float32) * row_freq_ref[...]
    angle += (image % GRID_W).astype(jnp.float32) * col_freq_ref[...]
    angle = jnp.where(block == 0, 0.0, angle)
    cosine, sine = jnp.cos(angle), jnp.sin(angle)
    odd = lax.broadcasted_iota(jnp.int32, shape, 1) % 2 == 1
    for gain_ref, c_ref, s_ref in ((q_ref, cq_ref, sq_ref), (k_ref, ck_ref, sk_ref)):
        gain = jnp.broadcast_to(gain_ref[...], shape)
        partner = jnp.where(odd, pltpu.roll(gain, 1, 1), -pltpu.roll(gain, HEAD_DIM - 1, 1))
        c_ref[...] = cosine * gain
        s_ref[...] = sine * partner
    block, slot = place(1, (1, rows))
    mask_ref[...] = jnp.where((block > 0) | (slot < len_ref[0]), 0.0, -jnp.inf)
    square = (HEAD_DIM, HEAD_DIM)
    column = lax.broadcasted_iota(jnp.int32, square, 1)
    other = column + 1 - 2 * (column % 2)
    swap_ref[...] = jnp.where(lax.broadcasted_iota(jnp.int32, square, 0) == other, 1.0, 0.0).astype(jnp.bfloat16)


def make_tables(half, text_len, q_gain, k_gain, rows):
    pairs_zero = HEAD_DIM // 16
    pairs_axis = (HEAD_DIM // 2 - pairs_zero) // 2
    freqs = 10000.0 ** (-np.arange(pairs_axis, dtype=np.float32) / np.float32(pairs_axis))
    row_freq, col_freq = np.zeros((2, 1, HEAD_DIM // 2), np.float32)
    row_freq[0, pairs_zero : pairs_zero + pairs_axis] = freqs
    col_freq[0, pairs_zero + pairs_axis :] = freqs
    scalars = pl.BlockSpec(memory_space=pltpu.SMEM)
    table = jax.ShapeDtypeStruct((rows, HEAD_DIM), jnp.float32)
    return pl.pallas_call(
        tables_kernel,
        in_specs=[scalars, scalars] + [pl.BlockSpec(memory_space=pltpu.VMEM)] * 4,
        out_shape=[
            table,
            table,
            table,
            table,
            jax.ShapeDtypeStruct((1, rows), jnp.float32),
            jax.ShapeDtypeStruct((HEAD_DIM, HEAD_DIM), jnp.bfloat16),
        ],
        compiler_params=pltpu.CompilerParams(vmem_limit_bytes=VMEM),
        cost_estimate=pl.CostEstimate(flops=rows * HEAD_DIM * 8, bytes_accessed=rows * HEAD_DIM * 4, transcendentals=0),
        name="tables",
    )(
        half,
        text_len,
        np.repeat(row_freq, 2, axis=1),
        np.repeat(col_freq, 2, axis=1),
        q_gain[None, :],
        k_gain[None, :],
    )


def attend_kernel(half_ref, own_ref, far_ref, cq_ref, sq_ref, ck_ref, sk_ref, mask_ref, swap_ref, *refs):
    out_ref = refs[-1]
    rows = own_ref.shape[0] * own_ref.shape[2]

    def load(part):
        return jnp.concatenate(
            [own_ref[:, part].reshape(rows, HEAD_DIM), far_ref[:, part].reshape(rows, HEAD_DIM)], axis=0
        )

    def turn(raw, straight, crossed):
        wide = raw.astype(jnp.float32)
        scale = lax.rsqrt(jnp.mean(wide * wide, axis=-1, keepdims=True) + EPS)
        partner = jnp.dot(raw, swap_ref[...], preferred_element_type=jnp.float32)
        return ((wide * straight + partner * crossed) * scale).astype(jnp.bfloat16)

    queries = turn(load(0), cq_ref[...], sq_ref[...])
    keys = turn(load(1), ck_ref[...], sk_ref[...])
    scores = lax.dot_general(queries, keys, NT, preferred_element_type=jnp.float32)
    scores = scores * SCALE + mask_ref[...]
    weights = jnp.exp2(scores - jnp.max(scores, axis=-1, keepdims=True))
    total = jnp.sum(weights, axis=-1, keepdims=True)
    mixed = jnp.dot(weights.astype(jnp.bfloat16), load(2), preferred_element_type=jnp.float32)
    out_ref[...] = (mixed / total).astype(jnp.bfloat16)


def attend(half, own, far, tables, part, parts, into=None):
    blocks, kinds, slots, width = far.shape
    heads = width // HEAD_DIM
    count = heads // parts
    first = part * count
    rows = 2 * blocks * slots
    shape = (blocks, kinds, slots, HEAD_DIM)
    whole = pl.BlockSpec((rows, HEAD_DIM), lambda g, half: (0, 0))
    return pl.pallas_call(
        attend_kernel,
        grid_spec=pltpu.PrefetchScalarGridSpec(
            num_scalar_prefetch=1,
            grid=(count,),
            in_specs=[
                pl.BlockSpec(shape, lambda g, half: (0, 0, 0, half[0] * heads + first + g)),
                pl.BlockSpec(shape, lambda g, half: (0, 0, 0, first + g)),
                whole,
                whole,
                whole,
                whole,
                pl.BlockSpec((1, rows), lambda g, half: (0, 0)),
                pl.BlockSpec((HEAD_DIM, HEAD_DIM), lambda g, half: (0, 0)),
            ]
            + ([] if into is None else [pl.BlockSpec(memory_space=pl.ANY)]),
            out_specs=pl.BlockSpec((rows, HEAD_DIM), lambda g, half: (0, first + g)),
        ),
        out_shape=jax.ShapeDtypeStruct((rows, width), jnp.bfloat16),
        input_output_aliases={} if into is None else {9: 0},
        compiler_params=pltpu.CompilerParams(vmem_limit_bytes=VMEM),
        cost_estimate=pl.CostEstimate(
            flops=count * rows * rows * HEAD_DIM * 4,
            bytes_accessed=rows * width * 8,
            transcendentals=0,
        ),
        name="attend",
    )(half, own, far, *tables, *([] if into is None else [into]))


def gelu_kernel(part_ref, units_ref, *refs):
    refs[-1][...] = jax.nn.gelu(units_ref[0].astype(jnp.float32), approximate=True).astype(jnp.bfloat16)


def activate(part, units, width, into=None):
    blocks, slots, _ = units.shape
    first = 0 if into is None else blocks
    return pl.pallas_call(
        gelu_kernel,
        grid_spec=pltpu.PrefetchScalarGridSpec(
            num_scalar_prefetch=1,
            grid=(blocks,),
            in_specs=[pl.BlockSpec((1, slots, width), lambda b, part: (b, 0, part[0]))]
            + ([] if into is None else [pl.BlockSpec(memory_space=pl.ANY)]),
            out_specs=pl.BlockSpec((slots, width), lambda b, part: (first + b, 0)),
        ),
        out_shape=jax.ShapeDtypeStruct((2 * blocks * slots, width), jnp.bfloat16),
        input_output_aliases={} if into is None else {2: 0},
        compiler_params=pltpu.CompilerParams(vmem_limit_bytes=LESS),
        cost_estimate=pl.CostEstimate(
            flops=blocks * slots * width * 4, bytes_accessed=blocks * slots * width, transcendentals=0
        ),
        name="activate",
    )(part, units, *([] if into is None else [into]))


def project_kernel(layout, sides, core_ref, attn_ref, act_ref, *refs):
    pieces, outs, (w_ref, sems) = refs[: len(layout)], refs[len(layout) : -2], refs[-2:]
    depth = attn_ref.shape[1]
    rows, columns = outs[0].shape
    taken = pl.ds(rows * sides[0], rows * len(sides))
    core = core_ref[0]
    copies = []
    for (base, here, share), piece in zip(layout, pieces):
        start = base + (core if here else 1 - core) * share
        place = pl.ds(pl.multiple_of(start, 16), piece.shape[0])
        copies.append(pltpu.make_async_copy(piece, w_ref.at[place], sems.at[len(copies)]))
        copies[-1].start()
    pending = [base // (2 * share) * 2 * share for base, _, share in layout]
    for first in range(0, columns, 256):
        end = min(first + 256, columns)
        while pending and pending[0] < end:
            copies[-len(pending)].wait()
            pending.pop(0)
        total = lax.dot_general(attn_ref[taken], w_ref[first:end, :depth], NT, preferred_element_type=jnp.float32)
        total += lax.dot_general(act_ref[taken], w_ref[first:end, depth:], NT, preferred_element_type=jnp.float32)
        for index, out_ref in enumerate(outs):
            out_ref[:, first:end] = total[rows * index : rows * (index + 1)].astype(out_ref.dtype)


def project(core, attn, act, chips, sides=(0, 1)):
    share = sum(piece.shape[0] for here, _, piece in chips[0] if here)
    layout, flat = [], []
    for index, pieces in enumerate(chips):
        for here, first, piece in pieces:
            layout.append((2 * share * index + first, here, share))
            flat.append(piece)
    rows, depth = attn.shape[0] // 2, attn.shape[1] + act.shape[1]
    columns = 2 * share * len(chips)
    inside = pl.BlockSpec(memory_space=pltpu.VMEM)
    return pl.pallas_call(
        functools.partial(project_kernel, layout, sides),
        in_specs=[pl.BlockSpec(memory_space=pltpu.SMEM), inside, inside]
        + [pl.BlockSpec(memory_space=pl.ANY)] * len(flat),
        out_specs=[inside] * len(sides),
        out_shape=[jax.ShapeDtypeStruct((rows, columns), jnp.bfloat16)] * len(sides),
        scratch_shapes=[
            pltpu.VMEM((columns, depth), jnp.bfloat16),
            pltpu.SemaphoreType.DMA((len(flat),)),
        ],
        compiler_params=pltpu.CompilerParams(vmem_limit_bytes=LESS),
        cost_estimate=pl.CostEstimate(
            flops=rows * columns * depth // 2, bytes_accessed=columns * depth // 4, transcendentals=0
        ),
        name="project",
    )(core, attn, act, *flat)


def finish_kernel(chunks, tile_ref, place_ref, step_ref, *refs):
    pairs = [refs[2 * i : 2 * i + 2] for i in range(chunks)]
    (
        stream_ref, bias_ref, gate_ref, scale_ref, shift_ref, w_ref, b_ref, latent_ref, hidden_ref, next_ref, proj_ref,
    ) = refs[2 * chunks :]
    slots, width = proj_ref.shape
    places = len(PATH)
    chip = width // places
    mine = place_ref[places + tile_ref[0] // 2]
    behind = [0] + [distance for step in range(1, places // 2) for distance in (step, -step)] + [places // 2]
    total = jnp.zeros((slots, chip), jnp.float32)
    for own_ref, far_ref in pairs:
        for first in range(0, own_ref.shape[1], chip):
            source = place_ref[(mine - behind.pop(0) + places) % places]
            target = pl.ds(pl.multiple_of(chip * source, 128), chip)
            part = slice(first, first + chip)
            proj = own_ref[:, part].astype(jnp.float32) + far_ref[:, part].astype(jnp.float32)
            updated = stream_ref[0, :, target].astype(jnp.float32) + gate_ref[:, target] * (proj + bias_ref[:, target])
            hidden_ref[0, :, target] = updated.astype(jnp.bfloat16)
            proj_ref[:, target] = updated
            total += updated

    @pl.when(pl.program_id(0) > 0)
    def _():
        parts = [slice(chip * index, chip * (index + 1)) for index in range(places)]
        mean = jnp.sum(total, axis=-1, keepdims=True) / width
        square = jnp.zeros((slots, chip), jnp.float32)
        for part in parts:
            center = proj_ref[:, part] - mean
            square += center * center
        inverse = lax.rsqrt(jnp.sum(square, axis=-1, keepdims=True) / width + EPS)
        velocity = b_ref[...]
        for part in parts:
            normed = (proj_ref[:, part] - mean) * inverse
            modulated = ((1.0 + scale_ref[:, part]) * normed + shift_ref[:, part]).astype(jnp.bfloat16)
            velocity += lax.dot_general(w_ref[:, part], modulated, NT, preferred_element_type=jnp.float32)
        next_ref[0] = latent_ref[0] + step_ref[0] * velocity


def finish(tile, step, chunks, stream, bias, gate, scale, shift, w_final, b_final, latent):
    blocks, slots, width = stream.shape
    channels = w_final.shape[0]
    flat = [array for pair in chunks for array in pair]

    def whole(array):
        return pl.BlockSpec(array.shape, lambda b, *_: (0, 0))

    tokens = pl.BlockSpec((1, slots, width), lambda b, *_: (b, 0, 0))
    image = pl.BlockSpec((1, channels, slots), lambda b, *_: (jnp.maximum(b - 1, 0), 0, 0))
    return pl.pallas_call(
        functools.partial(finish_kernel, len(chunks)),
        grid_spec=pltpu.PrefetchScalarGridSpec(
            num_scalar_prefetch=3,
            grid=(blocks,),
            in_specs=[pl.BlockSpec((slots, array.shape[1]), lambda b, *_: (b, 0)) for array in flat]
            + [
                tokens,
                whole(bias),
                whole(gate),
                whole(scale),
                whole(shift),
                whole(w_final),
                whole(b_final),
                image,
            ],
            out_specs=[tokens, image],
            scratch_shapes=[pltpu.VMEM((slots, width), jnp.float32)],
        ),
        out_shape=[
            jax.ShapeDtypeStruct(stream.shape, jnp.bfloat16),
            jax.ShapeDtypeStruct(latent.shape, jnp.float32),
        ],
        compiler_params=pltpu.CompilerParams(vmem_limit_bytes=LIGHT),
        cost_estimate=pl.CostEstimate(
            flops=blocks * slots * width * 160, bytes_accessed=blocks * slots * width * 10, transcendentals=0
        ),
        name="finish",
    )(tile, np.array(PATH + PLACE, np.int32), step, *flat, stream, bias, gate, scale, shift, w_final, b_final, latent)


PATH = (0, 1, 3, 5, 7, 6, 4, 2)
PLACE = tuple(PATH.index(chip) for chip in range(len(PATH)))


def hop(array, by):
    places = len(PATH)
    pairs = [(2 * PATH[i] + c, 2 * PATH[(i + by) % places] + c) for i in range(places) for c in range(2)]
    return lax.ppermute(array, "tile", pairs)


def both_cores(array, first=0):
    other = lax.ppermute(array, "tile", [(t, t ^ 1) for t in range(2 * len(PATH))])
    return [(True, first, array), (False, first, other)]


def paired(
    partners,
    attn_proj,
    mlp_proj,
    stream,
    text_len,
    q_gain,
    k_gain,
    w_out_attn,
    w_out_mlp,
    bias_out,
    gate_mod,
    final_shift,
    final_scale,
    w_final,
    b_final,
    latent,
    step_size,
):
    me = lax.axis_index("head")
    half = me[None].astype(jnp.int32)
    trade = functools.partial(lax.ppermute, axis_name="head", perm=[(0, 1), (1, 0)])

    tile = lax.axis_index("tile").astype(jnp.int32)
    core = (tile % 2)[None]
    own_attn = jnp.transpose(attn_proj[0], (0, 2, 1, 3))
    own_units = mlp_proj[0]
    slots = own_attn.shape[2]
    units = own_units.shape[2] // partners
    width = own_attn.shape[3] // partners
    sent_attn = lax.dynamic_slice_in_dim(own_attn, (1 - me) * width, width, axis=3)
    block = jnp.concatenate([w_out_attn.T, w_out_mlp.T], axis=1)

    onward, back = hop(block, 1), hop(block, -1)
    far_attn = trade(sent_attn)
    chips = [both_cores(block)]

    tables = make_tables(half, text_len, q_gain, k_gain, 6 * slots)
    act_near = activate(half, own_units, units)
    sent_units = lax.dynamic_slice_in_dim(own_units, (1 - me) * units, units, axis=2)

    onward, back, tables, act_near, sent_units, chips = lax.optimization_barrier(
        (onward, back, tables, act_near, sent_units, [[piece[2] for piece in chip] for chip in chips])
    )
    chips = [[(True, 0, chip[0]), (False, 0, chip[1])] for chip in chips]
    chips += [both_cores(onward), both_cores(back)]
    onward, back = hop(onward, 1), hop(back, -1)
    far_attn, sent_units = lax.optimization_barrier((far_attn, sent_units))
    far_units = trade(sent_units)
    attn = attend(half, own_attn, far_attn, tables, 0, 2)
    blocks = [piece[2] for chip in chips[1:] for piece in chip]
    attn, onward, back, blocks = lax.optimization_barrier((attn, onward, back, blocks))
    chips[1:] = [[(True, 0, blocks[i]), (False, 0, blocks[i + 1])] for i in (0, 2)]
    chips += [both_cores(onward), both_cores(back)]
    onward, back = hop(onward, 1), hop(back, -1)
    attn = attend(half, own_attn, far_attn, tables, 1, 2, attn)
    far_units, attn = lax.optimization_barrier((far_units, attn))
    act = activate(jnp.zeros_like(half), far_units, units, act_near)

    chunks = []

    def send(group):
        own, sent = project(core, attn, act, group)
        chunks.append((own, trade(sent)))
        return sent

    (sent,) = project(core, attn, act, chips[0:1], (1,))
    chunks.append([None, trade(sent)])
    attn, sent = lax.optimization_barrier((attn, sent))
    sent = send(chips[1:3])
    onward, back, attn, sent, chunks[0][1] = lax.optimization_barrier((onward, back, attn, sent, chunks[0][1]))
    middle = block.shape[0] // 2
    last = hop(onward[:middle], 1), hop(back[middle:], -1)
    chips += [both_cores(onward), both_cores(back)]
    sent = send(chips[3:5])
    attn, sent, chunks[1] = lax.optimization_barrier((attn, sent, chunks[1]))
    sent = send(chips[5:7])
    onward, back, attn, sent, chunks[2] = lax.optimization_barrier((*last, attn, sent, chunks[2]))
    chips.append(both_cores(onward) + both_cores(back, middle))
    sent = send(chips[7:8])
    attn, sent = lax.optimization_barrier((attn, sent))
    (chunks[0][0],) = project(core, attn, act, chips[0:1], (0,))

    hidden, following = finish(
        tile[None],
        step_size,
        chunks,
        stream[0],
        bias_out[None, :],
        gate_mod,
        final_scale,
        final_shift,
        w_final.T,
        b_final[:, None],
        jnp.transpose(latent[0], (0, 2, 1)),
    )
    return hidden[None], jnp.transpose(following, (0, 2, 1))[None]


def solution(mesh):
    placed = (
        P("tile", None, "head", None, None),
        P("tile", None, "head", None),
        P("tile", None, "head", None),
        P("tile"),
        P(),
        P(),
        P("head", "tile"),
        P("head", "tile"),
        P(),
        P("tile", None),
        P("tile", None),
        P("tile", None),
        P(),
        P(),
        P("tile", None, "head", None),
        P("tile"),
    )
    return jax.shard_map(
        functools.partial(paired, mesh.shape["head"]) if fits(mesh.shape) else general,
        mesh=mesh,
        in_specs=placed,
        out_specs=(P("tile", None, "head", None), P("tile", None, "head", None)),
        check_vma=False,
    )
```

```python
import functools
import math

import jax
import jax.numpy as jnp
import numpy as np
from jax import lax
from jax.experimental import pallas as pl
from jax.experimental.pallas import tpu as pltpu
from jax.sharding import PartitionSpec as P

HEAD_DIM = 128
SLOTS = 192
GRID_W = 32


def rope_tables(positions):
    pairs_zero = HEAD_DIM // 16
    pairs_axis = (HEAD_DIM // 2 - pairs_zero) // 2
    freqs = 10000.0 ** (-jnp.arange(pairs_axis, dtype=jnp.float32) / pairs_axis)
    count = positions.shape[0]
    angles = [jnp.zeros((count, HEAD_DIM // 2), jnp.float32)]
    for block in range(1, 3):
        image_index = (block - 1) * SLOTS + positions
        rows = (image_index // GRID_W).astype(jnp.float32)
        columns = (image_index % GRID_W).astype(jnp.float32)
        angles.append(
            jnp.concatenate(
                [
                    jnp.zeros((count, pairs_zero), jnp.float32),
                    rows[:, None] * freqs[None, :],
                    columns[:, None] * freqs[None, :],
                ],
                axis=1,
            )
        )
    stacked = jnp.stack(angles)
    return (jnp.cos(stacked), jnp.sin(stacked))


def prepare(raw, gain, cosine, sine):
    normed = raw * lax.rsqrt(jnp.mean(raw * raw, axis=-1, keepdims=True) + 1e-06) * gain
    halves = normed.reshape(normed.shape[:-1] + (HEAD_DIM // 2, 2))
    first = halves[..., 0]
    second = halves[..., 1]
    cosine = cosine[None, :, :, None, :]
    sine = sine[None, :, :, None, :]
    rotated = jnp.stack([first * cosine - second * sine, first * sine + second * cosine], axis=-1)
    return rotated.reshape(raw.shape).astype(jnp.bfloat16)


def attend_head(inputs):
    queries, keys, values, live = inputs
    scores = jnp.einsum("qd,kd->qk", queries, keys, preferred_element_type=jnp.float32) / math.sqrt(
        HEAD_DIM
    )
    scores = jnp.where(live[None, :], scores, -jnp.inf)
    top = jnp.max(scores, axis=-1, keepdims=True)
    weights = jnp.exp(scores - top)
    total = jnp.sum(weights, axis=-1, keepdims=True)
    mixed = jnp.dot(weights.astype(jnp.bfloat16), values, preferred_element_type=jnp.float32)
    return (mixed / total).astype(jnp.bfloat16)


def attend_request(inputs):
    queries, keys, values, live = inputs
    count = queries.shape[1]
    broad_live = jnp.broadcast_to(live[None, :], (count, live.shape[0]))
    result = lax.map(
        attend_head,
        (
            jnp.moveaxis(queries, 1, 0),
            jnp.moveaxis(keys, 1, 0),
            jnp.moveaxis(values, 1, 0),
            broad_live,
        ),
    )
    return jnp.moveaxis(result, 0, 1)


def general(
    attn_proj,
    mlp_proj,
    stream,
    text_len,
    q_gain,
    k_gain,
    w_out_attn,
    w_out_mlp,
    bias_out,
    gate_mod,
    final_shift,
    final_scale,
    w_final,
    b_final,
    latent,
    step_size,
):
    requests = attn_proj.shape[0]
    own_slots = attn_proj.shape[2]
    width = attn_proj.shape[4]
    heads = width // HEAD_DIM
    start_slot = lax.axis_index("head") * own_slots
    positions = start_slot + jnp.arange(own_slots, dtype=jnp.int32)
    cosine, sine = rope_tables(positions)
    head_shape = (requests, 3, own_slots, heads, HEAD_DIM)
    queries = prepare(
        attn_proj[:, :, :, 0].astype(jnp.float32).reshape(head_shape), q_gain, cosine, sine
    )
    keys = prepare(
        attn_proj[:, :, :, 1].astype(jnp.float32).reshape(head_shape), k_gain, cosine, sine
    )
    packed = jnp.stack(
        [
            queries.reshape(requests, 3, own_slots, width),
            keys.reshape(requests, 3, own_slots, width),
            attn_proj[:, :, :, 2],
        ],
        axis=3,
    )
    units = mlp_proj[:, :, :, None, :]
    moved, hidden_units = (
        lax.all_to_all(packed, "head", split_axis=4, concat_axis=2, tiled=True),
        lax.all_to_all(units, "head", split_axis=4, concat_axis=2, tiled=True),
    )
    hidden_units = hidden_units[:, :, :, 0]
    tile_slots = moved.shape[2]
    local_width = moved.shape[4]
    local_heads = local_width // HEAD_DIM
    flat_shape = (requests, 3 * tile_slots, local_heads, HEAD_DIM)
    all_positions = jnp.arange(tile_slots, dtype=jnp.int32)
    text_live = all_positions[None, :] < text_len[:, None]
    image_live = jnp.ones_like(text_live)
    live = jnp.stack([text_live, image_live, image_live], axis=1).reshape(requests, 3 * tile_slots)
    attn_out = lax.map(
        attend_request,
        (
            moved[:, :, :, 0].reshape(flat_shape),
            moved[:, :, :, 1].reshape(flat_shape),
            moved[:, :, :, 2].reshape(flat_shape),
            live,
        ),
    )
    attn_out = attn_out.reshape(requests, 3, tile_slots, local_width)
    mlp_act = jax.nn.gelu(hidden_units.astype(jnp.float32), approximate=True).astype(jnp.bfloat16)
    term = jnp.einsum(
        "rbsk,kd->rbsd",
        attn_out,
        lax.all_gather(w_out_attn, "tile", axis=1, tiled=True),
        preferred_element_type=jnp.float32,
    )
    term = term + jnp.einsum(
        "rbsk,kd->rbsd",
        mlp_act,
        lax.all_gather(w_out_mlp, "tile", axis=1, tiled=True),
        preferred_element_type=jnp.float32,
    )
    proj = lax.psum_scatter(term, "head", scatter_dimension=2, tiled=True)
    updated = stream.astype(jnp.float32) + gate_mod[:, None, None, :] * (proj + bias_out)
    hidden_out = updated.astype(jnp.bfloat16)
    image = updated[:, 1:]
    center = image - jnp.mean(image, axis=-1, keepdims=True)
    variance = jnp.mean(center * center, axis=-1, keepdims=True)
    normed = center * lax.rsqrt(variance + 1e-06)
    modulated = (
        (1.0 + final_scale[:, None, None, :]) * normed + final_shift[:, None, None, :]
    ).astype(jnp.bfloat16)
    velocity = (
        jnp.einsum("rbsd,dc->rbsc", modulated, w_final, preferred_element_type=jnp.float32)
        + b_final
    )
    latent_next = latent + step_size[:, None, None, None] * velocity
    return (hidden_out, latent_next)


EPS = 1e-06
SCALE = math.log2(math.e) / math.sqrt(HEAD_DIM)
VMEM = 60 * 1024 * 1024
LIGHT = 24 * 1024 * 1024
LESS = 34 * 1024 * 1024
NT = (((1,), (1,)), ((), ()))


def fits(sizes):
    return sizes["head"] == 2 and sizes["tile"] == 2 * len(PATH)


def tables_kernel(half_ref, len_ref, row_freq_ref, col_freq_ref, q_ref, k_ref, cq_ref, sq_ref, ck_ref, sk_ref, mask_ref, swap_ref):
    rows = cq_ref.shape[0]
    slots = rows // 6

    def place(axis, shape):
        index = lax.broadcasted_iota(jnp.int32, shape, axis)
        away = index >= rows // 2
        block = (index - jnp.where(away, rows // 2, 0)) // slots
        slot = index % slots + slots * jnp.where(away, 1 - half_ref[0], half_ref[0])
        return block, slot

    shape = (rows, HEAD_DIM)
    block, slot = place(0, shape)
    image = (block - 1) * SLOTS + slot
    angle = (image // GRID_W).astype(jnp.float32) * row_freq_ref[...]
    angle += (image % GRID_W).astype(jnp.float32) * col_freq_ref[...]
    angle = jnp.where(block == 0, 0.0, angle)
    cosine, sine = jnp.cos(angle), jnp.sin(angle)
    odd = lax.broadcasted_iota(jnp.int32, shape, 1) % 2 == 1
    for gain_ref, c_ref, s_ref in ((q_ref, cq_ref, sq_ref), (k_ref, ck_ref, sk_ref)):
        gain = jnp.broadcast_to(gain_ref[...], shape)
        partner = jnp.where(odd, pltpu.roll(gain, 1, 1), -pltpu.roll(gain, HEAD_DIM - 1, 1))
        c_ref[...] = cosine * gain
        s_ref[...] = sine * partner
    block, slot = place(1, (1, rows))
    mask_ref[...] = jnp.where((block > 0) | (slot < len_ref[0]), 0.0, -jnp.inf)
    square = (HEAD_DIM, HEAD_DIM)
    column = lax.broadcasted_iota(jnp.int32, square, 1)
    other = column + 1 - 2 * (column % 2)
    swap_ref[...] = jnp.where(lax.broadcasted_iota(jnp.int32, square, 0) == other, 1.0, 0.0).astype(jnp.bfloat16)


def make_tables(half, text_len, q_gain, k_gain, rows):
    pairs_zero = HEAD_DIM // 16
    pairs_axis = (HEAD_DIM // 2 - pairs_zero) // 2
    freqs = 10000.0 ** (-np.arange(pairs_axis, dtype=np.float32) / np.float32(pairs_axis))
    row_freq, col_freq = np.zeros((2, 1, HEAD_DIM // 2), np.float32)
    row_freq[0, pairs_zero : pairs_zero + pairs_axis] = freqs
    col_freq[0, pairs_zero + pairs_axis :] = freqs
    scalars = pl.BlockSpec(memory_space=pltpu.SMEM)
    table = jax.ShapeDtypeStruct((rows, HEAD_DIM), jnp.float32)
    return pl.pallas_call(
        tables_kernel,
        in_specs=[scalars, scalars] + [pl.BlockSpec(memory_space=pltpu.VMEM)] * 4,
        out_shape=[
            table,
            table,
            table,
            table,
            jax.ShapeDtypeStruct((1, rows), jnp.float32),
            jax.ShapeDtypeStruct((HEAD_DIM, HEAD_DIM), jnp.bfloat16),
        ],
        compiler_params=pltpu.CompilerParams(vmem_limit_bytes=VMEM),
        cost_estimate=pl.CostEstimate(flops=rows * HEAD_DIM * 8, bytes_accessed=rows * HEAD_DIM * 4, transcendentals=0),
        name="tables",
    )(
        half,
        text_len,
        np.repeat(row_freq, 2, axis=1),
        np.repeat(col_freq, 2, axis=1),
        q_gain[None, :],
        k_gain[None, :],
    )


def attend_kernel(half_ref, own_ref, far_ref, cq_ref, sq_ref, ck_ref, sk_ref, mask_ref, swap_ref, *refs):
    out_ref = refs[-1]
    rows = own_ref.shape[0] * own_ref.shape[2]

    def load(part):
        return jnp.concatenate(
            [own_ref[:, part].reshape(rows, HEAD_DIM), far_ref[:, part].reshape(rows, HEAD_DIM)], axis=0
        )

    def turn(raw, straight, crossed):
        wide = raw.astype(jnp.float32)
        scale = lax.rsqrt(jnp.mean(wide * wide, axis=-1, keepdims=True) + EPS)
        partner = jnp.dot(raw, swap_ref[...], preferred_element_type=jnp.float32)
        return ((wide * straight + partner * crossed) * scale).astype(jnp.bfloat16)

    queries = turn(load(0), cq_ref[...], sq_ref[...])
    keys = turn(load(1), ck_ref[...], sk_ref[...])
    scores = lax.dot_general(queries, keys, NT, preferred_element_type=jnp.float32)
    scores = scores * SCALE + mask_ref[...]
    weights = jnp.exp2(scores - jnp.max(scores, axis=-1, keepdims=True))
    total = jnp.sum(weights, axis=-1, keepdims=True)
    mixed = jnp.dot(weights.astype(jnp.bfloat16), load(2), preferred_element_type=jnp.float32)
    out_ref[...] = (mixed / total).astype(jnp.bfloat16)


def attend(half, own, far, tables, part, parts, into=None):
    blocks, kinds, slots, width = far.shape
    heads = width // HEAD_DIM
    count = heads // parts
    first = part * count
    rows = 2 * blocks * slots
    shape = (blocks, kinds, slots, HEAD_DIM)
    whole = pl.BlockSpec((rows, HEAD_DIM), lambda g, half: (0, 0))
    return pl.pallas_call(
        attend_kernel,
        grid_spec=pltpu.PrefetchScalarGridSpec(
            num_scalar_prefetch=1,
            grid=(count,),
            in_specs=[
                pl.BlockSpec(shape, lambda g, half: (0, 0, 0, half[0] * heads + first + g)),
                pl.BlockSpec(shape, lambda g, half: (0, 0, 0, first + g)),
                whole,
                whole,
                whole,
                whole,
                pl.BlockSpec((1, rows), lambda g, half: (0, 0)),
                pl.BlockSpec((HEAD_DIM, HEAD_DIM), lambda g, half: (0, 0)),
            ]
            + ([] if into is None else [pl.BlockSpec(memory_space=pl.ANY)]),
            out_specs=pl.BlockSpec((rows, HEAD_DIM), lambda g, half: (0, first + g)),
        ),
        out_shape=jax.ShapeDtypeStruct((rows, width), jnp.bfloat16),
        input_output_aliases={} if into is None else {9: 0},
        compiler_params=pltpu.CompilerParams(vmem_limit_bytes=VMEM),
        cost_estimate=pl.CostEstimate(
            flops=count * rows * rows * HEAD_DIM * 4,
            bytes_accessed=rows * width * 8,
            transcendentals=0,
        ),
        name="attend",
    )(half, own, far, *tables, *([] if into is None else [into]))


def gelu_kernel(part_ref, units_ref, *refs):
    refs[-1][...] = jax.nn.gelu(units_ref[0].astype(jnp.float32), approximate=True).astype(jnp.bfloat16)


def activate(part, units, width, into=None):
    blocks, slots, _ = units.shape
    first = 0 if into is None else blocks
    return pl.pallas_call(
        gelu_kernel,
        grid_spec=pltpu.PrefetchScalarGridSpec(
            num_scalar_prefetch=1,
            grid=(blocks,),
            in_specs=[pl.BlockSpec((1, slots, width), lambda b, part: (b, 0, part[0]))]
            + ([] if into is None else [pl.BlockSpec(memory_space=pl.ANY)]),
            out_specs=pl.BlockSpec((slots, width), lambda b, part: (first + b, 0)),
        ),
        out_shape=jax.ShapeDtypeStruct((2 * blocks * slots, width), jnp.bfloat16),
        input_output_aliases={} if into is None else {2: 0},
        compiler_params=pltpu.CompilerParams(vmem_limit_bytes=LESS),
        cost_estimate=pl.CostEstimate(
            flops=blocks * slots * width * 4, bytes_accessed=blocks * slots * width, transcendentals=0
        ),
        name="activate",
    )(part, units, *([] if into is None else [into]))


def project_kernel(layout, sides, core_ref, attn_ref, act_ref, *refs):
    pieces, outs, (w_ref, sems) = refs[: len(layout)], refs[len(layout) : -2], refs[-2:]
    depth = attn_ref.shape[1]
    rows, columns = outs[0].shape
    taken = pl.ds(rows * sides[0], rows * len(sides))
    core = core_ref[0]
    copies = []
    for (base, here, share), piece in zip(layout, pieces):
        start = base + (core if here else 1 - core) * share
        place = pl.ds(pl.multiple_of(start, 16), piece.shape[0])
        copies.append(pltpu.make_async_copy(piece, w_ref.at[place], sems.at[len(copies)]))
        copies[-1].start()
    pending = [base // (2 * share) * 2 * share for base, _, share in layout]
    for first in range(0, columns, 256):
        end = min(first + 256, columns)
        while pending and pending[0] < end:
            copies[-len(pending)].wait()
            pending.pop(0)
        total = lax.dot_general(attn_ref[taken], w_ref[first:end, :depth], NT, preferred_element_type=jnp.float32)
        total += lax.dot_general(act_ref[taken], w_ref[first:end, depth:], NT, preferred_element_type=jnp.float32)
        for index, out_ref in enumerate(outs):
            out_ref[:, first:end] = total[rows * index : rows * (index + 1)].astype(out_ref.dtype)


def project(core, attn, act, chips, sides=(0, 1)):
    share = sum(piece.shape[0] for here, _, piece in chips[0] if here)
    layout, flat = [], []
    for index, pieces in enumerate(chips):
        for here, first, piece in pieces:
            layout.append((2 * share * index + first, here, share))
            flat.append(piece)
    rows, depth = attn.shape[0] // 2, attn.shape[1] + act.shape[1]
    columns = 2 * share * len(chips)
    inside = pl.BlockSpec(memory_space=pltpu.VMEM)
    return pl.pallas_call(
        functools.partial(project_kernel, layout, sides),
        in_specs=[pl.BlockSpec(memory_space=pltpu.SMEM), inside, inside]
        + [pl.BlockSpec(memory_space=pl.ANY)] * len(flat),
        out_specs=[inside] * len(sides),
        out_shape=[jax.ShapeDtypeStruct((rows, columns), jnp.bfloat16)] * len(sides),
        scratch_shapes=[
            pltpu.VMEM((columns, depth), jnp.bfloat16),
            pltpu.SemaphoreType.DMA((len(flat),)),
        ],
        compiler_params=pltpu.CompilerParams(vmem_limit_bytes=LESS),
        cost_estimate=pl.CostEstimate(
            flops=rows * columns * depth // 2, bytes_accessed=columns * depth // 4, transcendentals=0
        ),
        name="project",
    )(core, attn, act, *flat)


def finish_kernel(chunks, tile_ref, place_ref, step_ref, *refs):
    pairs = [refs[2 * i : 2 * i + 2] for i in range(chunks)]
    (
        stream_ref, bias_ref, gate_ref, scale_ref, shift_ref, w_ref, b_ref, latent_ref, hidden_ref, next_ref, proj_ref,
    ) = refs[2 * chunks :]
    slots, width = proj_ref.shape
    rows = pl.ds(pl.multiple_of(pl.program_id(0) * slots, slots), slots)
    places = len(PATH)
    chip = width // places
    mine = place_ref[places + tile_ref[0] // 2]
    behind = [0] + [distance for step in range(1, places // 2) for distance in (step, -step)] + [places // 2]
    total = jnp.zeros((slots, chip), jnp.float32)
    for own_ref, far_ref in pairs:
        for first in range(0, own_ref.shape[1], chip):
            source = place_ref[(mine - behind.pop(0) + places) % places]
            target = pl.ds(pl.multiple_of(chip * source, 128), chip)
            part = slice(first, first + chip)
            proj = own_ref[rows, part].astype(jnp.float32) + far_ref[rows, part].astype(jnp.float32)
            updated = stream_ref[rows, target].astype(jnp.float32) + gate_ref[:, target] * (proj + bias_ref[:, target])
            hidden_ref[0, :, target] = updated.astype(jnp.bfloat16)
            proj_ref[:, target] = updated
            total += updated

    @pl.when(pl.program_id(0) > 0)
    def _():
        parts = [slice(chip * index, chip * (index + 1)) for index in range(places)]
        mean = jnp.sum(total, axis=-1, keepdims=True) / width
        square = jnp.zeros((slots, chip), jnp.float32)
        for part in parts:
            center = proj_ref[:, part] - mean
            square += center * center
        inverse = lax.rsqrt(jnp.sum(square, axis=-1, keepdims=True) / width + EPS)
        velocity = b_ref[...]
        for part in parts:
            normed = (proj_ref[:, part] - mean) * inverse
            modulated = ((1.0 + scale_ref[:, part]) * normed + shift_ref[:, part]).astype(jnp.bfloat16)
            velocity += lax.dot_general(w_ref[:, part], modulated, NT, preferred_element_type=jnp.float32)
        next_ref[0] = latent_ref[0] + step_ref[0] * velocity


def finish(tile, step, chunks, stream, bias, gate, scale, shift, w_final, b_final, latent):
    blocks, slots, width = stream.shape
    channels = w_final.shape[0]
    flat = [array for pair in chunks for array in pair]

    def whole(array):
        return pl.BlockSpec(array.shape, lambda b, *_: (0, 0))

    tokens = pl.BlockSpec((1, slots, width), lambda b, *_: (b, 0, 0))
    image = pl.BlockSpec((1, channels, slots), lambda b, *_: (jnp.maximum(b - 1, 0), 0, 0))
    return pl.pallas_call(
        functools.partial(finish_kernel, len(chunks)),
        grid_spec=pltpu.PrefetchScalarGridSpec(
            num_scalar_prefetch=3,
            grid=(blocks,),
            in_specs=[pl.BlockSpec(memory_space=pltpu.VMEM)] * (len(flat) + 1)
            + [
                whole(bias),
                whole(gate),
                whole(scale),
                whole(shift),
                whole(w_final),
                whole(b_final),
                image,
            ],
            out_specs=[tokens, image],
            scratch_shapes=[pltpu.VMEM((slots, width), jnp.float32)],
        ),
        out_shape=[
            jax.ShapeDtypeStruct(stream.shape, jnp.bfloat16),
            jax.ShapeDtypeStruct(latent.shape, jnp.float32),
        ],
        compiler_params=pltpu.CompilerParams(vmem_limit_bytes=LIGHT),
        cost_estimate=pl.CostEstimate(
            flops=blocks * slots * width * 160, bytes_accessed=blocks * slots * width * 10, transcendentals=0
        ),
        name="finish",
    )(tile, np.array(PATH + PLACE, np.int32), step, *flat, stream.reshape(blocks * slots, width), bias, gate, scale, shift, w_final, b_final, latent)


PATH = (0, 1, 3, 5, 7, 6, 4, 2)
PLACE = tuple(PATH.index(chip) for chip in range(len(PATH)))


def hop(array, by):
    places = len(PATH)
    pairs = [(2 * PATH[i] + c, 2 * PATH[(i + by) % places] + c) for i in range(places) for c in range(2)]
    return lax.ppermute(array, "tile", pairs)


def both_cores(array, first=0):
    other = lax.ppermute(array, "tile", [(t, t ^ 1) for t in range(2 * len(PATH))])
    return [(True, first, array), (False, first, other)]


def paired(
    partners,
    attn_proj,
    mlp_proj,
    stream,
    text_len,
    q_gain,
    k_gain,
    w_out_attn,
    w_out_mlp,
    bias_out,
    gate_mod,
    final_shift,
    final_scale,
    w_final,
    b_final,
    latent,
    step_size,
):
    me = lax.axis_index("head")
    half = me[None].astype(jnp.int32)
    trade = functools.partial(lax.ppermute, axis_name="head", perm=[(0, 1), (1, 0)])

    tile = lax.axis_index("tile").astype(jnp.int32)
    core = (tile % 2)[None]
    own_attn = jnp.transpose(attn_proj[0], (0, 2, 1, 3))
    own_units = mlp_proj[0]
    slots = own_attn.shape[2]
    units = own_units.shape[2] // partners
    width = own_attn.shape[3] // partners
    sent_attn = lax.dynamic_slice_in_dim(own_attn, (1 - me) * width, width, axis=3)
    block = jnp.concatenate([w_out_attn.T, w_out_mlp.T], axis=1)

    onward, back = hop(block, 1), hop(block, -1)
    far_attn = trade(sent_attn)
    chips = [both_cores(block)]

    tables = make_tables(half, text_len, q_gain, k_gain, 6 * slots)
    act_near = activate(half, own_units, units)
    sent_units = lax.dynamic_slice_in_dim(own_units, (1 - me) * units, units, axis=2)

    onward, back, tables, act_near, sent_units, chips = lax.optimization_barrier(
        (onward, back, tables, act_near, sent_units, [[piece[2] for piece in chip] for chip in chips])
    )
    chips = [[(True, 0, chip[0]), (False, 0, chip[1])] for chip in chips]
    chips += [both_cores(onward), both_cores(back)]
    onward, back = hop(onward, 1), hop(back, -1)
    far_attn, sent_units = lax.optimization_barrier((far_attn, sent_units))
    far_units = trade(sent_units)
    attn = attend(half, own_attn, far_attn, tables, 0, 2)
    blocks = [piece[2] for chip in chips[1:] for piece in chip]
    attn, onward, back, blocks = lax.optimization_barrier((attn, onward, back, blocks))
    chips[1:] = [[(True, 0, blocks[i]), (False, 0, blocks[i + 1])] for i in (0, 2)]
    chips += [both_cores(onward), both_cores(back)]
    onward, back = hop(onward, 1), hop(back, -1)
    attn = attend(half, own_attn, far_attn, tables, 1, 2, attn)
    far_units, attn = lax.optimization_barrier((far_units, attn))
    act = activate(jnp.zeros_like(half), far_units, units, act_near)

    chunks = []

    def send(group):
        own, sent = project(core, attn, act, group)
        chunks.append((own, trade(sent)))
        return sent

    (sent,) = project(core, attn, act, chips[0:1], (1,))
    chunks.append([None, trade(sent)])
    attn, sent = lax.optimization_barrier((attn, sent))
    sent = send(chips[1:3])
    onward, back, attn, sent, chunks[0][1] = lax.optimization_barrier((onward, back, attn, sent, chunks[0][1]))
    middle = block.shape[0] // 2
    last = hop(onward[:middle], 1), hop(back[middle:], -1)
    chips += [both_cores(onward), both_cores(back)]
    sent = send(chips[3:5])
    attn, sent, chunks[1] = lax.optimization_barrier((attn, sent, chunks[1]))
    sent = send(chips[5:7])
    onward, back, attn, sent, chunks[2] = lax.optimization_barrier((*last, attn, sent, chunks[2]))
    chips.append(both_cores(onward) + both_cores(back, middle))
    sent = send(chips[7:8])
    attn, sent = lax.optimization_barrier((attn, sent))
    (chunks[0][0],) = project(core, attn, act, chips[0:1], (0,))

    hidden, following = finish(
        tile[None],
        step_size,
        chunks,
        stream[0],
        bias_out[None, :],
        gate_mod,
        final_scale,
        final_shift,
        w_final.T,
        b_final[:, None],
        jnp.transpose(latent[0], (0, 2, 1)),
    )
    return hidden[None], jnp.transpose(following, (0, 2, 1))[None]


def solution(mesh):
    placed = (
        P("tile", None, "head", None, None),
        P("tile", None, "head", None),
        P("tile", None, "head", None),
        P("tile"),
        P(),
        P(),
        P("head", "tile"),
        P("head", "tile"),
        P(),
        P("tile", None),
        P("tile", None),
        P("tile", None),
        P(),
        P(),
        P("tile", None, "head", None),
        P("tile"),
    )
    return jax.shard_map(
        functools.partial(paired, mesh.shape["head"]) if fits(mesh.shape) else general,
        mesh=mesh,
        in_specs=placed,
        out_specs=(P("tile", None, "head", None), P("tile", None, "head", None)),
        check_vma=False,
    )
```

```python
import functools
import math

import jax
import jax.numpy as jnp
import numpy as np
from jax import lax
from jax.experimental import pallas as pl
from jax.experimental.pallas import tpu as pltpu
from jax.sharding import PartitionSpec as P

HEAD_DIM = 128
SLOTS = 192
GRID_W = 32


def rope_tables(positions):
    pairs_zero = HEAD_DIM // 16
    pairs_axis = (HEAD_DIM // 2 - pairs_zero) // 2
    freqs = 10000.0 ** (-jnp.arange(pairs_axis, dtype=jnp.float32) / pairs_axis)
    count = positions.shape[0]
    angles = [jnp.zeros((count, HEAD_DIM // 2), jnp.float32)]
    for block in range(1, 3):
        image_index = (block - 1) * SLOTS + positions
        rows = (image_index // GRID_W).astype(jnp.float32)
        columns = (image_index % GRID_W).astype(jnp.float32)
        angles.append(
            jnp.concatenate(
                [
                    jnp.zeros((count, pairs_zero), jnp.float32),
                    rows[:, None] * freqs[None, :],
                    columns[:, None] * freqs[None, :],
                ],
                axis=1,
            )
        )
    stacked = jnp.stack(angles)
    return (jnp.cos(stacked), jnp.sin(stacked))


def prepare(raw, gain, cosine, sine):
    normed = raw * lax.rsqrt(jnp.mean(raw * raw, axis=-1, keepdims=True) + 1e-06) * gain
    halves = normed.reshape(normed.shape[:-1] + (HEAD_DIM // 2, 2))
    first = halves[..., 0]
    second = halves[..., 1]
    cosine = cosine[None, :, :, None, :]
    sine = sine[None, :, :, None, :]
    rotated = jnp.stack([first * cosine - second * sine, first * sine + second * cosine], axis=-1)
    return rotated.reshape(raw.shape).astype(jnp.bfloat16)


def attend_head(inputs):
    queries, keys, values, live = inputs
    scores = jnp.einsum("qd,kd->qk", queries, keys, preferred_element_type=jnp.float32) / math.sqrt(
        HEAD_DIM
    )
    scores = jnp.where(live[None, :], scores, -jnp.inf)
    top = jnp.max(scores, axis=-1, keepdims=True)
    weights = jnp.exp(scores - top)
    total = jnp.sum(weights, axis=-1, keepdims=True)
    mixed = jnp.dot(weights.astype(jnp.bfloat16), values, preferred_element_type=jnp.float32)
    return (mixed / total).astype(jnp.bfloat16)


def attend_request(inputs):
    queries, keys, values, live = inputs
    count = queries.shape[1]
    broad_live = jnp.broadcast_to(live[None, :], (count, live.shape[0]))
    result = lax.map(
        attend_head,
        (
            jnp.moveaxis(queries, 1, 0),
            jnp.moveaxis(keys, 1, 0),
            jnp.moveaxis(values, 1, 0),
            broad_live,
        ),
    )
    return jnp.moveaxis(result, 0, 1)


def general(
    attn_proj,
    mlp_proj,
    stream,
    text_len,
    q_gain,
    k_gain,
    w_out_attn,
    w_out_mlp,
    bias_out,
    gate_mod,
    final_shift,
    final_scale,
    w_final,
    b_final,
    latent,
    step_size,
):
    requests = attn_proj.shape[0]
    own_slots = attn_proj.shape[2]
    width = attn_proj.shape[4]
    heads = width // HEAD_DIM
    start_slot = lax.axis_index("head") * own_slots
    positions = start_slot + jnp.arange(own_slots, dtype=jnp.int32)
    cosine, sine = rope_tables(positions)
    head_shape = (requests, 3, own_slots, heads, HEAD_DIM)
    queries = prepare(
        attn_proj[:, :, :, 0].astype(jnp.float32).reshape(head_shape), q_gain, cosine, sine
    )
    keys = prepare(
        attn_proj[:, :, :, 1].astype(jnp.float32).reshape(head_shape), k_gain, cosine, sine
    )
    packed = jnp.stack(
        [
            queries.reshape(requests, 3, own_slots, width),
            keys.reshape(requests, 3, own_slots, width),
            attn_proj[:, :, :, 2],
        ],
        axis=3,
    )
    units = mlp_proj[:, :, :, None, :]
    moved, hidden_units = (
        lax.all_to_all(packed, "head", split_axis=4, concat_axis=2, tiled=True),
        lax.all_to_all(units, "head", split_axis=4, concat_axis=2, tiled=True),
    )
    hidden_units = hidden_units[:, :, :, 0]
    tile_slots = moved.shape[2]
    local_width = moved.shape[4]
    local_heads = local_width // HEAD_DIM
    flat_shape = (requests, 3 * tile_slots, local_heads, HEAD_DIM)
    all_positions = jnp.arange(tile_slots, dtype=jnp.int32)
    text_live = all_positions[None, :] < text_len[:, None]
    image_live = jnp.ones_like(text_live)
    live = jnp.stack([text_live, image_live, image_live], axis=1).reshape(requests, 3 * tile_slots)
    attn_out = lax.map(
        attend_request,
        (
            moved[:, :, :, 0].reshape(flat_shape),
            moved[:, :, :, 1].reshape(flat_shape),
            moved[:, :, :, 2].reshape(flat_shape),
            live,
        ),
    )
    attn_out = attn_out.reshape(requests, 3, tile_slots, local_width)
    mlp_act = jax.nn.gelu(hidden_units.astype(jnp.float32), approximate=True).astype(jnp.bfloat16)
    term = jnp.einsum(
        "rbsk,kd->rbsd",
        attn_out,
        lax.all_gather(w_out_attn, "tile", axis=1, tiled=True),
        preferred_element_type=jnp.float32,
    )
    term = term + jnp.einsum(
        "rbsk,kd->rbsd",
        mlp_act,
        lax.all_gather(w_out_mlp, "tile", axis=1, tiled=True),
        preferred_element_type=jnp.float32,
    )
    proj = lax.psum_scatter(term, "head", scatter_dimension=2, tiled=True)
    updated = stream.astype(jnp.float32) + gate_mod[:, None, None, :] * (proj + bias_out)
    hidden_out = updated.astype(jnp.bfloat16)
    image = updated[:, 1:]
    center = image - jnp.mean(image, axis=-1, keepdims=True)
    variance = jnp.mean(center * center, axis=-1, keepdims=True)
    normed = center * lax.rsqrt(variance + 1e-06)
    modulated = (
        (1.0 + final_scale[:, None, None, :]) * normed + final_shift[:, None, None, :]
    ).astype(jnp.bfloat16)
    velocity = (
        jnp.einsum("rbsd,dc->rbsc", modulated, w_final, preferred_element_type=jnp.float32)
        + b_final
    )
    latent_next = latent + step_size[:, None, None, None] * velocity
    return (hidden_out, latent_next)


EPS = 1e-06
SCALE = math.log2(math.e) / math.sqrt(HEAD_DIM)
VMEM = 60 * 1024 * 1024
LIGHT = 24 * 1024 * 1024
LESS = 34 * 1024 * 1024
NT = (((1,), (1,)), ((), ()))


def fits(sizes):
    return sizes["head"] == 2 and sizes["tile"] == 2 * len(PATH)


def tables_kernel(half_ref, len_ref, row_freq_ref, col_freq_ref, q_ref, k_ref, cq_ref, sq_ref, ck_ref, sk_ref, mask_ref, swap_ref):
    rows = cq_ref.shape[0]
    slots = rows // 6

    def place(axis, shape):
        index = lax.broadcasted_iota(jnp.int32, shape, axis)
        away = index >= rows // 2
        block = (index - jnp.where(away, rows // 2, 0)) // slots
        slot = index % slots + slots * jnp.where(away, 1 - half_ref[0], half_ref[0])
        return block, slot

    shape = (rows, HEAD_DIM)
    block, slot = place(0, shape)
    image = (block - 1) * SLOTS + slot
    angle = (image // GRID_W).astype(jnp.float32) * row_freq_ref[...]
    angle += (image % GRID_W).astype(jnp.float32) * col_freq_ref[...]
    angle = jnp.where(block == 0, 0.0, angle)
    cosine, sine = jnp.cos(angle), jnp.sin(angle)
    odd = lax.broadcasted_iota(jnp.int32, shape, 1) % 2 == 1
    for gain_ref, c_ref, s_ref in ((q_ref, cq_ref, sq_ref), (k_ref, ck_ref, sk_ref)):
        gain = jnp.broadcast_to(gain_ref[...], shape)
        partner = jnp.where(odd, pltpu.roll(gain, 1, 1), -pltpu.roll(gain, HEAD_DIM - 1, 1))
        c_ref[...] = cosine * gain
        s_ref[...] = sine * partner
    block, slot = place(1, (1, rows))
    mask_ref[...] = jnp.where((block > 0) | (slot < len_ref[0]), 0.0, -jnp.inf)
    square = (HEAD_DIM, HEAD_DIM)
    column = lax.broadcasted_iota(jnp.int32, square, 1)
    other = column + 1 - 2 * (column % 2)
    swap_ref[...] = jnp.where(lax.broadcasted_iota(jnp.int32, square, 0) == other, 1.0, 0.0).astype(jnp.bfloat16)


def make_tables(half, text_len, q_gain, k_gain, rows):
    pairs_zero = HEAD_DIM // 16
    pairs_axis = (HEAD_DIM // 2 - pairs_zero) // 2
    freqs = 10000.0 ** (-np.arange(pairs_axis, dtype=np.float32) / np.float32(pairs_axis))
    row_freq, col_freq = np.zeros((2, 1, HEAD_DIM // 2), np.float32)
    row_freq[0, pairs_zero : pairs_zero + pairs_axis] = freqs
    col_freq[0, pairs_zero + pairs_axis :] = freqs
    scalars = pl.BlockSpec(memory_space=pltpu.SMEM)
    table = jax.ShapeDtypeStruct((rows, HEAD_DIM), jnp.float32)
    return pl.pallas_call(
        tables_kernel,
        in_specs=[scalars, scalars] + [pl.BlockSpec(memory_space=pltpu.VMEM)] * 4,
        out_shape=[
            table,
            table,
            table,
            table,
            jax.ShapeDtypeStruct((1, rows), jnp.float32),
            jax.ShapeDtypeStruct((HEAD_DIM, HEAD_DIM), jnp.bfloat16),
        ],
        compiler_params=pltpu.CompilerParams(vmem_limit_bytes=VMEM),
        cost_estimate=pl.CostEstimate(flops=rows * HEAD_DIM * 8, bytes_accessed=rows * HEAD_DIM * 4, transcendentals=0),
        name="tables",
    )(
        half,
        text_len,
        np.repeat(row_freq, 2, axis=1),
        np.repeat(col_freq, 2, axis=1),
        q_gain[None, :],
        k_gain[None, :],
    )


def attend_kernel(half_ref, own_ref, far_q_ref, far_kv_ref, cq_ref, sq_ref, ck_ref, sk_ref, mask_ref, swap_ref, *refs):
    out_ref = refs[-1]
    rows = own_ref.shape[0] * own_ref.shape[2]

    def load(part):
        far = far_q_ref[...] if part == 0 else far_kv_ref[:, part - 1]
        return jnp.concatenate([own_ref[:, part].reshape(rows, HEAD_DIM), far.reshape(rows, HEAD_DIM)], axis=0)

    def turn(raw, straight, crossed):
        wide = raw.astype(jnp.float32)
        scale = lax.rsqrt(jnp.mean(wide * wide, axis=-1, keepdims=True) + EPS)
        partner = jnp.dot(raw, swap_ref[...], preferred_element_type=jnp.float32)
        return ((wide * straight + partner * crossed) * scale).astype(jnp.bfloat16)

    queries = turn(load(0), cq_ref[...], sq_ref[...])
    keys = turn(load(1), ck_ref[...], sk_ref[...])
    scores = lax.dot_general(queries, keys, NT, preferred_element_type=jnp.float32)
    scores = scores * SCALE + mask_ref[...]
    weights = jnp.exp2(scores - jnp.max(scores, axis=-1, keepdims=True))
    total = jnp.sum(weights, axis=-1, keepdims=True)
    mixed = jnp.dot(weights.astype(jnp.bfloat16), load(2), preferred_element_type=jnp.float32)
    out_ref[...] = (mixed / total).astype(jnp.bfloat16)


def attend(half, own, far, tables, part, parts, into=None):
    far_q, far_kv = far
    blocks, slots, width = far_q.shape
    heads = width // HEAD_DIM
    count = heads // parts
    first = part * count
    rows = 2 * blocks * slots
    whole = pl.BlockSpec((rows, HEAD_DIM), lambda g, half: (0, 0))
    return pl.pallas_call(
        attend_kernel,
        grid_spec=pltpu.PrefetchScalarGridSpec(
            num_scalar_prefetch=1,
            grid=(count,),
            in_specs=[
                pl.BlockSpec((blocks, 3, slots, HEAD_DIM), lambda g, half: (0, 0, 0, half[0] * heads + first + g)),
                pl.BlockSpec((blocks, slots, HEAD_DIM), lambda g, half: (0, 0, first + g)),
                pl.BlockSpec((blocks, 2, slots, HEAD_DIM), lambda g, half: (0, 0, 0, first + g)),
                whole,
                whole,
                whole,
                whole,
                pl.BlockSpec((1, rows), lambda g, half: (0, 0)),
                pl.BlockSpec((HEAD_DIM, HEAD_DIM), lambda g, half: (0, 0)),
            ]
            + ([] if into is None else [pl.BlockSpec(memory_space=pl.ANY)]),
            out_specs=pl.BlockSpec((rows, HEAD_DIM), lambda g, half: (0, first + g)),
        ),
        out_shape=jax.ShapeDtypeStruct((rows, width), jnp.bfloat16),
        input_output_aliases={} if into is None else {10: 0},
        compiler_params=pltpu.CompilerParams(vmem_limit_bytes=VMEM),
        cost_estimate=pl.CostEstimate(
            flops=count * rows * rows * HEAD_DIM * 4,
            bytes_accessed=rows * width * 8,
            transcendentals=0,
        ),
        name="attend",
    )(half, own, far_q, far_kv, *tables, *([] if into is None else [into]))


def gelu_kernel(part_ref, units_ref, *refs):
    refs[-1][...] = jax.nn.gelu(units_ref[0].astype(jnp.float32), approximate=True).astype(jnp.bfloat16)


def activate(part, units, width, into=None):
    blocks, slots, _ = units.shape
    first = 0 if into is None else blocks
    return pl.pallas_call(
        gelu_kernel,
        grid_spec=pltpu.PrefetchScalarGridSpec(
            num_scalar_prefetch=1,
            grid=(blocks,),
            in_specs=[pl.BlockSpec((1, slots, width), lambda b, part: (b, 0, part[0]))]
            + ([] if into is None else [pl.BlockSpec(memory_space=pl.ANY)]),
            out_specs=pl.BlockSpec((slots, width), lambda b, part: (first + b, 0)),
        ),
        out_shape=jax.ShapeDtypeStruct((2 * blocks * slots, width), jnp.bfloat16),
        input_output_aliases={} if into is None else {2: 0},
        compiler_params=pltpu.CompilerParams(vmem_limit_bytes=LESS),
        cost_estimate=pl.CostEstimate(
            flops=blocks * slots * width * 4, bytes_accessed=blocks * slots * width, transcendentals=0
        ),
        name="activate",
    )(part, units, *([] if into is None else [into]))


def project_kernel(layout, sides, core_ref, attn_ref, act_ref, *refs):
    pieces, outs, (w_ref, sems) = refs[: len(layout)], refs[len(layout) : -2], refs[-2:]
    depth = attn_ref.shape[1]
    rows, columns = outs[0].shape
    taken = pl.ds(rows * sides[0], rows * len(sides))
    core = core_ref[0]
    copies = []
    for (base, here, share), piece in zip(layout, pieces):
        start = base + (core if here else 1 - core) * share
        place = pl.ds(pl.multiple_of(start, 16), piece.shape[0])
        copies.append(pltpu.make_async_copy(piece, w_ref.at[place], sems.at[len(copies)]))
        copies[-1].start()
    pending = [base // (2 * share) * 2 * share for base, _, share in layout]
    for first in range(0, columns, 256):
        end = min(first + 256, columns)
        while pending and pending[0] < end:
            copies[-len(pending)].wait()
            pending.pop(0)
        total = lax.dot_general(attn_ref[taken], w_ref[first:end, :depth], NT, preferred_element_type=jnp.float32)
        total += lax.dot_general(act_ref[taken], w_ref[first:end, depth:], NT, preferred_element_type=jnp.float32)
        for index, out_ref in enumerate(outs):
            out_ref[:, first:end] = total[rows * index : rows * (index + 1)].astype(out_ref.dtype)


def project(core, attn, act, chips, sides=(0, 1)):
    share = sum(piece.shape[0] for here, _, piece in chips[0] if here)
    layout, flat = [], []
    for index, pieces in enumerate(chips):
        for here, first, piece in pieces:
            layout.append((2 * share * index + first, here, share))
            flat.append(piece)
    rows, depth = attn.shape[0] // 2, attn.shape[1] + act.shape[1]
    columns = 2 * share * len(chips)
    inside = pl.BlockSpec(memory_space=pltpu.VMEM)
    return pl.pallas_call(
        functools.partial(project_kernel, layout, sides),
        in_specs=[pl.BlockSpec(memory_space=pltpu.SMEM), inside, inside]
        + [pl.BlockSpec(memory_space=pl.ANY)] * len(flat),
        out_specs=[inside] * len(sides),
        out_shape=[jax.ShapeDtypeStruct((rows, columns), jnp.bfloat16)] * len(sides),
        scratch_shapes=[
            pltpu.VMEM((columns, depth), jnp.bfloat16),
            pltpu.SemaphoreType.DMA((len(flat),)),
        ],
        compiler_params=pltpu.CompilerParams(vmem_limit_bytes=LESS),
        cost_estimate=pl.CostEstimate(
            flops=rows * columns * depth // 2, bytes_accessed=columns * depth // 4, transcendentals=0
        ),
        name="project",
    )(core, attn, act, *flat)


def finish_kernel(chunks, tile_ref, place_ref, step_ref, *refs):
    pairs = [refs[2 * i : 2 * i + 2] for i in range(chunks)]
    (
        stream_ref, bias_ref, gate_ref, scale_ref, shift_ref, w_ref, b_ref, latent_ref, hidden_ref, next_ref, proj_ref,
    ) = refs[2 * chunks :]
    slots, width = proj_ref.shape
    rows = pl.ds(pl.multiple_of(pl.program_id(0) * slots, slots), slots)
    places = len(PATH)
    chip = width // places
    mine = place_ref[places + tile_ref[0] // 2]
    behind = [0] + [distance for step in range(1, places // 2) for distance in (step, -step)] + [places // 2]
    total = jnp.zeros((slots, chip), jnp.float32)
    for own_ref, far_ref in pairs:
        for first in range(0, own_ref.shape[1], chip):
            source = place_ref[(mine - behind.pop(0) + places) % places]
            target = pl.ds(pl.multiple_of(chip * source, 128), chip)
            part = slice(first, first + chip)
            proj = own_ref[rows, part].astype(jnp.float32) + far_ref[rows, part].astype(jnp.float32)
            updated = stream_ref[rows, target].astype(jnp.float32) + gate_ref[:, target] * (proj + bias_ref[:, target])
            hidden_ref[0, :, target] = updated.astype(jnp.bfloat16)
            proj_ref[:, target] = updated
            total += updated

    @pl.when(pl.program_id(0) > 0)
    def _():
        parts = [slice(chip * index, chip * (index + 1)) for index in range(places)]
        mean = jnp.sum(total, axis=-1, keepdims=True) / width
        square = jnp.zeros((slots, chip), jnp.float32)
        for part in parts:
            center = proj_ref[:, part] - mean
            square += center * center
        inverse = lax.rsqrt(jnp.sum(square, axis=-1, keepdims=True) / width + EPS)
        velocity = b_ref[...]
        for part in parts:
            normed = (proj_ref[:, part] - mean) * inverse
            modulated = ((1.0 + scale_ref[:, part]) * normed + shift_ref[:, part]).astype(jnp.bfloat16)
            velocity += lax.dot_general(w_ref[:, part], modulated, NT, preferred_element_type=jnp.float32)
        next_ref[0] = latent_ref[0] + step_ref[0] * velocity


def finish(tile, step, chunks, stream, bias, gate, scale, shift, w_final, b_final, latent):
    blocks, slots, width = stream.shape
    channels = w_final.shape[0]
    flat = [array for pair in chunks for array in pair]

    def whole(array):
        return pl.BlockSpec(array.shape, lambda b, *_: (0, 0))

    tokens = pl.BlockSpec((1, slots, width), lambda b, *_: (b, 0, 0))
    image = pl.BlockSpec((1, channels, slots), lambda b, *_: (jnp.maximum(b - 1, 0), 0, 0))
    return pl.pallas_call(
        functools.partial(finish_kernel, len(chunks)),
        grid_spec=pltpu.PrefetchScalarGridSpec(
            num_scalar_prefetch=3,
            grid=(blocks,),
            in_specs=[pl.BlockSpec(memory_space=pltpu.VMEM)] * (len(flat) + 1)
            + [
                whole(bias),
                whole(gate),
                whole(scale),
                whole(shift),
                whole(w_final),
                whole(b_final),
                image,
            ],
            out_specs=[tokens, image],
            scratch_shapes=[pltpu.VMEM((slots, width), jnp.float32)],
        ),
        out_shape=[
            jax.ShapeDtypeStruct(stream.shape, jnp.bfloat16),
            jax.ShapeDtypeStruct(latent.shape, jnp.float32),
        ],
        compiler_params=pltpu.CompilerParams(vmem_limit_bytes=LIGHT),
        cost_estimate=pl.CostEstimate(
            flops=blocks * slots * width * 160, bytes_accessed=blocks * slots * width * 10, transcendentals=0
        ),
        name="finish",
    )(tile, np.array(PATH + PLACE, np.int32), step, *flat, stream.reshape(blocks * slots, width), bias, gate, scale, shift, w_final, b_final, latent)


PATH = (0, 1, 3, 5, 7, 6, 4, 2)
PLACE = tuple(PATH.index(chip) for chip in range(len(PATH)))


def hop(array, by):
    places = len(PATH)
    pairs = [(2 * PATH[i] + c, 2 * PATH[(i + by) % places] + c) for i in range(places) for c in range(2)]
    return lax.ppermute(array, "tile", pairs)


def both_cores(array, first=0):
    other = lax.ppermute(array, "tile", [(t, t ^ 1) for t in range(2 * len(PATH))])
    return [(True, first, array), (False, first, other)]


def paired(
    partners,
    attn_proj,
    mlp_proj,
    stream,
    text_len,
    q_gain,
    k_gain,
    w_out_attn,
    w_out_mlp,
    bias_out,
    gate_mod,
    final_shift,
    final_scale,
    w_final,
    b_final,
    latent,
    step_size,
):
    me = lax.axis_index("head")
    half = me[None].astype(jnp.int32)
    trade = functools.partial(lax.ppermute, axis_name="head", perm=[(0, 1), (1, 0)])

    tile = lax.axis_index("tile").astype(jnp.int32)
    core = (tile % 2)[None]
    own_attn = jnp.transpose(attn_proj[0], (0, 2, 1, 3))
    own_units = mlp_proj[0]
    slots = own_attn.shape[2]
    units = own_units.shape[2] // partners
    width = own_attn.shape[3] // partners
    blocks, kinds, slots, _ = own_attn.shape
    sent_attn = [
        lax.dynamic_slice(own_attn, (0, first, 0, (1 - me) * width), (blocks, count, slots, width))
        for first, count in ((0, 1), (1, kinds - 1))
    ]
    block = jnp.concatenate([w_out_attn.T, w_out_mlp.T], axis=1)

    onward, back = hop(block, 1), hop(block, -1)
    far_attn = [trade(part) for part in sent_attn]
    far_attn[0] = far_attn[0][:, 0]
    chips = [both_cores(block)]

    tables = make_tables(half, text_len, q_gain, k_gain, 6 * slots)
    act_near = activate(half, own_units, units)
    sent_units = lax.dynamic_slice_in_dim(own_units, (1 - me) * units, units, axis=2)

    onward, back, tables, act_near, sent_units, chips = lax.optimization_barrier(
        (onward, back, tables, act_near, sent_units, [[piece[2] for piece in chip] for chip in chips])
    )
    chips = [[(True, 0, chip[0]), (False, 0, chip[1])] for chip in chips]
    chips += [both_cores(onward), both_cores(back)]
    onward, back = hop(onward, 1), hop(back, -1)
    far_attn, sent_units = lax.optimization_barrier((far_attn, sent_units))
    far_units = trade(sent_units)
    attn = attend(half, own_attn, far_attn, tables, 0, 2)
    blocks = [piece[2] for chip in chips[1:] for piece in chip]
    attn, onward, back, blocks = lax.optimization_barrier((attn, onward, back, blocks))
    chips[1:] = [[(True, 0, blocks[i]), (False, 0, blocks[i + 1])] for i in (0, 2)]
    chips += [both_cores(onward), both_cores(back)]
    onward, back = hop(onward, 1), hop(back, -1)
    attn = attend(half, own_attn, far_attn, tables, 1, 2, attn)
    far_units, attn = lax.optimization_barrier((far_units, attn))
    act = activate(jnp.zeros_like(half), far_units, units, act_near)

    chunks = []

    def send(group):
        own, sent = project(core, attn, act, group)
        chunks.append((own, trade(sent)))
        return sent

    (sent,) = project(core, attn, act, chips[0:1], (1,))
    chunks.append([None, trade(sent)])
    attn, sent = lax.optimization_barrier((attn, sent))
    sent = send(chips[1:3])
    onward, back, attn, sent, chunks[0][1] = lax.optimization_barrier((onward, back, attn, sent, chunks[0][1]))
    middle = block.shape[0] // 2
    last = hop(onward[:middle], 1), hop(back[middle:], -1)
    chips += [both_cores(onward), both_cores(back)]
    sent = send(chips[3:5])
    attn, sent, chunks[1] = lax.optimization_barrier((attn, sent, chunks[1]))
    sent = send(chips[5:7])
    onward, back, attn, sent, chunks[2] = lax.optimization_barrier((*last, attn, sent, chunks[2]))
    chips.append(both_cores(onward) + both_cores(back, middle))
    sent = send(chips[7:8])
    attn, sent = lax.optimization_barrier((attn, sent))
    (chunks[0][0],) = project(core, attn, act, chips[0:1], (0,))

    hidden, following = finish(
        tile[None],
        step_size,
        chunks,
        stream[0],
        bias_out[None, :],
        gate_mod,
        final_scale,
        final_shift,
        w_final.T,
        b_final[:, None],
        jnp.transpose(latent[0], (0, 2, 1)),
    )
    return hidden[None], jnp.transpose(following, (0, 2, 1))[None]


def solution(mesh):
    placed = (
        P("tile", None, "head", None, None),
        P("tile", None, "head", None),
        P("tile", None, "head", None),
        P("tile"),
        P(),
        P(),
        P("head", "tile"),
        P("head", "tile"),
        P(),
        P("tile", None),
        P("tile", None),
        P("tile", None),
        P(),
        P(),
        P("tile", None, "head", None),
        P("tile"),
    )
    return jax.shard_map(
        functools.partial(paired, mesh.shape["head"]) if fits(mesh.shape) else general,
        mesh=mesh,
        in_specs=placed,
        out_specs=(P("tile", None, "head", None), P("tile", None, "head", None)),
        check_vma=False,
    )
```

```python
import functools
import math

import jax
import jax.numpy as jnp
import numpy as np
from jax import lax
from jax.experimental import pallas as pl
from jax.experimental.pallas import tpu as pltpu
from jax.sharding import PartitionSpec as P

HEAD_DIM = 128
SLOTS = 192
GRID_W = 32


def rope_tables(positions):
    pairs_zero = HEAD_DIM // 16
    pairs_axis = (HEAD_DIM // 2 - pairs_zero) // 2
    freqs = 10000.0 ** (-jnp.arange(pairs_axis, dtype=jnp.float32) / pairs_axis)
    count = positions.shape[0]
    angles = [jnp.zeros((count, HEAD_DIM // 2), jnp.float32)]
    for block in range(1, 3):
        image_index = (block - 1) * SLOTS + positions
        rows = (image_index // GRID_W).astype(jnp.float32)
        columns = (image_index % GRID_W).astype(jnp.float32)
        angles.append(
            jnp.concatenate(
                [
                    jnp.zeros((count, pairs_zero), jnp.float32),
                    rows[:, None] * freqs[None, :],
                    columns[:, None] * freqs[None, :],
                ],
                axis=1,
            )
        )
    stacked = jnp.stack(angles)
    return (jnp.cos(stacked), jnp.sin(stacked))


def prepare(raw, gain, cosine, sine):
    normed = raw * lax.rsqrt(jnp.mean(raw * raw, axis=-1, keepdims=True) + 1e-06) * gain
    halves = normed.reshape(normed.shape[:-1] + (HEAD_DIM // 2, 2))
    first = halves[..., 0]
    second = halves[..., 1]
    cosine = cosine[None, :, :, None, :]
    sine = sine[None, :, :, None, :]
    rotated = jnp.stack([first * cosine - second * sine, first * sine + second * cosine], axis=-1)
    return rotated.reshape(raw.shape).astype(jnp.bfloat16)


def attend_head(inputs):
    queries, keys, values, live = inputs
    scores = jnp.einsum("qd,kd->qk", queries, keys, preferred_element_type=jnp.float32) / math.sqrt(
        HEAD_DIM
    )
    scores = jnp.where(live[None, :], scores, -jnp.inf)
    top = jnp.max(scores, axis=-1, keepdims=True)
    weights = jnp.exp(scores - top)
    total = jnp.sum(weights, axis=-1, keepdims=True)
    mixed = jnp.dot(weights.astype(jnp.bfloat16), values, preferred_element_type=jnp.float32)
    return (mixed / total).astype(jnp.bfloat16)


def attend_request(inputs):
    queries, keys, values, live = inputs
    count = queries.shape[1]
    broad_live = jnp.broadcast_to(live[None, :], (count, live.shape[0]))
    result = lax.map(
        attend_head,
        (
            jnp.moveaxis(queries, 1, 0),
            jnp.moveaxis(keys, 1, 0),
            jnp.moveaxis(values, 1, 0),
            broad_live,
        ),
    )
    return jnp.moveaxis(result, 0, 1)


def general(
    attn_proj,
    mlp_proj,
    stream,
    text_len,
    q_gain,
    k_gain,
    w_out_attn,
    w_out_mlp,
    bias_out,
    gate_mod,
    final_shift,
    final_scale,
    w_final,
    b_final,
    latent,
    step_size,
):
    requests = attn_proj.shape[0]
    own_slots = attn_proj.shape[2]
    width = attn_proj.shape[4]
    heads = width // HEAD_DIM
    start_slot = lax.axis_index("head") * own_slots
    positions = start_slot + jnp.arange(own_slots, dtype=jnp.int32)
    cosine, sine = rope_tables(positions)
    head_shape = (requests, 3, own_slots, heads, HEAD_DIM)
    queries = prepare(
        attn_proj[:, :, :, 0].astype(jnp.float32).reshape(head_shape), q_gain, cosine, sine
    )
    keys = prepare(
        attn_proj[:, :, :, 1].astype(jnp.float32).reshape(head_shape), k_gain, cosine, sine
    )
    packed = jnp.stack(
        [
            queries.reshape(requests, 3, own_slots, width),
            keys.reshape(requests, 3, own_slots, width),
            attn_proj[:, :, :, 2],
        ],
        axis=3,
    )
    units = mlp_proj[:, :, :, None, :]
    moved, hidden_units = (
        lax.all_to_all(packed, "head", split_axis=4, concat_axis=2, tiled=True),
        lax.all_to_all(units, "head", split_axis=4, concat_axis=2, tiled=True),
    )
    hidden_units = hidden_units[:, :, :, 0]
    tile_slots = moved.shape[2]
    local_width = moved.shape[4]
    local_heads = local_width // HEAD_DIM
    flat_shape = (requests, 3 * tile_slots, local_heads, HEAD_DIM)
    all_positions = jnp.arange(tile_slots, dtype=jnp.int32)
    text_live = all_positions[None, :] < text_len[:, None]
    image_live = jnp.ones_like(text_live)
    live = jnp.stack([text_live, image_live, image_live], axis=1).reshape(requests, 3 * tile_slots)
    attn_out = lax.map(
        attend_request,
        (
            moved[:, :, :, 0].reshape(flat_shape),
            moved[:, :, :, 1].reshape(flat_shape),
            moved[:, :, :, 2].reshape(flat_shape),
            live,
        ),
    )
    attn_out = attn_out.reshape(requests, 3, tile_slots, local_width)
    mlp_act = jax.nn.gelu(hidden_units.astype(jnp.float32), approximate=True).astype(jnp.bfloat16)
    term = jnp.einsum(
        "rbsk,kd->rbsd",
        attn_out,
        lax.all_gather(w_out_attn, "tile", axis=1, tiled=True),
        preferred_element_type=jnp.float32,
    )
    term = term + jnp.einsum(
        "rbsk,kd->rbsd",
        mlp_act,
        lax.all_gather(w_out_mlp, "tile", axis=1, tiled=True),
        preferred_element_type=jnp.float32,
    )
    proj = lax.psum_scatter(term, "head", scatter_dimension=2, tiled=True)
    updated = stream.astype(jnp.float32) + gate_mod[:, None, None, :] * (proj + bias_out)
    hidden_out = updated.astype(jnp.bfloat16)
    image = updated[:, 1:]
    center = image - jnp.mean(image, axis=-1, keepdims=True)
    variance = jnp.mean(center * center, axis=-1, keepdims=True)
    normed = center * lax.rsqrt(variance + 1e-06)
    modulated = (
        (1.0 + final_scale[:, None, None, :]) * normed + final_shift[:, None, None, :]
    ).astype(jnp.bfloat16)
    velocity = (
        jnp.einsum("rbsd,dc->rbsc", modulated, w_final, preferred_element_type=jnp.float32)
        + b_final
    )
    latent_next = latent + step_size[:, None, None, None] * velocity
    return (hidden_out, latent_next)


EPS = 1e-06
SCALE = math.log2(math.e) / math.sqrt(HEAD_DIM)
VMEM = 60 * 1024 * 1024
LIGHT = 24 * 1024 * 1024
LESS = 34 * 1024 * 1024
NT = (((1,), (1,)), ((), ()))


def fits(sizes):
    return sizes["head"] == 2 and sizes["tile"] == 2 * len(PATH)


def tables_kernel(half_ref, len_ref, row_freq_ref, col_freq_ref, q_ref, k_ref, cq_ref, sq_ref, ck_ref, sk_ref, mask_ref, swap_ref):
    rows = cq_ref.shape[0]
    slots = rows // 6

    def place(axis, shape):
        index = lax.broadcasted_iota(jnp.int32, shape, axis)
        away = index >= rows // 2
        block = (index - jnp.where(away, rows // 2, 0)) // slots
        slot = index % slots + slots * jnp.where(away, 1 - half_ref[0], half_ref[0])
        return block, slot

    shape = (rows, HEAD_DIM)
    block, slot = place(0, shape)
    image = (block - 1) * SLOTS + slot
    angle = (image // GRID_W).astype(jnp.float32) * row_freq_ref[...]
    angle += (image % GRID_W).astype(jnp.float32) * col_freq_ref[...]
    angle = jnp.where(block == 0, 0.0, angle)
    cosine, sine = jnp.cos(angle), jnp.sin(angle)
    odd = lax.broadcasted_iota(jnp.int32, shape, 1) % 2 == 1
    for gain_ref, c_ref, s_ref in ((q_ref, cq_ref, sq_ref), (k_ref, ck_ref, sk_ref)):
        gain = jnp.broadcast_to(gain_ref[...], shape)
        partner = jnp.where(odd, pltpu.roll(gain, 1, 1), -pltpu.roll(gain, HEAD_DIM - 1, 1))
        c_ref[...] = cosine * gain
        s_ref[...] = sine * partner
    block, slot = place(1, (1, rows))
    mask_ref[...] = jnp.where((block > 0) | (slot < len_ref[0]), 0.0, -jnp.inf)
    square = (HEAD_DIM, HEAD_DIM)
    column = lax.broadcasted_iota(jnp.int32, square, 1)
    other = column + 1 - 2 * (column % 2)
    swap_ref[...] = jnp.where(lax.broadcasted_iota(jnp.int32, square, 0) == other, 1.0, 0.0).astype(jnp.bfloat16)


def make_tables(half, text_len, q_gain, k_gain, rows):
    pairs_zero = HEAD_DIM // 16
    pairs_axis = (HEAD_DIM // 2 - pairs_zero) // 2
    freqs = 10000.0 ** (-np.arange(pairs_axis, dtype=np.float32) / np.float32(pairs_axis))
    row_freq, col_freq = np.zeros((2, 1, HEAD_DIM // 2), np.float32)
    row_freq[0, pairs_zero : pairs_zero + pairs_axis] = freqs
    col_freq[0, pairs_zero + pairs_axis :] = freqs
    scalars = pl.BlockSpec(memory_space=pltpu.SMEM)
    table = jax.ShapeDtypeStruct((rows, HEAD_DIM), jnp.float32)
    return pl.pallas_call(
        tables_kernel,
        in_specs=[scalars, scalars] + [pl.BlockSpec(memory_space=pltpu.VMEM)] * 4,
        out_shape=[
            table,
            table,
            table,
            table,
            jax.ShapeDtypeStruct((1, rows), jnp.float32),
            jax.ShapeDtypeStruct((HEAD_DIM, HEAD_DIM), jnp.bfloat16),
        ],
        compiler_params=pltpu.CompilerParams(vmem_limit_bytes=VMEM),
        cost_estimate=pl.CostEstimate(flops=rows * HEAD_DIM * 8, bytes_accessed=rows * HEAD_DIM * 4, transcendentals=0),
        name="tables",
    )(
        half,
        text_len,
        np.repeat(row_freq, 2, axis=1),
        np.repeat(col_freq, 2, axis=1),
        q_gain[None, :],
        k_gain[None, :],
    )


def attend_kernel(half_ref, own_ref, far_ref, cq_ref, sq_ref, ck_ref, sk_ref, mask_ref, swap_ref, *refs):
    out_ref = refs[-1]
    rows = own_ref.shape[0] * own_ref.shape[2]

    def load(part):
        return jnp.concatenate(
            [own_ref[:, part].reshape(rows, HEAD_DIM), far_ref[:, part].reshape(rows, HEAD_DIM)], axis=0
        )

    def turn(raw, straight, crossed):
        wide = raw.astype(jnp.float32)
        scale = lax.rsqrt(jnp.mean(wide * wide, axis=-1, keepdims=True) + EPS)
        partner = jnp.dot(raw, swap_ref[...], preferred_element_type=jnp.float32)
        return ((wide * straight + partner * crossed) * scale).astype(jnp.bfloat16)

    queries = turn(load(0), cq_ref[...], sq_ref[...])
    keys = turn(load(1), ck_ref[...], sk_ref[...])
    scores = lax.dot_general(queries, keys, NT, preferred_element_type=jnp.float32)
    scores = scores * SCALE + mask_ref[...]
    weights = jnp.exp2(scores - jnp.max(scores, axis=-1, keepdims=True))
    total = jnp.sum(weights, axis=-1, keepdims=True)
    mixed = jnp.dot(weights.astype(jnp.bfloat16), load(2), preferred_element_type=jnp.float32)
    out_ref[...] = (mixed / total).astype(jnp.bfloat16)


def attend(half, own, far, tables, part, parts, into=None):
    blocks, kinds, slots, width = far.shape
    heads = width // HEAD_DIM
    count = heads // parts
    first = part * count
    rows = 2 * blocks * slots
    shape = (blocks, kinds, slots, HEAD_DIM)
    whole = pl.BlockSpec((rows, HEAD_DIM), lambda g, half: (0, 0))
    return pl.pallas_call(
        attend_kernel,
        grid_spec=pltpu.PrefetchScalarGridSpec(
            num_scalar_prefetch=1,
            grid=(count,),
            in_specs=[
                pl.BlockSpec(shape, lambda g, half: (0, 0, 0, half[0] * heads + first + g)),
                pl.BlockSpec(shape, lambda g, half: (0, 0, 0, first + g)),
                whole,
                whole,
                whole,
                whole,
                pl.BlockSpec((1, rows), lambda g, half: (0, 0)),
                pl.BlockSpec((HEAD_DIM, HEAD_DIM), lambda g, half: (0, 0)),
            ]
            + ([] if into is None else [pl.BlockSpec(memory_space=pl.ANY)]),
            out_specs=pl.BlockSpec((rows, HEAD_DIM), lambda g, half: (0, first + g)),
        ),
        out_shape=jax.ShapeDtypeStruct((rows, width), jnp.bfloat16),
        input_output_aliases={} if into is None else {9: 0},
        compiler_params=pltpu.CompilerParams(vmem_limit_bytes=VMEM),
        cost_estimate=pl.CostEstimate(
            flops=count * rows * rows * HEAD_DIM * 4,
            bytes_accessed=rows * width * 8,
            transcendentals=0,
        ),
        name="attend",
    )(half, own, far, *tables, *([] if into is None else [into]))


def gelu_kernel(part_ref, units_ref, *refs):
    refs[-1][...] = jax.nn.gelu(units_ref[0].astype(jnp.float32), approximate=True).astype(jnp.bfloat16)


def activate(part, units, width, into=None):
    blocks, slots, _ = units.shape
    first = 0 if into is None else blocks
    return pl.pallas_call(
        gelu_kernel,
        grid_spec=pltpu.PrefetchScalarGridSpec(
            num_scalar_prefetch=1,
            grid=(blocks,),
            in_specs=[pl.BlockSpec((1, slots, width), lambda b, part: (b, 0, part[0]))]
            + ([] if into is None else [pl.BlockSpec(memory_space=pl.ANY)]),
            out_specs=pl.BlockSpec((slots, width), lambda b, part: (first + b, 0)),
        ),
        out_shape=jax.ShapeDtypeStruct((2 * blocks * slots, width), jnp.bfloat16),
        input_output_aliases={} if into is None else {2: 0},
        compiler_params=pltpu.CompilerParams(vmem_limit_bytes=LESS),
        cost_estimate=pl.CostEstimate(
            flops=blocks * slots * width * 4, bytes_accessed=blocks * slots * width, transcendentals=0
        ),
        name="activate",
    )(part, units, *([] if into is None else [into]))


def project_kernel(layout, sides, core_ref, attn_ref, act_ref, *refs):
    pieces, outs, (w_ref, sems) = refs[: len(layout)], refs[len(layout) : -2], refs[-2:]
    depth = attn_ref.shape[1]
    rows, columns = outs[0].shape
    taken = pl.ds(rows * sides[0], rows * len(sides))
    core = core_ref[0]
    copies = []
    for (base, here, share), piece in zip(layout, pieces):
        start = base + (core if here else 1 - core) * share
        place = pl.ds(pl.multiple_of(start, 16), piece.shape[0])
        copies.append(pltpu.make_async_copy(piece, w_ref.at[place], sems.at[len(copies)]))
        copies[-1].start()
    pending = [base // (2 * share) * 2 * share for base, _, share in layout]
    for first in range(0, columns, 256):
        end = min(first + 256, columns)
        while pending and pending[0] < end:
            copies[-len(pending)].wait()
            pending.pop(0)
        total = lax.dot_general(attn_ref[taken], w_ref[first:end, :depth], NT, preferred_element_type=jnp.float32)
        total += lax.dot_general(act_ref[taken], w_ref[first:end, depth:], NT, preferred_element_type=jnp.float32)
        for index, out_ref in enumerate(outs):
            out_ref[:, first:end] = total[rows * index : rows * (index + 1)].astype(out_ref.dtype)


def project(core, attn, act, chips, sides=(0, 1)):
    share = sum(piece.shape[0] for here, _, piece in chips[0] if here)
    layout, flat = [], []
    for index, pieces in enumerate(chips):
        for here, first, piece in pieces:
            layout.append((2 * share * index + first, here, share))
            flat.append(piece)
    rows, depth = attn.shape[0] // 2, attn.shape[1] + act.shape[1]
    columns = 2 * share * len(chips)
    inside = pl.BlockSpec(memory_space=pltpu.VMEM)
    return pl.pallas_call(
        functools.partial(project_kernel, layout, sides),
        in_specs=[pl.BlockSpec(memory_space=pltpu.SMEM), inside, inside]
        + [pl.BlockSpec(memory_space=pl.ANY)] * len(flat),
        out_specs=[inside] * len(sides),
        out_shape=[jax.ShapeDtypeStruct((rows, columns), jnp.bfloat16)] * len(sides),
        scratch_shapes=[
            pltpu.VMEM((columns, depth), jnp.bfloat16),
            pltpu.SemaphoreType.DMA((len(flat),)),
        ],
        compiler_params=pltpu.CompilerParams(vmem_limit_bytes=LESS),
        cost_estimate=pl.CostEstimate(
            flops=rows * columns * depth // 2, bytes_accessed=columns * depth // 4, transcendentals=0
        ),
        name="project",
    )(core, attn, act, *flat)


def finish_kernel(chunks, tile_ref, place_ref, step_ref, *refs):
    pairs = [refs[2 * i : 2 * i + 2] for i in range(chunks)]
    (
        stream_ref, bias_ref, gate_ref, scale_ref, shift_ref, w_ref, b_ref, latent_ref, hidden_ref, next_ref, proj_ref,
    ) = refs[2 * chunks :]
    slots, width = proj_ref.shape
    rows = pl.ds(pl.multiple_of(pl.program_id(0) * slots, slots), slots)
    places = len(PATH)
    chip = width // places
    mine = place_ref[places + tile_ref[0] // 2]
    behind = [0] + [distance for step in range(1, places // 2) for distance in (step, -step)] + [places // 2]
    total = jnp.zeros((slots, chip), jnp.float32)
    for own_ref, far_ref in pairs:
        for first in range(0, own_ref.shape[1], chip):
            source = place_ref[(mine - behind.pop(0) + places) % places]
            target = pl.ds(pl.multiple_of(chip * source, 128), chip)
            part = slice(first, first + chip)
            proj = own_ref[rows, part].astype(jnp.float32) + far_ref[rows, part].astype(jnp.float32)
            updated = stream_ref[rows, target].astype(jnp.float32) + gate_ref[:, target] * (proj + bias_ref[:, target])
            hidden_ref[0, :, target] = updated.astype(jnp.bfloat16)
            proj_ref[:, target] = updated
            total += updated

    @pl.when(pl.program_id(0) > 0)
    def _():
        parts = [slice(chip * index, chip * (index + 1)) for index in range(places)]
        mean = jnp.sum(total, axis=-1, keepdims=True) / width
        square = jnp.zeros((slots, chip), jnp.float32)
        for part in parts:
            center = proj_ref[:, part] - mean
            square += center * center
        inverse = lax.rsqrt(jnp.sum(square, axis=-1, keepdims=True) / width + EPS)
        velocity = b_ref[...]
        for part in parts:
            normed = (proj_ref[:, part] - mean) * inverse
            modulated = ((1.0 + scale_ref[:, part]) * normed + shift_ref[:, part]).astype(jnp.bfloat16)
            velocity += lax.dot_general(w_ref[:, part], modulated, NT, preferred_element_type=jnp.float32)
        next_ref[0] = latent_ref[0] + step_ref[0] * velocity


def finish(tile, step, chunks, stream, bias, gate, scale, shift, w_final, b_final, latent):
    blocks, slots, width = stream.shape
    channels = w_final.shape[0]
    flat = [array for pair in chunks for array in pair]

    def whole(array):
        return pl.BlockSpec(array.shape, lambda b, *_: (0, 0))

    tokens = pl.BlockSpec((1, slots, width), lambda b, *_: (b, 0, 0))
    image = pl.BlockSpec((1, channels, slots), lambda b, *_: (jnp.maximum(b - 1, 0), 0, 0))
    return pl.pallas_call(
        functools.partial(finish_kernel, len(chunks)),
        grid_spec=pltpu.PrefetchScalarGridSpec(
            num_scalar_prefetch=3,
            grid=(blocks,),
            in_specs=[pl.BlockSpec(memory_space=pltpu.VMEM)] * (len(flat) + 1)
            + [
                whole(bias),
                whole(gate),
                whole(scale),
                whole(shift),
                whole(w_final),
                whole(b_final),
                image,
            ],
            out_specs=[tokens, image],
            scratch_shapes=[pltpu.VMEM((slots, width), jnp.float32)],
        ),
        out_shape=[
            jax.ShapeDtypeStruct(stream.shape, jnp.bfloat16),
            jax.ShapeDtypeStruct(latent.shape, jnp.float32),
        ],
        compiler_params=pltpu.CompilerParams(vmem_limit_bytes=LIGHT),
        cost_estimate=pl.CostEstimate(
            flops=blocks * slots * width * 160, bytes_accessed=blocks * slots * width * 10, transcendentals=0
        ),
        name="finish",
    )(tile, np.array(PATH + PLACE, np.int32), step, *flat, stream.reshape(blocks * slots, width), bias, gate, scale, shift, w_final, b_final, latent)


PATH = (0, 1, 3, 5, 7, 6, 4, 2)
PLACE = tuple(PATH.index(chip) for chip in range(len(PATH)))


def hop(array, by):
    places = len(PATH)
    pairs = [(2 * PATH[i] + c, 2 * PATH[(i + by) % places] + c) for i in range(places) for c in range(2)]
    return lax.ppermute(array, "tile", pairs)


def both_cores(array, first=0):
    other = lax.ppermute(array, "tile", [(t, t ^ 1) for t in range(2 * len(PATH))])
    return [(True, first, array), (False, first, other)]


def paired(
    partners,
    attn_proj,
    mlp_proj,
    stream,
    text_len,
    q_gain,
    k_gain,
    w_out_attn,
    w_out_mlp,
    bias_out,
    gate_mod,
    final_shift,
    final_scale,
    w_final,
    b_final,
    latent,
    step_size,
):
    me = lax.axis_index("head")
    half = me[None].astype(jnp.int32)
    trade = functools.partial(lax.ppermute, axis_name="head", perm=[(0, 1), (1, 0)])

    tile = lax.axis_index("tile").astype(jnp.int32)
    core = (tile % 2)[None]
    own_attn = jnp.transpose(attn_proj[0], (0, 2, 1, 3))
    own_units = mlp_proj[0]
    slots = own_attn.shape[2]
    units = own_units.shape[2] // partners
    width = own_attn.shape[3] // partners
    sent_attn = lax.dynamic_slice_in_dim(own_attn, (1 - me) * width, width, axis=3)
    block = jnp.concatenate([w_out_attn.T, w_out_mlp.T], axis=1)

    onward, back = hop(block, 1), hop(block, -1)
    far_attn = trade(sent_attn)
    chips = [both_cores(block)]

    tables = make_tables(half, text_len, q_gain, k_gain, 6 * slots)
    act_near = activate(half, own_units, units)
    sent_units = lax.dynamic_slice_in_dim(own_units, (1 - me) * units, units, axis=2)

    onward, back, tables, act_near, sent_units, chips = lax.optimization_barrier(
        (onward, back, tables, act_near, sent_units, [[piece[2] for piece in chip] for chip in chips])
    )
    chips = [[(True, 0, chip[0]), (False, 0, chip[1])] for chip in chips]
    chips += [both_cores(onward), both_cores(back)]
    onward, back = hop(onward, 1), hop(back, -1)
    far_attn, sent_units = lax.optimization_barrier((far_attn, sent_units))
    far_units = trade(sent_units)
    attn = attend(half, own_attn, far_attn, tables, 0, 2)
    blocks = [piece[2] for chip in chips[1:] for piece in chip]
    attn, onward, back, blocks = lax.optimization_barrier((attn, onward, back, blocks))
    chips[1:] = [[(True, 0, blocks[i]), (False, 0, blocks[i + 1])] for i in (0, 2)]
    chips += [both_cores(onward), both_cores(back)]
    onward, back = hop(onward, 1), hop(back, -1)
    attn = attend(half, own_attn, far_attn, tables, 1, 2, attn)
    far_units, attn = lax.optimization_barrier((far_units, attn))
    act = activate(jnp.zeros_like(half), far_units, units, act_near)

    chunks = []

    def send(group):
        own, sent = project(core, attn, act, group)
        chunks.append((own, trade(sent)))
        return sent

    (sent,) = project(core, attn, act, chips[0:1], (1,))
    chunks.append([None, trade(sent)])
    attn, sent = lax.optimization_barrier((attn, sent))
    sent = send(chips[1:3])
    onward, back, attn, sent, chunks[0][1] = lax.optimization_barrier((onward, back, attn, sent, chunks[0][1]))
    middle = block.shape[0] // 2
    last = hop(onward[:middle], 1), hop(back[middle:], -1)
    chips += [both_cores(onward), both_cores(back)]
    sent = send(chips[3:5])
    attn, sent, chunks[1] = lax.optimization_barrier((attn, sent, chunks[1]))
    sent = send(chips[5:7])
    attn, sent = lax.optimization_barrier((attn, sent))
    (chunks[0][0],) = project(core, attn, act, chips[0:1], (0,))
    attn, chunks[0] = lax.optimization_barrier((attn, chunks[0]))
    onward, back, attn, sent, chunks[2] = lax.optimization_barrier((*last, attn, sent, chunks[2]))
    chips.append(both_cores(onward) + both_cores(back, middle))
    (sent,) = project(core, attn, act, chips[7:8], (1,))
    far = trade(sent)
    attn, sent = lax.optimization_barrier((attn, sent))
    chunks.append([project(core, attn, act, chips[7:8], (0,))[0], far])

    hidden, following = finish(
        tile[None],
        step_size,
        chunks,
        stream[0],
        bias_out[None, :],
        gate_mod,
        final_scale,
        final_shift,
        w_final.T,
        b_final[:, None],
        jnp.transpose(latent[0], (0, 2, 1)),
    )
    return hidden[None], jnp.transpose(following, (0, 2, 1))[None]


def solution(mesh):
    placed = (
        P("tile", None, "head", None, None),
        P("tile", None, "head", None),
        P("tile", None, "head", None),
        P("tile"),
        P(),
        P(),
        P("head", "tile"),
        P("head", "tile"),
        P(),
        P("tile", None),
        P("tile", None),
        P("tile", None),
        P(),
        P(),
        P("tile", None, "head", None),
        P("tile"),
    )
    return jax.shard_map(
        functools.partial(paired, mesh.shape["head"]) if fits(mesh.shape) else general,
        mesh=mesh,
        in_specs=placed,
        out_specs=(P("tile", None, "head", None), P("tile", None, "head", None)),
        check_vma=False,
    )
```
